32 devices in a mesh: dp: 8 (over y, x, core), vocab: 4 (over z).
Axes of the slice: x: 2, y: 2, z: 4, core: 2. Of those that a mesh axis runs over, the one named last changes fastest.
Arguments:
- token_ids: int32 [32, 512], P('dp'), may hold values from 0 to 65535
- seq_lengths: int32 [8, 4], P('dp'), may hold values from 256 to 512, as said below
- pair_order: int32 [8, 4], P('dp'), may hold values from 0 to 3, each once within a row
- table_master: float32 [65536, 1024], P(('dp', 'vocab')), may hold values from -0.3125 to 0.3125
- table_first: float32 [65536, 1024], P(('dp', 'vocab')), may hold values from -3.8146973e-06 to 3.8146973e-06
- table_second: float32 [65536, 1024], P(('dp', 'vocab')), may hold values from 1.9609928e-12 to 7.838011e-12
- square_master: float32 [7, 1024, 1024], P(None, ('dp', 'vocab'))
- square_moment: float32 [7, 1024, 1024], P(None, ('dp', 'vocab')), may hold values from -3.33786e-06 to 3.33786e-06
- wide_master: float32 [3, 4608, 1024], P(None, ('dp', 'vocab'))
- wide_moment: float32 [3, 4608, 1024], P(None, ('dp', 'vocab')), may hold values from -3.33786e-06 to 3.33786e-06
- vector_master: float32 [7, 1024], P(None, ('dp', 'vocab'))
- vector_first: float32 [7, 1024], P(None, ('dp', 'vocab')), may hold values from -1.9073486e-05 to 1.9073486e-05
- vector_second: float32 [7, 1024], P(None, ('dp', 'vocab')), may hold values from 1.8359375e-11 to 7.33817e-11
- norm_gains: float32 [2, 64], replicated, may hold values from 0.5 to 1.5
- norm_first: float32 [2, 64], replicated, may hold values from -1.9073486e-05 to 1.9073486e-05
- norm_second: float32 [2, 64], replicated, may hold values from 2.05625e-11 to 8.21875e-11
- adam_count: int32 [], replicated, may hold values from 1 to 20
Outputs:
- pair_loss: float32 [], replicated
- grad_norm: float32 [], replicated
- square_new: float32 [7, 1024, 1024], P(None, ('dp', 'vocab'))
- square_moment_new: float32 [7, 1024, 1024], P(None, ('dp', 'vocab'))
- square_copy: bfloat16 [7, 1024, 1024], P(None, ('dp', 'vocab'))
- wide_new: float32 [3, 4608, 1024], P(None, ('dp', 'vocab'))
- wide_moment_new: float32 [3, 4608, 1024], P(None, ('dp', 'vocab'))
- wide_copy: bfloat16 [3, 4608, 1024], P(None, ('dp', 'vocab'))
- table_step: float32 [65536, 1024], P(('dp', 'vocab'))
- table_first_new: float32 [65536, 1024], P(('dp', 'vocab'))
- table_second_new: float32 [65536, 1024], P(('dp', 'vocab'))
- vector_step: float32 [7, 1024], P(None, ('dp', 'vocab'))
- vector_first_new: float32 [7, 1024], P(None, ('dp', 'vocab'))
- vector_second_new: float32 [7, 1024], P(None, ('dp', 'vocab'))
- norm_step: float32 [2, 64], replicated
- norm_first_new: float32 [2, 64], replicated
- norm_second_new: float32 [2, 64], replicated
- final_gain_grad: float32 [1024], P(('dp', 'vocab'))
The draws below stay inside these ranges and needn't reach their ends.
Inputs may be any that keep to these rules, and one draw needn't show every extreme that they name: `seq_lengths`: in every draw some sequence has length exactly 512. `pair_order`: each row is a permutation of 0 to 3.
All inputs are finite; a program needn't handle non-finite values.
Results may differ from the reference program's by a relative error of at most 0.03.
Values may be sent and summed in bfloat16 or wider, within the bound.
No kernel may reach another device: no remote copies, remote signals or barrier semaphores. Data moves between devices by JAX's collectives and lax.ppermute only.
A program may use at most 448 MiB of HBM per device.

```python
import math
import jax
import jax.numpy as jnp
import numpy as np
from jax import lax

D = 1024
HEADS = 16
KV = 8
HD = 64
FF = 4608
V = 65536
SEQ = 512
RESP = 96
NS_ITERS = 3
SEQS = 32
N_DP = 8
N_VOCAB = 4


def draw_seq_lengths(key, part):
    first_key = jax.random.fold_in(key, 11)
    second_key = jax.random.fold_in(key, 12)
    lengths = jax.random.randint(first_key, (N_DP * N_VOCAB,), SEQ // 2, SEQ + 1, dtype=jnp.int32)
    place = jax.random.randint(second_key, (), 0, N_DP * N_VOCAB, dtype=jnp.int32)
    lengths = lengths.at[place].set(SEQ)
    return lengths.reshape(N_DP, N_VOCAB)


def draw_square_master(key, part):
    scales = jnp.array([1.0, 1.0, 1.0, 1.0, 1.0, 1.0, 4.0], jnp.float32) * D ** (-0.5)
    values = jnp.clip(jax.random.normal(jax.random.fold_in(key, 21), (7, D, D), jnp.float32), -6.0, 6.0)
    return values * scales[:, None, None]


def draw_wide_master(key, part):
    scales = jnp.array([D ** (-0.5), D ** (-0.5), FF ** (-0.5)], jnp.float32)
    values = jnp.clip(jax.random.normal(jax.random.fold_in(key, 31), (3, FF, D), jnp.float32), -6.0, 6.0)
    return values * scales[:, None, None]


def draw_vector_master(key, part):
    gain_rows = 1.0 + 0.1 * jax.random.uniform(jax.random.fold_in(key, 41), (4, D), jnp.float32, -1.0, 1.0)
    lead_tap = jax.random.uniform(jax.random.fold_in(key, 42), (1, D), jnp.float32, 0.6, 1.2)
    later_taps = jax.random.uniform(jax.random.fold_in(key, 43), (2, D), jnp.float32, -0.8, 0.8)
    return jnp.concatenate([gain_rows, lead_tap, later_taps], axis=0)


def with_ends(drawn, own_key, low, top_value):
    index_at = [jax.random.randint(jax.random.fold_in(own_key, axis), (), 0, length) for axis, length in enumerate(drawn.shape)]
    main_axis = drawn.shape.index(max(drawn.shape))
    neighbour = index_at[:main_axis] + [(index_at[main_axis] + 1) % drawn.shape[main_axis]] + index_at[main_axis + 1:]
    return drawn.at[tuple(index_at)].set(low).at[tuple(neighbour)].set(top_value)


def level_of(own_key, dims, split, smallest, high):
    factor_of = 1.0
    for dim, parts in split:
        steps = jax.random.uniform(jax.random.fold_in(jax.random.fold_in(own_key, 6), dim), (parts,), jnp.float32, smallest / len(split), high / len(split))
        factor_of = factor_of * jnp.repeat(jnp.exp(steps), dims[dim] // parts).reshape((-1,) + (1,) * (len(dims) - 1 - dim))
    return factor_of


def cumulative_ranks(count, skew):
    loads = [(1 << 20) // math.isqrt(rank ** skew) + 1 for rank in range(1, count + 1)]
    scale = 1 + sum(loads) // (1 << 30)
    return np.cumsum(np.array([max(1, weight // scale) for weight in loads]))


def ranked_ids(key, extent, count, lean):
    listing = cumulative_ranks(count, lean)
    lot = jax.random.randint(jax.random.fold_in(key, 1), extent, 0, int(listing[count - 1]))
    standing = jnp.searchsorted(jnp.asarray(listing, jnp.int32), lot, side="right")
    return jax.random.permutation(jax.random.fold_in(key, 2), count)[standing].astype(jnp.int32)


def noise(stream_key, shape, scale, most, pieces=(), kind=jnp.bfloat16):
    drawn = jax.random.normal(stream_key, shape, jnp.float32) * scale
    if len(pieces) > 0:
        drawn = level_of(stream_key, shape, pieces, -0.22, 0.18) * drawn
    return jnp.clip(drawn, min=-most, max=most).astype(kind)


def setup_inputs(seed: int = 0) -> dict:
    splits = jax.random.split(jax.random.key(seed), 18)
    return {
        "token_ids": with_ends(ranked_ids(splits[0], (SEQS, SEQ), V, 2), jax.random.fold_in(splits[0], 3), 0, V - 1).astype(jnp.int32),
        "seq_lengths": draw_seq_lengths(jax.random.fold_in(splits[17], 71), 0),
        "pair_order": jax.vmap(lambda own: jax.random.permutation(own, N_VOCAB))(jax.random.split(splits[2], N_DP)).reshape((N_DP, N_VOCAB)).astype(jnp.int32),
        "table_master": noise(splits[3], (V, D), 0.05, 0.3125, ((0, 32),), jnp.float32),
        "table_first": noise(splits[4], (V, D), (0.00556 / (V * D) ** 0.5), 3.814697265625e-06, ((0, 32),), jnp.float32),
        "table_second": jnp.clip(jnp.exp(math.log(7.838010622485125e-12) - 1.3855342 * jax.random.uniform(splits[5], (V, D), jnp.float32) ** level_of(splits[5], (V, D), ((0, 32),), -0.2, 0.2)), 1.9609927830871454e-12, 7.838010622485125e-12),
        "square_master": draw_square_master(jax.random.fold_in(splits[17], 71), 0),
        "square_moment": noise(splits[7], (7, D, D), (0.00263 / (7 * D * D + 3 * FF * D) ** 0.5), 3.337860107421875e-06, ((1, 32),), jnp.float32),
        "wide_master": draw_wide_master(jax.random.fold_in(splits[17], 71), 0),
        "wide_moment": noise(splits[9], (3, FF, D), (0.00263 / (7 * D * D + 3 * FF * D) ** 0.5), 3.337860107421875e-06, ((1, 32),), jnp.float32),
        "vector_master": draw_vector_master(jax.random.fold_in(splits[17], 71), 0),
        "vector_first": noise(splits[11], (7, D), (0.000278 / (7 * D) ** 0.5), 1.9073486328125e-05, ((1, 32),), jnp.float32),
        "vector_second": jnp.clip(jnp.exp(math.log(7.338169655257687e-11) - 1.3855342 * jax.random.uniform(splits[12], (7, D), jnp.float32) ** level_of(splits[12], (7, D), ((1, 32),), -0.2, 0.2)), 1.8359374784338023e-11, 7.338169655257687e-11),
        "norm_gains": jnp.clip(1.0 + 0.1 * jax.random.normal(splits[13], (2, HD), jnp.float32), 0.5, 1.5),
        "norm_first": noise(splits[14], (2, HD), (0.000037 / (2 * HD) ** 0.5), 1.9073486328125e-05, (), jnp.float32),
        "norm_second": jnp.clip(jnp.exp(jax.random.uniform(splits[15], (2, HD), jnp.float32, math.log(2.0562499619680707e-11), math.log(8.218749986133034e-11))), 2.0562499619680707e-11, 8.218749986133034e-11),
        "adam_count": jax.random.randint(splits[16], (), 1, 21).astype(jnp.int32),
    }


norm_epsilon = 1e-05
rope_base = 1000000.0
pref_beta = 2.0
clip_limit = 0.05
muon_decay = 0.95
muon_rate = 0.5
first_decay = 0.9
second_decay = 0.95
adam_rate = 0.02
adam_epsilon = 1e-08
weight_decay = 0.1
leading_coefficient = 3.4445
coef_second = -4.775
coef_third = 2.0315
ortho_epsilon = 1e-07
masked_score = -1e+30
top_precision = lax.Precision.HIGHEST

@jax.custom_vjp
def low(v):
    return lax.optimization_barrier(v.astype(jnp.bfloat16)).astype(jnp.float32)

@jax.custom_vjp
def low_back(v):
    return v

def low_keep(v):
    return (low(v), None)

def low_pass(kept, grad):
    return (grad,)

def back_keep(v):
    return (v, None)

def back_low(kept, grad):
    return (low(grad),)
low.defvjp(low_keep, low_pass)
low_back.defvjp(back_keep, back_low)

def rms_scale(inputs, gain):
    mean_square = lax.optimization_barrier(jnp.mean(inputs * inputs, axis=-1, keepdims=True))
    return inputs * lax.rsqrt(mean_square + norm_epsilon) * gain

def rope_tables(length, half):
    position = jnp.arange(length, dtype=jnp.float32)
    inverse = rope_base ** (-jnp.arange(half, dtype=jnp.float32) / half)
    angle = position[:, None] * inverse[None, :]
    return (jnp.cos(angle)[:, None, :], jnp.sin(angle)[:, None, :])

def rotate(inputs, cosine, sine):
    half = inputs.shape[-1] // 2
    first = inputs[..., :half]
    second = inputs[..., half:]
    return jnp.concatenate([first * cosine - second * sine, second * cosine + first * sine], axis=-1)

def project(inputs, weight):
    return jnp.einsum('bsi,oi->bso', inputs, weight, precision=top_precision)

def delayed(values, offset):
    return jnp.pad(values, ((0, 0), (offset, 0), (0, 0)))[:, :values.shape[1]]

def group_logps(weight_params, ids_group, lengths_group):
    table_reduced, square_low, wide_low, vector_low, gains_low = weight_params
    batch = ids_group.shape[0]
    cosine, sine = rope_tables(SEQ, HD // 2)
    hidden0 = low_back(table_reduced[ids_group])
    act1 = low(rms_scale(hidden0, vector_low[0]))
    inner = low_back(project(act1, square_low[0:3].reshape(3 * D, D)))
    entry = inner[..., :D]
    leave = inner[..., D:2 * D]
    conv_in = inner[..., 2 * D:]
    product = entry * conv_in
    convolved = vector_low[4] * product + vector_low[5] * delayed(product, 1) + vector_low[6] * delayed(product, 2)
    mixer = low(leave * convolved)
    hidden1 = hidden0 + low_back(project(mixer, square_low[3]))
    act2 = low(rms_scale(hidden1, vector_low[1]))
    query_raw = low_back(project(act2, square_low[4])).reshape(batch, SEQ, HEADS, HD)
    pair_raw = low_back(project(act2, square_low[5]))
    key_raw = pair_raw[..., :KV * HD].reshape(batch, SEQ, KV, HD)
    values = low(pair_raw[..., KV * HD:].reshape(batch, SEQ, KV, HD))
    query = low(rotate(rms_scale(query_raw, gains_low[0]), cosine, sine)).reshape(batch, SEQ, KV, HEADS // KV, HD)
    keys = low(rotate(rms_scale(key_raw, gains_low[1]), cosine, sine))
    scores = low_back(jnp.einsum('bsgrd,btgd->bgrst', query, keys, precision=top_precision) * HD ** (-0.5))
    causal = jnp.arange(SEQ)[:, None] >= jnp.arange(SEQ)[None, :]
    scores = jnp.where(causal, scores, masked_score)
    peak = lax.optimization_barrier(jnp.max(scores, axis=-1, keepdims=True))
    expo = jnp.exp(scores - peak)
    probs = expo / lax.optimization_barrier(jnp.sum(expo, axis=-1, keepdims=True))
    attended = jnp.einsum('bgrst,btgd->bsgrd', low(probs), values, precision=top_precision).reshape(batch, SEQ, D)
    attended = low(low_back(attended))
    hidden2 = hidden1 + low_back(project(attended, square_low[6]))
    act3 = low(rms_scale(hidden2, vector_low[2]))
    gate_up = low_back(project(act3, wide_low[0:2].reshape(2 * FF, D)))
    inner_ffn = low(jax.nn.silu(gate_up[..., :FF]) * gate_up[..., FF:])
    hidden3 = hidden2 + low_back(jnp.einsum('bsf,fd->bsd', inner_ffn, wide_low[2], precision=top_precision))
    final = low(rms_scale(hidden3, vector_low[3]))
    starts = (lengths_group - 1 - RESP).astype(jnp.int32)
    response_tokens = jax.vmap(lambda rows, first: lax.dynamic_slice_in_dim(rows, first, RESP, 0))(final, starts)
    targets = jax.vmap(lambda row, first: lax.dynamic_slice_in_dim(row, (first + 1).astype(jnp.int32), RESP, 0))(ids_group, starts)
    logit_scores = low_back(jnp.einsum('goz,qz->goq', response_tokens, table_reduced, precision=top_precision))
    top = lax.optimization_barrier(jnp.max(logit_scores, axis=-1, keepdims=True))
    log_total = top[..., 0] + jnp.log(lax.optimization_barrier(jnp.sum(jnp.exp(logit_scores - top), axis=-1)))
    picked = jnp.take_along_axis(logit_scores, targets[..., None], axis=-1)[..., 0]
    return lax.optimization_barrier(jnp.sum(picked - log_total, axis=-1))

def pair_objective(logps, pair_order):
    chosen = jnp.take_along_axis(logps, pair_order[:, 0::2], axis=1)
    rejected = jnp.take_along_axis(logps, pair_order[:, 1::2], axis=1)
    margin = pref_beta * (chosen - rejected) / RESP
    return jnp.sum(jax.nn.softplus(-margin))

def total_loss(table, square, wide, vector, gains, token_ids, seq_lengths, pair_order):
    weight_params = (low(table), low(square), low(wide), low(vector), low(gains))
    grouped_ids = token_ids.reshape(N_DP, N_VOCAB, SEQ)
    per_group = jax.checkpoint(group_logps)

    def visit(carry, inputs):
        return (carry, per_group(weight_params, inputs[0], inputs[1]))
    _, logps = lax.scan(visit, jnp.zeros((), jnp.float32), (grouped_ids, seq_lengths))
    return pair_objective(logps, pair_order)

def orthogonalize(moment):
    value = moment / (jnp.sqrt(jnp.sum(moment * moment)) + ortho_epsilon)
    for turn in range(NS_ITERS):
        narrow = low(value)
        gram = low(jnp.dot(narrow.T, narrow, precision=top_precision))
        first = jnp.dot(narrow, gram, precision=top_precision)
        second = jnp.dot(low(first), gram, precision=top_precision)
        value = leading_coefficient * value + coef_second * first + coef_third * second
    return value

def adam_step(master, first, second, grad, factor, count):
    scaled = factor * grad
    first_new = first_decay * first + (1.0 - first_decay) * scaled
    second_new = second_decay * second + (1.0 - second_decay) * scaled * scaled
    steps = count.astype(jnp.float32)
    first_hat = first_new / (1.0 - first_decay ** steps)
    second_hat = second_new / (1.0 - second_decay ** steps)
    change = -adam_rate * (first_hat / (jnp.sqrt(second_hat) + adam_epsilon) + weight_decay * master)
    return (change, first_new, second_new)

def reference(token_ids, seq_lengths, pair_order, table_master, table_first, table_second, square_master, square_moment, wide_master, wide_moment, vector_master, vector_first, vector_second, norm_gains, norm_first, norm_second, adam_count):

    def objective(table, square, wide, vector, gains):
        return total_loss(table, square, wide, vector, gains, token_ids, seq_lengths, pair_order)
    pair_loss, pullback = jax.vjp(objective, table_master, square_master, wide_master, vector_master, norm_gains)
    grads = pullback(jnp.ones((), jnp.float32))
    squares = sum((jnp.sum(grad * grad) for grad in grads))
    grad_norm = jnp.sqrt(squares)
    factor = jnp.minimum(1.0, clip_limit / grad_norm)
    table_grad, square_grad, wide_grad, vector_grad, gains_grad = grads
    square_moment_new = muon_decay * square_moment + (1.0 - muon_decay) * (factor * square_grad)
    wide_moment_new = muon_decay * wide_moment + (1.0 - muon_decay) * (factor * wide_grad)
    square_ortho = lax.map(orthogonalize, square_moment_new)
    wide_ortho = lax.map(orthogonalize, wide_moment_new)
    wide_scale = jnp.array([math.sqrt(FF / D), math.sqrt(FF / D), 1.0], jnp.float32)
    square_new = square_master - muon_rate * square_ortho
    wide_new = wide_master - muon_rate * wide_scale[:, None, None] * wide_ortho
    table_step, table_first_new, table_second_new = adam_step(table_master, table_first, table_second, table_grad, factor, adam_count)
    vector_step, vector_first_new, vector_second_new = adam_step(vector_master, vector_first, vector_second, vector_grad, factor, adam_count)
    norm_step, norm_first_new, norm_second_new = adam_step(norm_gains, norm_first, norm_second, gains_grad, factor, adam_count)
    return (pair_loss, grad_norm, square_new, square_moment_new, square_new.astype(jnp.bfloat16), wide_new, wide_moment_new, wide_new.astype(jnp.bfloat16), table_step, table_first_new, table_second_new, vector_step, vector_first_new, vector_second_new, norm_step, norm_first_new, norm_second_new, vector_grad[3])
```

```python
import math

import jax
import jax.numpy as jnp
from jax import lax
from jax.sharding import Mesh
from jax.sharding import PartitionSpec as P

D = 1024
HEADS = 16
KV = 8
HD = 64
FF = 4608
SEQ = 512
RESP = 96
NS_ITERS = 3


norm_epsilon = 1e-05
rope_base = 1000000.0
pref_beta = 2.0
clip_limit = 0.05
muon_decay = 0.95
muon_rate = 0.5
first_decay = 0.9
second_decay = 0.95
adam_rate = 0.02
adam_epsilon = 1e-08
weight_decay = 0.1
leading_coefficient = 3.4445
coef_second = -4.775
coef_third = 2.0315
ortho_epsilon = 1e-07
masked_score = -1e30


def rms_scale(inputs, gain):
    mean_square = jnp.mean(inputs * inputs, axis=-1, keepdims=True)
    return inputs * lax.rsqrt(mean_square + norm_epsilon) * gain


def rope_tables(length, half):
    position = jnp.arange(length, dtype=jnp.float32)
    inverse = rope_base ** (-jnp.arange(half, dtype=jnp.float32) / half)
    angle = position[:, None] * inverse[None, :]
    return (jnp.cos(angle)[:, None, :], jnp.sin(angle)[:, None, :])


def rotate(inputs, cosine, sine):
    half = inputs.shape[-1] // 2
    first = inputs[..., :half]
    second = inputs[..., half:]
    return jnp.concatenate(
        [first * cosine - second * sine, second * cosine + first * sine], axis=-1
    )


def dense(inputs, weight):
    return lax.dot_general(
        inputs, weight, (((1,), (1,)), ((), ())), preferred_element_type=jnp.float32
    )


def outer(grads, inputs):
    return lax.dot_general(
        grads, inputs, (((0,), (0,)), ((), ())), preferred_element_type=jnp.float32
    )


def back_dense(grads, weight):
    return jnp.dot(grads, weight, preferred_element_type=jnp.float32)


def delayed(values, offset):
    return jnp.pad(values, ((offset, 0), (0, 0)))[: values.shape[0]]


def advanced(values, offset):
    return jnp.pad(values, ((0, offset), (0, 0)))[offset:]


def norm_back(inputs, gain, grad_out):
    _, pullback = jax.vjp(rms_scale, inputs, gain)
    return pullback(grad_out)


def low_copy(values):
    return lax.optimization_barrier(values.astype(jnp.bfloat16)).astype(jnp.float32)


def adam_step(master, first, second, grad, factor, count):
    scaled = factor * grad
    first_new = first_decay * first + (1.0 - first_decay) * scaled
    second_new = second_decay * second + (1.0 - second_decay) * scaled * scaled
    steps = count.astype(jnp.float32)
    first_hat = first_new / (1.0 - first_decay**steps)
    second_hat = second_new / (1.0 - second_decay**steps)
    change = -adam_rate * (
        first_hat / (jnp.sqrt(second_hat) + adam_epsilon) + weight_decay * master
    )
    return (change, first_new, second_new)

DP = ("chip", "core")
ALL = ("chip", "core", "vocab")
SLOTS = 32


def scatter_sum(values, dimension):
    part = lax.psum_scatter(values, DP, scatter_dimension=dimension, tiled=True)
    return lax.psum_scatter(part, "vocab", scatter_dimension=dimension, tiled=True)


def onehot_rows(index, count):
    return (index[:, None] == jnp.arange(count)[None, :]).astype(jnp.bfloat16)


def token_slots(ids, block_rows):
    owner = ids // block_rows
    place = jnp.arange(ids.shape[0])
    earlier = place[:, None] > place[None, :]
    equal = ids[:, None] == ids[None, :]
    first = jnp.logical_not(jnp.any(equal & earlier, axis=1))
    ahead = (owner[:, None] == owner[None, :]) & earlier & first[None, :]
    rank = jnp.sum(ahead.astype(jnp.int32), axis=1)
    slot = jnp.sum(jnp.where(equal & first[None, :], rank[None, :], 0), axis=1)
    return owner, first, slot


def round_keys(owner, slot, turn):
    within = slot - turn * SLOTS
    return jnp.where((within >= 0) & (within < SLOTS), owner * SLOTS + within, -1)


def round_asks(keys, first, local, count):
    hits = (keys[None, :] == jnp.arange(count)[:, None]) & first[None, :]
    return jnp.sum(jnp.where(hits, local[None, :] + 1, 0), axis=1) - 1


def square_product(left, right):
    return jnp.dot(
        left.astype(jnp.bfloat16), right.astype(jnp.bfloat16), preferred_element_type=jnp.float32
    )


def ortho_rest(gram):
    lead = leading_coefficient
    power, rest = 1.0, None
    for turn in range(NS_ITERS):
        change = coef_second * gram + coef_third * square_product(gram, gram)
        if turn + 1 < NS_ITERS:
            mixed = square_product(change, gram)
            gram = lead * lead * gram + 2.0 * lead * mixed + square_product(mixed, change)
        if rest is None:
            rest = change
        else:
            rest = lead * rest + power * change + square_product(rest, change)
        power = power * lead
    return power, rest


def body(
    token_ids,
    seq_lengths,
    pair_order,
    table_master,
    table_first,
    table_second,
    square_master,
    square_moment,
    wide_master,
    wide_moment,
    vector_master,
    vector_first,
    vector_second,
    norm_gains,
    norm_first,
    norm_second,
    adam_count,
):
    members = lax.axis_size("vocab")
    member = lax.axis_index("vocab")
    block_rows = table_master.shape[0]
    lengths = seq_lengths[0]
    order = pair_order[0]
    groups_per = HEADS // KV
    scale = HD ** (-0.5)

    devices = lax.axis_size(ALL)
    device = lax.axis_index(ALL)
    groups = devices // members

    own_ids = lax.dynamic_index_in_dim(token_ids, member, 0, keepdims=False)
    own_length = lengths[member]
    start = own_length - 1 - RESP
    owner, first_seen, slot = token_slots(own_ids, block_rows)
    local_ids = own_ids % block_rows
    keys = round_keys(owner, slot, 0)
    asks = round_asks(keys, first_seen, local_ids, devices * SLOTS)
    own_targets = lax.dynamic_slice_in_dim(own_ids, start + 1, RESP, 0)
    vector_low = vector_master.astype(jnp.bfloat16).astype(jnp.float32)
    whole_numbers = jnp.concatenate([asks, own_targets, order, jnp.max(slot)[None] + 1])
    vectors_count = vector_low.size
    notes = jnp.concatenate([vector_low.reshape(-1), whole_numbers.astype(jnp.float32)])
    notes = lax.all_gather(notes, ALL, axis=0)
    square_b = lax.all_gather(square_master.astype(jnp.bfloat16), ALL, axis=1, tiled=True)
    wide_b = lax.all_gather(wide_master.astype(jnp.bfloat16), ALL, axis=1, tiled=True)
    gains = (
        notes[:, :vectors_count]
        .reshape(devices, vector_master.shape[0], vector_master.shape[1])
        .transpose(1, 0, 2)
        .reshape(vector_master.shape[0], D)
    )
    numbers = notes[:, vectors_count:].astype(jnp.int32)
    asked = lax.dynamic_slice_in_dim(numbers, device * SLOTS, SLOTS, 1).reshape(-1)
    numbers = numbers[:, devices * SLOTS :]
    targets = numbers[:, :RESP].reshape(-1)
    orders = numbers[:, RESP : RESP + members].reshape(groups, members, members)[:, 0]
    turns = (jnp.max(numbers[:, RESP + members]) + SLOTS - 1) // SLOTS
    table_b = table_master.astype(jnp.bfloat16)
    head_gains = low_copy(norm_gains)
    cosine, sine = rope_tables(SEQ, HD // 2)

    def exchanged(rows):
        return lax.all_to_all(rows, ALL, 0, 0, tiled=True)

    def fetched(wanted, row_keys):
        rows = jnp.dot(
            onehot_rows(wanted, block_rows), table_b, preferred_element_type=jnp.float32
        ).astype(jnp.bfloat16)
        return jnp.dot(
            onehot_rows(row_keys, devices * SLOTS),
            exchanged(rows),
            preferred_element_type=jnp.float32,
        )

    def later_round(turn):
        later_keys = round_keys(owner, slot, turn)
        later_asks = round_asks(later_keys, first_seen, local_ids, devices * SLOTS)
        return later_keys, exchanged(later_asks)

    def fetch_more(turn, rows):
        later_keys, later_asked = later_round(turn)
        return rows + fetched(later_asked, later_keys)

    hidden0 = lax.fori_loop(1, turns, fetch_more, fetched(asked, keys))
    act1 = rms_scale(hidden0, gains[0]).astype(jnp.bfloat16)
    inner = dense(act1, square_b[0:3].reshape(3 * D, D))
    entry = inner[:, :D]
    leave = inner[:, D : 2 * D]
    conv_in = inner[:, 2 * D :]
    product = entry * conv_in
    convolved = gains[4] * product + gains[5] * delayed(product, 1) + gains[6] * delayed(product, 2)
    mixer = (leave * convolved).astype(jnp.bfloat16)
    hidden1 = hidden0 + dense(mixer, square_b[3])
    act2 = rms_scale(hidden1, gains[1]).astype(jnp.bfloat16)
    query_raw = dense(act2, square_b[4]).reshape(SEQ, HEADS, HD)
    pair_raw = dense(act2, square_b[5])
    key_raw = pair_raw[:, : KV * HD].reshape(SEQ, KV, HD)
    value_b = pair_raw[:, KV * HD :].astype(jnp.bfloat16).reshape(SEQ, KV, HD)

    def query_prep(raw, gain):
        return rotate(rms_scale(raw, gain), cosine, sine)

    query_b = (
        query_prep(query_raw, head_gains[0]).astype(jnp.bfloat16).reshape(SEQ, KV, groups_per, HD)
    )
    key_b = query_prep(key_raw, head_gains[1]).astype(jnp.bfloat16)
    causal = jnp.arange(SEQ)[:, None] >= jnp.arange(SEQ)[None, :]
    scores = (
        jnp.einsum("sgrd,tgd->grst", query_b, key_b, preferred_element_type=jnp.float32) * scale
    )
    scores = jnp.where(causal, scores, masked_score)
    peak = jnp.max(scores, axis=-1, keepdims=True)
    expo = jnp.exp(scores - peak)
    total = jnp.sum(expo, axis=-1, keepdims=True)
    log_norm = peak + jnp.log(total)
    probs_b = (expo / total).astype(jnp.bfloat16)
    attended = jnp.einsum(
        "grst,tgd->sgrd", probs_b, value_b, preferred_element_type=jnp.float32
    ).reshape(SEQ, D)
    attended_b = attended.astype(jnp.bfloat16)
    hidden2 = hidden1 + dense(attended_b, square_b[6])
    act3 = rms_scale(hidden2, gains[2]).astype(jnp.bfloat16)
    gate_up = dense(act3, wide_b[0:2].reshape(2 * FF, D))
    gate_part = gate_up[:, :FF]
    up_part = gate_up[:, FF:]
    inner_b = (jax.nn.silu(gate_part) * up_part).astype(jnp.bfloat16)
    hidden3 = hidden2 + jnp.dot(inner_b, wide_b[2], preferred_element_type=jnp.float32)
    final_b = rms_scale(hidden3, gains[3]).astype(jnp.bfloat16)
    answer_b = lax.dynamic_slice_in_dim(final_b, start, RESP, 0)
    response_tokens = lax.all_gather(answer_b, ALL, axis=0, tiled=True)
    logit_scores = dense(response_tokens, table_b)
    local_target = jnp.where(targets // block_rows == device, targets % block_rows, -1)
    onehot = jnp.arange(block_rows)[None, :] == local_target[:, None]
    top = jnp.max(logit_scores, axis=-1)
    exp_total = jnp.sum(jnp.exp(logit_scores - top[:, None]), axis=-1)
    picked = jnp.sum(jnp.where(onehot, logit_scores, 0.0), axis=-1)
    stats = lax.all_gather(jnp.stack([top, exp_total, picked]), ALL, axis=0)
    top = jnp.max(stats[:, 0], axis=0)
    exp_total = jnp.sum(stats[:, 1] * jnp.exp(stats[:, 0] - top[None, :]), axis=0)
    picked = jnp.sum(stats[:, 2], axis=0)
    log_total = top + jnp.log(exp_total)
    seq_logp = jnp.sum((picked - log_total).reshape(groups, members, RESP), axis=-1)
    slots = jnp.arange(members)
    chosen_mask = (orders[:, 0::2, None] == slots[None, None, :]).astype(jnp.float32)
    rejected_mask = (orders[:, 1::2, None] == slots[None, None, :]).astype(jnp.float32)
    margin = (
        pref_beta * jnp.sum((chosen_mask - rejected_mask) * seq_logp[:, None, :], axis=2) / RESP
    )
    pair_loss = jnp.sum(jax.nn.softplus(-margin))
    pull = jax.nn.sigmoid(-margin) * pref_beta / RESP
    grad_logp = jnp.sum((rejected_mask - chosen_mask) * pull[:, :, None], axis=1)
    row_weight = jnp.repeat(grad_logp.reshape(-1), RESP)
    softmax_rows = jnp.exp(logit_scores - log_total[:, None])
    grad_logits = (row_weight[:, None] * (onehot.astype(jnp.float32) - softmax_rows)).astype(
        jnp.bfloat16
    )
    grad_answers = jnp.dot(grad_logits, table_b, preferred_element_type=jnp.float32)
    grad_table = outer(grad_logits, response_tokens)
    grad_answer_own = scatter_sum(grad_answers.astype(jnp.bfloat16), 0).astype(jnp.float32)
    grad_final = lax.dynamic_update_slice_in_dim(
        jnp.zeros((SEQ, D), jnp.float32), grad_answer_own, start, 0
    )
    grad_hidden3, grad_gain3 = norm_back(hidden3, gains[3], grad_final)
    grad_ffn_out = grad_hidden3.astype(jnp.bfloat16)
    grad_inner = dense(grad_ffn_out, wide_b[2])
    grad_down_w = outer(inner_b, grad_ffn_out)
    _, silu_pull = jax.vjp(lambda gate_in, up_in: jax.nn.silu(gate_in) * up_in, gate_part, up_part)
    grad_gate, grad_up = silu_pull(grad_inner)
    grad_gate_up = jnp.concatenate([grad_gate, grad_up], axis=1).astype(jnp.bfloat16)
    grad_act3 = back_dense(grad_gate_up, wide_b[0:2].reshape(2 * FF, D))
    grad_gate_up_w = outer(grad_gate_up, act3)
    grad_norm2, grad_gain2 = norm_back(hidden2, gains[2], grad_act3)
    grad_hidden2 = grad_hidden3 + grad_norm2
    grad_attn_out = grad_hidden2.astype(jnp.bfloat16)
    grad_attended = (
        back_dense(grad_attn_out, square_b[6]).astype(jnp.bfloat16).reshape(SEQ, KV, groups_per, HD)
    )
    grad_out_w = outer(grad_attn_out, attended_b)
    scores = (
        jnp.einsum("sgrd,tgd->grst", query_b, key_b, preferred_element_type=jnp.float32) * scale
    )
    probs = jnp.exp(jnp.where(causal, scores, masked_score) - log_norm)
    grad_probs = jnp.einsum(
        "sgrd,tgd->grst", grad_attended, value_b, preferred_element_type=jnp.float32
    )
    grad_values = jnp.einsum(
        "grst,sgrd->tgd", probs_b, grad_attended, preferred_element_type=jnp.float32
    )
    delta = jnp.sum(probs * grad_probs, axis=-1, keepdims=True)
    grad_scores = (probs * (grad_probs - delta)).astype(jnp.bfloat16)
    grad_query = (
        jnp.einsum("grst,tgd->sgrd", grad_scores, key_b, preferred_element_type=jnp.float32) * scale
    ).reshape(SEQ, HEADS, HD)
    grad_keys = (
        jnp.einsum("grst,sgrd->tgd", grad_scores, query_b, preferred_element_type=jnp.float32)
        * scale
    )
    _, query_pull = jax.vjp(query_prep, query_raw, head_gains[0])
    grad_query_raw, grad_query_gain = query_pull(grad_query)
    _, key_pull = jax.vjp(query_prep, key_raw, head_gains[1])
    grad_key_raw, grad_key_gain = key_pull(grad_keys)
    grad_query_b = grad_query_raw.reshape(SEQ, D).astype(jnp.bfloat16)
    grad_pair_b = jnp.concatenate(
        [grad_key_raw.reshape(SEQ, KV * HD), grad_values.reshape(SEQ, KV * HD)], axis=1
    ).astype(jnp.bfloat16)
    grad_act2 = back_dense(grad_query_b, square_b[4]) + back_dense(grad_pair_b, square_b[5])
    grad_query_w = outer(grad_query_b, act2)
    grad_pair_w = outer(grad_pair_b, act2)
    grad_norm1, grad_gain1 = norm_back(hidden1, gains[1], grad_act2)
    grad_hidden1 = grad_hidden2 + grad_norm1
    grad_mix_out = grad_hidden1.astype(jnp.bfloat16)
    grad_mixer = back_dense(grad_mix_out, square_b[3])
    grad_mixer_w = outer(grad_mix_out, mixer)
    grad_leave = grad_mixer * convolved
    grad_conv = grad_mixer * leave
    grad_tap0 = jnp.sum(grad_conv * product, axis=0)
    grad_tap1 = jnp.sum(grad_conv * delayed(product, 1), axis=0)
    grad_tap2 = jnp.sum(grad_conv * delayed(product, 2), axis=0)
    grad_product = (
        gains[4] * grad_conv + gains[5] * advanced(grad_conv, 1) + gains[6] * advanced(grad_conv, 2)
    )
    grad_inner_b = jnp.concatenate(
        [grad_product * conv_in, grad_leave, grad_product * entry], axis=1
    ).astype(jnp.bfloat16)
    grad_act1 = back_dense(grad_inner_b, square_b[0:3].reshape(3 * D, D))
    grad_inner_w = outer(grad_inner_b, act1)
    grad_norm0, grad_gain0 = norm_back(hidden0, gains[0], grad_act1)
    grad_embed_b = (grad_hidden1 + grad_norm0).astype(jnp.bfloat16)

    def returned(wanted, row_keys):
        rows = outer(onehot_rows(row_keys, devices * SLOTS), grad_embed_b)
        rows = exchanged(rows.astype(jnp.bfloat16))
        return outer(onehot_rows(wanted, block_rows), rows)

    def return_more(turn, total):
        later_keys, later_asked = later_round(turn)
        return total + returned(later_asked, later_keys)

    share_table = lax.fori_loop(1, turns, return_more, grad_table + returned(asked, keys))
    grad_square = jnp.concatenate(
        [
            grad_inner_w.astype(jnp.bfloat16).reshape(3, D, D),
            grad_mixer_w.astype(jnp.bfloat16)[None],
            grad_query_w.astype(jnp.bfloat16)[None],
            grad_pair_w.astype(jnp.bfloat16)[None],
            grad_out_w.astype(jnp.bfloat16)[None],
        ],
        axis=0,
    )
    grad_vector = jnp.stack(
        [grad_gain0, grad_gain1, grad_gain2, grad_gain3, grad_tap0, grad_tap1, grad_tap2]
    )
    grad_head_gains = jnp.stack([grad_query_gain, grad_key_gain])
    share_square = scatter_sum(grad_square, 1).astype(jnp.float32)
    share_gate_up = scatter_sum(grad_gate_up_w.astype(jnp.bfloat16).reshape(2, FF, D), 1)
    share_down = scatter_sum(grad_down_w.astype(jnp.bfloat16), 0)
    share_wide = jnp.concatenate([share_gate_up, share_down[None]], axis=0).astype(jnp.float32)
    vector_total, gains_total = lax.psum((grad_vector, grad_head_gains), ALL)
    width = vector_master.shape[1]
    share_vector = lax.dynamic_slice_in_dim(vector_total, device * width, width, 1)
    own_squares = (
        jnp.sum(share_square * share_square)
        + jnp.sum(share_wide * share_wide)
        + jnp.sum(share_table * share_table)
    )
    moment_squares = jnp.concatenate(
        [
            jnp.sum(square_moment * square_moment, axis=(1, 2)),
            jnp.sum(wide_moment * wide_moment, axis=(1, 2)),
        ]
    )
    moment_cross = jnp.concatenate(
        [
            jnp.sum(square_moment * share_square, axis=(1, 2)),
            jnp.sum(wide_moment * share_wide, axis=(1, 2)),
        ]
    )
    grad_squares = jnp.concatenate(
        [
            jnp.sum(share_square * share_square, axis=(1, 2)),
            jnp.sum(share_wide * share_wide, axis=(1, 2)),
        ]
    )
    moment_stats = jnp.stack([moment_squares, moment_cross, grad_squares])
    stats_total, squares_total = lax.psum((moment_stats, own_squares), ALL)
    grad_norm = jnp.sqrt(
        squares_total + jnp.sum(vector_total * vector_total) + jnp.sum(gains_total * gains_total)
    )
    factor = jnp.minimum(1.0, clip_limit / grad_norm)
    square_moment_new = muon_decay * square_moment + (1.0 - muon_decay) * (factor * share_square)
    wide_moment_new = muon_decay * wide_moment + (1.0 - muon_decay) * (factor * share_wide)
    moment_norm = jnp.sqrt(
        muon_decay * muon_decay * stats_total[0]
        + 2.0 * muon_decay * (1.0 - muon_decay) * factor * stats_total[1]
        + (1.0 - muon_decay) * (1.0 - muon_decay) * factor * factor * stats_total[2]
    )
    ortho_square = square_moment_new / (moment_norm[:7][:, None, None] + ortho_epsilon)
    ortho_wide = wide_moment_new / (moment_norm[7:][:, None, None] + ortho_epsilon)
    squares, square_rows = square_master.shape[0], square_master.shape[1]
    wides, wide_rows = wide_master.shape[0], wide_master.shape[1]
    chunk = max(squares * square_rows, wide_rows)
    wide_jobs = jnp.pad(ortho_wide.astype(jnp.bfloat16), ((0, 0), (0, chunk - wide_rows), (0, 0)))
    square_jobs = ortho_square.astype(jnp.bfloat16).reshape(1, squares * square_rows, D)
    square_jobs = jnp.pad(square_jobs, ((0, 0), (0, chunk - squares * square_rows), (0, 0)))
    jobs = jnp.concatenate([wide_jobs, square_jobs], axis=0).reshape(members * chunk, D)
    jobs = lax.all_to_all(jobs, "vocab", 0, 0, tiled=True).reshape(members, chunk, D)
    on_square = member == wides
    group_square = (
        jobs[:, : squares * square_rows]
        .reshape(members, squares, square_rows, D)
        .transpose(1, 0, 2, 3)
        .reshape(squares, members * square_rows, D)
    )
    group_square = jnp.pad(group_square, ((0, groups - squares), (0, 0), (0, 0)))
    whole_square = lax.all_to_all(
        group_square.reshape(groups * members * square_rows, D), DP, 0, 0, tiled=True
    )
    wide_part = jobs[:, :wide_rows].reshape(members * wide_rows, D)
    wide_part = jnp.pad(wide_part, ((0, D - members * wide_rows), (0, 0)))
    job = jnp.where(on_square, whole_square, wide_part)
    gram = outer(job, job)
    gram_sum = lax.psum(gram.astype(jnp.bfloat16), DP).astype(jnp.float32)
    gram = jnp.where(on_square, gram, gram_sum)
    power, rest = ortho_rest(gram)
    product_rows = square_product(job, rest).astype(jnp.bfloat16)
    back_square = lax.all_to_all(product_rows, DP, 0, 0, tiled=True)
    back_square = (
        back_square.reshape(groups, members, square_rows, D)[:squares]
        .transpose(1, 0, 2, 3)
        .reshape(members, squares * square_rows, D)
    )
    back_square = jnp.pad(back_square, ((0, 0), (0, chunk - squares * square_rows), (0, 0)))
    back_wide = product_rows[: members * wide_rows].reshape(members, wide_rows, D)
    back_wide = jnp.pad(back_wide, ((0, 0), (0, chunk - wide_rows), (0, 0)))
    backs = jnp.where(on_square, back_square, back_wide).reshape(members * chunk, D)
    backs = lax.all_to_all(backs, "vocab", 0, 0, tiled=True).reshape(members, chunk, D)
    ortho_wide = power * ortho_wide + backs[:wides, :wide_rows].astype(jnp.float32)
    ortho_square = power * ortho_square + backs[wides, : squares * square_rows].reshape(
        squares, square_rows, D
    ).astype(jnp.float32)
    wide_scale = jnp.array([math.sqrt(FF / D), math.sqrt(FF / D), 1.0], jnp.float32)
    square_new = square_master - muon_rate * ortho_square
    wide_new = wide_master - muon_rate * wide_scale[:, None, None] * ortho_wide
    table_step, table_first_new, table_second_new = adam_step(
        table_master, table_first, table_second, share_table, factor, adam_count
    )
    vector_step, vector_first_new, vector_second_new = adam_step(
        vector_master, vector_first, vector_second, share_vector, factor, adam_count
    )
    norm_step, norm_first_new, norm_second_new = adam_step(
        norm_gains, norm_first, norm_second, gains_total, factor, adam_count
    )
    return (
        pair_loss,
        grad_norm,
        square_new,
        square_moment_new,
        square_new.astype(jnp.bfloat16),
        wide_new,
        wide_moment_new,
        wide_new.astype(jnp.bfloat16),
        table_step,
        table_first_new,
        table_second_new,
        vector_step,
        vector_first_new,
        vector_second_new,
        norm_step,
        norm_first_new,
        norm_second_new,
        share_vector[3],
    )


def solution(mesh):
    groups, members = mesh.shape["dp"], mesh.shape["vocab"]
    cores = 2
    split_mesh = Mesh(mesh.devices.reshape(groups // cores, cores, members), ALL)
    return jax.shard_map(
        body,
        mesh=split_mesh,
        in_specs=(
            P(DP, None),
            P(DP, None),
            P(DP, None),
            P(ALL, None),
            P(ALL, None),
            P(ALL, None),
            P(None, ALL, None),
            P(None, ALL, None),
            P(None, ALL, None),
            P(None, ALL, None),
            P(None, ALL),
            P(None, ALL),
            P(None, ALL),
            P(),
            P(),
            P(),
            P(),
        ),
        out_specs=(
            P(),
            P(),
            P(None, ALL, None),
            P(None, ALL, None),
            P(None, ALL, None),
            P(None, ALL, None),
            P(None, ALL, None),
            P(None, ALL, None),
            P(ALL, None),
            P(ALL, None),
            P(ALL, None),
            P(None, ALL),
            P(None, ALL),
            P(None, ALL),
            P(),
            P(),
            P(),
            P(ALL),
        ),
        check_vma=False,
    )
```

```python
import math

import jax
import jax.numpy as jnp
from jax import lax
from jax.sharding import Mesh
from jax.sharding import PartitionSpec as P

D = 1024
HEADS = 16
KV = 8
HD = 64
FF = 4608
SEQ = 512
RESP = 96
NS_ITERS = 3


norm_epsilon = 1e-05
rope_base = 1000000.0
pref_beta = 2.0
clip_limit = 0.05
muon_decay = 0.95
muon_rate = 0.5
first_decay = 0.9
second_decay = 0.95
adam_rate = 0.02
adam_epsilon = 1e-08
weight_decay = 0.1
leading_coefficient = 3.4445
coef_second = -4.775
coef_third = 2.0315
ortho_epsilon = 1e-07
masked_score = -1e30


def rms_scale(inputs, gain):
    mean_square = jnp.mean(inputs * inputs, axis=-1, keepdims=True)
    return inputs * lax.rsqrt(mean_square + norm_epsilon) * gain


def rope_tables(length, half):
    position = jnp.arange(length, dtype=jnp.float32)
    inverse = rope_base ** (-jnp.arange(half, dtype=jnp.float32) / half)
    angle = position[:, None] * inverse[None, :]
    return (jnp.cos(angle)[:, None, :], jnp.sin(angle)[:, None, :])


def rotate(inputs, cosine, sine):
    half = inputs.shape[-1] // 2
    first = inputs[..., :half]
    second = inputs[..., half:]
    return jnp.concatenate(
        [first * cosine - second * sine, second * cosine + first * sine], axis=-1
    )


def dense(inputs, weight):
    return lax.dot_general(
        inputs, weight, (((1,), (1,)), ((), ())), preferred_element_type=jnp.float32
    )


def outer(grads, inputs):
    return lax.dot_general(
        grads, inputs, (((0,), (0,)), ((), ())), preferred_element_type=jnp.float32
    )


def back_dense(grads, weight):
    return jnp.dot(grads, weight, preferred_element_type=jnp.float32)


def delayed(values, offset):
    return jnp.pad(values, ((offset, 0), (0, 0)))[: values.shape[0]]


def advanced(values, offset):
    return jnp.pad(values, ((0, offset), (0, 0)))[offset:]


def norm_back(inputs, gain, grad_out):
    _, pullback = jax.vjp(rms_scale, inputs, gain)
    return pullback(grad_out)


def low_copy(values):
    return lax.optimization_barrier(values.astype(jnp.bfloat16)).astype(jnp.float32)


def adam_step(master, first, second, grad, factor, count):
    scaled = factor * grad
    first_new = first_decay * first + (1.0 - first_decay) * scaled
    second_new = second_decay * second + (1.0 - second_decay) * scaled * scaled
    steps = count.astype(jnp.float32)
    first_hat = first_new / (1.0 - first_decay**steps)
    second_hat = second_new / (1.0 - second_decay**steps)
    change = -adam_rate * (
        first_hat / (jnp.sqrt(second_hat) + adam_epsilon) + weight_decay * master
    )
    return (change, first_new, second_new)

DP = ("chip", "core")
ALL = ("chip", "core", "vocab")
SLOTS = 32


def exchanged(rows):
    return lax.all_to_all(rows, ALL, 0, 0, tiled=True)


def spread(values):
    count = lax.axis_size(ALL)
    return lax.all_to_all(jnp.broadcast_to(values[None], (count,) + values.shape), ALL, 0, 0)


def turned(values, step):
    count = lax.axis_size("vocab")
    return lax.ppermute(values, "vocab", [(i, (i + step) % count) for i in range(count)])


def member_gather(values):
    return jnp.concatenate(
        [values] + [turned(values, step) for step in range(1, lax.axis_size("vocab"))], axis=0
    )


def member_return(blocks):
    total = blocks[0].astype(jnp.float32)
    for step in range(1, len(blocks)):
        total = total + turned(blocks[step], -step).astype(jnp.float32)
    return total


def member_scatter(blocks, member):
    count = blocks.shape[0]
    return member_return(
        [
            lax.dynamic_index_in_dim(blocks, (member - step) % count, 0, keepdims=False)
            for step in range(count)
        ]
    )


def onehot_rows(index, count):
    return (index[:, None] == jnp.arange(count)[None, :]).astype(jnp.bfloat16)


def token_slots(ids, block_rows):
    owner = ids // block_rows
    place = jnp.arange(ids.shape[0])
    earlier = place[:, None] > place[None, :]
    equal = ids[:, None] == ids[None, :]
    first = jnp.logical_not(jnp.any(equal & earlier, axis=1))
    ahead = (owner[:, None] == owner[None, :]) & earlier & first[None, :]
    rank = jnp.sum(ahead.astype(jnp.int32), axis=1)
    slot = jnp.sum(jnp.where(equal & first[None, :], rank[None, :], 0), axis=1)
    return owner, first, slot


def round_keys(owner, slot, turn):
    within = slot - turn * SLOTS
    return jnp.where((within >= 0) & (within < SLOTS), owner * SLOTS + within, -1)


def round_asks(keys, first, local, count):
    hits = (keys[None, :] == jnp.arange(count)[:, None]) & first[None, :]
    return jnp.sum(jnp.where(hits, local[None, :] + 1, 0), axis=1) - 1


def square_product(left, right):
    return jnp.dot(
        left.astype(jnp.bfloat16), right.astype(jnp.bfloat16), preferred_element_type=jnp.float32
    )


def ortho_rest(gram):
    lead = leading_coefficient
    power, rest = 1.0, None
    for turn in range(NS_ITERS):
        change = coef_second * gram + coef_third * square_product(gram, gram)
        if turn + 1 < NS_ITERS:
            mixed = square_product(change, gram)
            gram = lead * lead * gram + 2.0 * lead * mixed + square_product(mixed, change)
        if rest is None:
            rest = change
        else:
            rest = lead * rest + power * change + square_product(rest, change)
        power = power * lead
    return power, rest


def body(
    token_ids,
    seq_lengths,
    pair_order,
    table_master,
    table_first,
    table_second,
    square_master,
    square_moment,
    wide_master,
    wide_moment,
    vector_master,
    vector_first,
    vector_second,
    norm_gains,
    norm_first,
    norm_second,
    adam_count,
):
    members = lax.axis_size("vocab")
    member = lax.axis_index("vocab")
    block_rows = table_master.shape[0]
    lengths = seq_lengths[0]
    order = pair_order[0]
    groups_per = HEADS // KV
    scale = HD ** (-0.5)

    devices = lax.axis_size(ALL)
    device = lax.axis_index(ALL)
    groups = devices // members

    own_ids = lax.dynamic_index_in_dim(token_ids, member, 0, keepdims=False)
    own_length = lengths[member]
    start = own_length - 1 - RESP
    owner, first_seen, slot = token_slots(own_ids, block_rows)
    local_ids = own_ids % block_rows
    keys = round_keys(owner, slot, 0)
    asks = round_asks(keys, first_seen, local_ids, devices * SLOTS)
    own_targets = lax.dynamic_slice_in_dim(own_ids, start + 1, RESP, 0)
    vector_low = vector_master.astype(jnp.bfloat16).astype(jnp.float32)
    shared_notes = jnp.concatenate(
        [
            vector_low.reshape(-1),
            jnp.concatenate([own_targets, order, jnp.max(slot)[None] + 1]).astype(jnp.float32),
        ]
    )
    notes = jnp.concatenate(
        [
            asks.reshape(devices, SLOTS).astype(jnp.float32),
            jnp.broadcast_to(shared_notes[None, :], (devices, shared_notes.size)),
        ],
        axis=1,
    )
    notes = exchanged(notes)
    square_b = lax.all_gather(square_master.astype(jnp.bfloat16), ALL, axis=1, tiled=True)
    wide_b = lax.all_gather(wide_master.astype(jnp.bfloat16), DP, axis=1, tiled=True)
    hidden_units = wide_b.shape[1]
    asked = notes[:, :SLOTS].astype(jnp.int32).reshape(-1)
    gains = (
        notes[:, SLOTS : SLOTS + vector_low.size]
        .reshape(devices, vector_low.shape[0], vector_low.shape[1])
        .transpose(1, 0, 2)
        .reshape(vector_low.shape[0], D)
    )
    numbers = notes[:, SLOTS + vector_low.size :].astype(jnp.int32)
    targets = numbers[:, :RESP].reshape(-1)
    orders = numbers[:, RESP : RESP + members].reshape(groups, members, members)[:, 0]
    turns = (jnp.max(numbers[:, RESP + members]) + SLOTS - 1) // SLOTS
    table_b = table_master.astype(jnp.bfloat16)
    head_gains = low_copy(norm_gains)
    cosine, sine = rope_tables(SEQ, HD // 2)

    def fetched(wanted, row_keys):
        rows = jnp.dot(
            onehot_rows(wanted, block_rows), table_b, preferred_element_type=jnp.float32
        ).astype(jnp.bfloat16)
        return jnp.dot(
            onehot_rows(row_keys, devices * SLOTS),
            exchanged(rows),
            preferred_element_type=jnp.float32,
        )

    def later_round(turn):
        later_keys = round_keys(owner, slot, turn)
        later_asks = round_asks(later_keys, first_seen, local_ids, devices * SLOTS)
        return later_keys, exchanged(later_asks)

    def fetch_more(turn, rows):
        later_keys, later_asked = later_round(turn)
        return rows + fetched(later_asked, later_keys)

    hidden0 = lax.fori_loop(1, turns, fetch_more, fetched(asked, keys))
    act1 = rms_scale(hidden0, gains[0]).astype(jnp.bfloat16)
    inner = dense(act1, square_b[0:3].reshape(3 * D, D))
    entry = inner[:, :D]
    leave = inner[:, D : 2 * D]
    conv_in = inner[:, 2 * D :]
    product = entry * conv_in
    convolved = gains[4] * product + gains[5] * delayed(product, 1) + gains[6] * delayed(product, 2)
    mixer = (leave * convolved).astype(jnp.bfloat16)
    hidden1 = hidden0 + dense(mixer, square_b[3])
    act2 = rms_scale(hidden1, gains[1]).astype(jnp.bfloat16)

    def answers(values):
        return lax.dynamic_slice_in_dim(values, start, RESP, 0)

    def placed(values):
        return lax.dynamic_update_slice_in_dim(
            jnp.zeros((SEQ, values.shape[1]), values.dtype), values, start, 0
        )

    answer_act2 = answers(act2)
    query_raw = dense(answer_act2, square_b[4]).reshape(RESP, HEADS, HD)
    pair_raw = dense(act2, square_b[5])
    key_raw = pair_raw[:, : KV * HD].reshape(SEQ, KV, HD)
    value_b = pair_raw[:, KV * HD :].astype(jnp.bfloat16).reshape(SEQ, KV, HD)

    answer_cosine, answer_sine = answers(cosine), answers(sine)

    def query_prep(raw, gain):
        return rotate(rms_scale(raw, gain), answer_cosine, answer_sine)

    def key_prep(raw, gain):
        return rotate(rms_scale(raw, gain), cosine, sine)

    query_b = (
        query_prep(query_raw, head_gains[0]).astype(jnp.bfloat16).reshape(RESP, KV, groups_per, HD)
    )
    key_b = key_prep(key_raw, head_gains[1]).astype(jnp.bfloat16)
    causal = start + jnp.arange(RESP)[:, None] >= jnp.arange(SEQ)[None, :]
    scores = (
        jnp.einsum("sgrd,tgd->grst", query_b, key_b, preferred_element_type=jnp.float32) * scale
    )
    scores = jnp.where(causal, scores, masked_score)
    peak = jnp.max(scores, axis=-1, keepdims=True)
    expo = jnp.exp(scores - peak)
    total = jnp.sum(expo, axis=-1, keepdims=True)
    log_norm = peak + jnp.log(total)
    probs_b = (expo / total).astype(jnp.bfloat16)
    attended = jnp.einsum(
        "grst,tgd->sgrd", probs_b, value_b, preferred_element_type=jnp.float32
    ).reshape(RESP, D)
    attended_b = attended.astype(jnp.bfloat16)
    hidden2 = answers(hidden1) + dense(attended_b, square_b[6])
    act3 = member_gather(rms_scale(hidden2, gains[2]).astype(jnp.bfloat16))
    gate_up = dense(act3, wide_b[0:2].reshape(2 * hidden_units, D))
    gate_part = gate_up[:, :hidden_units]
    up_part = gate_up[:, hidden_units:]
    inner_b = (jax.nn.silu(gate_part) * up_part).astype(jnp.bfloat16)
    ffn_part = jnp.dot(inner_b, wide_b[2], preferred_element_type=jnp.float32)
    hidden3 = hidden2 + member_return(ffn_part.astype(jnp.bfloat16).reshape(members, RESP, D))
    final_b = rms_scale(hidden3, gains[3]).astype(jnp.bfloat16)
    response_tokens = lax.all_gather(final_b, ALL, axis=0, tiled=True)
    logit_scores = dense(response_tokens, table_b)
    local_target = jnp.where(targets // block_rows == device, targets % block_rows, -1)
    onehot = jnp.arange(block_rows)[None, :] == local_target[:, None]
    top = jnp.max(logit_scores, axis=-1)
    exp_total = jnp.sum(jnp.exp(logit_scores - top[:, None]), axis=-1)
    picked = jnp.sum(jnp.where(onehot, logit_scores, 0.0), axis=-1)
    stats = jnp.stack([top, exp_total, picked]).reshape(3, devices, RESP).transpose(1, 0, 2)
    stats = exchanged(stats)
    top = jnp.max(stats[:, 0], axis=0)
    exp_total = jnp.sum(stats[:, 1] * jnp.exp(stats[:, 0] - top[None, :]), axis=0)
    own_log_total = top + jnp.log(exp_total)
    own_logp = jnp.sum(jnp.sum(stats[:, 2], axis=0) - own_log_total)
    joined = spread(jnp.concatenate([own_log_total, own_logp[None]]))
    log_total = joined[:, :RESP].reshape(-1)
    seq_logp = joined[:, RESP].reshape(groups, members)
    slots = jnp.arange(members)
    chosen_mask = (orders[:, 0::2, None] == slots[None, None, :]).astype(jnp.float32)
    rejected_mask = (orders[:, 1::2, None] == slots[None, None, :]).astype(jnp.float32)
    margin = (
        pref_beta * jnp.sum((chosen_mask - rejected_mask) * seq_logp[:, None, :], axis=2) / RESP
    )
    pair_loss = jnp.sum(jax.nn.softplus(-margin))
    pull = jax.nn.sigmoid(-margin) * pref_beta / RESP
    grad_logp = jnp.sum((rejected_mask - chosen_mask) * pull[:, :, None], axis=1)
    row_weight = jnp.repeat(grad_logp.reshape(-1), RESP)
    softmax_rows = jnp.exp(logit_scores - log_total[:, None])
    grad_logits = (row_weight[:, None] * (onehot.astype(jnp.float32) - softmax_rows)).astype(
        jnp.bfloat16
    )
    grad_answers = jnp.dot(grad_logits, table_b, preferred_element_type=jnp.float32)
    grad_table = outer(grad_logits, response_tokens)
    grad_answer_group = lax.psum_scatter(
        grad_answers.astype(jnp.bfloat16), DP, scatter_dimension=0, tiled=True
    )
    grad_final = member_scatter(grad_answer_group.reshape(members, RESP, D), member)
    grad_hidden3, grad_gain3 = norm_back(hidden3, gains[3], grad_final)
    grad_ffn_out = member_gather(grad_hidden3.astype(jnp.bfloat16))
    grad_inner = dense(grad_ffn_out, wide_b[2])
    grad_down_w = outer(inner_b, grad_ffn_out)
    _, silu_pull = jax.vjp(lambda gate_in, up_in: jax.nn.silu(gate_in) * up_in, gate_part, up_part)
    grad_gate, grad_up = silu_pull(grad_inner)
    grad_gate_up = jnp.concatenate([grad_gate, grad_up], axis=1).astype(jnp.bfloat16)
    grad_act3_part = back_dense(grad_gate_up, wide_b[0:2].reshape(2 * hidden_units, D))
    grad_act3 = member_return(grad_act3_part.astype(jnp.bfloat16).reshape(members, RESP, D))
    grad_gate_up_w = outer(grad_gate_up, act3)
    grad_norm2, grad_gain2 = norm_back(hidden2, gains[2], grad_act3)
    grad_hidden2 = grad_hidden3 + grad_norm2
    grad_attn_out = grad_hidden2.astype(jnp.bfloat16)
    grad_attended = (
        back_dense(grad_attn_out, square_b[6])
        .astype(jnp.bfloat16)
        .reshape(RESP, KV, groups_per, HD)
    )
    grad_out_w = outer(grad_attn_out, attended_b)
    scores = (
        jnp.einsum("sgrd,tgd->grst", query_b, key_b, preferred_element_type=jnp.float32) * scale
    )
    probs = jnp.exp(jnp.where(causal, scores, masked_score) - log_norm)
    grad_probs = jnp.einsum(
        "sgrd,tgd->grst", grad_attended, value_b, preferred_element_type=jnp.float32
    )
    grad_values = jnp.einsum(
        "grst,sgrd->tgd", probs_b, grad_attended, preferred_element_type=jnp.float32
    )
    delta = jnp.sum(probs * grad_probs, axis=-1, keepdims=True)
    grad_scores = (probs * (grad_probs - delta)).astype(jnp.bfloat16)
    grad_query = (
        jnp.einsum("grst,tgd->sgrd", grad_scores, key_b, preferred_element_type=jnp.float32) * scale
    ).reshape(RESP, HEADS, HD)
    grad_keys = (
        jnp.einsum("grst,sgrd->tgd", grad_scores, query_b, preferred_element_type=jnp.float32)
        * scale
    )
    _, query_pull = jax.vjp(query_prep, query_raw, head_gains[0])
    grad_query_raw, grad_query_gain = query_pull(grad_query)
    _, key_pull = jax.vjp(key_prep, key_raw, head_gains[1])
    grad_key_raw, grad_key_gain = key_pull(grad_keys)
    grad_query_b = grad_query_raw.reshape(RESP, D).astype(jnp.bfloat16)
    grad_pair_b = jnp.concatenate(
        [grad_key_raw.reshape(SEQ, KV * HD), grad_values.reshape(SEQ, KV * HD)], axis=1
    ).astype(jnp.bfloat16)
    grad_act2 = back_dense(grad_pair_b, square_b[5]) + placed(back_dense(grad_query_b, square_b[4]))
    grad_query_w = outer(grad_query_b, answer_act2)
    grad_pair_w = outer(grad_pair_b, act2)
    grad_norm1, grad_gain1 = norm_back(hidden1, gains[1], grad_act2)
    grad_hidden1 = placed(grad_hidden2) + grad_norm1
    grad_mix_out = grad_hidden1.astype(jnp.bfloat16)
    grad_mixer = back_dense(grad_mix_out, square_b[3])
    grad_mixer_w = outer(grad_mix_out, mixer)
    grad_leave = grad_mixer * convolved
    grad_conv = grad_mixer * leave
    grad_tap0 = jnp.sum(grad_conv * product, axis=0)
    grad_tap1 = jnp.sum(grad_conv * delayed(product, 1), axis=0)
    grad_tap2 = jnp.sum(grad_conv * delayed(product, 2), axis=0)
    grad_product = (
        gains[4] * grad_conv + gains[5] * advanced(grad_conv, 1) + gains[6] * advanced(grad_conv, 2)
    )
    grad_inner_b = jnp.concatenate(
        [grad_product * conv_in, grad_leave, grad_product * entry], axis=1
    ).astype(jnp.bfloat16)
    grad_act1 = back_dense(grad_inner_b, square_b[0:3].reshape(3 * D, D))
    grad_inner_w = outer(grad_inner_b, act1)
    grad_norm0, grad_gain0 = norm_back(hidden0, gains[0], grad_act1)
    grad_embed_b = (grad_hidden1 + grad_norm0).astype(jnp.bfloat16)

    def returned(wanted, row_keys):
        rows = outer(onehot_rows(row_keys, devices * SLOTS), grad_embed_b)
        rows = exchanged(rows.astype(jnp.bfloat16))
        return outer(onehot_rows(wanted, block_rows), rows)

    def return_more(turn, total):
        later_keys, later_asked = later_round(turn)
        return total + returned(later_asked, later_keys)

    share_table = lax.fori_loop(1, turns, return_more, grad_table + returned(asked, keys))
    grad_square = jnp.concatenate(
        [
            grad_inner_w.astype(jnp.bfloat16).reshape(3, D, D),
            grad_mixer_w.astype(jnp.bfloat16)[None],
            grad_query_w.astype(jnp.bfloat16)[None],
            grad_pair_w.astype(jnp.bfloat16)[None],
            grad_out_w.astype(jnp.bfloat16)[None],
        ],
        axis=0,
    )
    grad_vector = jnp.stack(
        [grad_gain0, grad_gain1, grad_gain2, grad_gain3, grad_tap0, grad_tap1, grad_tap2]
    )
    grad_head_gains = jnp.stack([grad_query_gain, grad_key_gain])
    grad_wide = jnp.concatenate(
        [
            grad_gate_up_w.astype(jnp.bfloat16).reshape(2, hidden_units, D),
            grad_down_w.astype(jnp.bfloat16)[None],
        ],
        axis=0,
    )
    share_wide_b = lax.psum_scatter(grad_wide, DP, scatter_dimension=1, tiled=True)
    share_wide = share_wide_b.astype(jnp.float32)
    squares, square_rows = square_master.shape[0], square_master.shape[1]
    wides, wide_rows = wide_master.shape[0], wide_master.shape[1]
    group_square = lax.psum_scatter(grad_square, DP, scatter_dimension=1, tiled=True)
    share_square = member_scatter(
        group_square.reshape(squares, members, square_rows, D).transpose(1, 0, 2, 3), member
    )
    width = vector_master.shape[1]
    vector_notes = grad_vector.reshape(-1, devices, width).transpose(1, 0, 2).reshape(devices, -1)
    vector_notes = jnp.concatenate(
        [
            vector_notes,
            jnp.broadcast_to(grad_head_gains.reshape(1, -1), (devices, grad_head_gains.size)),
        ],
        axis=1,
    )
    vector_notes = jnp.sum(exchanged(vector_notes), axis=0)
    share_vector = vector_notes[: vector_master.size].reshape(vector_master.shape)
    gains_total = vector_notes[vector_master.size :].reshape(grad_head_gains.shape)
    own_squares = (
        jnp.sum(share_square * share_square)
        + jnp.sum(share_wide * share_wide)
        + jnp.sum(share_vector * share_vector)
        + jnp.sum(share_table * share_table)
    )
    moment_squares = jnp.concatenate(
        [
            jnp.sum(square_moment * square_moment, axis=(1, 2)),
            jnp.sum(wide_moment * wide_moment, axis=(1, 2)),
        ]
    )
    moment_cross = jnp.concatenate(
        [
            jnp.sum(square_moment * share_square, axis=(1, 2)),
            jnp.sum(wide_moment * share_wide, axis=(1, 2)),
        ]
    )
    grad_squares = jnp.concatenate(
        [
            jnp.sum(share_square * share_square, axis=(1, 2)),
            jnp.sum(share_wide * share_wide, axis=(1, 2)),
        ]
    )
    moment_stats = jnp.stack([moment_squares, moment_cross, grad_squares])
    sums = jnp.concatenate([moment_stats.reshape(-1), own_squares[None]])
    sums = jnp.sum(spread(sums), axis=0)
    stats_total = sums[:-1].reshape(moment_stats.shape)
    grad_norm = jnp.sqrt(sums[-1] + jnp.sum(gains_total * gains_total))
    factor = jnp.minimum(1.0, clip_limit / grad_norm)
    square_moment_new = muon_decay * square_moment + (1.0 - muon_decay) * (factor * share_square)
    wide_moment_new = muon_decay * wide_moment + (1.0 - muon_decay) * (factor * share_wide)
    moment_norm = jnp.sqrt(
        muon_decay * muon_decay * stats_total[0]
        + 2.0 * muon_decay * (1.0 - muon_decay) * factor * stats_total[1]
        + (1.0 - muon_decay) * (1.0 - muon_decay) * factor * factor * stats_total[2]
    )
    ortho_square = square_moment_new / (moment_norm[:7][:, None, None] + ortho_epsilon)
    ortho_wide = wide_moment_new / (moment_norm[7:][:, None, None] + ortho_epsilon)
    core = lax.axis_index("core")
    per_member = -(-squares // members)
    wide_early = jnp.stack([wide_moment.astype(jnp.bfloat16), share_wide_b], axis=1)
    wide_early = jnp.pad(wide_early, ((0, members - wides), (0, 0), (0, 0), (0, 0)))
    wide_early = lax.all_to_all(wide_early, "vocab", 0, 0, tiled=True).astype(jnp.float32)
    wide_inverse = 1.0 / (moment_norm[squares:] + ortho_epsilon)
    wide_inverse = jnp.pad(wide_inverse, (0, members - wides))[member]
    wide_job = (
        (
            (muon_decay * wide_inverse) * wide_early[:, 0]
            + ((1.0 - muon_decay) * factor * wide_inverse) * wide_early[:, 1]
        )
        .reshape(members * wide_rows, D)
        .astype(jnp.bfloat16)
    )
    wide_gram = lax.psum(outer(wide_job, wide_job).astype(jnp.bfloat16), DP)

    def to_members(values):
        values = jnp.pad(values, ((0, per_member * members - squares), (0, 0), (0, 0)))
        values = values.reshape(per_member, members, square_rows, D).transpose(1, 0, 2, 3)
        return lax.all_to_all(values, "vocab", 0, 0, tiled=True)

    def from_members(values):
        values = lax.all_to_all(values, "vocab", 0, 0, tiled=True).transpose(1, 0, 2, 3)
        return values.reshape(per_member * members, square_rows, D)[:squares]

    group_rows = members * square_rows
    square_part = to_members(ortho_square.astype(jnp.bfloat16)).transpose(1, 0, 2, 3)
    square_part = square_part.reshape(per_member, 1, group_rows, D)
    square_part = jnp.pad(
        square_part, ((0, groups // 2 - per_member), (1, 0), (0, 0), (0, 0))
    ).reshape(groups * group_rows, D)
    square_job = lax.all_to_all(square_part, DP, 0, 0, tiled=True)
    square_gram = outer(square_job, square_job)
    gram = jnp.where(core == 0, wide_gram.astype(jnp.float32), square_gram)
    power, rest = ortho_rest(gram)
    rest_b = rest.astype(jnp.bfloat16)
    wide_rest = jnp.where(core == 0, rest_b, lax.ppermute(rest_b, "core", [(0, 1), (1, 0)]))
    back_square = lax.all_to_all(
        square_product(square_job, rest_b).astype(jnp.bfloat16), DP, 0, 0, tiled=True
    )
    back_square = back_square.reshape(groups // 2, 2, members, square_rows, D)[:per_member, 1]
    back_square = from_members(back_square.transpose(1, 0, 2, 3))
    back_wide = square_product(wide_job, wide_rest).astype(jnp.bfloat16)
    back_wide = lax.all_to_all(
        back_wide.reshape(members, wide_rows, D), "vocab", 0, 0, tiled=True
    )[:wides]
    ortho_wide = power * ortho_wide + back_wide.astype(jnp.float32)
    ortho_square = power * ortho_square + back_square.astype(jnp.float32)
    wide_scale = jnp.array([math.sqrt(FF / D), math.sqrt(FF / D), 1.0], jnp.float32)
    square_new = square_master - muon_rate * ortho_square
    wide_new = wide_master - muon_rate * wide_scale[:, None, None] * ortho_wide
    table_step, table_first_new, table_second_new = adam_step(
        table_master, table_first, table_second, share_table, factor, adam_count
    )
    vector_step, vector_first_new, vector_second_new = adam_step(
        vector_master, vector_first, vector_second, share_vector, factor, adam_count
    )
    norm_step, norm_first_new, norm_second_new = adam_step(
        norm_gains, norm_first, norm_second, gains_total, factor, adam_count
    )
    return (
        pair_loss,
        grad_norm,
        square_new,
        square_moment_new,
        square_new.astype(jnp.bfloat16),
        wide_new,
        wide_moment_new,
        wide_new.astype(jnp.bfloat16),
        table_step,
        table_first_new,
        table_second_new,
        vector_step,
        vector_first_new,
        vector_second_new,
        norm_step,
        norm_first_new,
        norm_second_new,
        share_vector[3],
    )


def solution(mesh):
    groups, members = mesh.shape["dp"], mesh.shape["vocab"]
    cores = 2
    split_mesh = Mesh(mesh.devices.reshape(groups // cores, cores, members), ALL)
    return jax.shard_map(
        body,
        mesh=split_mesh,
        in_specs=(
            P(DP, None),
            P(DP, None),
            P(DP, None),
            P(ALL, None),
            P(ALL, None),
            P(ALL, None),
            P(None, ALL, None),
            P(None, ALL, None),
            P(None, ALL, None),
            P(None, ALL, None),
            P(None, ALL),
            P(None, ALL),
            P(None, ALL),
            P(),
            P(),
            P(),
            P(),
        ),
        out_specs=(
            P(),
            P(),
            P(None, ALL, None),
            P(None, ALL, None),
            P(None, ALL, None),
            P(None, ALL, None),
            P(None, ALL, None),
            P(None, ALL, None),
            P(ALL, None),
            P(ALL, None),
            P(ALL, None),
            P(None, ALL),
            P(None, ALL),
            P(None, ALL),
            P(),
            P(),
            P(),
            P(ALL),
        ),
        check_vma=False,
    )
```

```python
import math

import jax
import jax.numpy as jnp
from jax import lax
from jax.experimental import pallas as pl
from jax.experimental.pallas import tpu as pltpu
from jax.sharding import Mesh
from jax.sharding import PartitionSpec as P

D = 1024
HEADS = 16
KV = 8
HD = 64
FF = 4608
SEQ = 512
RESP = 96
NS_ITERS = 3


norm_epsilon = 1e-05
rope_base = 1000000.0
pref_beta = 2.0
clip_limit = 0.05
muon_decay = 0.95
muon_rate = 0.5
first_decay = 0.9
second_decay = 0.95
adam_rate = 0.02
adam_epsilon = 1e-08
weight_decay = 0.1
leading_coefficient = 3.4445
coef_second = -4.775
coef_third = 2.0315
ortho_epsilon = 1e-07
masked_score = -1e30


def rms_scale(inputs, gain):
    mean_square = jnp.mean(inputs * inputs, axis=-1, keepdims=True)
    return inputs * lax.rsqrt(mean_square + norm_epsilon) * gain


def rope_tables(length, half):
    position = jnp.arange(length, dtype=jnp.float32)
    inverse = rope_base ** (-jnp.arange(half, dtype=jnp.float32) / half)
    angle = position[:, None] * inverse[None, :]
    return (jnp.cos(angle)[:, None, :], jnp.sin(angle)[:, None, :])


def rotate(inputs, cosine, sine):
    half = inputs.shape[-1] // 2
    first = inputs[..., :half]
    second = inputs[..., half:]
    return jnp.concatenate(
        [first * cosine - second * sine, second * cosine + first * sine], axis=-1
    )


def dense(inputs, weight):
    return lax.dot_general(
        inputs, weight, (((1,), (1,)), ((), ())), preferred_element_type=jnp.float32
    )


def outer(grads, inputs):
    return lax.dot_general(
        grads, inputs, (((0,), (0,)), ((), ())), preferred_element_type=jnp.float32
    )


def back_dense(grads, weight):
    return jnp.dot(grads, weight, preferred_element_type=jnp.float32)


def delayed(values, offset):
    return jnp.pad(values, ((offset, 0), (0, 0)))[: values.shape[0]]


def advanced(values, offset):
    return jnp.pad(values, ((0, offset), (0, 0)))[offset:]


def norm_back(inputs, gain, grad_out):
    _, pullback = jax.vjp(rms_scale, inputs, gain)
    return pullback(grad_out)


def low_copy(values):
    return lax.optimization_barrier(values.astype(jnp.bfloat16)).astype(jnp.float32)


def adam_step(master, first, second, grad, factor, count):
    scaled = factor * grad
    first_new = first_decay * first + (1.0 - first_decay) * scaled
    second_new = second_decay * second + (1.0 - second_decay) * scaled * scaled
    steps = count.astype(jnp.float32)
    first_hat = first_new / (1.0 - first_decay**steps)
    second_hat = second_new / (1.0 - second_decay**steps)
    change = -adam_rate * (
        first_hat / (jnp.sqrt(second_hat) + adam_epsilon) + weight_decay * master
    )
    return (change, first_new, second_new)

DP = ("chip", "core")
ALL = ("chip", "core", "vocab")
SLOTS = 32


def exchanged(rows):
    return lax.all_to_all(rows, ALL, 0, 0, tiled=True)


def spread(values):
    count = lax.axis_size(ALL)
    return lax.all_to_all(jnp.broadcast_to(values[None], (count,) + values.shape), ALL, 0, 0)


def turned(values, step):
    count = lax.axis_size("vocab")
    return lax.ppermute(values, "vocab", [(i, (i + step) % count) for i in range(count)])


def other_core(values):
    return lax.ppermute(values, "core", [(0, 1), (1, 0)])


def pair_sum(halves, core):
    given = lax.dynamic_index_in_dim(halves, 1 - core, 0, keepdims=False)
    kept = lax.dynamic_index_in_dim(halves, core, 0, keepdims=False)
    total = kept.astype(jnp.float32) + other_core(given).astype(jnp.float32)
    return total.astype(jnp.bfloat16)


def chip_sum(blocks):
    blocks = lax.all_to_all(blocks, "chip", 0, 0, tiled=True)
    return jnp.sum(blocks.astype(jnp.float32), axis=0)


def group_sum(values, core):
    rows = values.shape[0] // 2
    chips = lax.axis_size("chip")
    half = pair_sum(values.reshape(2, rows, -1), core).reshape(chips, rows // chips, -1)
    part = chip_sum(half).astype(jnp.bfloat16)
    half = lax.all_to_all(
        jnp.broadcast_to(part[None], (chips,) + part.shape), "chip", 0, 0, tiled=True
    ).reshape(rows, -1)
    other = other_core(half)
    first = jnp.where(core == 0, half, other)
    second = jnp.where(core == 0, other, half)
    return jnp.concatenate([first, second], axis=0)


def member_gather(values):
    return jnp.concatenate(
        [values] + [turned(values, step) for step in range(1, lax.axis_size("vocab"))], axis=0
    )


def member_return(blocks):
    total = blocks[0].astype(jnp.float32)
    for step in range(1, len(blocks)):
        total = total + turned(blocks[step], -step).astype(jnp.float32)
    return total


def member_scatter(blocks, member):
    count = blocks.shape[0]
    return member_return(
        [
            lax.dynamic_index_in_dim(blocks, (member - step) % count, 0, keepdims=False)
            for step in range(count)
        ]
    )


def onehot_rows(index, count):
    return (index[:, None] == jnp.arange(count)[None, :]).astype(jnp.bfloat16)


def token_slots(ids, block_rows):
    owner = ids // block_rows
    place = jnp.arange(ids.shape[0])
    earlier = place[:, None] > place[None, :]
    equal = ids[:, None] == ids[None, :]
    first = jnp.logical_not(jnp.any(equal & earlier, axis=1))
    ahead = (owner[:, None] == owner[None, :]) & earlier & first[None, :]
    rank = jnp.sum(ahead.astype(jnp.int32), axis=1)
    slot = jnp.sum(jnp.where(equal & first[None, :], rank[None, :], 0), axis=1)
    return owner, first, slot


def round_keys(owner, slot, turn):
    within = slot - turn * SLOTS
    return jnp.where((within >= 0) & (within < SLOTS), owner * SLOTS + within, -1)


def round_asks(keys, first, local, count):
    hits = (keys[None, :] == jnp.arange(count)[:, None]) & first[None, :]
    return jnp.sum(jnp.where(hits, local[None, :] + 1, 0), axis=1) - 1


def square_product(left, right):
    return jnp.dot(
        left.astype(jnp.bfloat16), right.astype(jnp.bfloat16), preferred_element_type=jnp.float32
    )


def rest_kernel(
    gram_ref, rest_ref, gram_scratch, change_scratch, rest_scratch, grams, change_b, rest_b
):
    lead = leading_coefficient
    size = gram_ref.shape[0]
    tile = 256

    def dot(left, right):
        return jnp.dot(left, right, preferred_element_type=jnp.float32)

    @pl.loop(0, size // tile)
    def _(step):
        rows = pl.ds(pl.multiple_of(step * tile, tile), tile)
        gram_scratch[rows, :] = gram_ref[rows, :]
        grams[0, rows, :] = gram_ref[rows, :].astype(jnp.bfloat16)

    power = 1.0
    for turn in range(NS_ITERS):
        now, later = turn % 2, (turn + 1) % 2

        @pl.loop(0, size // tile)
        def _(step):
            rows = pl.ds(pl.multiple_of(step * tile, tile), tile)
            change = coef_second * gram_scratch[rows, :] + coef_third * dot(
                grams[now, rows, :], grams[now]
            )
            change_scratch[rows, :] = change
            change_b[rows, :] = change.astype(jnp.bfloat16)

        @pl.loop(0, size // tile)
        def _(step):
            rows = pl.ds(pl.multiple_of(step * tile, tile), tile)
            if turn == 0:
                rest = change_scratch[rows, :]
            else:
                rest = (
                    lead * rest_scratch[rows, :]
                    + power * change_scratch[rows, :]
                    + dot(rest_b[rows, :], change_b[...])
                )
            if turn + 1 < NS_ITERS:
                rest_scratch[rows, :] = rest
                rest_b[rows, :] = rest.astype(jnp.bfloat16)
                mixed = dot(change_b[rows, :], grams[now])
                gram = (
                    lead * lead * gram_scratch[rows, :]
                    + 2.0 * lead * mixed
                    + dot(mixed.astype(jnp.bfloat16), change_b[...])
                )
                gram_scratch[rows, :] = gram
                grams[later, rows, :] = gram.astype(jnp.bfloat16)
            else:
                rest_ref[rows, :] = rest.astype(jnp.bfloat16)

        power = power * lead


def ortho_rest(gram):
    size = gram.shape[0]
    wide = pltpu.VMEM((size, size), jnp.float32)
    narrow = pltpu.VMEM((size, size), jnp.bfloat16)
    return pl.pallas_call(
        rest_kernel,
        out_shape=jax.ShapeDtypeStruct((size, size), jnp.bfloat16),
        in_specs=[pl.BlockSpec(memory_space=pltpu.VMEM)],
        out_specs=pl.BlockSpec(memory_space=pltpu.VMEM),
        scratch_shapes=[
            wide,
            wide,
            wide,
            pltpu.VMEM((2, size, size), jnp.bfloat16),
            narrow,
            narrow,
        ],
        compiler_params=pltpu.CompilerParams(vmem_limit_bytes=44 * 1024 * 1024),
        cost_estimate=pl.CostEstimate(
            flops=18 * size**3, bytes_accessed=6 * size * size, transcendentals=0
        ),
    )(gram)


def body(
    token_ids,
    seq_lengths,
    pair_order,
    table_master,
    table_first,
    table_second,
    square_master,
    square_moment,
    wide_master,
    wide_moment,
    vector_master,
    vector_first,
    vector_second,
    norm_gains,
    norm_first,
    norm_second,
    adam_count,
):
    members = lax.axis_size("vocab")
    member = lax.axis_index("vocab")
    block_rows = table_master.shape[0]
    lengths = seq_lengths[0]
    order = pair_order[0]
    groups_per = HEADS // KV
    scale = HD ** (-0.5)

    core = lax.axis_index("core")
    devices = lax.axis_size(ALL)
    device = lax.axis_index(ALL)
    groups = devices // members

    own_ids = lax.dynamic_index_in_dim(token_ids, member, 0, keepdims=False)
    own_length = lengths[member]
    start = own_length - 1 - RESP
    owner, first_seen, slot = token_slots(own_ids, block_rows)
    local_ids = own_ids % block_rows
    keys = round_keys(owner, slot, 0)
    asks = round_asks(keys, first_seen, local_ids, devices * SLOTS)
    own_targets = lax.dynamic_slice_in_dim(own_ids, start + 1, RESP, 0)
    vector_low = vector_master.astype(jnp.bfloat16).astype(jnp.float32)
    shared_notes = jnp.concatenate(
        [
            vector_low.reshape(-1),
            jnp.concatenate([own_targets, order, jnp.max(slot)[None] + 1]).astype(jnp.float32),
        ]
    )
    notes = jnp.concatenate(
        [
            asks.reshape(devices, SLOTS).astype(jnp.float32),
            jnp.broadcast_to(shared_notes[None, :], (devices, shared_notes.size)),
        ],
        axis=1,
    )
    notes = exchanged(notes)
    square_b = lax.all_gather(square_master.astype(jnp.bfloat16), ALL, axis=1, tiled=True)
    wide_b = lax.all_gather(wide_master.astype(jnp.bfloat16), DP, axis=1, tiled=True)
    hidden_units = wide_b.shape[1]
    asked = notes[:, :SLOTS].astype(jnp.int32).reshape(-1)
    gains = (
        notes[:, SLOTS : SLOTS + vector_low.size]
        .reshape(devices, vector_low.shape[0], vector_low.shape[1])
        .transpose(1, 0, 2)
        .reshape(vector_low.shape[0], D)
    )
    numbers = notes[:, SLOTS + vector_low.size :].astype(jnp.int32)
    targets = numbers[:, :RESP].reshape(-1)
    orders = numbers[:, RESP : RESP + members].reshape(groups, members, members)[:, 0]
    turns = (jnp.max(numbers[:, RESP + members]) + SLOTS - 1) // SLOTS
    table_b = table_master.astype(jnp.bfloat16)
    head_gains = low_copy(norm_gains)
    cosine, sine = rope_tables(SEQ, HD // 2)

    def fetched(wanted, row_keys):
        rows = jnp.dot(
            onehot_rows(wanted, block_rows), table_b, preferred_element_type=jnp.float32
        ).astype(jnp.bfloat16)
        return jnp.dot(
            onehot_rows(row_keys, devices * SLOTS),
            exchanged(rows),
            preferred_element_type=jnp.float32,
        )

    def later_round(turn):
        later_keys = round_keys(owner, slot, turn)
        later_asks = round_asks(later_keys, first_seen, local_ids, devices * SLOTS)
        return later_keys, exchanged(later_asks)

    def fetch_more(turn, rows):
        later_keys, later_asked = later_round(turn)
        return rows + fetched(later_asked, later_keys)

    hidden0 = lax.fori_loop(1, turns, fetch_more, fetched(asked, keys))
    act1 = rms_scale(hidden0, gains[0]).astype(jnp.bfloat16)
    inner = dense(act1, square_b[0:3].reshape(3 * D, D))
    entry = inner[:, :D]
    leave = inner[:, D : 2 * D]
    conv_in = inner[:, 2 * D :]
    product = entry * conv_in
    convolved = gains[4] * product + gains[5] * delayed(product, 1) + gains[6] * delayed(product, 2)
    mixer = (leave * convolved).astype(jnp.bfloat16)
    hidden1 = hidden0 + dense(mixer, square_b[3])
    act2 = rms_scale(hidden1, gains[1]).astype(jnp.bfloat16)

    def answers(values):
        return lax.dynamic_slice_in_dim(values, start, RESP, 0)

    def placed(values):
        return lax.dynamic_update_slice_in_dim(
            jnp.zeros((SEQ, values.shape[1]), values.dtype), values, start, 0
        )

    answer_act2 = answers(act2)
    query_raw = dense(answer_act2, square_b[4]).reshape(RESP, HEADS, HD)
    pair_raw = dense(act2, square_b[5])
    key_raw = pair_raw[:, : KV * HD].reshape(SEQ, KV, HD)
    value_b = pair_raw[:, KV * HD :].astype(jnp.bfloat16).reshape(SEQ, KV, HD)

    answer_cosine, answer_sine = answers(cosine), answers(sine)

    def query_prep(raw, gain):
        return rotate(rms_scale(raw, gain), answer_cosine, answer_sine)

    def key_prep(raw, gain):
        return rotate(rms_scale(raw, gain), cosine, sine)

    query_b = (
        query_prep(query_raw, head_gains[0]).astype(jnp.bfloat16).reshape(RESP, KV, groups_per, HD)
    )
    key_b = key_prep(key_raw, head_gains[1]).astype(jnp.bfloat16)
    causal = start + jnp.arange(RESP)[:, None] >= jnp.arange(SEQ)[None, :]
    scores = (
        jnp.einsum("sgrd,tgd->grst", query_b, key_b, preferred_element_type=jnp.float32) * scale
    )
    scores = jnp.where(causal, scores, masked_score)
    peak = jnp.max(scores, axis=-1, keepdims=True)
    expo = jnp.exp(scores - peak)
    total = jnp.sum(expo, axis=-1, keepdims=True)
    log_norm = peak + jnp.log(total)
    probs_b = (expo / total).astype(jnp.bfloat16)
    attended = jnp.einsum(
        "grst,tgd->sgrd", probs_b, value_b, preferred_element_type=jnp.float32
    ).reshape(RESP, D)
    attended_b = attended.astype(jnp.bfloat16)
    hidden2 = answers(hidden1) + dense(attended_b, square_b[6])
    act3 = member_gather(rms_scale(hidden2, gains[2]).astype(jnp.bfloat16))
    gate_up = dense(act3, wide_b[0:2].reshape(2 * hidden_units, D))
    gate_part = gate_up[:, :hidden_units]
    up_part = gate_up[:, hidden_units:]
    inner_b = (jax.nn.silu(gate_part) * up_part).astype(jnp.bfloat16)
    ffn_part = jnp.dot(inner_b, wide_b[2], preferred_element_type=jnp.float32)
    hidden3 = hidden2 + member_return(ffn_part.astype(jnp.bfloat16).reshape(members, RESP, D))
    final_b = rms_scale(hidden3, gains[3]).astype(jnp.bfloat16)
    response_tokens = lax.all_gather(final_b, ALL, axis=0, tiled=True)
    logit_scores = dense(response_tokens, table_b)
    local_target = jnp.where(targets // block_rows == device, targets % block_rows, -1)
    onehot = jnp.arange(block_rows)[None, :] == local_target[:, None]
    top = jnp.max(logit_scores, axis=-1)
    exp_total = jnp.sum(jnp.exp(logit_scores - top[:, None]), axis=-1)
    picked = jnp.sum(jnp.where(onehot, logit_scores, 0.0), axis=-1)
    stats = jnp.stack([top, exp_total, picked]).reshape(3, devices, RESP).transpose(1, 0, 2)
    stats = exchanged(stats)
    top = jnp.max(stats[:, 0], axis=0)
    exp_total = jnp.sum(stats[:, 1] * jnp.exp(stats[:, 0] - top[None, :]), axis=0)
    own_log_total = top + jnp.log(exp_total)
    own_logp = jnp.sum(jnp.sum(stats[:, 2], axis=0) - own_log_total)
    joined = spread(jnp.concatenate([own_log_total, own_logp[None]]))
    log_total = joined[:, :RESP].reshape(-1)
    seq_logp = joined[:, RESP].reshape(groups, members)
    slots = jnp.arange(members)
    chosen_mask = (orders[:, 0::2, None] == slots[None, None, :]).astype(jnp.float32)
    rejected_mask = (orders[:, 1::2, None] == slots[None, None, :]).astype(jnp.float32)
    margin = (
        pref_beta * jnp.sum((chosen_mask - rejected_mask) * seq_logp[:, None, :], axis=2) / RESP
    )
    pair_loss = jnp.sum(jax.nn.softplus(-margin))
    pull = jax.nn.sigmoid(-margin) * pref_beta / RESP
    grad_logp = jnp.sum((rejected_mask - chosen_mask) * pull[:, :, None], axis=1)
    row_weight = jnp.repeat(grad_logp.reshape(-1), RESP)
    softmax_rows = jnp.exp(logit_scores - log_total[:, None])
    grad_logits = (row_weight[:, None] * (onehot.astype(jnp.float32) - softmax_rows)).astype(
        jnp.bfloat16
    )
    grad_answers = jnp.dot(grad_logits, table_b, preferred_element_type=jnp.float32)
    grad_table = outer(grad_logits, response_tokens)
    grad_answer_pair = pair_sum(
        grad_answers.astype(jnp.bfloat16)
        .reshape(groups // 2, 2, members * RESP, D)
        .transpose(1, 0, 2, 3),
        core,
    )
    grad_answer_group = chip_sum(grad_answer_pair).astype(jnp.bfloat16)
    grad_final = member_scatter(grad_answer_group.reshape(members, RESP, D), member)
    grad_hidden3, grad_gain3 = norm_back(hidden3, gains[3], grad_final)
    grad_ffn_out = member_gather(grad_hidden3.astype(jnp.bfloat16))
    grad_inner = dense(grad_ffn_out, wide_b[2])
    grad_down_w = outer(inner_b, grad_ffn_out)
    _, silu_pull = jax.vjp(lambda gate_in, up_in: jax.nn.silu(gate_in) * up_in, gate_part, up_part)
    grad_gate, grad_up = silu_pull(grad_inner)
    grad_gate_up = jnp.concatenate([grad_gate, grad_up], axis=1).astype(jnp.bfloat16)
    grad_act3_part = back_dense(grad_gate_up, wide_b[0:2].reshape(2 * hidden_units, D))
    grad_act3 = member_return(grad_act3_part.astype(jnp.bfloat16).reshape(members, RESP, D))
    grad_gate_up_w = outer(grad_gate_up, act3)
    grad_norm2, grad_gain2 = norm_back(hidden2, gains[2], grad_act3)
    grad_hidden2 = grad_hidden3 + grad_norm2
    grad_attn_out = grad_hidden2.astype(jnp.bfloat16)
    grad_attended = (
        back_dense(grad_attn_out, square_b[6])
        .astype(jnp.bfloat16)
        .reshape(RESP, KV, groups_per, HD)
    )
    grad_out_w = outer(grad_attn_out, attended_b)
    scores = (
        jnp.einsum("sgrd,tgd->grst", query_b, key_b, preferred_element_type=jnp.float32) * scale
    )
    probs = jnp.exp(jnp.where(causal, scores, masked_score) - log_norm)
    grad_probs = jnp.einsum(
        "sgrd,tgd->grst", grad_attended, value_b, preferred_element_type=jnp.float32
    )
    grad_values = jnp.einsum(
        "grst,sgrd->tgd", probs_b, grad_attended, preferred_element_type=jnp.float32
    )
    delta = jnp.sum(probs * grad_probs, axis=-1, keepdims=True)
    grad_scores = (probs * (grad_probs - delta)).astype(jnp.bfloat16)
    grad_query = (
        jnp.einsum("grst,tgd->sgrd", grad_scores, key_b, preferred_element_type=jnp.float32) * scale
    ).reshape(RESP, HEADS, HD)
    grad_keys = (
        jnp.einsum("grst,sgrd->tgd", grad_scores, query_b, preferred_element_type=jnp.float32)
        * scale
    )
    _, query_pull = jax.vjp(query_prep, query_raw, head_gains[0])
    grad_query_raw, grad_query_gain = query_pull(grad_query)
    _, key_pull = jax.vjp(key_prep, key_raw, head_gains[1])
    grad_key_raw, grad_key_gain = key_pull(grad_keys)
    grad_query_b = grad_query_raw.reshape(RESP, D).astype(jnp.bfloat16)
    grad_pair_b = jnp.concatenate(
        [grad_key_raw.reshape(SEQ, KV * HD), grad_values.reshape(SEQ, KV * HD)], axis=1
    ).astype(jnp.bfloat16)
    grad_act2 = back_dense(grad_pair_b, square_b[5]) + placed(back_dense(grad_query_b, square_b[4]))
    grad_query_w = outer(grad_query_b, answer_act2)
    grad_pair_w = outer(grad_pair_b, act2)
    grad_norm1, grad_gain1 = norm_back(hidden1, gains[1], grad_act2)
    grad_hidden1 = placed(grad_hidden2) + grad_norm1
    grad_mix_out = grad_hidden1.astype(jnp.bfloat16)
    grad_mixer = back_dense(grad_mix_out, square_b[3])
    grad_mixer_w = outer(grad_mix_out, mixer)
    grad_leave = grad_mixer * convolved
    grad_conv = grad_mixer * leave
    grad_tap0 = jnp.sum(grad_conv * product, axis=0)
    grad_tap1 = jnp.sum(grad_conv * delayed(product, 1), axis=0)
    grad_tap2 = jnp.sum(grad_conv * delayed(product, 2), axis=0)
    grad_product = (
        gains[4] * grad_conv + gains[5] * advanced(grad_conv, 1) + gains[6] * advanced(grad_conv, 2)
    )
    grad_inner_b = jnp.concatenate(
        [grad_product * conv_in, grad_leave, grad_product * entry], axis=1
    ).astype(jnp.bfloat16)
    grad_act1 = back_dense(grad_inner_b, square_b[0:3].reshape(3 * D, D))
    grad_inner_w = outer(grad_inner_b, act1)
    grad_norm0, grad_gain0 = norm_back(hidden0, gains[0], grad_act1)
    grad_embed_b = (grad_hidden1 + grad_norm0).astype(jnp.bfloat16)

    def returned(wanted, row_keys):
        rows = outer(onehot_rows(row_keys, devices * SLOTS), grad_embed_b)
        rows = exchanged(rows.astype(jnp.bfloat16))
        return outer(onehot_rows(wanted, block_rows), rows)

    def return_more(turn, total):
        later_keys, later_asked = later_round(turn)
        return total + returned(later_asked, later_keys)

    share_table = lax.fori_loop(1, turns, return_more, grad_table + returned(asked, keys))
    grad_square = jnp.concatenate(
        [
            grad_inner_w.astype(jnp.bfloat16).reshape(3, D, D),
            grad_mixer_w.astype(jnp.bfloat16)[None],
            grad_query_w.astype(jnp.bfloat16)[None],
            grad_pair_w.astype(jnp.bfloat16)[None],
            grad_out_w.astype(jnp.bfloat16)[None],
        ],
        axis=0,
    )
    grad_vector = jnp.stack(
        [grad_gain0, grad_gain1, grad_gain2, grad_gain3, grad_tap0, grad_tap1, grad_tap2]
    )
    grad_head_gains = jnp.stack([grad_query_gain, grad_key_gain])
    grad_wide = jnp.concatenate(
        [
            grad_gate_up_w.astype(jnp.bfloat16).reshape(2, hidden_units, D),
            grad_down_w.astype(jnp.bfloat16)[None],
        ],
        axis=0,
    )
    share_wide_b = lax.psum_scatter(grad_wide, DP, scatter_dimension=1, tiled=True)
    share_wide = share_wide_b.astype(jnp.float32)
    squares, square_rows = square_master.shape[0], square_master.shape[1]
    wides, wide_rows = wide_master.shape[0], wide_master.shape[1]
    wide_early = jnp.stack([wide_moment.astype(jnp.bfloat16), share_wide_b], axis=1)
    wide_early = jnp.pad(wide_early, ((0, members - wides), (0, 0), (0, 0), (0, 0)))
    wide_early = lax.all_to_all(wide_early, "vocab", 0, 0, tiled=True)
    per_member = -(-squares // members)
    group_rows = members * square_rows

    def by_member(values):
        values = jnp.pad(values, ((0, per_member * members - squares), (0, 0), (0, 0)))
        return values.reshape(per_member, members, -1, D).transpose(1, 0, 2, 3)

    square_moment_job = lax.all_to_all(
        by_member(square_moment.astype(jnp.bfloat16)), "vocab", 0, 0, tiled=True
    )
    square_moment_job = square_moment_job.transpose(1, 0, 2, 3).reshape(per_member, group_rows, D)
    grad_square, share_wide_b = lax.optimization_barrier((grad_square, share_wide_b))
    group_square = lax.psum_scatter(grad_square, DP, scatter_dimension=1, tiled=True)
    group_square, wide_early, square_moment_job = lax.optimization_barrier(
        (group_square, wide_early, square_moment_job)
    )
    square_grad_job = member_scatter(by_member(group_square), member)

    def from_members(values):
        values = values.reshape(per_member, members, square_rows, D).transpose(1, 0, 2, 3)
        values = lax.all_to_all(values.astype(jnp.bfloat16), "vocab", 0, 0, tiled=True)
        values = values.transpose(1, 0, 2, 3).reshape(per_member * members, square_rows, D)
        return values[:squares].astype(jnp.float32)

    share_square = from_members(square_grad_job)
    width = vector_master.shape[1]
    vector_notes = grad_vector.reshape(-1, devices, width).transpose(1, 0, 2).reshape(devices, -1)
    vector_notes = jnp.concatenate(
        [
            vector_notes,
            jnp.broadcast_to(grad_head_gains.reshape(1, -1), (devices, grad_head_gains.size)),
        ],
        axis=1,
    )
    vector_notes = jnp.sum(exchanged(vector_notes), axis=0)
    share_vector = vector_notes[: vector_master.size].reshape(vector_master.shape)
    gains_total = vector_notes[vector_master.size :].reshape(grad_head_gains.shape)

    def job_sums(values):
        sums = jnp.sum(values, axis=(1, 2))[:, None]
        sums = jnp.where(jnp.arange(members)[None, :] == member, sums, 0.0)
        return sums.reshape(-1)[:squares]

    moment_squares = jnp.concatenate(
        [
            jnp.sum(square_moment * square_moment, axis=(1, 2)),
            jnp.sum(wide_moment * wide_moment, axis=(1, 2)),
        ]
    )
    moment_cross = jnp.concatenate(
        [
            job_sums(square_moment_job.astype(jnp.float32) * square_grad_job),
            jnp.sum(wide_moment * share_wide, axis=(1, 2)),
        ]
    )
    grad_squares = jnp.concatenate(
        [
            job_sums(square_grad_job * square_grad_job),
            jnp.sum(share_wide * share_wide, axis=(1, 2)),
        ]
    )
    moment_stats = jnp.stack([moment_squares, moment_cross, grad_squares])
    own_squares = (
        jnp.sum(grad_squares)
        + jnp.sum(share_vector * share_vector)
        + jnp.sum(share_table * share_table)
    )
    sums = jnp.concatenate([moment_stats.reshape(-1), own_squares[None]])
    sums = jnp.sum(spread(sums), axis=0)
    stats_total = sums[:-1].reshape(moment_stats.shape)
    grad_norm = jnp.sqrt(sums[-1] + jnp.sum(gains_total * gains_total))
    factor = jnp.minimum(1.0, clip_limit / grad_norm)
    square_moment_new = muon_decay * square_moment + (1.0 - muon_decay) * (factor * share_square)
    wide_moment_new = muon_decay * wide_moment + (1.0 - muon_decay) * (factor * share_wide)
    moment_norm = jnp.sqrt(
        muon_decay * muon_decay * stats_total[0]
        + 2.0 * muon_decay * (1.0 - muon_decay) * factor * stats_total[1]
        + (1.0 - muon_decay) * (1.0 - muon_decay) * factor * factor * stats_total[2]
    )
    ortho_square = square_moment_new / (moment_norm[:7][:, None, None] + ortho_epsilon)
    ortho_wide = wide_moment_new / (moment_norm[7:][:, None, None] + ortho_epsilon)
    table_step, table_first_new, table_second_new = adam_step(
        table_master, table_first, table_second, share_table, factor, adam_count
    )
    wide_inverse = 1.0 / (moment_norm[squares:] + ortho_epsilon)
    wide_inverse = jnp.pad(wide_inverse, (0, members - wides))[member]
    wide_early = wide_early.astype(jnp.float32)
    wide_job = (
        (
            (muon_decay * wide_inverse) * wide_early[:, 0]
            + ((1.0 - muon_decay) * factor * wide_inverse) * wide_early[:, 1]
        )
        .reshape(members * wide_rows, D)
        .astype(jnp.bfloat16)
    )
    wide_gram = group_sum(outer(wide_job, wide_job).astype(jnp.bfloat16), core)
    square_inverse = 1.0 / (moment_norm[:squares] + ortho_epsilon)
    square_inverse = jnp.pad(square_inverse, (0, per_member * members - squares))
    square_inverse = square_inverse.reshape(per_member, members)[:, member][:, None, None]
    square_part = (muon_decay * square_inverse) * square_moment_job.astype(jnp.float32) + (
        (1.0 - muon_decay) * factor * square_inverse
    ) * square_grad_job
    square_part = square_part.astype(jnp.bfloat16).reshape(per_member, 1, group_rows, D)
    square_part = jnp.pad(
        square_part, ((0, groups // 2 - per_member), (1, 0), (0, 0), (0, 0))
    ).reshape(groups * group_rows, D)
    square_job = lax.all_to_all(square_part, DP, 0, 0, tiled=True)
    square_gram = outer(square_job, square_job)
    gram = jnp.where(core == 0, wide_gram.astype(jnp.float32), square_gram)
    gram, table_step, table_first_new, table_second_new = lax.optimization_barrier(
        (gram, table_step, table_first_new, table_second_new)
    )
    rest_b = ortho_rest(gram)
    power = leading_coefficient**NS_ITERS
    wide_rest = jnp.where(core == 0, rest_b, other_core(rest_b))
    back_square = lax.all_to_all(
        square_product(square_job, rest_b).astype(jnp.bfloat16), DP, 0, 0, tiled=True
    )
    back_square = back_square.reshape(groups // 2, 2, group_rows, D)[:per_member, 1]
    back_square = from_members(back_square)
    back_wide = square_product(wide_job, wide_rest).astype(jnp.bfloat16)
    back_wide = lax.all_to_all(
        back_wide.reshape(members, wide_rows, D), "vocab", 0, 0, tiled=True
    )[:wides]
    ortho_wide = power * ortho_wide + back_wide.astype(jnp.float32)
    ortho_square = power * ortho_square + back_square
    wide_scale = jnp.array([math.sqrt(FF / D), math.sqrt(FF / D), 1.0], jnp.float32)
    square_new = square_master - muon_rate * ortho_square
    wide_new = wide_master - muon_rate * wide_scale[:, None, None] * ortho_wide
    vector_step, vector_first_new, vector_second_new = adam_step(
        vector_master, vector_first, vector_second, share_vector, factor, adam_count
    )
    norm_step, norm_first_new, norm_second_new = adam_step(
        norm_gains, norm_first, norm_second, gains_total, factor, adam_count
    )
    return (
        pair_loss,
        grad_norm,
        square_new,
        square_moment_new,
        square_new.astype(jnp.bfloat16),
        wide_new,
        wide_moment_new,
        wide_new.astype(jnp.bfloat16),
        table_step,
        table_first_new,
        table_second_new,
        vector_step,
        vector_first_new,
        vector_second_new,
        norm_step,
        norm_first_new,
        norm_second_new,
        share_vector[3],
    )


def solution(mesh):
    groups, members = mesh.shape["dp"], mesh.shape["vocab"]
    cores = 2
    split_mesh = Mesh(mesh.devices.reshape(groups // cores, cores, members), ALL)
    return jax.shard_map(
        body,
        mesh=split_mesh,
        in_specs=(
            P(DP, None),
            P(DP, None),
            P(DP, None),
            P(ALL, None),
            P(ALL, None),
            P(ALL, None),
            P(None, ALL, None),
            P(None, ALL, None),
            P(None, ALL, None),
            P(None, ALL, None),
            P(None, ALL),
            P(None, ALL),
            P(None, ALL),
            P(),
            P(),
            P(),
            P(),
        ),
        out_specs=(
            P(),
            P(),
            P(None, ALL, None),
            P(None, ALL, None),
            P(None, ALL, None),
            P(None, ALL, None),
            P(None, ALL, None),
            P(None, ALL, None),
            P(ALL, None),
            P(ALL, None),
            P(ALL, None),
            P(None, ALL),
            P(None, ALL),
            P(None, ALL),
            P(),
            P(),
            P(),
            P(ALL),
        ),
        check_vma=False,
    )
```

```python
import math

import jax
import jax.numpy as jnp
from jax import lax
from jax.experimental import pallas as pl
from jax.experimental.pallas import tpu as pltpu
from jax.sharding import Mesh
from jax.sharding import PartitionSpec as P

D = 1024
HEADS = 16
KV = 8
HD = 64
FF = 4608
SEQ = 512
RESP = 96
NS_ITERS = 3


norm_epsilon = 1e-05
rope_base = 1000000.0
pref_beta = 2.0
clip_limit = 0.05
muon_decay = 0.95
muon_rate = 0.5
first_decay = 0.9
second_decay = 0.95
adam_rate = 0.02
adam_epsilon = 1e-08
weight_decay = 0.1
leading_coefficient = 3.4445
coef_second = -4.775
coef_third = 2.0315
ortho_epsilon = 1e-07
masked_score = -1e30


def rms_scale(inputs, gain):
    mean_square = jnp.mean(inputs * inputs, axis=-1, keepdims=True)
    return inputs * lax.rsqrt(mean_square + norm_epsilon) * gain


def rope_tables(length, half):
    position = jnp.arange(length, dtype=jnp.float32)
    inverse = rope_base ** (-jnp.arange(half, dtype=jnp.float32) / half)
    angle = position[:, None] * inverse[None, :]
    return (jnp.cos(angle)[:, None, :], jnp.sin(angle)[:, None, :])


def rotate(inputs, cosine, sine):
    half = inputs.shape[-1] // 2
    first = inputs[..., :half]
    second = inputs[..., half:]
    return jnp.concatenate(
        [first * cosine - second * sine, second * cosine + first * sine], axis=-1
    )


def dense(inputs, weight):
    return lax.dot_general(
        inputs, weight, (((1,), (1,)), ((), ())), preferred_element_type=jnp.float32
    )


def outer(grads, inputs):
    return lax.dot_general(
        grads, inputs, (((0,), (0,)), ((), ())), preferred_element_type=jnp.float32
    )


def back_dense(grads, weight):
    return jnp.dot(grads, weight, preferred_element_type=jnp.float32)


def delayed(values, offset):
    return jnp.pad(values, ((offset, 0), (0, 0)))[: values.shape[0]]


def advanced(values, offset):
    return jnp.pad(values, ((0, offset), (0, 0)))[offset:]


def norm_back(inputs, gain, grad_out):
    _, pullback = jax.vjp(rms_scale, inputs, gain)
    return pullback(grad_out)


def low_copy(values):
    return lax.optimization_barrier(values.astype(jnp.bfloat16)).astype(jnp.float32)


def adam_step(master, first, second, grad, factor, count):
    scaled = factor * grad
    first_new = first_decay * first + (1.0 - first_decay) * scaled
    second_new = second_decay * second + (1.0 - second_decay) * scaled * scaled
    steps = count.astype(jnp.float32)
    first_hat = first_new / (1.0 - first_decay**steps)
    second_hat = second_new / (1.0 - second_decay**steps)
    change = -adam_rate * (
        first_hat / (jnp.sqrt(second_hat) + adam_epsilon) + weight_decay * master
    )
    return (change, first_new, second_new)

DP = ("chip", "core")
ALL = ("chip", "core", "vocab")
SLOTS = 32


def exchanged(rows):
    return lax.all_to_all(rows, ALL, 0, 0, tiled=True)


def spread(values):
    count = lax.axis_size(ALL)
    return lax.all_to_all(jnp.broadcast_to(values[None], (count,) + values.shape), ALL, 0, 0)


def turned(values, axis, step):
    count = lax.axis_size(axis)
    return lax.ppermute(values, axis, [(i, (i + step) % count) for i in range(count)])


def block_at(blocks, index):
    return lax.dynamic_index_in_dim(blocks, index % blocks.shape[0], 0, keepdims=False)


def handed_out(blocks, axis):
    place, count = lax.axis_index(axis), lax.axis_size(axis)
    return [block_at(blocks, place)] + [
        turned(block_at(blocks, place + step), axis, step) for step in range(1, count)
    ]


def handed_back(pieces, axis):
    return [pieces[0]] + [turned(pieces[step], axis, -step) for step in range(1, len(pieces))]


def gathered(values, axis):
    return [values] + [turned(values, axis, step) for step in range(1, lax.axis_size(axis))]


def placed_before(pieces, axis):
    pieces, place = jnp.stack(pieces), lax.axis_index(axis)
    return jnp.stack([block_at(pieces, place - j) for j in range(pieces.shape[0])])


def placed_after(pieces, axis):
    pieces, place = jnp.stack(pieces), lax.axis_index(axis)
    return jnp.stack([block_at(pieces, j - place) for j in range(pieces.shape[0])])


def added(pieces):
    total = pieces[0].astype(jnp.float32)
    for piece in pieces[1:]:
        total = total + piece.astype(jnp.float32)
    return total


def other_core(values):
    return lax.ppermute(values, "core", [(0, 1), (1, 0)])


def pair_sum(halves, core):
    given = lax.dynamic_index_in_dim(halves, 1 - core, 0, keepdims=False)
    kept = lax.dynamic_index_in_dim(halves, core, 0, keepdims=False)
    total = kept.astype(jnp.float32) + other_core(given).astype(jnp.float32)
    return total.astype(jnp.bfloat16)


def chip_sum(blocks):
    return added(handed_out(blocks, "chip"))


def group_sum(values, core):
    rows = values.shape[0] // 2
    chips = lax.axis_size("chip")
    half = pair_sum(values.reshape(2, rows, -1), core).reshape(chips, rows // chips, -1)
    part = chip_sum(half).astype(jnp.bfloat16)
    half = placed_before(gathered(part, "chip"), "chip").reshape(rows, -1)
    other = other_core(half)
    first = jnp.where(core == 0, half, other)
    second = jnp.where(core == 0, other, half)
    return jnp.concatenate([first, second], axis=0)


def member_gather(values):
    return jnp.concatenate(gathered(values, "vocab"), axis=0)


def member_return(pieces):
    return added(handed_back(pieces, "vocab"))


def member_scatter(blocks):
    return added(handed_out(blocks, "vocab"))


def onehot_rows(index, count):
    return (index[:, None] == jnp.arange(count)[None, :]).astype(jnp.bfloat16)


def token_slots(ids, block_rows):
    owner = ids // block_rows
    place = jnp.arange(ids.shape[0])
    earlier = place[:, None] > place[None, :]
    equal = ids[:, None] == ids[None, :]
    first = jnp.logical_not(jnp.any(equal & earlier, axis=1))
    ahead = (owner[:, None] == owner[None, :]) & earlier & first[None, :]
    rank = jnp.sum(ahead.astype(jnp.int32), axis=1)
    slot = jnp.sum(jnp.where(equal & first[None, :], rank[None, :], 0), axis=1)
    return owner, first, slot


def round_keys(owner, slot, turn):
    within = slot - turn * SLOTS
    return jnp.where((within >= 0) & (within < SLOTS), owner * SLOTS + within, -1)


def round_asks(keys, first, local, count):
    hits = (keys[None, :] == jnp.arange(count)[:, None]) & first[None, :]
    return jnp.sum(jnp.where(hits, local[None, :] + 1, 0), axis=1) - 1


def square_product(left, right):
    return jnp.dot(
        left.astype(jnp.bfloat16), right.astype(jnp.bfloat16), preferred_element_type=jnp.float32
    )


def rest_kernel(
    gram_ref, rest_ref, gram_scratch, change_scratch, rest_scratch, grams, change_b, rest_b
):
    lead = leading_coefficient
    size = gram_ref.shape[0]
    tile = 256

    def dot(left, right):
        return jnp.dot(left, right, preferred_element_type=jnp.float32)

    @pl.loop(0, size // tile)
    def _(step):
        rows = pl.ds(pl.multiple_of(step * tile, tile), tile)
        gram_scratch[rows, :] = gram_ref[rows, :]
        grams[0, rows, :] = gram_ref[rows, :].astype(jnp.bfloat16)

    power = 1.0
    for turn in range(NS_ITERS):
        now, later = turn % 2, (turn + 1) % 2

        @pl.loop(0, size // tile)
        def _(step):
            rows = pl.ds(pl.multiple_of(step * tile, tile), tile)
            change = coef_second * gram_scratch[rows, :] + coef_third * dot(
                grams[now, rows, :], grams[now]
            )
            change_scratch[rows, :] = change
            change_b[rows, :] = change.astype(jnp.bfloat16)

        @pl.loop(0, size // tile)
        def _(step):
            rows = pl.ds(pl.multiple_of(step * tile, tile), tile)
            if turn == 0:
                rest = change_scratch[rows, :]
            else:
                rest = (
                    lead * rest_scratch[rows, :]
                    + power * change_scratch[rows, :]
                    + dot(rest_b[rows, :], change_b[...])
                )
            if turn + 1 < NS_ITERS:
                rest_scratch[rows, :] = rest
                rest_b[rows, :] = rest.astype(jnp.bfloat16)
                mixed = dot(change_b[rows, :], grams[now])
                gram = (
                    lead * lead * gram_scratch[rows, :]
                    + 2.0 * lead * mixed
                    + dot(mixed.astype(jnp.bfloat16), change_b[...])
                )
                gram_scratch[rows, :] = gram
                grams[later, rows, :] = gram.astype(jnp.bfloat16)
            else:
                rest_ref[rows, :] = rest.astype(jnp.bfloat16)

        power = power * lead


def ortho_rest(gram):
    size = gram.shape[0]
    wide = pltpu.VMEM((size, size), jnp.float32)
    narrow = pltpu.VMEM((size, size), jnp.bfloat16)
    return pl.pallas_call(
        rest_kernel,
        out_shape=jax.ShapeDtypeStruct((size, size), jnp.bfloat16),
        in_specs=[pl.BlockSpec(memory_space=pltpu.VMEM)],
        out_specs=pl.BlockSpec(memory_space=pltpu.VMEM),
        scratch_shapes=[
            wide,
            wide,
            wide,
            pltpu.VMEM((2, size, size), jnp.bfloat16),
            narrow,
            narrow,
        ],
        compiler_params=pltpu.CompilerParams(vmem_limit_bytes=44 * 1024 * 1024),
        cost_estimate=pl.CostEstimate(
            flops=18 * size**3, bytes_accessed=6 * size * size, transcendentals=0
        ),
    )(gram)


def body(
    token_ids,
    seq_lengths,
    pair_order,
    table_master,
    table_first,
    table_second,
    square_master,
    square_moment,
    wide_master,
    wide_moment,
    vector_master,
    vector_first,
    vector_second,
    norm_gains,
    norm_first,
    norm_second,
    adam_count,
):
    members = lax.axis_size("vocab")
    member = lax.axis_index("vocab")
    block_rows = table_master.shape[0]
    lengths = seq_lengths[0]
    order = pair_order[0]
    groups_per = HEADS // KV
    scale = HD ** (-0.5)

    core = lax.axis_index("core")
    devices = lax.axis_size(ALL)
    device = lax.axis_index(ALL)
    groups = devices // members

    own_ids = lax.dynamic_index_in_dim(token_ids, member, 0, keepdims=False)
    own_length = lengths[member]
    start = own_length - 1 - RESP
    owner, first_seen, slot = token_slots(own_ids, block_rows)
    local_ids = own_ids % block_rows
    keys = round_keys(owner, slot, 0)
    asks = round_asks(keys, first_seen, local_ids, devices * SLOTS)
    own_targets = lax.dynamic_slice_in_dim(own_ids, start + 1, RESP, 0)
    vector_low = vector_master.astype(jnp.bfloat16).astype(jnp.float32)
    shared_notes = jnp.concatenate(
        [
            vector_low.reshape(-1),
            jnp.concatenate([own_targets, order, jnp.max(slot)[None] + 1]).astype(jnp.float32),
        ]
    )
    notes = jnp.concatenate(
        [
            asks.reshape(devices, SLOTS).astype(jnp.float32),
            jnp.broadcast_to(shared_notes[None, :], (devices, shared_notes.size)),
        ],
        axis=1,
    )
    notes = exchanged(notes)
    square_b = lax.all_gather(square_master.astype(jnp.bfloat16), ALL, axis=1, tiled=True)
    wide_b = lax.all_gather(wide_master.astype(jnp.bfloat16), DP, axis=1, tiled=True)
    hidden_units = wide_b.shape[1]
    asked = notes[:, :SLOTS].astype(jnp.int32).reshape(-1)
    gains = (
        notes[:, SLOTS : SLOTS + vector_low.size]
        .reshape(devices, vector_low.shape[0], vector_low.shape[1])
        .transpose(1, 0, 2)
        .reshape(vector_low.shape[0], D)
    )
    numbers = notes[:, SLOTS + vector_low.size :].astype(jnp.int32)
    targets = numbers[:, :RESP].reshape(-1)
    orders = numbers[:, RESP : RESP + members].reshape(groups, members, members)[:, 0]
    turns = (jnp.max(numbers[:, RESP + members]) + SLOTS - 1) // SLOTS
    slots = jnp.arange(members)
    chosen_mask = (orders[:, 0::2, None] == slots[None, None, :]).astype(jnp.float32)
    rejected_mask = (orders[:, 1::2, None] == slots[None, None, :]).astype(jnp.float32)
    pair_rows = jnp.sum(
        (chosen_mask + rejected_mask)[:, :, :, None] * (chosen_mask - rejected_mask)[:, :, None, :],
        axis=1,
    )
    same_group = jnp.arange(groups)[:, None] == jnp.arange(groups)[None, :]
    pair_rows = jnp.where(same_group[:, None, :, None], pair_rows[:, :, None, :], 0.0)
    pair_rows = pair_rows.reshape(devices, devices) * (pref_beta / RESP)
    chosen_sign = jnp.sum(chosen_mask - rejected_mask, axis=1).reshape(devices, 1)
    table_b = table_master.astype(jnp.bfloat16)
    head_gains = low_copy(norm_gains)
    cosine, sine = rope_tables(SEQ, HD // 2)

    def fetched(wanted, row_keys):
        rows = jnp.dot(
            onehot_rows(wanted, block_rows), table_b, preferred_element_type=jnp.float32
        ).astype(jnp.bfloat16)
        return jnp.dot(
            onehot_rows(row_keys, devices * SLOTS),
            exchanged(rows),
            preferred_element_type=jnp.float32,
        )

    def later_round(turn):
        later_keys = round_keys(owner, slot, turn)
        later_asks = round_asks(later_keys, first_seen, local_ids, devices * SLOTS)
        return later_keys, exchanged(later_asks)

    def fetch_more(turn, rows):
        later_keys, later_asked = later_round(turn)
        return rows + fetched(later_asked, later_keys)

    hidden0 = lax.fori_loop(1, turns, fetch_more, fetched(asked, keys))
    act1 = rms_scale(hidden0, gains[0]).astype(jnp.bfloat16)
    inner = dense(act1, square_b[0:3].reshape(3 * D, D))
    entry = inner[:, :D]
    leave = inner[:, D : 2 * D]
    conv_in = inner[:, 2 * D :]
    product = entry * conv_in
    convolved = gains[4] * product + gains[5] * delayed(product, 1) + gains[6] * delayed(product, 2)
    mixer = (leave * convolved).astype(jnp.bfloat16)
    hidden1 = hidden0 + dense(mixer, square_b[3])
    act2 = rms_scale(hidden1, gains[1]).astype(jnp.bfloat16)

    def answers(values):
        return lax.dynamic_slice_in_dim(values, start, RESP, 0)

    def placed(values):
        return lax.dynamic_update_slice_in_dim(
            jnp.zeros((SEQ, values.shape[1]), values.dtype), values, start, 0
        )

    answer_act2 = answers(act2)
    query_raw = dense(answer_act2, square_b[4]).reshape(RESP, HEADS, HD)
    pair_raw = dense(act2, square_b[5])
    key_raw = pair_raw[:, : KV * HD].reshape(SEQ, KV, HD)
    value_b = pair_raw[:, KV * HD :].astype(jnp.bfloat16).reshape(SEQ, KV, HD)

    answer_cosine, answer_sine = answers(cosine), answers(sine)

    def query_prep(raw, gain):
        return rotate(rms_scale(raw, gain), answer_cosine, answer_sine)

    def key_prep(raw, gain):
        return rotate(rms_scale(raw, gain), cosine, sine)

    query_b = (
        query_prep(query_raw, head_gains[0]).astype(jnp.bfloat16).reshape(RESP, KV, groups_per, HD)
    )
    key_b = key_prep(key_raw, head_gains[1]).astype(jnp.bfloat16)
    causal = start + jnp.arange(RESP)[:, None] >= jnp.arange(SEQ)[None, :]
    scores = (
        jnp.einsum("sgrd,tgd->grst", query_b, key_b, preferred_element_type=jnp.float32) * scale
    )
    scores = jnp.where(causal, scores, masked_score)
    peak = jnp.max(scores, axis=-1, keepdims=True)
    expo = jnp.exp(scores - peak)
    total = jnp.sum(expo, axis=-1, keepdims=True)
    log_norm = peak + jnp.log(total)
    probs_b = (expo / total).astype(jnp.bfloat16)
    attended = jnp.einsum(
        "grst,tgd->sgrd", probs_b, value_b, preferred_element_type=jnp.float32
    ).reshape(RESP, D)
    attended_b = attended.astype(jnp.bfloat16)
    hidden2 = answers(hidden1) + dense(attended_b, square_b[6])
    act3 = member_gather(rms_scale(hidden2, gains[2]).astype(jnp.bfloat16))
    gate_up = dense(act3, wide_b[0:2].reshape(2 * hidden_units, D))
    gate_part = gate_up[:, :hidden_units]
    up_part = gate_up[:, hidden_units:]
    inner_b = (jax.nn.silu(gate_part) * up_part).astype(jnp.bfloat16)
    ffn_part = jnp.dot(inner_b, wide_b[2], preferred_element_type=jnp.float32)
    hidden3 = hidden2 + member_return(ffn_part.astype(jnp.bfloat16).reshape(members, RESP, D))
    final_b = rms_scale(hidden3, gains[3]).astype(jnp.bfloat16)
    response_tokens = lax.all_gather(final_b, ALL, axis=0, tiled=True)
    logit_scores = dense(response_tokens, table_b)
    local_target = jnp.where(targets // block_rows == device, targets % block_rows, -1)
    onehot = jnp.arange(block_rows)[None, :] == local_target[:, None]
    top = jnp.max(logit_scores, axis=-1)
    exp_total = jnp.sum(jnp.exp(logit_scores - top[:, None]), axis=-1)
    picked = jnp.sum(jnp.where(onehot, logit_scores, 0.0), axis=-1)
    stats = jnp.stack([top, exp_total, picked]).reshape(3, devices, RESP).transpose(1, 0, 2)
    stats = exchanged(stats)
    top = jnp.max(stats[:, 0], axis=0)
    exp_total = jnp.sum(stats[:, 1] * jnp.exp(stats[:, 0] - top[None, :]), axis=0)
    own_log_total = top + jnp.log(exp_total)
    own_logp = jnp.sum(jnp.sum(stats[:, 2], axis=0) - own_log_total)
    joined = spread(jnp.concatenate([own_log_total, own_logp[None]]))
    log_total = joined[:, :RESP].reshape(-1)
    margin = jnp.sum(pair_rows * joined[:, RESP][None, :], axis=1, keepdims=True)
    pair_loss = 0.5 * jnp.sum(jax.nn.softplus(-margin))
    grad_logp = chosen_sign * jax.nn.sigmoid(-margin) * (-pref_beta / RESP)
    row_weight = jnp.broadcast_to(grad_logp, (devices, RESP)).reshape(-1)
    softmax_rows = jnp.exp(logit_scores - log_total[:, None])
    grad_logits = (row_weight[:, None] * (onehot.astype(jnp.float32) - softmax_rows)).astype(
        jnp.bfloat16
    )
    grad_answers = jnp.dot(grad_logits, table_b, preferred_element_type=jnp.float32)
    grad_table = outer(grad_logits, response_tokens)
    grad_answer_pair = pair_sum(
        grad_answers.astype(jnp.bfloat16)
        .reshape(groups // 2, 2, members * RESP, D)
        .transpose(1, 0, 2, 3),
        core,
    )
    grad_answer_group = chip_sum(grad_answer_pair).astype(jnp.bfloat16)
    grad_final = member_scatter(grad_answer_group.reshape(members, RESP, D))
    grad_hidden3, grad_gain3 = norm_back(hidden3, gains[3], grad_final)
    grad_ffn_out = member_gather(grad_hidden3.astype(jnp.bfloat16))
    grad_inner = dense(grad_ffn_out, wide_b[2])
    grad_down_w = outer(inner_b, grad_ffn_out)
    _, silu_pull = jax.vjp(lambda gate_in, up_in: jax.nn.silu(gate_in) * up_in, gate_part, up_part)
    grad_gate, grad_up = silu_pull(grad_inner)
    grad_gate_up = jnp.concatenate([grad_gate, grad_up], axis=1).astype(jnp.bfloat16)
    grad_act3_part = back_dense(grad_gate_up, wide_b[0:2].reshape(2 * hidden_units, D))
    grad_act3 = member_return(grad_act3_part.astype(jnp.bfloat16).reshape(members, RESP, D))
    grad_gate_up_w = outer(grad_gate_up, act3)
    grad_norm2, grad_gain2 = norm_back(hidden2, gains[2], grad_act3)
    grad_hidden2 = grad_hidden3 + grad_norm2
    grad_attn_out = grad_hidden2.astype(jnp.bfloat16)
    grad_attended = (
        back_dense(grad_attn_out, square_b[6])
        .astype(jnp.bfloat16)
        .reshape(RESP, KV, groups_per, HD)
    )
    grad_out_w = outer(grad_attn_out, attended_b)
    scores = (
        jnp.einsum("sgrd,tgd->grst", query_b, key_b, preferred_element_type=jnp.float32) * scale
    )
    probs = jnp.exp(jnp.where(causal, scores, masked_score) - log_norm)
    grad_probs = jnp.einsum(
        "sgrd,tgd->grst", grad_attended, value_b, preferred_element_type=jnp.float32
    )
    grad_values = jnp.einsum(
        "grst,sgrd->tgd", probs_b, grad_attended, preferred_element_type=jnp.float32
    )
    delta = jnp.sum(probs * grad_probs, axis=-1, keepdims=True)
    grad_scores = (probs * (grad_probs - delta)).astype(jnp.bfloat16)
    grad_query = (
        jnp.einsum("grst,tgd->sgrd", grad_scores, key_b, preferred_element_type=jnp.float32) * scale
    ).reshape(RESP, HEADS, HD)
    grad_keys = (
        jnp.einsum("grst,sgrd->tgd", grad_scores, query_b, preferred_element_type=jnp.float32)
        * scale
    )
    _, query_pull = jax.vjp(query_prep, query_raw, head_gains[0])
    grad_query_raw, grad_query_gain = query_pull(grad_query)
    _, key_pull = jax.vjp(key_prep, key_raw, head_gains[1])
    grad_key_raw, grad_key_gain = key_pull(grad_keys)
    grad_query_b = grad_query_raw.reshape(RESP, D).astype(jnp.bfloat16)
    grad_pair_b = jnp.concatenate(
        [grad_key_raw.reshape(SEQ, KV * HD), grad_values.reshape(SEQ, KV * HD)], axis=1
    ).astype(jnp.bfloat16)
    grad_act2 = back_dense(grad_pair_b, square_b[5]) + placed(back_dense(grad_query_b, square_b[4]))
    grad_query_w = outer(grad_query_b, answer_act2)
    grad_pair_w = outer(grad_pair_b, act2)
    grad_norm1, grad_gain1 = norm_back(hidden1, gains[1], grad_act2)
    grad_hidden1 = placed(grad_hidden2) + grad_norm1
    grad_mix_out = grad_hidden1.astype(jnp.bfloat16)
    grad_mixer = back_dense(grad_mix_out, square_b[3])
    grad_mixer_w = outer(grad_mix_out, mixer)
    grad_leave = grad_mixer * convolved
    grad_conv = grad_mixer * leave
    grad_tap0 = jnp.sum(grad_conv * product, axis=0)
    grad_tap1 = jnp.sum(grad_conv * delayed(product, 1), axis=0)
    grad_tap2 = jnp.sum(grad_conv * delayed(product, 2), axis=0)
    grad_product = (
        gains[4] * grad_conv + gains[5] * advanced(grad_conv, 1) + gains[6] * advanced(grad_conv, 2)
    )
    grad_inner_b = jnp.concatenate(
        [grad_product * conv_in, grad_leave, grad_product * entry], axis=1
    ).astype(jnp.bfloat16)
    grad_act1 = back_dense(grad_inner_b, square_b[0:3].reshape(3 * D, D))
    grad_inner_w = outer(grad_inner_b, act1)
    grad_norm0, grad_gain0 = norm_back(hidden0, gains[0], grad_act1)
    grad_embed_b = (grad_hidden1 + grad_norm0).astype(jnp.bfloat16)

    grad_square = jnp.concatenate(
        [
            grad_inner_w.astype(jnp.bfloat16).reshape(3, D, D),
            grad_mixer_w.astype(jnp.bfloat16)[None],
            grad_query_w.astype(jnp.bfloat16)[None],
            grad_pair_w.astype(jnp.bfloat16)[None],
            grad_out_w.astype(jnp.bfloat16)[None],
        ],
        axis=0,
    )
    grad_vector = jnp.stack(
        [grad_gain0, grad_gain1, grad_gain2, grad_gain3, grad_tap0, grad_tap1, grad_tap2]
    )
    grad_head_gains = jnp.stack([grad_query_gain, grad_key_gain])
    grad_wide = jnp.concatenate(
        [
            grad_gate_up_w.astype(jnp.bfloat16).reshape(2, hidden_units, D),
            grad_down_w.astype(jnp.bfloat16)[None],
        ],
        axis=0,
    )
    share_wide_b = lax.psum_scatter(grad_wide, DP, scatter_dimension=1, tiled=True)
    share_wide = share_wide_b.astype(jnp.float32)
    squares, square_rows = square_master.shape[0], square_master.shape[1]
    wides, wide_rows = wide_master.shape[0], wide_master.shape[1]
    per_member = -(-squares // members)
    group_rows = members * square_rows

    def by_member(values):
        values = jnp.pad(values, ((0, per_member * members - squares), (0, 0), (0, 0)))
        return values.reshape(per_member, members, -1, D).transpose(1, 0, 2, 3)

    def wide_by_member(values):
        return jnp.pad(values, ((0, members - wides), (0, 0), (0, 0)))

    moment_jobs = jnp.concatenate(
        [
            wide_by_member(wide_moment.astype(jnp.bfloat16)),
            by_member(square_moment.astype(jnp.bfloat16)).reshape(members, -1, D),
        ],
        axis=1,
    )
    moment_jobs = jnp.stack(handed_out(moment_jobs, "vocab"))
    grad_square, share_wide_b, moment_jobs = lax.optimization_barrier(
        (grad_square, share_wide_b, moment_jobs)
    )
    wide_moment_job = moment_jobs[:, :wide_rows]
    square_moment_job = placed_before(list(moment_jobs[:, wide_rows:]), "vocab")
    square_moment_job = square_moment_job.reshape(members, per_member, square_rows, D)
    square_moment_job = square_moment_job.transpose(1, 0, 2, 3).reshape(per_member, group_rows, D)
    wide_grad_job = jnp.stack(handed_out(wide_by_member(share_wide_b), "vocab"))
    grad_embed_b, wide_grad_job = lax.optimization_barrier((grad_embed_b, wide_grad_job))
    group_square = lax.psum_scatter(grad_square, DP, scatter_dimension=1, tiled=True)
    square_grad_job = member_scatter(by_member(group_square))

    def from_members(values):
        values = values.reshape(per_member, members, square_rows, D).transpose(1, 0, 2, 3)
        values = placed_before(handed_out(values.astype(jnp.bfloat16), "vocab"), "vocab")
        values = values.transpose(1, 0, 2, 3).reshape(per_member * members, square_rows, D)
        return values[:squares].astype(jnp.float32)

    share_square = from_members(square_grad_job)

    def returned(wanted, row_keys):
        rows = outer(onehot_rows(row_keys, devices * SLOTS), grad_embed_b)
        rows = exchanged(rows.astype(jnp.bfloat16))
        return outer(onehot_rows(wanted, block_rows), rows)

    def return_more(turn, total):
        later_keys, later_asked = later_round(turn)
        return total + returned(later_asked, later_keys)

    share_table = lax.fori_loop(1, turns, return_more, grad_table + returned(asked, keys))
    width = vector_master.shape[1]
    vector_notes = grad_vector.reshape(-1, devices, width).transpose(1, 0, 2).reshape(devices, -1)
    vector_notes = jnp.concatenate(
        [
            vector_notes,
            jnp.broadcast_to(grad_head_gains.reshape(1, -1), (devices, grad_head_gains.size)),
        ],
        axis=1,
    )
    vector_notes = jnp.sum(exchanged(vector_notes), axis=0)
    share_vector = vector_notes[: vector_master.size].reshape(vector_master.shape)
    gains_total = vector_notes[vector_master.size :].reshape(grad_head_gains.shape)

    def job_sums(values):
        sums = jnp.sum(values, axis=(1, 2))[:, None]
        sums = jnp.where(jnp.arange(members)[None, :] == member, sums, 0.0)
        return sums.reshape(-1)[:squares]

    moment_squares = jnp.concatenate(
        [
            jnp.sum(square_moment * square_moment, axis=(1, 2)),
            jnp.sum(wide_moment * wide_moment, axis=(1, 2)),
        ]
    )
    moment_cross = jnp.concatenate(
        [
            job_sums(square_moment_job.astype(jnp.float32) * square_grad_job),
            jnp.sum(wide_moment * share_wide, axis=(1, 2)),
        ]
    )
    grad_squares = jnp.concatenate(
        [
            job_sums(square_grad_job * square_grad_job),
            jnp.sum(share_wide * share_wide, axis=(1, 2)),
        ]
    )
    moment_stats = jnp.stack([moment_squares, moment_cross, grad_squares])
    own_squares = (
        jnp.sum(grad_squares)
        + jnp.sum(share_vector * share_vector)
        + jnp.sum(share_table * share_table)
    )
    sums = jnp.concatenate([moment_stats.reshape(-1), own_squares[None]])
    sums = jnp.sum(spread(sums), axis=0)
    stats_total = sums[:-1].reshape(moment_stats.shape)
    grad_norm = jnp.sqrt(sums[-1] + jnp.sum(gains_total * gains_total))
    factor = jnp.minimum(1.0, clip_limit / grad_norm)
    square_moment_new = muon_decay * square_moment + (1.0 - muon_decay) * (factor * share_square)
    wide_moment_new = muon_decay * wide_moment + (1.0 - muon_decay) * (factor * share_wide)
    moment_norm = jnp.sqrt(
        muon_decay * muon_decay * stats_total[0]
        + 2.0 * muon_decay * (1.0 - muon_decay) * factor * stats_total[1]
        + (1.0 - muon_decay) * (1.0 - muon_decay) * factor * factor * stats_total[2]
    )
    ortho_square = square_moment_new / (moment_norm[:7][:, None, None] + ortho_epsilon)
    ortho_wide = wide_moment_new / (moment_norm[7:][:, None, None] + ortho_epsilon)
    table_step, table_first_new, table_second_new = adam_step(
        table_master, table_first, table_second, share_table, factor, adam_count
    )
    wide_inverse = 1.0 / (moment_norm[squares:] + ortho_epsilon)
    wide_inverse = jnp.pad(wide_inverse, (0, members - wides))[member]
    square_inverse = 1.0 / (moment_norm[:squares] + ortho_epsilon)
    square_inverse = jnp.pad(square_inverse, (0, per_member * members - squares))
    square_inverse = square_inverse.reshape(per_member, members)[:, member][:, None, None]
    square_part = (muon_decay * square_inverse) * square_moment_job.astype(jnp.float32) + (
        (1.0 - muon_decay) * factor * square_inverse
    ) * square_grad_job
    square_part, wide_grad_job = lax.optimization_barrier(
        (square_part.astype(jnp.bfloat16), wide_grad_job)
    )
    square_part = jnp.pad(square_part, ((0, groups // 2 - per_member), (0, 0), (0, 0)))
    square_half = jnp.concatenate(handed_out(square_part, "chip"), axis=0)
    square_job = jnp.concatenate([square_half, other_core(square_half)], axis=0)
    wide_job = (
        (muon_decay * wide_inverse) * wide_moment_job.astype(jnp.float32)
        + ((1.0 - muon_decay) * factor * wide_inverse) * wide_grad_job.astype(jnp.float32)
    )
    wide_job = wide_job.reshape(members * wide_rows, D).astype(jnp.bfloat16)
    wide_gram = group_sum(outer(wide_job, wide_job).astype(jnp.bfloat16), core)
    square_gram = outer(square_job, square_job)
    gram = jnp.where(core == 0, wide_gram.astype(jnp.float32), square_gram)
    gram, share_square, table_step, table_first_new, table_second_new = lax.optimization_barrier(
        (gram, share_square, table_step, table_first_new, table_second_new)
    )
    rest_b = ortho_rest(gram)
    power = leading_coefficient**NS_ITERS
    wide_rest = jnp.where(core == 0, rest_b, other_core(rest_b))
    back_square = square_product(square_job, rest_b).astype(jnp.bfloat16)
    half_rows = square_half.shape[0]
    back_square = jnp.where(
        core == 0, other_core(back_square[half_rows:]), back_square[:half_rows]
    )
    back_square = handed_back(list(back_square.reshape(-1, group_rows, D)), "chip")
    back_square = placed_after(back_square, "chip")[:per_member]
    back_wide = square_product(wide_job, wide_rest).astype(jnp.bfloat16)
    back_wide = handed_back(list(back_wide.reshape(members, wide_rows, D)), "vocab")
    back_wide = placed_after(back_wide, "vocab")[:wides]
    back_square, back_wide = lax.optimization_barrier((back_square, back_wide))
    back_square = from_members(back_square)
    ortho_wide = power * ortho_wide + back_wide.astype(jnp.float32)
    ortho_square = power * ortho_square + back_square
    wide_scale = jnp.array([math.sqrt(FF / D), math.sqrt(FF / D), 1.0], jnp.float32)
    square_new = square_master - muon_rate * ortho_square
    wide_new = wide_master - muon_rate * wide_scale[:, None, None] * ortho_wide
    vector_step, vector_first_new, vector_second_new = adam_step(
        vector_master, vector_first, vector_second, share_vector, factor, adam_count
    )
    norm_step, norm_first_new, norm_second_new = adam_step(
        norm_gains, norm_first, norm_second, gains_total, factor, adam_count
    )
    return (
        pair_loss,
        grad_norm,
        square_new,
        square_moment_new,
        square_new.astype(jnp.bfloat16),
        wide_new,
        wide_moment_new,
        wide_new.astype(jnp.bfloat16),
        table_step,
        table_first_new,
        table_second_new,
        vector_step,
        vector_first_new,
        vector_second_new,
        norm_step,
        norm_first_new,
        norm_second_new,
        share_vector[3],
    )


def solution(mesh):
    groups, members = mesh.shape["dp"], mesh.shape["vocab"]
    cores = 2
    split_mesh = Mesh(mesh.devices.reshape(groups // cores, cores, members), ALL)
    return jax.shard_map(
        body,
        mesh=split_mesh,
        in_specs=(
            P(DP, None),
            P(DP, None),
            P(DP, None),
            P(ALL, None),
            P(ALL, None),
            P(ALL, None),
            P(None, ALL, None),
            P(None, ALL, None),
            P(None, ALL, None),
            P(None, ALL, None),
            P(None, ALL),
            P(None, ALL),
            P(None, ALL),
            P(),
            P(),
            P(),
            P(),
        ),
        out_specs=(
            P(),
            P(),
            P(None, ALL, None),
            P(None, ALL, None),
            P(None, ALL, None),
            P(None, ALL, None),
            P(None, ALL, None),
            P(None, ALL, None),
            P(ALL, None),
            P(ALL, None),
            P(ALL, None),
            P(None, ALL),
            P(None, ALL),
            P(None, ALL),
            P(),
            P(),
            P(),
            P(ALL),
        ),
        check_vma=False,
    )
```

```python
import math

import jax
import jax.numpy as jnp
from jax import lax
from jax.experimental import pallas as pl
from jax.experimental.pallas import tpu as pltpu
from jax.sharding import Mesh
from jax.sharding import PartitionSpec as P

D = 1024
HEADS = 16
KV = 8
HD = 64
FF = 4608
SEQ = 512
RESP = 96
NS_ITERS = 3


norm_epsilon = 1e-05
rope_base = 1000000.0
pref_beta = 2.0
clip_limit = 0.05
muon_decay = 0.95
muon_rate = 0.5
first_decay = 0.9
second_decay = 0.95
adam_rate = 0.02
adam_epsilon = 1e-08
weight_decay = 0.1
leading_coefficient = 3.4445
coef_second = -4.775
coef_third = 2.0315
ortho_epsilon = 1e-07
masked_score = -1e30


def rms_scale(inputs, gain):
    mean_square = jnp.mean(inputs * inputs, axis=-1, keepdims=True)
    return inputs * lax.rsqrt(mean_square + norm_epsilon) * gain


def rope_tables(length, half):
    position = jnp.arange(length, dtype=jnp.float32)
    inverse = rope_base ** (-jnp.arange(half, dtype=jnp.float32) / half)
    angle = position[:, None] * inverse[None, :]
    return (jnp.cos(angle)[:, None, :], jnp.sin(angle)[:, None, :])


def rotate(inputs, cosine, sine):
    half = inputs.shape[-1] // 2
    first = inputs[..., :half]
    second = inputs[..., half:]
    return jnp.concatenate(
        [first * cosine - second * sine, second * cosine + first * sine], axis=-1
    )


def dense(inputs, weight):
    return lax.dot_general(
        inputs, weight, (((1,), (1,)), ((), ())), preferred_element_type=jnp.float32
    )


def outer(grads, inputs):
    return lax.dot_general(
        grads, inputs, (((0,), (0,)), ((), ())), preferred_element_type=jnp.float32
    )


def back_dense(grads, weight):
    return jnp.dot(grads, weight, preferred_element_type=jnp.float32)


def delayed(values, offset):
    return jnp.pad(values, ((offset, 0), (0, 0)))[: values.shape[0]]


def advanced(values, offset):
    return jnp.pad(values, ((0, offset), (0, 0)))[offset:]


def norm_back(inputs, gain, grad_out):
    _, pullback = jax.vjp(rms_scale, inputs, gain)
    return pullback(grad_out)


def low_copy(values):
    return lax.optimization_barrier(values.astype(jnp.bfloat16)).astype(jnp.float32)


def adam_step(master, first, second, grad, factor, count):
    scaled = factor * grad
    first_new = first_decay * first + (1.0 - first_decay) * scaled
    second_new = second_decay * second + (1.0 - second_decay) * scaled * scaled
    steps = count.astype(jnp.float32)
    first_hat = first_new / (1.0 - first_decay**steps)
    second_hat = second_new / (1.0 - second_decay**steps)
    change = -adam_rate * (
        first_hat / (jnp.sqrt(second_hat) + adam_epsilon) + weight_decay * master
    )
    return (change, first_new, second_new)

DP = ("chip", "core")
ALL = ("chip", "core", "vocab")
SLOTS = 32


def exchanged(rows):
    return lax.all_to_all(rows, ALL, 0, 0, tiled=True)


def spread(values):
    count = lax.axis_size(ALL)
    return lax.all_to_all(jnp.broadcast_to(values[None], (count,) + values.shape), ALL, 0, 0)


def turned(values, axis, step):
    count = lax.axis_size(axis)
    return lax.ppermute(values, axis, [(i, (i + step) % count) for i in range(count)])


def block_at(blocks, index):
    return lax.dynamic_index_in_dim(blocks, index % blocks.shape[0], 0, keepdims=False)


def handed_out(blocks, axis):
    place, count = lax.axis_index(axis), lax.axis_size(axis)
    return [block_at(blocks, place)] + [
        turned(block_at(blocks, place + step), axis, step) for step in range(1, count)
    ]


def handed_back(pieces, axis):
    return [pieces[0]] + [turned(pieces[step], axis, -step) for step in range(1, len(pieces))]


def gathered(values, axis):
    return [values] + [turned(values, axis, step) for step in range(1, lax.axis_size(axis))]


def placed_before(pieces, axis):
    pieces, place = jnp.stack(pieces), lax.axis_index(axis)
    return jnp.stack([block_at(pieces, place - j) for j in range(pieces.shape[0])])


def placed_after(pieces, axis):
    pieces, place = jnp.stack(pieces), lax.axis_index(axis)
    return jnp.stack([block_at(pieces, j - place) for j in range(pieces.shape[0])])


def added(pieces):
    total = pieces[0].astype(jnp.float32)
    for piece in pieces[1:]:
        total = total + piece.astype(jnp.float32)
    return total


def other_core(values):
    return lax.ppermute(values, "core", [(0, 1), (1, 0)])


def pair_sum(halves, core):
    given = lax.dynamic_index_in_dim(halves, 1 - core, 0, keepdims=False)
    kept = lax.dynamic_index_in_dim(halves, core, 0, keepdims=False)
    total = kept.astype(jnp.float32) + other_core(given).astype(jnp.float32)
    return total.astype(jnp.bfloat16)


def chip_sum(blocks):
    return added(handed_out(blocks, "chip"))


def group_sum(values, core):
    rows = values.shape[0] // 2
    chips = lax.axis_size("chip")
    half = pair_sum(values.reshape(2, rows, -1), core).reshape(chips, rows // chips, -1)
    part = chip_sum(half).astype(jnp.bfloat16)
    half = placed_before(gathered(part, "chip"), "chip").reshape(rows, -1)
    other = other_core(half)
    first = jnp.where(core == 0, half, other)
    second = jnp.where(core == 0, other, half)
    return jnp.concatenate([first, second], axis=0)


def member_gather(values):
    return jnp.concatenate(gathered(values, "vocab"), axis=0)


def member_return(pieces):
    return added(handed_back(pieces, "vocab"))


def member_scatter(blocks):
    return added(handed_out(blocks, "vocab"))


def onehot_rows(index, count):
    return (index[:, None] == jnp.arange(count)[None, :]).astype(jnp.bfloat16)


def token_slots(ids, block_rows):
    owner = ids // block_rows
    place = jnp.arange(ids.shape[0])
    earlier = place[:, None] > place[None, :]
    equal = ids[:, None] == ids[None, :]
    first = jnp.logical_not(jnp.any(equal & earlier, axis=1))
    ahead = (owner[:, None] == owner[None, :]) & earlier & first[None, :]
    rank = jnp.sum(ahead.astype(jnp.int32), axis=1)
    slot = jnp.sum(jnp.where(equal & first[None, :], rank[None, :], 0), axis=1)
    return owner, first, slot


def round_keys(owner, slot, turn):
    within = slot - turn * SLOTS
    return jnp.where((within >= 0) & (within < SLOTS), owner * SLOTS + within, -1)


def round_asks(keys, first, local, count):
    hits = (keys[None, :] == jnp.arange(count)[:, None]) & first[None, :]
    return jnp.sum(jnp.where(hits, local[None, :] + 1, 0), axis=1) - 1


def square_product(left, right):
    return jnp.dot(
        left.astype(jnp.bfloat16), right.astype(jnp.bfloat16), preferred_element_type=jnp.float32
    )


def rest_kernel(
    gram_ref, rest_ref, gram_scratch, change_scratch, rest_scratch, grams, change_b, rest_b
):
    lead = leading_coefficient
    size = gram_ref.shape[0]
    tile = 256

    def dot(left, right):
        return jnp.dot(left, right, preferred_element_type=jnp.float32)

    @pl.loop(0, size // tile)
    def _(step):
        rows = pl.ds(pl.multiple_of(step * tile, tile), tile)
        gram_scratch[rows, :] = gram_ref[rows, :]
        grams[0, rows, :] = gram_ref[rows, :].astype(jnp.bfloat16)

    power = 1.0
    for turn in range(NS_ITERS):
        now, later = turn % 2, (turn + 1) % 2

        @pl.loop(0, size // tile)
        def _(step):
            rows = pl.ds(pl.multiple_of(step * tile, tile), tile)
            change = coef_second * gram_scratch[rows, :] + coef_third * dot(
                grams[now, rows, :], grams[now]
            )
            change_scratch[rows, :] = change
            change_b[rows, :] = change.astype(jnp.bfloat16)

        @pl.loop(0, size // tile)
        def _(step):
            rows = pl.ds(pl.multiple_of(step * tile, tile), tile)
            if turn == 0:
                rest = change_scratch[rows, :]
            else:
                rest = (
                    lead * rest_scratch[rows, :]
                    + power * change_scratch[rows, :]
                    + dot(rest_b[rows, :], change_b[...])
                )
            if turn + 1 < NS_ITERS:
                rest_scratch[rows, :] = rest
                rest_b[rows, :] = rest.astype(jnp.bfloat16)
                mixed = dot(change_b[rows, :], grams[now])
                gram = (
                    lead * lead * gram_scratch[rows, :]
                    + 2.0 * lead * mixed
                    + dot(mixed.astype(jnp.bfloat16), change_b[...])
                )
                gram_scratch[rows, :] = gram
                grams[later, rows, :] = gram.astype(jnp.bfloat16)
            else:
                rest_ref[rows, :] = rest.astype(jnp.bfloat16)

        power = power * lead


def ortho_rest(gram):
    size = gram.shape[0]
    wide = pltpu.VMEM((size, size), jnp.float32)
    narrow = pltpu.VMEM((size, size), jnp.bfloat16)
    return pl.pallas_call(
        rest_kernel,
        out_shape=jax.ShapeDtypeStruct((size, size), jnp.bfloat16),
        in_specs=[pl.BlockSpec(memory_space=pltpu.VMEM)],
        out_specs=pl.BlockSpec(memory_space=pltpu.VMEM),
        scratch_shapes=[
            wide,
            wide,
            wide,
            pltpu.VMEM((2, size, size), jnp.bfloat16),
            narrow,
            narrow,
        ],
        compiler_params=pltpu.CompilerParams(vmem_limit_bytes=44 * 1024 * 1024),
        cost_estimate=pl.CostEstimate(
            flops=18 * size**3, bytes_accessed=6 * size * size, transcendentals=0
        ),
    )(gram)


def logits_kernel(target_ref, answers_ref, table_ref, shares_ref, stats_ref, logits):
    rows, width = logits.shape
    piece = 256
    target = target_ref[...]
    top = jnp.full((8, width), -jnp.inf, jnp.float32)
    total = jnp.zeros((8, width), jnp.float32)
    picked = jnp.zeros((8, width), jnp.float32)
    for first in range(0, rows, piece):
        scores = lax.dot_general(
            table_ref[first : first + piece, :],
            answers_ref[...],
            (((1,), (1,)), ((), ())),
            preferred_element_type=jnp.float32,
        )
        logits[first : first + piece, :] = scores
        top = jnp.maximum(top, jnp.max(scores.reshape(-1, 8, width), axis=0))
    top = jnp.max(top, axis=0, keepdims=True)
    for first in range(0, rows, piece):
        scores = logits[first : first + piece, :]
        share = jnp.exp(scores - top)
        shares_ref[first : first + piece, :] = share.astype(jnp.bfloat16)
        total = total + jnp.sum(share.reshape(-1, 8, width), axis=0)
        place = lax.broadcasted_iota(jnp.int32, (piece, width), 0)
        hit = jnp.where(place == target - first, scores, 0.0)
        picked = picked + jnp.sum(hit.reshape(-1, 8, width), axis=0)
    stats_ref[0:1, :] = top
    stats_ref[1:2, :] = jnp.sum(total, axis=0, keepdims=True)
    stats_ref[2:3, :] = jnp.sum(picked, axis=0, keepdims=True)
    stats_ref[3:8, :] = jnp.zeros((5, width), jnp.float32)


def answer_shares(target, answers, table):
    count, rows = answers.shape[0], table.shape[0]
    tile = 256
    return pl.pallas_call(
        logits_kernel,
        grid=(count // tile,),
        in_specs=[
            pl.BlockSpec((1, tile), lambda i: (0, i)),
            pl.BlockSpec((tile, D), lambda i: (i, 0)),
            pl.BlockSpec((rows, D), lambda i: (0, 0)),
        ],
        out_specs=[
            pl.BlockSpec((rows, tile), lambda i: (0, i)),
            pl.BlockSpec((8, tile), lambda i: (0, i)),
        ],
        out_shape=[
            jax.ShapeDtypeStruct((rows, count), jnp.bfloat16),
            jax.ShapeDtypeStruct((8, count), jnp.float32),
        ],
        scratch_shapes=[pltpu.VMEM((rows, tile), jnp.float32)],
        compiler_params=pltpu.CompilerParams(vmem_limit_bytes=40 * 1024 * 1024),
        cost_estimate=pl.CostEstimate(
            flops=2 * count * rows * D,
            bytes_accessed=2 * count * (rows + D),
            transcendentals=count * rows,
        ),
    )(target, answers, table)


def logit_grads(place, target, scale, value, shares):
    return jnp.where(place == target, value, shares.astype(jnp.float32) * scale).astype(jnp.bfloat16)


def grads_kernel(core_ref, target_ref, scale_ref, value_ref, shares_ref, table_ref, grads_ref):
    place = lax.broadcasted_iota(jnp.int32, shares_ref.shape, 0)
    grads = logit_grads(place, target_ref[...], scale_ref[...], value_ref[...], shares_ref[...])
    grads_ref[...] = lax.dot_general(
        grads, table_ref[...], (((0,), (0,)), ((), ())), preferred_element_type=jnp.float32
    ).astype(jnp.bfloat16)


def answer_grads(core, target, scale, value, shares, table, width):
    rows, count = shares.shape
    steps = count // (2 * width)
    row = pl.BlockSpec((1, width), lambda i, core_ref: (0, 2 * i + core_ref[0]))
    return pl.pallas_call(
        grads_kernel,
        grid_spec=pltpu.PrefetchScalarGridSpec(
            num_scalar_prefetch=1,
            grid=(steps,),
            in_specs=[
                row,
                row,
                row,
                pl.BlockSpec((rows, width), lambda i, core_ref: (0, 2 * i + core_ref[0])),
                pl.BlockSpec((rows, D), lambda i, core_ref: (0, 0)),
            ],
            out_specs=pl.BlockSpec((width, D), lambda i, core_ref: (i, 0)),
        ),
        out_shape=jax.ShapeDtypeStruct((steps * width, D), jnp.bfloat16),
        compiler_params=pltpu.CompilerParams(vmem_limit_bytes=40 * 1024 * 1024),
        cost_estimate=pl.CostEstimate(
            flops=2 * steps * width * rows * D,
            bytes_accessed=2 * steps * width * (rows + D),
            transcendentals=0,
        ),
    )(core.reshape(1), target, scale, value, shares, table)


def body(
    token_ids,
    seq_lengths,
    pair_order,
    table_master,
    table_first,
    table_second,
    square_master,
    square_moment,
    wide_master,
    wide_moment,
    vector_master,
    vector_first,
    vector_second,
    norm_gains,
    norm_first,
    norm_second,
    adam_count,
):
    members = lax.axis_size("vocab")
    member = lax.axis_index("vocab")
    block_rows = table_master.shape[0]
    lengths = seq_lengths[0]
    order = pair_order[0]
    groups_per = HEADS // KV
    scale = HD ** (-0.5)

    core = lax.axis_index("core")
    devices = lax.axis_size(ALL)
    device = lax.axis_index(ALL)
    groups = devices // members

    own_ids = lax.dynamic_index_in_dim(token_ids, member, 0, keepdims=False)
    own_length = lengths[member]
    start = own_length - 1 - RESP
    owner, first_seen, slot = token_slots(own_ids, block_rows)
    local_ids = own_ids % block_rows
    keys = round_keys(owner, slot, 0)
    asks = round_asks(keys, first_seen, local_ids, devices * SLOTS)
    own_targets = lax.dynamic_slice_in_dim(own_ids, start + 1, RESP, 0)
    vector_low = vector_master.astype(jnp.bfloat16).astype(jnp.float32)
    shared_notes = jnp.concatenate(
        [
            vector_low.reshape(-1),
            jnp.concatenate([own_targets, order, jnp.max(slot)[None] + 1]).astype(jnp.float32),
        ]
    )
    notes = jnp.concatenate(
        [
            asks.reshape(devices, SLOTS).astype(jnp.float32),
            jnp.broadcast_to(shared_notes[None, :], (devices, shared_notes.size)),
        ],
        axis=1,
    )
    notes = exchanged(notes)
    square_b = lax.all_gather(square_master.astype(jnp.bfloat16), ALL, axis=1, tiled=True)
    wide_b = lax.all_gather(wide_master.astype(jnp.bfloat16), DP, axis=1, tiled=True)
    hidden_units = wide_b.shape[1]
    asked = notes[:, :SLOTS].astype(jnp.int32).reshape(-1)
    gains = (
        notes[:, SLOTS : SLOTS + vector_low.size]
        .reshape(devices, vector_low.shape[0], vector_low.shape[1])
        .transpose(1, 0, 2)
        .reshape(vector_low.shape[0], D)
    )
    numbers = notes[:, SLOTS + vector_low.size :].astype(jnp.int32)
    targets = numbers[:, :RESP].reshape(-1)
    orders = numbers[:, RESP : RESP + members].reshape(groups, members, members)[:, 0]
    turns = (jnp.max(numbers[:, RESP + members]) + SLOTS - 1) // SLOTS
    slots = jnp.arange(members)
    chosen_mask = (orders[:, 0::2, None] == slots[None, None, :]).astype(jnp.float32)
    rejected_mask = (orders[:, 1::2, None] == slots[None, None, :]).astype(jnp.float32)
    pair_rows = jnp.sum(
        (chosen_mask + rejected_mask)[:, :, :, None] * (chosen_mask - rejected_mask)[:, :, None, :],
        axis=1,
    )
    same_group = jnp.arange(groups)[:, None] == jnp.arange(groups)[None, :]
    pair_rows = jnp.where(same_group[:, None, :, None], pair_rows[:, :, None, :], 0.0)
    pair_rows = pair_rows.reshape(devices, devices) * (pref_beta / RESP)
    chosen_sign = jnp.sum(chosen_mask - rejected_mask, axis=1).reshape(devices, 1)
    table_b = table_master.astype(jnp.bfloat16)
    head_gains = low_copy(norm_gains)
    cosine, sine = rope_tables(SEQ, HD // 2)

    def fetched(wanted, row_keys):
        rows = jnp.dot(
            onehot_rows(wanted, block_rows), table_b, preferred_element_type=jnp.float32
        ).astype(jnp.bfloat16)
        return jnp.dot(
            onehot_rows(row_keys, devices * SLOTS),
            exchanged(rows),
            preferred_element_type=jnp.float32,
        )

    def later_round(turn):
        later_keys = round_keys(owner, slot, turn)
        later_asks = round_asks(later_keys, first_seen, local_ids, devices * SLOTS)
        return later_keys, exchanged(later_asks)

    def fetch_more(turn, rows):
        later_keys, later_asked = later_round(turn)
        return rows + fetched(later_asked, later_keys)

    hidden0 = lax.fori_loop(1, turns, fetch_more, fetched(asked, keys))
    act1 = rms_scale(hidden0, gains[0]).astype(jnp.bfloat16)
    inner = dense(act1, square_b[0:3].reshape(3 * D, D))
    entry = inner[:, :D]
    leave = inner[:, D : 2 * D]
    conv_in = inner[:, 2 * D :]
    product = entry * conv_in
    convolved = gains[4] * product + gains[5] * delayed(product, 1) + gains[6] * delayed(product, 2)
    mixer = (leave * convolved).astype(jnp.bfloat16)
    hidden1 = hidden0 + dense(mixer, square_b[3])
    act2 = rms_scale(hidden1, gains[1]).astype(jnp.bfloat16)

    def answers(values):
        return lax.dynamic_slice_in_dim(values, start, RESP, 0)

    def placed(values):
        return lax.dynamic_update_slice_in_dim(
            jnp.zeros((SEQ, values.shape[1]), values.dtype), values, start, 0
        )

    answer_act2 = answers(act2)
    query_raw = dense(answer_act2, square_b[4]).reshape(RESP, HEADS, HD)
    pair_raw = dense(act2, square_b[5])
    key_raw = pair_raw[:, : KV * HD].reshape(SEQ, KV, HD)
    value_b = pair_raw[:, KV * HD :].astype(jnp.bfloat16).reshape(SEQ, KV, HD)

    answer_cosine, answer_sine = answers(cosine), answers(sine)

    def query_prep(raw, gain):
        return rotate(rms_scale(raw, gain), answer_cosine, answer_sine)

    def key_prep(raw, gain):
        return rotate(rms_scale(raw, gain), cosine, sine)

    query_b = (
        query_prep(query_raw, head_gains[0]).astype(jnp.bfloat16).reshape(RESP, KV, groups_per, HD)
    )
    key_b = key_prep(key_raw, head_gains[1]).astype(jnp.bfloat16)
    causal = start + jnp.arange(RESP)[:, None] >= jnp.arange(SEQ)[None, :]
    scores = (
        jnp.einsum("sgrd,tgd->grst", query_b, key_b, preferred_element_type=jnp.float32) * scale
    )
    scores = jnp.where(causal, scores, masked_score)
    peak = jnp.max(scores, axis=-1, keepdims=True)
    expo = jnp.exp(scores - peak)
    total = jnp.sum(expo, axis=-1, keepdims=True)
    log_norm = peak + jnp.log(total)
    probs_b = (expo / total).astype(jnp.bfloat16)
    attended = jnp.einsum(
        "grst,tgd->sgrd", probs_b, value_b, preferred_element_type=jnp.float32
    ).reshape(RESP, D)
    attended_b = attended.astype(jnp.bfloat16)
    hidden2 = answers(hidden1) + dense(attended_b, square_b[6])
    act3 = member_gather(rms_scale(hidden2, gains[2]).astype(jnp.bfloat16))
    gate_up = dense(act3, wide_b[0:2].reshape(2 * hidden_units, D))
    gate_part = gate_up[:, :hidden_units]
    up_part = gate_up[:, hidden_units:]
    inner_b = (jax.nn.silu(gate_part) * up_part).astype(jnp.bfloat16)
    ffn_part = jnp.dot(inner_b, wide_b[2], preferred_element_type=jnp.float32)
    hidden3 = hidden2 + member_return(ffn_part.astype(jnp.bfloat16).reshape(members, RESP, D))
    final_b = rms_scale(hidden3, gains[3]).astype(jnp.bfloat16)
    response_tokens = lax.all_gather(final_b, ALL, axis=0, tiled=True)
    local_target = jnp.where(targets // block_rows == device, targets % block_rows, -1)[None, :]
    shares, own_stats = answer_shares(local_target, response_tokens, table_b)
    stats = own_stats[:3].reshape(3, devices, RESP).transpose(1, 0, 2)
    stats = exchanged(stats)
    top = jnp.max(stats[:, 0], axis=0)
    exp_total = jnp.sum(stats[:, 1] * jnp.exp(stats[:, 0] - top[None, :]), axis=0)
    own_log_total = top + jnp.log(exp_total)
    own_logp = jnp.sum(jnp.sum(stats[:, 2], axis=0) - own_log_total)
    joined = spread(jnp.concatenate([own_log_total, own_logp[None]]))
    log_total = joined[:, :RESP].reshape(1, -1)
    margin = jnp.sum(pair_rows * joined[:, RESP][None, :], axis=1, keepdims=True)
    pair_loss = 0.5 * jnp.sum(jax.nn.softplus(-margin))
    grad_logp = chosen_sign * jax.nn.sigmoid(-margin) * (-pref_beta / RESP)
    row_weight = jnp.broadcast_to(grad_logp, (devices, RESP)).reshape(1, -1)
    share_scale = -row_weight * jnp.exp(own_stats[0:1] - log_total)
    target_value = row_weight * (1.0 - jnp.exp(own_stats[2:3] - log_total))
    given, kept = (
        answer_grads(
            which, local_target, share_scale, target_value, shares, table_b, members * RESP
        )
        for which in (1 - core, core)
    )
    grad_answer_pair = (kept.astype(jnp.float32) + other_core(given).astype(jnp.float32)).astype(
        jnp.bfloat16
    )
    grad_answer_group = chip_sum(grad_answer_pair.reshape(groups // 2, members * RESP, D))
    grad_table = jnp.dot(
        logit_grads(
            jnp.arange(block_rows)[:, None], local_target, share_scale, target_value, shares
        ),
        response_tokens,
        preferred_element_type=jnp.float32,
    )
    grad_answer_group, grad_table = lax.optimization_barrier(
        (grad_answer_group.astype(jnp.bfloat16), grad_table)
    )
    grad_final = member_scatter(grad_answer_group.reshape(members, RESP, D))
    grad_hidden3, grad_gain3 = norm_back(hidden3, gains[3], grad_final)
    grad_ffn_out = member_gather(grad_hidden3.astype(jnp.bfloat16))
    grad_inner = dense(grad_ffn_out, wide_b[2])
    grad_down_w = outer(inner_b, grad_ffn_out)
    _, silu_pull = jax.vjp(lambda gate_in, up_in: jax.nn.silu(gate_in) * up_in, gate_part, up_part)
    grad_gate, grad_up = silu_pull(grad_inner)
    grad_gate_up = jnp.concatenate([grad_gate, grad_up], axis=1).astype(jnp.bfloat16)
    grad_act3_part = back_dense(grad_gate_up, wide_b[0:2].reshape(2 * hidden_units, D))
    grad_act3 = member_return(grad_act3_part.astype(jnp.bfloat16).reshape(members, RESP, D))
    grad_gate_up_w = outer(grad_gate_up, act3)
    grad_norm2, grad_gain2 = norm_back(hidden2, gains[2], grad_act3)
    grad_hidden2 = grad_hidden3 + grad_norm2
    grad_attn_out = grad_hidden2.astype(jnp.bfloat16)
    grad_attended = (
        back_dense(grad_attn_out, square_b[6])
        .astype(jnp.bfloat16)
        .reshape(RESP, KV, groups_per, HD)
    )
    grad_out_w = outer(grad_attn_out, attended_b)
    scores = (
        jnp.einsum("sgrd,tgd->grst", query_b, key_b, preferred_element_type=jnp.float32) * scale
    )
    probs = jnp.exp(jnp.where(causal, scores, masked_score) - log_norm)
    grad_probs = jnp.einsum(
        "sgrd,tgd->grst", grad_attended, value_b, preferred_element_type=jnp.float32
    )
    grad_values = jnp.einsum(
        "grst,sgrd->tgd", probs_b, grad_attended, preferred_element_type=jnp.float32
    )
    delta = jnp.sum(probs * grad_probs, axis=-1, keepdims=True)
    grad_scores = (probs * (grad_probs - delta)).astype(jnp.bfloat16)
    grad_query = (
        jnp.einsum("grst,tgd->sgrd", grad_scores, key_b, preferred_element_type=jnp.float32) * scale
    ).reshape(RESP, HEADS, HD)
    grad_keys = (
        jnp.einsum("grst,sgrd->tgd", grad_scores, query_b, preferred_element_type=jnp.float32)
        * scale
    )
    _, query_pull = jax.vjp(query_prep, query_raw, head_gains[0])
    grad_query_raw, grad_query_gain = query_pull(grad_query)
    _, key_pull = jax.vjp(key_prep, key_raw, head_gains[1])
    grad_key_raw, grad_key_gain = key_pull(grad_keys)
    grad_query_b = grad_query_raw.reshape(RESP, D).astype(jnp.bfloat16)
    grad_pair_b = jnp.concatenate(
        [grad_key_raw.reshape(SEQ, KV * HD), grad_values.reshape(SEQ, KV * HD)], axis=1
    ).astype(jnp.bfloat16)
    grad_act2 = back_dense(grad_pair_b, square_b[5]) + placed(back_dense(grad_query_b, square_b[4]))
    grad_query_w = outer(grad_query_b, answer_act2)
    grad_pair_w = outer(grad_pair_b, act2)
    grad_norm1, grad_gain1 = norm_back(hidden1, gains[1], grad_act2)
    grad_hidden1 = placed(grad_hidden2) + grad_norm1
    squares, square_rows = square_master.shape[0], square_master.shape[1]
    wides, wide_rows = wide_master.shape[0], wide_master.shape[1]
    per_member = -(-squares // members)
    group_rows = members * square_rows

    def by_member(values):
        values = jnp.pad(values, ((0, per_member * members - squares), (0, 0), (0, 0)))
        return values.reshape(per_member, members, -1, D).transpose(1, 0, 2, 3)

    def wide_by_member(values):
        return jnp.pad(values, ((0, members - wides), (0, 0), (0, 0)))

    moment_jobs = jnp.concatenate(
        [
            wide_by_member(wide_moment.astype(jnp.bfloat16)),
            by_member(square_moment.astype(jnp.bfloat16)).reshape(members, -1, D),
        ],
        axis=1,
    )
    moment_jobs = jnp.stack(handed_out(moment_jobs, "vocab"))
    grad_hidden1, moment_jobs = lax.optimization_barrier((grad_hidden1, moment_jobs))
    wide_moment_job = moment_jobs[:, :wide_rows]
    square_moment_job = placed_before(list(moment_jobs[:, wide_rows:]), "vocab")
    square_moment_job = square_moment_job.reshape(members, per_member, square_rows, D)
    square_moment_job = square_moment_job.transpose(1, 0, 2, 3).reshape(per_member, group_rows, D)
    grad_mix_out = grad_hidden1.astype(jnp.bfloat16)
    grad_mixer = back_dense(grad_mix_out, square_b[3])
    grad_mixer_w = outer(grad_mix_out, mixer)
    grad_leave = grad_mixer * convolved
    grad_conv = grad_mixer * leave
    grad_tap0 = jnp.sum(grad_conv * product, axis=0)
    grad_tap1 = jnp.sum(grad_conv * delayed(product, 1), axis=0)
    grad_tap2 = jnp.sum(grad_conv * delayed(product, 2), axis=0)
    grad_product = (
        gains[4] * grad_conv + gains[5] * advanced(grad_conv, 1) + gains[6] * advanced(grad_conv, 2)
    )
    grad_inner_b = jnp.concatenate(
        [grad_product * conv_in, grad_leave, grad_product * entry], axis=1
    ).astype(jnp.bfloat16)
    grad_act1 = back_dense(grad_inner_b, square_b[0:3].reshape(3 * D, D))
    grad_inner_w = outer(grad_inner_b, act1)
    grad_norm0, grad_gain0 = norm_back(hidden0, gains[0], grad_act1)
    grad_embed_b = (grad_hidden1 + grad_norm0).astype(jnp.bfloat16)

    grad_square = jnp.concatenate(
        [
            grad_inner_w.astype(jnp.bfloat16).reshape(3, D, D),
            grad_mixer_w.astype(jnp.bfloat16)[None],
            grad_query_w.astype(jnp.bfloat16)[None],
            grad_pair_w.astype(jnp.bfloat16)[None],
            grad_out_w.astype(jnp.bfloat16)[None],
        ],
        axis=0,
    )
    grad_vector = jnp.stack(
        [grad_gain0, grad_gain1, grad_gain2, grad_gain3, grad_tap0, grad_tap1, grad_tap2]
    )
    grad_head_gains = jnp.stack([grad_query_gain, grad_key_gain])
    grad_wide = jnp.concatenate(
        [
            grad_gate_up_w.astype(jnp.bfloat16).reshape(2, hidden_units, D),
            grad_down_w.astype(jnp.bfloat16)[None],
        ],
        axis=0,
    )
    share_wide_b = lax.psum_scatter(grad_wide, DP, scatter_dimension=1, tiled=True)
    share_wide = share_wide_b.astype(jnp.float32)
    grad_square, share_wide_b = lax.optimization_barrier((grad_square, share_wide_b))
    wide_grad_job = jnp.stack(handed_out(wide_by_member(share_wide_b), "vocab"))
    group_square = lax.psum_scatter(grad_square, DP, scatter_dimension=1, tiled=True)
    square_grad_job = member_scatter(by_member(group_square))

    def from_members(values):
        values = values.reshape(per_member, members, square_rows, D).transpose(1, 0, 2, 3)
        values = placed_before(handed_out(values.astype(jnp.bfloat16), "vocab"), "vocab")
        values = values.transpose(1, 0, 2, 3).reshape(per_member * members, square_rows, D)
        return values[:squares].astype(jnp.float32)

    share_square = from_members(square_grad_job)

    def returned(row_keys):
        rows = outer(onehot_rows(row_keys, devices * SLOTS), grad_embed_b)
        return exchanged(rows.astype(jnp.bfloat16))

    def put(wanted, rows):
        return outer(onehot_rows(wanted, block_rows), rows)

    def return_more(turn, total):
        later_keys, later_asked = later_round(turn)
        return total + put(later_asked, returned(later_keys))

    returned_rows, wide_grad_job = lax.optimization_barrier((returned(keys), wide_grad_job))
    share_table = lax.fori_loop(1, turns, return_more, grad_table + put(asked, returned_rows))
    width = vector_master.shape[1]
    vector_notes = grad_vector.reshape(-1, devices, width).transpose(1, 0, 2).reshape(devices, -1)
    vector_notes = jnp.concatenate(
        [
            vector_notes,
            jnp.broadcast_to(grad_head_gains.reshape(1, -1), (devices, grad_head_gains.size)),
        ],
        axis=1,
    )
    vector_notes = jnp.sum(exchanged(vector_notes), axis=0)
    share_vector = vector_notes[: vector_master.size].reshape(vector_master.shape)
    gains_total = vector_notes[vector_master.size :].reshape(grad_head_gains.shape)

    def job_sums(values):
        sums = jnp.sum(values, axis=(1, 2))[:, None]
        sums = jnp.where(jnp.arange(members)[None, :] == member, sums, 0.0)
        return sums.reshape(-1)[:squares]

    moment_squares = jnp.concatenate(
        [
            jnp.sum(square_moment * square_moment, axis=(1, 2)),
            jnp.sum(wide_moment * wide_moment, axis=(1, 2)),
        ]
    )
    moment_cross = jnp.concatenate(
        [
            job_sums(square_moment_job.astype(jnp.float32) * square_grad_job),
            jnp.sum(wide_moment * share_wide, axis=(1, 2)),
        ]
    )
    grad_squares = jnp.concatenate(
        [
            job_sums(square_grad_job * square_grad_job),
            jnp.sum(share_wide * share_wide, axis=(1, 2)),
        ]
    )
    moment_stats = jnp.stack([moment_squares, moment_cross, grad_squares])
    own_squares = (
        jnp.sum(grad_squares)
        + jnp.sum(share_vector * share_vector)
        + jnp.sum(share_table * share_table)
    )
    sums = jnp.concatenate([moment_stats.reshape(-1), own_squares[None]])
    sums = jnp.sum(spread(sums), axis=0)
    stats_total = sums[:-1].reshape(moment_stats.shape)
    grad_norm = jnp.sqrt(sums[-1] + jnp.sum(gains_total * gains_total))
    factor = jnp.minimum(1.0, clip_limit / grad_norm)
    square_moment_new = muon_decay * square_moment + (1.0 - muon_decay) * (factor * share_square)
    wide_moment_new = muon_decay * wide_moment + (1.0 - muon_decay) * (factor * share_wide)
    moment_norm = jnp.sqrt(
        muon_decay * muon_decay * stats_total[0]
        + 2.0 * muon_decay * (1.0 - muon_decay) * factor * stats_total[1]
        + (1.0 - muon_decay) * (1.0 - muon_decay) * factor * factor * stats_total[2]
    )
    ortho_square = square_moment_new / (moment_norm[:7][:, None, None] + ortho_epsilon)
    ortho_wide = wide_moment_new / (moment_norm[7:][:, None, None] + ortho_epsilon)
    table_step, table_first_new, table_second_new = adam_step(
        table_master, table_first, table_second, share_table, factor, adam_count
    )
    wide_inverse = 1.0 / (moment_norm[squares:] + ortho_epsilon)
    wide_inverse = jnp.pad(wide_inverse, (0, members - wides))[member]
    square_inverse = 1.0 / (moment_norm[:squares] + ortho_epsilon)
    square_inverse = jnp.pad(square_inverse, (0, per_member * members - squares))
    square_inverse = square_inverse.reshape(per_member, members)[:, member][:, None, None]
    square_part = (muon_decay * square_inverse) * square_moment_job.astype(jnp.float32) + (
        (1.0 - muon_decay) * factor * square_inverse
    ) * square_grad_job
    square_part, wide_grad_job = lax.optimization_barrier(
        (square_part.astype(jnp.bfloat16), wide_grad_job)
    )
    square_part = jnp.pad(square_part, ((0, groups // 2 - per_member), (0, 0), (0, 0)))
    square_half = jnp.concatenate(handed_out(square_part, "chip"), axis=0)
    square_job = jnp.concatenate([square_half, other_core(square_half)], axis=0)
    wide_job = (
        (muon_decay * wide_inverse) * wide_moment_job.astype(jnp.float32)
        + ((1.0 - muon_decay) * factor * wide_inverse) * wide_grad_job.astype(jnp.float32)
    )
    wide_job = wide_job.reshape(members * wide_rows, D).astype(jnp.bfloat16)
    wide_gram = group_sum(outer(wide_job, wide_job).astype(jnp.bfloat16), core)
    square_gram = outer(square_job, square_job)
    gram = jnp.where(core == 0, wide_gram.astype(jnp.float32), square_gram)
    rest_b = ortho_rest(gram)
    power = leading_coefficient**NS_ITERS
    wide_rest = jnp.where(core == 0, rest_b, other_core(rest_b))
    back_square = square_product(square_job, rest_b).astype(jnp.bfloat16)
    half_rows = square_half.shape[0]
    back_square = jnp.where(
        core == 0, other_core(back_square[half_rows:]), back_square[:half_rows]
    )
    back_square = handed_back(list(back_square.reshape(-1, group_rows, D)), "chip")
    back_square = placed_after(back_square, "chip")[:per_member]
    back_wide = square_product(wide_job, wide_rest).astype(jnp.bfloat16)
    back_wide = handed_back(list(back_wide.reshape(members, wide_rows, D)), "vocab")
    back_wide = placed_after(back_wide, "vocab")[:wides]
    back_square, back_wide = lax.optimization_barrier((back_square, back_wide))
    back_square = from_members(back_square)
    ortho_wide = power * ortho_wide + back_wide.astype(jnp.float32)
    ortho_square = power * ortho_square + back_square
    wide_scale = jnp.array([math.sqrt(FF / D), math.sqrt(FF / D), 1.0], jnp.float32)
    square_new = square_master - muon_rate * ortho_square
    wide_new = wide_master - muon_rate * wide_scale[:, None, None] * ortho_wide
    vector_step, vector_first_new, vector_second_new = adam_step(
        vector_master, vector_first, vector_second, share_vector, factor, adam_count
    )
    norm_step, norm_first_new, norm_second_new = adam_step(
        norm_gains, norm_first, norm_second, gains_total, factor, adam_count
    )
    return (
        pair_loss,
        grad_norm,
        square_new,
        square_moment_new,
        square_new.astype(jnp.bfloat16),
        wide_new,
        wide_moment_new,
        wide_new.astype(jnp.bfloat16),
        table_step,
        table_first_new,
        table_second_new,
        vector_step,
        vector_first_new,
        vector_second_new,
        norm_step,
        norm_first_new,
        norm_second_new,
        share_vector[3],
    )


def solution(mesh):
    groups, members = mesh.shape["dp"], mesh.shape["vocab"]
    cores = 2
    split_mesh = Mesh(mesh.devices.reshape(groups // cores, cores, members), ALL)
    return jax.shard_map(
        body,
        mesh=split_mesh,
        in_specs=(
            P(DP, None),
            P(DP, None),
            P(DP, None),
            P(ALL, None),
            P(ALL, None),
            P(ALL, None),
            P(None, ALL, None),
            P(None, ALL, None),
            P(None, ALL, None),
            P(None, ALL, None),
            P(None, ALL),
            P(None, ALL),
            P(None, ALL),
            P(),
            P(),
            P(),
            P(),
        ),
        out_specs=(
            P(),
            P(),
            P(None, ALL, None),
            P(None, ALL, None),
            P(None, ALL, None),
            P(None, ALL, None),
            P(None, ALL, None),
            P(None, ALL, None),
            P(ALL, None),
            P(ALL, None),
            P(ALL, None),
            P(None, ALL),
            P(None, ALL),
            P(None, ALL),
            P(),
            P(),
            P(),
            P(ALL),
        ),
        check_vma=False,
    )
```

```python
import math

import jax
import jax.numpy as jnp
from jax import lax
from jax.experimental import pallas as pl
from jax.experimental.pallas import tpu as pltpu
from jax.sharding import Mesh
from jax.sharding import PartitionSpec as P

D = 1024
HEADS = 16
KV = 8
HD = 64
FF = 4608
SEQ = 512
RESP = 96
NS_ITERS = 3


norm_epsilon = 1e-05
rope_base = 1000000.0
pref_beta = 2.0
clip_limit = 0.05
muon_decay = 0.95
muon_rate = 0.5
first_decay = 0.9
second_decay = 0.95
adam_rate = 0.02
adam_epsilon = 1e-08
weight_decay = 0.1
leading_coefficient = 3.4445
coef_second = -4.775
coef_third = 2.0315
ortho_epsilon = 1e-07
masked_score = -1e30


def rms_scale(inputs, gain):
    mean_square = jnp.mean(inputs * inputs, axis=-1, keepdims=True)
    return inputs * lax.rsqrt(mean_square + norm_epsilon) * gain


def rope_tables(length, half):
    position = jnp.arange(length, dtype=jnp.float32)
    inverse = rope_base ** (-jnp.arange(half, dtype=jnp.float32) / half)
    angle = position[:, None] * inverse[None, :]
    return (jnp.cos(angle)[:, None, :], jnp.sin(angle)[:, None, :])


def rotate(inputs, cosine, sine):
    half = inputs.shape[-1] // 2
    first = inputs[..., :half]
    second = inputs[..., half:]
    return jnp.concatenate(
        [first * cosine - second * sine, second * cosine + first * sine], axis=-1
    )


def dense(inputs, weight):
    return lax.dot_general(
        inputs, weight, (((1,), (1,)), ((), ())), preferred_element_type=jnp.float32
    )


def outer(grads, inputs):
    return lax.dot_general(
        grads, inputs, (((0,), (0,)), ((), ())), preferred_element_type=jnp.float32
    )


def back_dense(grads, weight):
    return jnp.dot(grads, weight, preferred_element_type=jnp.float32)


def delayed(values, offset):
    return jnp.pad(values, ((offset, 0), (0, 0)))[: values.shape[0]]


def advanced(values, offset):
    return jnp.pad(values, ((0, offset), (0, 0)))[offset:]


def norm_back(inputs, gain, grad_out):
    _, pullback = jax.vjp(rms_scale, inputs, gain)
    return pullback(grad_out)


def low_copy(values):
    return lax.optimization_barrier(values.astype(jnp.bfloat16)).astype(jnp.float32)


def adam_step(master, first, second, grad, factor, count):
    scaled = factor * grad
    first_new = first_decay * first + (1.0 - first_decay) * scaled
    second_new = second_decay * second + (1.0 - second_decay) * scaled * scaled
    steps = count.astype(jnp.float32)
    first_hat = first_new / (1.0 - first_decay**steps)
    second_hat = second_new / (1.0 - second_decay**steps)
    change = -adam_rate * (
        first_hat / (jnp.sqrt(second_hat) + adam_epsilon) + weight_decay * master
    )
    return (change, first_new, second_new)

DP = ("chip", "core")
ALL = ("chip", "core", "vocab")
SLOTS = 24
LATER_SLOTS = 8


def exchanged(rows):
    return lax.all_to_all(rows, ALL, 0, 0, tiled=True)


def spread(values):
    count = lax.axis_size(ALL)
    return lax.all_to_all(jnp.broadcast_to(values[None], (count,) + values.shape), ALL, 0, 0)


def turned(values, axis, step):
    count = lax.axis_size(axis)
    return lax.ppermute(values, axis, [(i, (i + step) % count) for i in range(count)])


def block_at(blocks, index):
    return lax.dynamic_index_in_dim(blocks, index % blocks.shape[0], 0, keepdims=False)


def handed_out(blocks, axis):
    place, count = lax.axis_index(axis), lax.axis_size(axis)
    return [block_at(blocks, place)] + [
        turned(block_at(blocks, place + step), axis, step) for step in range(1, count)
    ]


def handed_back(pieces, axis):
    return [pieces[0]] + [turned(pieces[step], axis, -step) for step in range(1, len(pieces))]


def gathered(values, axis):
    return [values] + [turned(values, axis, step) for step in range(1, lax.axis_size(axis))]


def placed_before(pieces, axis):
    pieces, place = jnp.stack(pieces), lax.axis_index(axis)
    return jnp.stack([block_at(pieces, place - j) for j in range(pieces.shape[0])])


def placed_after(pieces, axis):
    pieces, place = jnp.stack(pieces), lax.axis_index(axis)
    return jnp.stack([block_at(pieces, j - place) for j in range(pieces.shape[0])])


def added(pieces):
    total = pieces[0].astype(jnp.float32)
    for piece in pieces[1:]:
        total = total + piece.astype(jnp.float32)
    return total


def other_core(values):
    return lax.ppermute(values, "core", [(0, 1), (1, 0)])


def pair_sum(halves, core):
    given = lax.dynamic_index_in_dim(halves, 1 - core, 0, keepdims=False)
    kept = lax.dynamic_index_in_dim(halves, core, 0, keepdims=False)
    total = kept.astype(jnp.float32) + other_core(given).astype(jnp.float32)
    return total.astype(jnp.bfloat16)


def chip_sum(blocks):
    return added(handed_out(blocks, "chip"))


def group_sum(values, core):
    rows = values.shape[0] // 2
    chips = lax.axis_size("chip")
    half = pair_sum(values.reshape(2, rows, -1), core).reshape(chips, rows // chips, -1)
    part = chip_sum(half).astype(jnp.bfloat16)
    half = placed_before(gathered(part, "chip"), "chip").reshape(rows, -1)
    other = other_core(half)
    first = jnp.where(core == 0, half, other)
    second = jnp.where(core == 0, other, half)
    return jnp.concatenate([first, second], axis=0)


def member_gather(values):
    return jnp.concatenate(gathered(values, "vocab"), axis=0)


def member_return(pieces):
    return added(handed_back(pieces, "vocab"))


def member_scatter(blocks):
    return added(handed_out(blocks, "vocab"))


def onehot_rows(index, count):
    return (index[:, None] == jnp.arange(count)[None, :]).astype(jnp.bfloat16)


def token_slots(ids, block_rows):
    owner = ids // block_rows
    place = jnp.arange(ids.shape[0])
    earlier = place[:, None] > place[None, :]
    equal = ids[:, None] == ids[None, :]
    first = jnp.logical_not(jnp.any(equal & earlier, axis=1))
    ahead = (owner[:, None] == owner[None, :]) & earlier & first[None, :]
    rank = jnp.sum(ahead.astype(jnp.int32), axis=1)
    slot = jnp.sum(jnp.where(equal & first[None, :], rank[None, :], 0), axis=1)
    return owner, first, slot


def round_keys(owner, slot, first, count):
    within = slot - first
    return jnp.where((within >= 0) & (within < count), owner * count + within, -1)


def round_asks(keys, first_seen, local, count):
    hits = (keys[None, :] == jnp.arange(count)[:, None]) & first_seen[None, :]
    return jnp.sum(jnp.where(hits, local[None, :] + 1, 0), axis=1) - 1


def square_product(left, right):
    return jnp.dot(
        left.astype(jnp.bfloat16), right.astype(jnp.bfloat16), preferred_element_type=jnp.float32
    )


def rest_kernel(
    gram_ref, rest_ref, gram_scratch, change_scratch, rest_scratch, grams, change_b, rest_b
):
    lead = leading_coefficient
    size = gram_ref.shape[0]
    tile = 256

    def dot(left, right):
        return jnp.dot(left, right, preferred_element_type=jnp.float32)

    @pl.loop(0, size // tile)
    def _(step):
        rows = pl.ds(pl.multiple_of(step * tile, tile), tile)
        gram_scratch[rows, :] = gram_ref[rows, :]
        grams[0, rows, :] = gram_ref[rows, :].astype(jnp.bfloat16)

    power = 1.0
    for turn in range(NS_ITERS):
        now, later = turn % 2, (turn + 1) % 2

        @pl.loop(0, size // tile)
        def _(step):
            rows = pl.ds(pl.multiple_of(step * tile, tile), tile)
            change = coef_second * gram_scratch[rows, :] + coef_third * dot(
                grams[now, rows, :], grams[now]
            )
            change_scratch[rows, :] = change
            change_b[rows, :] = change.astype(jnp.bfloat16)

        @pl.loop(0, size // tile)
        def _(step):
            rows = pl.ds(pl.multiple_of(step * tile, tile), tile)
            if turn == 0:
                rest = change_scratch[rows, :]
            else:
                rest = (
                    lead * rest_scratch[rows, :]
                    + power * change_scratch[rows, :]
                    + dot(rest_b[rows, :], change_b[...])
                )
            if turn + 1 < NS_ITERS:
                rest_scratch[rows, :] = rest
                rest_b[rows, :] = rest.astype(jnp.bfloat16)
                mixed = dot(change_b[rows, :], grams[now])
                gram = (
                    lead * lead * gram_scratch[rows, :]
                    + 2.0 * lead * mixed
                    + dot(mixed.astype(jnp.bfloat16), change_b[...])
                )
                gram_scratch[rows, :] = gram
                grams[later, rows, :] = gram.astype(jnp.bfloat16)
            else:
                rest_ref[rows, :] = rest.astype(jnp.bfloat16)

        power = power * lead


def ortho_rest(gram):
    size = gram.shape[0]
    wide = pltpu.VMEM((size, size), jnp.float32)
    narrow = pltpu.VMEM((size, size), jnp.bfloat16)
    return pl.pallas_call(
        rest_kernel,
        out_shape=jax.ShapeDtypeStruct((size, size), jnp.bfloat16),
        in_specs=[pl.BlockSpec(memory_space=pltpu.VMEM)],
        out_specs=pl.BlockSpec(memory_space=pltpu.VMEM),
        scratch_shapes=[
            wide,
            wide,
            wide,
            pltpu.VMEM((2, size, size), jnp.bfloat16),
            narrow,
            narrow,
        ],
        compiler_params=pltpu.CompilerParams(vmem_limit_bytes=44 * 1024 * 1024),
        cost_estimate=pl.CostEstimate(
            flops=18 * size**3, bytes_accessed=6 * size * size, transcendentals=0
        ),
    )(gram)


def logits_kernel(target_ref, answers_ref, table_ref, shares_ref, stats_ref, logits):
    rows, width = logits.shape
    piece = 256
    target = target_ref[...]
    top = jnp.full((8, width), -jnp.inf, jnp.float32)
    total = jnp.zeros((8, width), jnp.float32)
    picked = jnp.zeros((8, width), jnp.float32)
    for first in range(0, rows, piece):
        scores = lax.dot_general(
            table_ref[first : first + piece, :],
            answers_ref[...],
            (((1,), (1,)), ((), ())),
            preferred_element_type=jnp.float32,
        )
        logits[first : first + piece, :] = scores
        top = jnp.maximum(top, jnp.max(scores.reshape(-1, 8, width), axis=0))
    top = jnp.max(top, axis=0, keepdims=True)
    for first in range(0, rows, piece):
        scores = logits[first : first + piece, :]
        share = jnp.exp(scores - top)
        shares_ref[first : first + piece, :] = share.astype(jnp.bfloat16)
        total = total + jnp.sum(share.reshape(-1, 8, width), axis=0)
        place = lax.broadcasted_iota(jnp.int32, (piece, width), 0)
        hit = jnp.where(place == target - first, scores, 0.0)
        picked = picked + jnp.sum(hit.reshape(-1, 8, width), axis=0)
    stats_ref[0:1, :] = top
    stats_ref[1:2, :] = jnp.sum(total, axis=0, keepdims=True)
    stats_ref[2:3, :] = jnp.sum(picked, axis=0, keepdims=True)
    stats_ref[3:8, :] = jnp.zeros((5, width), jnp.float32)


def answer_shares(target, answers, table):
    count, rows = answers.shape[0], table.shape[0]
    tile = 256
    return pl.pallas_call(
        logits_kernel,
        grid=(count // tile,),
        in_specs=[
            pl.BlockSpec((1, tile), lambda i: (0, i)),
            pl.BlockSpec((tile, D), lambda i: (i, 0)),
            pl.BlockSpec((rows, D), lambda i: (0, 0)),
        ],
        out_specs=[
            pl.BlockSpec((rows, tile), lambda i: (0, i)),
            pl.BlockSpec((8, tile), lambda i: (0, i)),
        ],
        out_shape=[
            jax.ShapeDtypeStruct((rows, count), jnp.bfloat16),
            jax.ShapeDtypeStruct((8, count), jnp.float32),
        ],
        scratch_shapes=[pltpu.VMEM((rows, tile), jnp.float32)],
        compiler_params=pltpu.CompilerParams(vmem_limit_bytes=40 * 1024 * 1024),
        cost_estimate=pl.CostEstimate(
            flops=2 * count * rows * D,
            bytes_accessed=2 * count * (rows + D),
            transcendentals=count * rows,
        ),
    )(target, answers, table)


def logit_grads(place, target, scale, value, shares):
    return jnp.where(place == target, value, shares.astype(jnp.float32) * scale).astype(jnp.bfloat16)


def grads_kernel(core_ref, target_ref, scale_ref, value_ref, shares_ref, table_ref, grads_ref):
    place = lax.broadcasted_iota(jnp.int32, shares_ref.shape, 0)
    grads = logit_grads(place, target_ref[...], scale_ref[...], value_ref[...], shares_ref[...])
    grads_ref[...] = lax.dot_general(
        grads, table_ref[...], (((0,), (0,)), ((), ())), preferred_element_type=jnp.float32
    ).astype(jnp.bfloat16)


def answer_grads(core, target, scale, value, shares, table, width):
    rows, count = shares.shape
    steps = count // (2 * width)
    row = pl.BlockSpec((1, width), lambda i, core_ref: (0, 2 * i + core_ref[0]))
    return pl.pallas_call(
        grads_kernel,
        grid_spec=pltpu.PrefetchScalarGridSpec(
            num_scalar_prefetch=1,
            grid=(steps,),
            in_specs=[
                row,
                row,
                row,
                pl.BlockSpec((rows, width), lambda i, core_ref: (0, 2 * i + core_ref[0])),
                pl.BlockSpec((rows, D), lambda i, core_ref: (0, 0)),
            ],
            out_specs=pl.BlockSpec((width, D), lambda i, core_ref: (i, 0)),
        ),
        out_shape=jax.ShapeDtypeStruct((steps * width, D), jnp.bfloat16),
        compiler_params=pltpu.CompilerParams(vmem_limit_bytes=40 * 1024 * 1024),
        cost_estimate=pl.CostEstimate(
            flops=2 * steps * width * rows * D,
            bytes_accessed=2 * steps * width * (rows + D),
            transcendentals=0,
        ),
    )(core.reshape(1), target, scale, value, shares, table)


def body(
    token_ids,
    seq_lengths,
    pair_order,
    table_master,
    table_first,
    table_second,
    square_master,
    square_moment,
    wide_master,
    wide_moment,
    vector_master,
    vector_first,
    vector_second,
    norm_gains,
    norm_first,
    norm_second,
    adam_count,
):
    members = lax.axis_size("vocab")
    member = lax.axis_index("vocab")
    block_rows = table_master.shape[0]
    lengths = seq_lengths[0]
    order = pair_order[0]
    groups_per = HEADS // KV
    scale = HD ** (-0.5)

    core = lax.axis_index("core")
    devices = lax.axis_size(ALL)
    device = lax.axis_index(ALL)
    groups = devices // members

    own_ids = lax.dynamic_index_in_dim(token_ids, member, 0, keepdims=False)
    own_length = lengths[member]
    start = own_length - 1 - RESP
    owner, first_seen, slot = token_slots(own_ids, block_rows)
    local_ids = own_ids % block_rows
    keys = round_keys(owner, slot, 0, SLOTS)
    asks = round_asks(keys, first_seen, local_ids, devices * SLOTS)
    own_targets = lax.dynamic_slice_in_dim(own_ids, start + 1, RESP, 0)
    vector_low = vector_master.astype(jnp.bfloat16).astype(jnp.float32)
    shared_notes = jnp.concatenate(
        [
            vector_low.reshape(-1),
            jnp.concatenate([own_targets, order, jnp.max(slot)[None] + 1]).astype(jnp.float32),
        ]
    )
    notes = jnp.concatenate(
        [
            asks.reshape(devices, SLOTS).astype(jnp.float32),
            jnp.broadcast_to(shared_notes[None, :], (devices, shared_notes.size)),
        ],
        axis=1,
    )
    notes = exchanged(notes)
    square_b = lax.all_gather(square_master.astype(jnp.bfloat16), ALL, axis=1, tiled=True)
    wide_b = lax.all_gather(wide_master.astype(jnp.bfloat16), DP, axis=1, tiled=True)
    hidden_units = wide_b.shape[1]
    asked = notes[:, :SLOTS].astype(jnp.int32).reshape(-1)
    gains = (
        notes[:, SLOTS : SLOTS + vector_low.size]
        .reshape(devices, vector_low.shape[0], vector_low.shape[1])
        .transpose(1, 0, 2)
        .reshape(vector_low.shape[0], D)
    )
    numbers = notes[:, SLOTS + vector_low.size :].astype(jnp.int32)
    targets = numbers[:, :RESP].reshape(-1)
    orders = numbers[:, RESP : RESP + members].reshape(groups, members, members)[:, 0]
    later = jnp.maximum(jnp.max(numbers[:, RESP + members]) - SLOTS, 0)
    later_turns = (later + LATER_SLOTS - 1) // LATER_SLOTS
    slots = jnp.arange(members)
    chosen_mask = (orders[:, 0::2, None] == slots[None, None, :]).astype(jnp.float32)
    rejected_mask = (orders[:, 1::2, None] == slots[None, None, :]).astype(jnp.float32)
    pair_rows = jnp.sum(
        (chosen_mask + rejected_mask)[:, :, :, None] * (chosen_mask - rejected_mask)[:, :, None, :],
        axis=1,
    )
    same_group = jnp.arange(groups)[:, None] == jnp.arange(groups)[None, :]
    pair_rows = jnp.where(same_group[:, None, :, None], pair_rows[:, :, None, :], 0.0)
    pair_rows = pair_rows.reshape(devices, devices) * (pref_beta / RESP)
    chosen_sign = jnp.sum(chosen_mask - rejected_mask, axis=1).reshape(devices, 1)
    table_b = table_master.astype(jnp.bfloat16)
    head_gains = low_copy(norm_gains)
    cosine, sine = rope_tables(SEQ, HD // 2)

    def fetched(wanted, row_keys):
        rows = jnp.dot(
            onehot_rows(wanted, block_rows), table_b, preferred_element_type=jnp.float32
        ).astype(jnp.bfloat16)
        return jnp.dot(
            onehot_rows(row_keys, wanted.shape[0]),
            exchanged(rows),
            preferred_element_type=jnp.float32,
        )

    def later_round(turn):
        count = devices * LATER_SLOTS
        later_keys = round_keys(owner, slot, SLOTS + turn * LATER_SLOTS, LATER_SLOTS)
        return later_keys, exchanged(round_asks(later_keys, first_seen, local_ids, count))

    def fetch_more(turn, rows):
        later_keys, later_asked = later_round(turn)
        return rows + fetched(later_asked, later_keys)

    hidden0 = lax.fori_loop(0, later_turns, fetch_more, fetched(asked, keys))
    act1 = rms_scale(hidden0, gains[0]).astype(jnp.bfloat16)
    inner = dense(act1, square_b[0:3].reshape(3 * D, D))
    entry = inner[:, :D]
    leave = inner[:, D : 2 * D]
    conv_in = inner[:, 2 * D :]
    product = entry * conv_in
    convolved = gains[4] * product + gains[5] * delayed(product, 1) + gains[6] * delayed(product, 2)
    mixer = (leave * convolved).astype(jnp.bfloat16)
    hidden1 = hidden0 + dense(mixer, square_b[3])
    act2 = rms_scale(hidden1, gains[1]).astype(jnp.bfloat16)

    def answers(values):
        return lax.dynamic_slice_in_dim(values, start, RESP, 0)

    def placed(values):
        return lax.dynamic_update_slice_in_dim(
            jnp.zeros((SEQ, values.shape[1]), values.dtype), values, start, 0
        )

    answer_act2 = answers(act2)
    query_raw = dense(answer_act2, square_b[4]).reshape(RESP, HEADS, HD)
    pair_raw = dense(act2, square_b[5])
    key_raw = pair_raw[:, : KV * HD].reshape(SEQ, KV, HD)
    value_b = pair_raw[:, KV * HD :].astype(jnp.bfloat16).reshape(SEQ, KV, HD)

    answer_cosine, answer_sine = answers(cosine), answers(sine)

    def query_prep(raw, gain):
        return rotate(rms_scale(raw, gain), answer_cosine, answer_sine)

    def key_prep(raw, gain):
        return rotate(rms_scale(raw, gain), cosine, sine)

    query_b = (
        query_prep(query_raw, head_gains[0]).astype(jnp.bfloat16).reshape(RESP, KV, groups_per, HD)
    )
    key_b = key_prep(key_raw, head_gains[1]).astype(jnp.bfloat16)
    causal = start + jnp.arange(RESP)[:, None] >= jnp.arange(SEQ)[None, :]
    scores = (
        jnp.einsum("sgrd,tgd->grst", query_b, key_b, preferred_element_type=jnp.float32) * scale
    )
    scores = jnp.where(causal, scores, masked_score)
    peak = jnp.max(scores, axis=-1, keepdims=True)
    expo = jnp.exp(scores - peak)
    total = jnp.sum(expo, axis=-1, keepdims=True)
    log_norm = peak + jnp.log(total)
    probs_b = (expo / total).astype(jnp.bfloat16)
    attended = jnp.einsum(
        "grst,tgd->sgrd", probs_b, value_b, preferred_element_type=jnp.float32
    ).reshape(RESP, D)
    attended_b = attended.astype(jnp.bfloat16)
    hidden2 = answers(hidden1) + dense(attended_b, square_b[6])
    act3 = member_gather(rms_scale(hidden2, gains[2]).astype(jnp.bfloat16))
    gate_up = dense(act3, wide_b[0:2].reshape(2 * hidden_units, D))
    gate_part = gate_up[:, :hidden_units]
    up_part = gate_up[:, hidden_units:]
    inner_b = (jax.nn.silu(gate_part) * up_part).astype(jnp.bfloat16)
    ffn_part = jnp.dot(inner_b, wide_b[2], preferred_element_type=jnp.float32)
    hidden3 = hidden2 + member_return(ffn_part.astype(jnp.bfloat16).reshape(members, RESP, D))
    final_b = rms_scale(hidden3, gains[3]).astype(jnp.bfloat16)
    response_tokens = lax.all_gather(final_b, ALL, axis=0, tiled=True)
    squares, square_rows = square_master.shape[0], square_master.shape[1]
    wides, wide_rows = wide_master.shape[0], wide_master.shape[1]
    per_member = -(-squares // members)
    group_rows = members * square_rows

    def by_member(values):
        values = jnp.pad(values, ((0, per_member * members - squares), (0, 0), (0, 0)))
        return values.reshape(per_member, members, -1, D).transpose(1, 0, 2, 3)

    def wide_by_member(values):
        return jnp.pad(values, ((0, members - wides), (0, 0), (0, 0)))

    moment_rows = jnp.concatenate(
        [
            wide_by_member(wide_moment.astype(jnp.bfloat16)).reshape(-1, D),
            square_moment.astype(jnp.bfloat16).reshape(-1, D),
        ],
        axis=0,
    )
    moment_rows, response_tokens = lax.optimization_barrier((moment_rows, response_tokens))
    moment_rows = lax.all_gather(moment_rows, "vocab", axis=0)
    wide_moment_job = jnp.stack(
        [
            lax.dynamic_slice_in_dim(
                block_at(moment_rows, member - step), member * wide_rows, wide_rows, 0
            )
            for step in range(members)
        ]
    )
    square_moment_job = moment_rows[:, members * wide_rows :].reshape(
        members, squares, square_rows, D
    )
    square_moment_job = jnp.pad(
        square_moment_job, ((0, 0), (0, per_member * members - squares), (0, 0), (0, 0))
    ).reshape(members, per_member, members, square_rows, D)
    square_moment_job = lax.dynamic_index_in_dim(square_moment_job, member, 2, keepdims=False)
    square_moment_job = square_moment_job.transpose(1, 0, 2, 3).reshape(per_member, group_rows, D)
    local_target = jnp.where(targets // block_rows == device, targets % block_rows, -1)[None, :]
    shares, own_stats = answer_shares(local_target, response_tokens, table_b)
    stats = own_stats[:3].reshape(3, devices, RESP).transpose(1, 0, 2)
    stats = exchanged(stats)
    top = jnp.max(stats[:, 0], axis=0)
    exp_total = jnp.sum(stats[:, 1] * jnp.exp(stats[:, 0] - top[None, :]), axis=0)
    own_log_total = top + jnp.log(exp_total)
    own_logp = jnp.sum(jnp.sum(stats[:, 2], axis=0) - own_log_total)
    joined = spread(jnp.concatenate([own_log_total, own_logp[None]]))
    log_total = joined[:, :RESP].reshape(1, -1)
    margin = jnp.sum(pair_rows * joined[:, RESP][None, :], axis=1, keepdims=True)
    pair_loss = 0.5 * jnp.sum(jax.nn.softplus(-margin))
    grad_logp = chosen_sign * jax.nn.sigmoid(-margin) * (-pref_beta / RESP)
    row_weight = jnp.broadcast_to(grad_logp, (devices, RESP)).reshape(1, -1)
    share_scale = -row_weight * jnp.exp(own_stats[0:1] - log_total)
    target_value = row_weight * (1.0 - jnp.exp(own_stats[2:3] - log_total))
    given, kept = (
        answer_grads(
            which, local_target, share_scale, target_value, shares, table_b, members * RESP
        )
        for which in (1 - core, core)
    )
    grad_answer_pair = (kept.astype(jnp.float32) + other_core(given).astype(jnp.float32)).astype(
        jnp.bfloat16
    )
    grad_answer_group = chip_sum(grad_answer_pair.reshape(groups // 2, members * RESP, D))
    grad_table = jnp.dot(
        logit_grads(
            jnp.arange(block_rows)[:, None], local_target, share_scale, target_value, shares
        ),
        response_tokens,
        preferred_element_type=jnp.float32,
    )
    grad_answer_group, grad_table, wide_moment_job, square_moment_job = lax.optimization_barrier(
        (grad_answer_group.astype(jnp.bfloat16), grad_table, wide_moment_job, square_moment_job)
    )
    grad_final = member_scatter(grad_answer_group.reshape(members, RESP, D))
    grad_hidden3, grad_gain3 = norm_back(hidden3, gains[3], grad_final)
    grad_ffn_out = member_gather(grad_hidden3.astype(jnp.bfloat16))
    grad_inner = dense(grad_ffn_out, wide_b[2])
    grad_down_w = outer(inner_b, grad_ffn_out)
    _, silu_pull = jax.vjp(lambda gate_in, up_in: jax.nn.silu(gate_in) * up_in, gate_part, up_part)
    grad_gate, grad_up = silu_pull(grad_inner)
    grad_gate_up = jnp.concatenate([grad_gate, grad_up], axis=1).astype(jnp.bfloat16)
    grad_act3_part = back_dense(grad_gate_up, wide_b[0:2].reshape(2 * hidden_units, D))
    grad_act3 = member_return(grad_act3_part.astype(jnp.bfloat16).reshape(members, RESP, D))
    grad_gate_up_w = outer(grad_gate_up, act3)
    grad_norm2, grad_gain2 = norm_back(hidden2, gains[2], grad_act3)
    grad_hidden2 = grad_hidden3 + grad_norm2
    grad_attn_out = grad_hidden2.astype(jnp.bfloat16)
    grad_attended = (
        back_dense(grad_attn_out, square_b[6])
        .astype(jnp.bfloat16)
        .reshape(RESP, KV, groups_per, HD)
    )
    grad_out_w = outer(grad_attn_out, attended_b)
    scores = (
        jnp.einsum("sgrd,tgd->grst", query_b, key_b, preferred_element_type=jnp.float32) * scale
    )
    probs = jnp.exp(jnp.where(causal, scores, masked_score) - log_norm)
    grad_probs = jnp.einsum(
        "sgrd,tgd->grst", grad_attended, value_b, preferred_element_type=jnp.float32
    )
    grad_values = jnp.einsum(
        "grst,sgrd->tgd", probs_b, grad_attended, preferred_element_type=jnp.float32
    )
    delta = jnp.sum(probs * grad_probs, axis=-1, keepdims=True)
    grad_scores = (probs * (grad_probs - delta)).astype(jnp.bfloat16)
    grad_query = (
        jnp.einsum("grst,tgd->sgrd", grad_scores, key_b, preferred_element_type=jnp.float32) * scale
    ).reshape(RESP, HEADS, HD)
    grad_keys = (
        jnp.einsum("grst,sgrd->tgd", grad_scores, query_b, preferred_element_type=jnp.float32)
        * scale
    )
    _, query_pull = jax.vjp(query_prep, query_raw, head_gains[0])
    grad_query_raw, grad_query_gain = query_pull(grad_query)
    _, key_pull = jax.vjp(key_prep, key_raw, head_gains[1])
    grad_key_raw, grad_key_gain = key_pull(grad_keys)
    grad_query_b = grad_query_raw.reshape(RESP, D).astype(jnp.bfloat16)
    grad_pair_b = jnp.concatenate(
        [grad_key_raw.reshape(SEQ, KV * HD), grad_values.reshape(SEQ, KV * HD)], axis=1
    ).astype(jnp.bfloat16)
    grad_act2 = back_dense(grad_pair_b, square_b[5]) + placed(back_dense(grad_query_b, square_b[4]))
    grad_query_w = outer(grad_query_b, answer_act2)
    grad_pair_w = outer(grad_pair_b, act2)
    grad_norm1, grad_gain1 = norm_back(hidden1, gains[1], grad_act2)
    grad_hidden1 = placed(grad_hidden2) + grad_norm1
    grad_mix_out = grad_hidden1.astype(jnp.bfloat16)
    grad_mixer = back_dense(grad_mix_out, square_b[3])
    grad_mixer_w = outer(grad_mix_out, mixer)
    grad_leave = grad_mixer * convolved
    grad_conv = grad_mixer * leave
    grad_tap0 = jnp.sum(grad_conv * product, axis=0)
    grad_tap1 = jnp.sum(grad_conv * delayed(product, 1), axis=0)
    grad_tap2 = jnp.sum(grad_conv * delayed(product, 2), axis=0)
    grad_product = (
        gains[4] * grad_conv + gains[5] * advanced(grad_conv, 1) + gains[6] * advanced(grad_conv, 2)
    )
    grad_inner_b = jnp.concatenate(
        [grad_product * conv_in, grad_leave, grad_product * entry], axis=1
    ).astype(jnp.bfloat16)
    grad_act1 = back_dense(grad_inner_b, square_b[0:3].reshape(3 * D, D))
    grad_inner_w = outer(grad_inner_b, act1)
    grad_norm0, grad_gain0 = norm_back(hidden0, gains[0], grad_act1)
    grad_embed_b = (grad_hidden1 + grad_norm0).astype(jnp.bfloat16)

    grad_square = jnp.concatenate(
        [
            grad_inner_w.astype(jnp.bfloat16).reshape(3, D, D),
            grad_mixer_w.astype(jnp.bfloat16)[None],
            grad_query_w.astype(jnp.bfloat16)[None],
            grad_pair_w.astype(jnp.bfloat16)[None],
            grad_out_w.astype(jnp.bfloat16)[None],
        ],
        axis=0,
    )
    grad_vector = jnp.stack(
        [grad_gain0, grad_gain1, grad_gain2, grad_gain3, grad_tap0, grad_tap1, grad_tap2]
    )
    grad_head_gains = jnp.stack([grad_query_gain, grad_key_gain])
    grad_wide = jnp.concatenate(
        [
            grad_gate_up_w.astype(jnp.bfloat16).reshape(2, hidden_units, D),
            grad_down_w.astype(jnp.bfloat16)[None],
        ],
        axis=0,
    )
    share_wide_b = lax.psum_scatter(grad_wide, DP, scatter_dimension=1, tiled=True)
    grad_square, share_wide_b = lax.optimization_barrier((grad_square, share_wide_b))
    share_wide_b, grad_embed_b = lax.optimization_barrier((share_wide_b, grad_embed_b))
    share_wide = share_wide_b.astype(jnp.float32)
    wide_grad_job = jnp.stack(handed_out(wide_by_member(share_wide_b), "vocab"))
    group_square = lax.psum_scatter(grad_square, DP, scatter_dimension=1, tiled=True)
    square_grad_job = member_scatter(by_member(group_square))

    def from_members(values):
        values = values.reshape(per_member, members, square_rows, D).transpose(1, 0, 2, 3)
        values = placed_before(handed_out(values.astype(jnp.bfloat16), "vocab"), "vocab")
        values = values.transpose(1, 0, 2, 3).reshape(per_member * members, square_rows, D)
        return values[:squares].astype(jnp.float32)

    share_square = from_members(square_grad_job)

    def returned(row_keys, count):
        rows = outer(onehot_rows(row_keys, count), grad_embed_b)
        return exchanged(rows.astype(jnp.bfloat16))

    def put(wanted, rows):
        return outer(onehot_rows(wanted, block_rows), rows)

    def return_more(turn, total):
        later_keys, later_asked = later_round(turn)
        return total + put(later_asked, returned(later_keys, later_asked.shape[0]))

    returned_rows, wide_grad_job = lax.optimization_barrier(
        (returned(keys, devices * SLOTS), wide_grad_job)
    )
    share_table = lax.fori_loop(
        0, later_turns, return_more, grad_table + put(asked, returned_rows))
    width = vector_master.shape[1]
    vector_notes = grad_vector.reshape(-1, devices, width).transpose(1, 0, 2).reshape(devices, -1)
    vector_notes = jnp.concatenate(
        [
            vector_notes,
            jnp.broadcast_to(grad_head_gains.reshape(1, -1), (devices, grad_head_gains.size)),
        ],
        axis=1,
    )
    vector_notes = jnp.sum(exchanged(vector_notes), axis=0)
    share_vector = vector_notes[: vector_master.size].reshape(vector_master.shape)
    gains_total = vector_notes[vector_master.size :].reshape(grad_head_gains.shape)

    def job_sums(values):
        sums = jnp.sum(values, axis=(1, 2))[:, None]
        sums = jnp.where(jnp.arange(members)[None, :] == member, sums, 0.0)
        return sums.reshape(-1)[:squares]

    moment_squares = jnp.concatenate(
        [
            jnp.sum(square_moment * square_moment, axis=(1, 2)),
            jnp.sum(wide_moment * wide_moment, axis=(1, 2)),
        ]
    )
    moment_cross = jnp.concatenate(
        [
            job_sums(square_moment_job.astype(jnp.float32) * square_grad_job),
            jnp.sum(wide_moment * share_wide, axis=(1, 2)),
        ]
    )
    grad_squares = jnp.concatenate(
        [
            job_sums(square_grad_job * square_grad_job),
            jnp.sum(share_wide * share_wide, axis=(1, 2)),
        ]
    )
    moment_stats = jnp.stack([moment_squares, moment_cross, grad_squares])
    own_squares = (
        jnp.sum(grad_squares)
        + jnp.sum(share_vector * share_vector)
        + jnp.sum(share_table * share_table)
    )
    sums = jnp.concatenate([moment_stats.reshape(-1), own_squares[None]])
    sums = jnp.sum(spread(sums), axis=0)
    stats_total = sums[:-1].reshape(moment_stats.shape)
    grad_norm = jnp.sqrt(sums[-1] + jnp.sum(gains_total * gains_total))
    factor = jnp.minimum(1.0, clip_limit / grad_norm)
    square_moment_new = muon_decay * square_moment + (1.0 - muon_decay) * (factor * share_square)
    wide_moment_new = muon_decay * wide_moment + (1.0 - muon_decay) * (factor * share_wide)
    moment_norm = jnp.sqrt(
        muon_decay * muon_decay * stats_total[0]
        + 2.0 * muon_decay * (1.0 - muon_decay) * factor * stats_total[1]
        + (1.0 - muon_decay) * (1.0 - muon_decay) * factor * factor * stats_total[2]
    )
    ortho_square = square_moment_new / (moment_norm[:7][:, None, None] + ortho_epsilon)
    ortho_wide = wide_moment_new / (moment_norm[7:][:, None, None] + ortho_epsilon)
    wide_inverse = 1.0 / (moment_norm[squares:] + ortho_epsilon)
    wide_inverse = jnp.pad(wide_inverse, (0, members - wides))[member]
    square_inverse = 1.0 / (moment_norm[:squares] + ortho_epsilon)
    square_inverse = jnp.pad(square_inverse, (0, per_member * members - squares))
    square_inverse = square_inverse.reshape(per_member, members)[:, member][:, None, None]
    square_part = (muon_decay * square_inverse) * square_moment_job.astype(jnp.float32) + (
        (1.0 - muon_decay) * factor * square_inverse
    ) * square_grad_job
    square_part, wide_grad_job = lax.optimization_barrier(
        (square_part.astype(jnp.bfloat16), wide_grad_job)
    )
    square_part = jnp.pad(square_part, ((0, groups // 2 - per_member), (0, 0), (0, 0)))
    square_half = jnp.concatenate(handed_out(square_part, "chip"), axis=0)
    square_job = jnp.concatenate([square_half, other_core(square_half)], axis=0)
    wide_job = (
        (muon_decay * wide_inverse) * wide_moment_job.astype(jnp.float32)
        + ((1.0 - muon_decay) * factor * wide_inverse) * wide_grad_job.astype(jnp.float32)
    )
    wide_job = wide_job.reshape(members * wide_rows, D).astype(jnp.bfloat16)
    wide_gram = group_sum(outer(wide_job, wide_job).astype(jnp.bfloat16), core)
    square_gram = outer(square_job, square_job)
    gram = jnp.where(core == 0, wide_gram.astype(jnp.float32), square_gram)
    rest_b = ortho_rest(gram)
    power = leading_coefficient**NS_ITERS
    share_table, rest_b = lax.optimization_barrier((share_table, rest_b))
    table_step, table_first_new, table_second_new = adam_step(
        table_master, table_first, table_second, share_table, factor, adam_count
    )
    wide_rest = jnp.where(core == 0, rest_b, other_core(rest_b))
    back_square = square_product(square_job, rest_b).astype(jnp.bfloat16)
    half_rows = square_half.shape[0]
    back_square = jnp.where(
        core == 0, other_core(back_square[half_rows:]), back_square[:half_rows]
    )
    back_square = handed_back(list(back_square.reshape(-1, group_rows, D)), "chip")
    back_square = placed_after(back_square, "chip")[:per_member]
    back_wide = square_product(wide_job, wide_rest).astype(jnp.bfloat16)
    back_wide = handed_back(list(back_wide.reshape(members, wide_rows, D)), "vocab")
    back_wide = placed_after(back_wide, "vocab")[:wides]
    back_square, back_wide = lax.optimization_barrier((back_square, back_wide))
    back_square = from_members(back_square)
    ortho_wide = power * ortho_wide + back_wide.astype(jnp.float32)
    ortho_square = power * ortho_square + back_square
    wide_scale = jnp.array([math.sqrt(FF / D), math.sqrt(FF / D), 1.0], jnp.float32)
    square_new = square_master - muon_rate * ortho_square
    wide_new = wide_master - muon_rate * wide_scale[:, None, None] * ortho_wide
    vector_step, vector_first_new, vector_second_new = adam_step(
        vector_master, vector_first, vector_second, share_vector, factor, adam_count
    )
    norm_step, norm_first_new, norm_second_new = adam_step(
        norm_gains, norm_first, norm_second, gains_total, factor, adam_count
    )
    return (
        pair_loss,
        grad_norm,
        square_new,
        square_moment_new,
        square_new.astype(jnp.bfloat16),
        wide_new,
        wide_moment_new,
        wide_new.astype(jnp.bfloat16),
        table_step,
        table_first_new,
        table_second_new,
        vector_step,
        vector_first_new,
        vector_second_new,
        norm_step,
        norm_first_new,
        norm_second_new,
        share_vector[3],
    )


def solution(mesh):
    groups, members = mesh.shape["dp"], mesh.shape["vocab"]
    cores = 2
    split_mesh = Mesh(mesh.devices.reshape(groups // cores, cores, members), ALL)
    return jax.shard_map(
        body,
        mesh=split_mesh,
        in_specs=(
            P(DP, None),
            P(DP, None),
            P(DP, None),
            P(ALL, None),
            P(ALL, None),
            P(ALL, None),
            P(None, ALL, None),
            P(None, ALL, None),
            P(None, ALL, None),
            P(None, ALL, None),
            P(None, ALL),
            P(None, ALL),
            P(None, ALL),
            P(),
            P(),
            P(),
            P(),
        ),
        out_specs=(
            P(),
            P(),
            P(None, ALL, None),
            P(None, ALL, None),
            P(None, ALL, None),
            P(None, ALL, None),
            P(None, ALL, None),
            P(None, ALL, None),
            P(ALL, None),
            P(ALL, None),
            P(ALL, None),
            P(None, ALL),
            P(None, ALL),
            P(None, ALL),
            P(),
            P(),
            P(),
            P(ALL),
        ),
        check_vma=False,
    )
```

```python
import math

import jax
import jax.numpy as jnp
from jax import lax
from jax.experimental import pallas as pl
from jax.experimental.pallas import tpu as pltpu
from jax.sharding import Mesh
from jax.sharding import PartitionSpec as P

D = 1024
HEADS = 16
KV = 8
HD = 64
FF = 4608
SEQ = 512
RESP = 96
NS_ITERS = 3


norm_epsilon = 1e-05
rope_base = 1000000.0
pref_beta = 2.0
clip_limit = 0.05
muon_decay = 0.95
muon_rate = 0.5
first_decay = 0.9
second_decay = 0.95
adam_rate = 0.02
adam_epsilon = 1e-08
weight_decay = 0.1
leading_coefficient = 3.4445
coef_second = -4.775
coef_third = 2.0315
ortho_epsilon = 1e-07
masked_score = -1e30


def rms_scale(inputs, gain):
    mean_square = jnp.mean(inputs * inputs, axis=-1, keepdims=True)
    return inputs * lax.rsqrt(mean_square + norm_epsilon) * gain


def rope_tables(length, half):
    position = jnp.arange(length, dtype=jnp.float32)
    inverse = rope_base ** (-jnp.arange(half, dtype=jnp.float32) / half)
    angle = position[:, None] * inverse[None, :]
    return (jnp.cos(angle)[:, None, :], jnp.sin(angle)[:, None, :])


def rotate(inputs, cosine, sine):
    half = inputs.shape[-1] // 2
    first = inputs[..., :half]
    second = inputs[..., half:]
    return jnp.concatenate(
        [first * cosine - second * sine, second * cosine + first * sine], axis=-1
    )


def dense(inputs, weight):
    return lax.dot_general(
        inputs, weight, (((1,), (1,)), ((), ())), preferred_element_type=jnp.float32
    )


def outer(grads, inputs):
    return lax.dot_general(
        grads, inputs, (((0,), (0,)), ((), ())), preferred_element_type=jnp.float32
    )


def back_dense(grads, weight):
    return jnp.dot(grads, weight, preferred_element_type=jnp.float32)


def delayed(values, offset):
    return jnp.pad(values, ((offset, 0), (0, 0)))[: values.shape[0]]


def advanced(values, offset):
    return jnp.pad(values, ((0, offset), (0, 0)))[offset:]


def norm_back(inputs, gain, grad_out):
    _, pullback = jax.vjp(rms_scale, inputs, gain)
    return pullback(grad_out)


def low_copy(values):
    return lax.optimization_barrier(values.astype(jnp.bfloat16)).astype(jnp.float32)


def adam_step(master, first, second, grad, factor, count):
    scaled = factor * grad
    first_new = first_decay * first + (1.0 - first_decay) * scaled
    second_new = second_decay * second + (1.0 - second_decay) * scaled * scaled
    steps = count.astype(jnp.float32)
    first_hat = first_new / (1.0 - first_decay**steps)
    second_hat = second_new / (1.0 - second_decay**steps)
    change = -adam_rate * (
        first_hat / (jnp.sqrt(second_hat) + adam_epsilon) + weight_decay * master
    )
    return (change, first_new, second_new)

DP = ("chip", "core")
ALL = ("chip", "core", "vocab")
SLOTS = 24
LATER_SLOTS = 8


def exchanged(rows):
    return lax.all_to_all(rows, ALL, 0, 0, tiled=True)


def spread(values):
    count = lax.axis_size(ALL)
    return lax.all_to_all(jnp.broadcast_to(values[None], (count,) + values.shape), ALL, 0, 0)


def turned(values, axis, step):
    count = lax.axis_size(axis)
    return lax.ppermute(values, axis, [(i, (i + step) % count) for i in range(count)])


def block_at(blocks, index):
    return lax.dynamic_index_in_dim(blocks, index % blocks.shape[0], 0, keepdims=False)


def handed_out(blocks, axis):
    place, count = lax.axis_index(axis), lax.axis_size(axis)
    return [block_at(blocks, place)] + [
        turned(block_at(blocks, place + step), axis, step) for step in range(1, count)
    ]


def handed_back(pieces, axis):
    return [pieces[0]] + [turned(pieces[step], axis, -step) for step in range(1, len(pieces))]


def gathered(values, axis):
    return [values] + [turned(values, axis, step) for step in range(1, lax.axis_size(axis))]


def placed_before(pieces, axis):
    pieces, place = jnp.stack(pieces), lax.axis_index(axis)
    return jnp.stack([block_at(pieces, place - j) for j in range(pieces.shape[0])])


def placed_after(pieces, axis):
    pieces, place = jnp.stack(pieces), lax.axis_index(axis)
    return jnp.stack([block_at(pieces, j - place) for j in range(pieces.shape[0])])


def added(pieces):
    total = pieces[0].astype(jnp.float32)
    for piece in pieces[1:]:
        total = total + piece.astype(jnp.float32)
    return total


def other_core(values):
    return lax.ppermute(values, "core", [(0, 1), (1, 0)])


def pair_sum(halves, core):
    given = lax.dynamic_index_in_dim(halves, 1 - core, 0, keepdims=False)
    kept = lax.dynamic_index_in_dim(halves, core, 0, keepdims=False)
    total = kept.astype(jnp.float32) + other_core(given).astype(jnp.float32)
    return total.astype(jnp.bfloat16)


def chip_sum(blocks):
    return added(handed_out(blocks, "chip"))


def group_sum(values, core):
    rows = values.shape[0] // 2
    chips = lax.axis_size("chip")
    half = pair_sum(values.reshape(2, rows, -1), core).reshape(chips, rows // chips, -1)
    part = chip_sum(half).astype(jnp.bfloat16)
    half = placed_before(gathered(part, "chip"), "chip").reshape(rows, -1)
    other = other_core(half)
    first = jnp.where(core == 0, half, other)
    second = jnp.where(core == 0, other, half)
    return jnp.concatenate([first, second], axis=0)


def member_gather(values):
    return jnp.concatenate(gathered(values, "vocab"), axis=0)


def member_return(pieces):
    return added(handed_back(pieces, "vocab"))


def member_scatter(blocks):
    return added(handed_out(blocks, "vocab"))


def onehot_rows(index, count):
    return (index[:, None] == jnp.arange(count)[None, :]).astype(jnp.bfloat16)


def token_slots(ids, block_rows):
    owner = ids // block_rows
    place = jnp.arange(ids.shape[0])
    earlier = place[:, None] > place[None, :]
    equal = ids[:, None] == ids[None, :]
    first = jnp.logical_not(jnp.any(equal & earlier, axis=1))
    ahead = (owner[:, None] == owner[None, :]) & earlier & first[None, :]
    rank = jnp.sum(ahead.astype(jnp.int32), axis=1)
    slot = jnp.sum(jnp.where(equal & first[None, :], rank[None, :], 0), axis=1)
    return owner, first, slot


def round_keys(owner, slot, first, count):
    within = slot - first
    return jnp.where((within >= 0) & (within < count), owner * count + within, -1)


def round_asks(keys, first_seen, local, count):
    hits = (keys[None, :] == jnp.arange(count)[:, None]) & first_seen[None, :]
    return jnp.sum(jnp.where(hits, local[None, :] + 1, 0), axis=1) - 1


def square_product(left, right):
    return jnp.dot(
        left.astype(jnp.bfloat16), right.astype(jnp.bfloat16), preferred_element_type=jnp.float32
    )


def rest_kernel(
    gram_ref, rest_ref, gram_scratch, change_scratch, rest_scratch, grams, change_b, rest_b
):
    lead = leading_coefficient
    size = gram_ref.shape[0]
    tile = 256

    def dot(left, right):
        return jnp.dot(left, right, preferred_element_type=jnp.float32)

    @pl.loop(0, size // tile)
    def _(step):
        rows = pl.ds(pl.multiple_of(step * tile, tile), tile)
        gram_scratch[rows, :] = gram_ref[rows, :]
        grams[0, rows, :] = gram_ref[rows, :].astype(jnp.bfloat16)

    power = 1.0
    for turn in range(NS_ITERS):
        now, later = turn % 2, (turn + 1) % 2

        @pl.loop(0, size // tile)
        def _(step):
            rows = pl.ds(pl.multiple_of(step * tile, tile), tile)
            change = coef_second * gram_scratch[rows, :] + coef_third * dot(
                grams[now, rows, :], grams[now]
            )
            change_scratch[rows, :] = change
            change_b[rows, :] = change.astype(jnp.bfloat16)

        @pl.loop(0, size // tile)
        def _(step):
            rows = pl.ds(pl.multiple_of(step * tile, tile), tile)
            if turn == 0:
                rest = change_scratch[rows, :]
            else:
                rest = (
                    lead * rest_scratch[rows, :]
                    + power * change_scratch[rows, :]
                    + dot(rest_b[rows, :], change_b[...])
                )
            if turn + 1 < NS_ITERS:
                rest_scratch[rows, :] = rest
                rest_b[rows, :] = rest.astype(jnp.bfloat16)
                mixed = dot(change_b[rows, :], grams[now])
                gram = (
                    lead * lead * gram_scratch[rows, :]
                    + 2.0 * lead * mixed
                    + dot(mixed.astype(jnp.bfloat16), change_b[...])
                )
                gram_scratch[rows, :] = gram
                grams[later, rows, :] = gram.astype(jnp.bfloat16)
            else:
                rest_ref[rows, :] = rest.astype(jnp.bfloat16)

        power = power * lead


def ortho_rest(gram):
    size = gram.shape[0]
    wide = pltpu.VMEM((size, size), jnp.float32)
    narrow = pltpu.VMEM((size, size), jnp.bfloat16)
    return pl.pallas_call(
        rest_kernel,
        out_shape=jax.ShapeDtypeStruct((size, size), jnp.bfloat16),
        in_specs=[pl.BlockSpec(memory_space=pltpu.VMEM)],
        out_specs=pl.BlockSpec(memory_space=pltpu.VMEM),
        scratch_shapes=[
            wide,
            wide,
            wide,
            pltpu.VMEM((2, size, size), jnp.bfloat16),
            narrow,
            narrow,
        ],
        compiler_params=pltpu.CompilerParams(vmem_limit_bytes=44 * 1024 * 1024),
        cost_estimate=pl.CostEstimate(
            flops=18 * size**3, bytes_accessed=6 * size * size, transcendentals=0
        ),
    )(gram)


def logits_kernel(target_ref, answers_ref, table_ref, shares_ref, stats_ref, logits):
    rows, width = logits.shape
    piece = 256
    target = target_ref[...]
    top = jnp.full((8, width), -jnp.inf, jnp.float32)
    total = jnp.zeros((8, width), jnp.float32)
    picked = jnp.zeros((8, width), jnp.float32)
    for first in range(0, rows, piece):
        scores = lax.dot_general(
            table_ref[first : first + piece, :],
            answers_ref[...],
            (((1,), (1,)), ((), ())),
            preferred_element_type=jnp.float32,
        )
        logits[first : first + piece, :] = scores
        top = jnp.maximum(top, jnp.max(scores.reshape(-1, 8, width), axis=0))
    top = jnp.max(top, axis=0, keepdims=True)
    for first in range(0, rows, piece):
        scores = logits[first : first + piece, :]
        share = jnp.exp(scores - top)
        shares_ref[first : first + piece, :] = share.astype(jnp.bfloat16)
        total = total + jnp.sum(share.reshape(-1, 8, width), axis=0)
        place = lax.broadcasted_iota(jnp.int32, (piece, width), 0)
        hit = jnp.where(place == target - first, scores, 0.0)
        picked = picked + jnp.sum(hit.reshape(-1, 8, width), axis=0)
    stats_ref[0:1, :] = top
    stats_ref[1:2, :] = jnp.sum(total, axis=0, keepdims=True)
    stats_ref[2:3, :] = jnp.sum(picked, axis=0, keepdims=True)
    stats_ref[3:8, :] = jnp.zeros((5, width), jnp.float32)


def answer_shares(target, answers, table):
    count, rows = answers.shape[0], table.shape[0]
    tile = 256
    return pl.pallas_call(
        logits_kernel,
        grid=(count // tile,),
        in_specs=[
            pl.BlockSpec((1, tile), lambda i: (0, i)),
            pl.BlockSpec((tile, D), lambda i: (i, 0)),
            pl.BlockSpec((rows, D), lambda i: (0, 0)),
        ],
        out_specs=[
            pl.BlockSpec((rows, tile), lambda i: (0, i)),
            pl.BlockSpec((8, tile), lambda i: (0, i)),
        ],
        out_shape=[
            jax.ShapeDtypeStruct((rows, count), jnp.bfloat16),
            jax.ShapeDtypeStruct((8, count), jnp.float32),
        ],
        scratch_shapes=[pltpu.VMEM((rows, tile), jnp.float32)],
        compiler_params=pltpu.CompilerParams(vmem_limit_bytes=40 * 1024 * 1024),
        cost_estimate=pl.CostEstimate(
            flops=2 * count * rows * D,
            bytes_accessed=2 * count * (rows + D),
            transcendentals=count * rows,
        ),
    )(target, answers, table)


def logit_grads(place, target, scale, value, shares):
    return jnp.where(place == target, value, shares.astype(jnp.float32) * scale).astype(jnp.bfloat16)


def grads_kernel(core_ref, target_ref, scale_ref, value_ref, shares_ref, table_ref, grads_ref):
    place = lax.broadcasted_iota(jnp.int32, shares_ref.shape, 0)
    grads = logit_grads(place, target_ref[...], scale_ref[...], value_ref[...], shares_ref[...])
    grads_ref[...] = lax.dot_general(
        grads, table_ref[...], (((0,), (0,)), ((), ())), preferred_element_type=jnp.float32
    ).astype(jnp.bfloat16)


def answer_grads(core, target, scale, value, shares, table, width):
    rows, count = shares.shape
    steps = count // (2 * width)
    row = pl.BlockSpec((1, width), lambda i, core_ref: (0, 2 * i + core_ref[0]))
    return pl.pallas_call(
        grads_kernel,
        grid_spec=pltpu.PrefetchScalarGridSpec(
            num_scalar_prefetch=1,
            grid=(steps,),
            in_specs=[
                row,
                row,
                row,
                pl.BlockSpec((rows, width), lambda i, core_ref: (0, 2 * i + core_ref[0])),
                pl.BlockSpec((rows, D), lambda i, core_ref: (0, 0)),
            ],
            out_specs=pl.BlockSpec((width, D), lambda i, core_ref: (i, 0)),
        ),
        out_shape=jax.ShapeDtypeStruct((steps * width, D), jnp.bfloat16),
        compiler_params=pltpu.CompilerParams(vmem_limit_bytes=40 * 1024 * 1024),
        cost_estimate=pl.CostEstimate(
            flops=2 * steps * width * rows * D,
            bytes_accessed=2 * steps * width * (rows + D),
            transcendentals=0,
        ),
    )(core.reshape(1), target, scale, value, shares, table)


def body(
    token_ids,
    seq_lengths,
    pair_order,
    table_master,
    table_first,
    table_second,
    square_master,
    square_moment,
    wide_master,
    wide_moment,
    vector_master,
    vector_first,
    vector_second,
    norm_gains,
    norm_first,
    norm_second,
    adam_count,
):
    members = lax.axis_size("vocab")
    member = lax.axis_index("vocab")
    block_rows = table_master.shape[0]
    lengths = seq_lengths[0]
    order = pair_order[0]
    groups_per = HEADS // KV
    scale = HD ** (-0.5)

    core = lax.axis_index("core")
    devices = lax.axis_size(ALL)
    device = lax.axis_index(ALL)
    groups = devices // members

    own_ids = lax.dynamic_index_in_dim(token_ids, member, 0, keepdims=False)
    own_length = lengths[member]
    start = own_length - 1 - RESP
    owner, first_seen, slot = token_slots(own_ids, block_rows)
    local_ids = own_ids % block_rows
    keys = round_keys(owner, slot, 0, SLOTS)
    asks = round_asks(keys, first_seen, local_ids, devices * SLOTS)
    own_targets = lax.dynamic_slice_in_dim(own_ids, start + 1, RESP, 0)
    vector_low = vector_master.astype(jnp.bfloat16).astype(jnp.float32)
    shared_notes = jnp.concatenate(
        [
            vector_low.reshape(-1),
            jnp.concatenate([own_targets, order, jnp.max(slot)[None] + 1]).astype(jnp.float32),
        ]
    )
    notes = jnp.concatenate(
        [
            asks.reshape(devices, SLOTS).astype(jnp.float32),
            jnp.broadcast_to(shared_notes[None, :], (devices, shared_notes.size)),
        ],
        axis=1,
    )
    notes = exchanged(notes)
    square_b = lax.all_gather(square_master.astype(jnp.bfloat16), ALL, axis=1, tiled=True)
    wide_b = lax.all_gather(wide_master.astype(jnp.bfloat16), DP, axis=1, tiled=True)
    hidden_units = wide_b.shape[1]
    asked = notes[:, :SLOTS].astype(jnp.int32).reshape(-1)
    gains = (
        notes[:, SLOTS : SLOTS + vector_low.size]
        .reshape(devices, vector_low.shape[0], vector_low.shape[1])
        .transpose(1, 0, 2)
        .reshape(vector_low.shape[0], D)
    )
    numbers = notes[:, SLOTS + vector_low.size :].astype(jnp.int32)
    targets = numbers[:, :RESP].reshape(-1)
    orders = numbers[:, RESP : RESP + members].reshape(groups, members, members)[:, 0]
    later = jnp.maximum(jnp.max(numbers[:, RESP + members]) - SLOTS, 0)
    later_turns = (later + LATER_SLOTS - 1) // LATER_SLOTS
    slots = jnp.arange(members)
    chosen_mask = (orders[:, 0::2, None] == slots[None, None, :]).astype(jnp.float32)
    rejected_mask = (orders[:, 1::2, None] == slots[None, None, :]).astype(jnp.float32)
    pair_rows = jnp.sum(
        (chosen_mask + rejected_mask)[:, :, :, None] * (chosen_mask - rejected_mask)[:, :, None, :],
        axis=1,
    )
    same_group = jnp.arange(groups)[:, None] == jnp.arange(groups)[None, :]
    pair_rows = jnp.where(same_group[:, None, :, None], pair_rows[:, :, None, :], 0.0)
    pair_rows = pair_rows.reshape(devices, devices) * (pref_beta / RESP)
    chosen_sign = jnp.sum(chosen_mask - rejected_mask, axis=1).reshape(devices, 1)
    table_b = table_master.astype(jnp.bfloat16)
    head_gains = low_copy(norm_gains)
    cosine, sine = rope_tables(SEQ, HD // 2)

    def fetched(wanted, row_keys):
        rows = jnp.dot(
            onehot_rows(wanted, block_rows), table_b, preferred_element_type=jnp.float32
        ).astype(jnp.bfloat16)
        return jnp.dot(
            onehot_rows(row_keys, wanted.shape[0]),
            exchanged(rows),
            preferred_element_type=jnp.float32,
        )

    def later_round(turn):
        count = devices * LATER_SLOTS
        later_keys = round_keys(owner, slot, SLOTS + turn * LATER_SLOTS, LATER_SLOTS)
        return later_keys, exchanged(round_asks(later_keys, first_seen, local_ids, count))

    def fetch_more(turn, rows):
        later_keys, later_asked = later_round(turn)
        return rows + fetched(later_asked, later_keys)

    hidden0 = lax.fori_loop(0, later_turns, fetch_more, fetched(asked, keys))
    act1 = rms_scale(hidden0, gains[0]).astype(jnp.bfloat16)
    entry, leave, conv_in = (dense(act1, square_b[place]) for place in range(3))
    product = entry * conv_in
    convolved = gains[4] * product + gains[5] * delayed(product, 1) + gains[6] * delayed(product, 2)
    mixer = (leave * convolved).astype(jnp.bfloat16)
    hidden1 = hidden0 + dense(mixer, square_b[3])
    act2 = rms_scale(hidden1, gains[1]).astype(jnp.bfloat16)

    def answers(values):
        return lax.dynamic_slice_in_dim(values, start, RESP, 0)

    def placed(values):
        return lax.dynamic_update_slice_in_dim(
            jnp.zeros((SEQ, values.shape[1]), values.dtype), values, start, 0
        )

    answer_act2 = answers(act2)
    query_raw = dense(answer_act2, square_b[4]).reshape(RESP, HEADS, HD)
    pair_raw = dense(act2, square_b[5])
    key_raw = pair_raw[:, : KV * HD].reshape(SEQ, KV, HD)
    value_b = pair_raw[:, KV * HD :].astype(jnp.bfloat16).reshape(SEQ, KV, HD)

    answer_cosine, answer_sine = answers(cosine), answers(sine)

    def query_prep(raw, gain):
        return rotate(rms_scale(raw, gain), answer_cosine, answer_sine)

    def key_prep(raw, gain):
        return rotate(rms_scale(raw, gain), cosine, sine)

    query_b = (
        query_prep(query_raw, head_gains[0]).astype(jnp.bfloat16).reshape(RESP, KV, groups_per, HD)
    )
    key_b = key_prep(key_raw, head_gains[1]).astype(jnp.bfloat16)
    causal = start + jnp.arange(RESP)[:, None] >= jnp.arange(SEQ)[None, :]
    scores = (
        jnp.einsum("sgrd,tgd->grst", query_b, key_b, preferred_element_type=jnp.float32) * scale
    )
    scores = jnp.where(causal, scores, masked_score)
    peak = jnp.max(scores, axis=-1, keepdims=True)
    expo = jnp.exp(scores - peak)
    total = jnp.sum(expo, axis=-1, keepdims=True)
    log_norm = peak + jnp.log(total)
    probs_b = (expo / total).astype(jnp.bfloat16)
    attended = jnp.einsum(
        "grst,tgd->sgrd", probs_b, value_b, preferred_element_type=jnp.float32
    ).reshape(RESP, D)
    attended_b = attended.astype(jnp.bfloat16)
    hidden2 = answers(hidden1) + dense(attended_b, square_b[6])
    act3 = member_gather(rms_scale(hidden2, gains[2]).astype(jnp.bfloat16))
    gate_part, up_part = dense(act3, wide_b[0]), dense(act3, wide_b[1])
    inner_b = (jax.nn.silu(gate_part) * up_part).astype(jnp.bfloat16)
    ffn_part = jnp.dot(inner_b, wide_b[2], preferred_element_type=jnp.float32)
    hidden3 = hidden2 + member_return(ffn_part.astype(jnp.bfloat16).reshape(members, RESP, D))
    final_b = rms_scale(hidden3, gains[3]).astype(jnp.bfloat16)
    response_tokens = lax.all_gather(final_b, ALL, axis=0, tiled=True)
    squares, square_rows = square_master.shape[0], square_master.shape[1]
    wides, wide_rows = wide_master.shape[0], wide_master.shape[1]
    per_member = -(-squares // members)
    group_rows = members * square_rows

    def by_member(values):
        values = jnp.pad(values, ((0, per_member * members - squares), (0, 0), (0, 0)))
        return values.reshape(per_member, members, -1, D).transpose(1, 0, 2, 3)

    def wide_by_member(values):
        return jnp.pad(values, ((0, members - wides), (0, 0), (0, 0)))

    moment_rows = jnp.concatenate(
        [
            wide_moment.astype(jnp.bfloat16).reshape(-1, D),
            square_moment.astype(jnp.bfloat16).reshape(-1, D),
        ],
        axis=0,
    )
    moment_rows, response_tokens = lax.optimization_barrier((moment_rows, response_tokens))
    moment_rows = lax.all_gather(moment_rows, "vocab", axis=0)
    local_target = jnp.where(targets // block_rows == device, targets % block_rows, -1)[None, :]
    shares, own_stats = answer_shares(local_target, response_tokens, table_b)
    stats = own_stats[:3].reshape(3, devices, RESP).transpose(1, 0, 2)
    stats = exchanged(stats)
    top = jnp.max(stats[:, 0], axis=0)
    exp_total = jnp.sum(stats[:, 1] * jnp.exp(stats[:, 0] - top[None, :]), axis=0)
    own_log_total = top + jnp.log(exp_total)
    own_logp = jnp.sum(jnp.sum(stats[:, 2], axis=0) - own_log_total)
    joined = spread(jnp.concatenate([own_log_total, own_logp[None]]))
    log_total = joined[:, :RESP].reshape(1, -1)
    margin = jnp.sum(pair_rows * joined[:, RESP][None, :], axis=1, keepdims=True)
    pair_loss = 0.5 * jnp.sum(jax.nn.softplus(-margin))
    grad_logp = chosen_sign * jax.nn.sigmoid(-margin) * (-pref_beta / RESP)
    row_weight = jnp.broadcast_to(grad_logp, (devices, RESP)).reshape(1, -1)
    share_scale = -row_weight * jnp.exp(own_stats[0:1] - log_total)
    target_value = row_weight * (1.0 - jnp.exp(own_stats[2:3] - log_total))
    given, kept = (
        answer_grads(
            which, local_target, share_scale, target_value, shares, table_b, members * RESP
        )
        for which in (1 - core, core)
    )
    grad_answer_pair = (kept.astype(jnp.float32) + other_core(given).astype(jnp.float32)).astype(
        jnp.bfloat16
    )
    grad_answer_group = chip_sum(grad_answer_pair.reshape(groups // 2, members * RESP, D))
    grad_table = jnp.dot(
        logit_grads(
            jnp.arange(block_rows)[:, None], local_target, share_scale, target_value, shares
        ),
        response_tokens,
        preferred_element_type=jnp.float32,
    )
    grad_answer_group, grad_table = lax.optimization_barrier(
        (grad_answer_group.astype(jnp.bfloat16), grad_table)
    )
    grad_final = member_scatter(grad_answer_group.reshape(members, RESP, D))
    grad_hidden3, grad_gain3 = norm_back(hidden3, gains[3], grad_final)
    grad_ffn_out = member_gather(grad_hidden3.astype(jnp.bfloat16))
    grad_inner = dense(grad_ffn_out, wide_b[2])
    grad_down_w = outer(inner_b, grad_ffn_out)
    _, silu_pull = jax.vjp(lambda gate_in, up_in: jax.nn.silu(gate_in) * up_in, gate_part, up_part)
    grad_gate, grad_up = silu_pull(grad_inner)
    grad_gate_b, grad_up_b = grad_gate.astype(jnp.bfloat16), grad_up.astype(jnp.bfloat16)
    grad_act3_part = back_dense(grad_gate_b, wide_b[0]) + back_dense(grad_up_b, wide_b[1])
    grad_act3 = member_return(grad_act3_part.astype(jnp.bfloat16).reshape(members, RESP, D))
    grad_gate_w, grad_up_w = outer(grad_gate_b, act3), outer(grad_up_b, act3)
    grad_norm2, grad_gain2 = norm_back(hidden2, gains[2], grad_act3)
    grad_hidden2 = grad_hidden3 + grad_norm2
    grad_attn_out = grad_hidden2.astype(jnp.bfloat16)
    grad_attended = (
        back_dense(grad_attn_out, square_b[6])
        .astype(jnp.bfloat16)
        .reshape(RESP, KV, groups_per, HD)
    )
    grad_out_w = outer(grad_attn_out, attended_b)
    scores = (
        jnp.einsum("sgrd,tgd->grst", query_b, key_b, preferred_element_type=jnp.float32) * scale
    )
    probs = jnp.exp(jnp.where(causal, scores, masked_score) - log_norm)
    grad_probs = jnp.einsum(
        "sgrd,tgd->grst", grad_attended, value_b, preferred_element_type=jnp.float32
    )
    grad_values = jnp.einsum(
        "grst,sgrd->tgd", probs_b, grad_attended, preferred_element_type=jnp.float32
    )
    delta = jnp.sum(probs * grad_probs, axis=-1, keepdims=True)
    grad_scores = (probs * (grad_probs - delta)).astype(jnp.bfloat16)
    grad_query = (
        jnp.einsum("grst,tgd->sgrd", grad_scores, key_b, preferred_element_type=jnp.float32) * scale
    ).reshape(RESP, HEADS, HD)
    grad_keys = (
        jnp.einsum("grst,sgrd->tgd", grad_scores, query_b, preferred_element_type=jnp.float32)
        * scale
    )
    _, query_pull = jax.vjp(query_prep, query_raw, head_gains[0])
    grad_query_raw, grad_query_gain = query_pull(grad_query)
    _, key_pull = jax.vjp(key_prep, key_raw, head_gains[1])
    grad_key_raw, grad_key_gain = key_pull(grad_keys)
    grad_query_b = grad_query_raw.reshape(RESP, D).astype(jnp.bfloat16)
    grad_pair_b = jnp.concatenate(
        [grad_key_raw.reshape(SEQ, KV * HD), grad_values.reshape(SEQ, KV * HD)], axis=1
    ).astype(jnp.bfloat16)
    grad_act2 = back_dense(grad_pair_b, square_b[5]) + placed(back_dense(grad_query_b, square_b[4]))
    grad_query_w = outer(grad_query_b, answer_act2)
    grad_pair_w = outer(grad_pair_b, act2)
    grad_norm1, grad_gain1 = norm_back(hidden1, gains[1], grad_act2)
    grad_hidden1 = placed(grad_hidden2) + grad_norm1
    grad_mix_out = grad_hidden1.astype(jnp.bfloat16)
    grad_mixer = back_dense(grad_mix_out, square_b[3])
    grad_mixer_w = outer(grad_mix_out, mixer)
    grad_leave = grad_mixer * convolved
    grad_conv = grad_mixer * leave
    grad_tap0 = jnp.sum(grad_conv * product, axis=0)
    grad_tap1 = jnp.sum(grad_conv * delayed(product, 1), axis=0)
    grad_tap2 = jnp.sum(grad_conv * delayed(product, 2), axis=0)
    grad_product = (
        gains[4] * grad_conv + gains[5] * advanced(grad_conv, 1) + gains[6] * advanced(grad_conv, 2)
    )
    grad_inner = [
        part.astype(jnp.bfloat16)
        for part in (grad_product * conv_in, grad_leave, grad_product * entry)
    ]
    grad_act1 = sum(back_dense(grad_inner[place], square_b[place]) for place in range(3))
    grad_inner_w = [outer(part, act1) for part in grad_inner]
    grad_norm0, grad_gain0 = norm_back(hidden0, gains[0], grad_act1)
    grad_embed_b = (grad_hidden1 + grad_norm0).astype(jnp.bfloat16)

    grad_square = jnp.stack(
        [
            part.astype(jnp.bfloat16)
            for part in (*grad_inner_w, grad_mixer_w, grad_query_w, grad_pair_w, grad_out_w)
        ]
    )
    grad_vector = jnp.stack(
        [grad_gain0, grad_gain1, grad_gain2, grad_gain3, grad_tap0, grad_tap1, grad_tap2]
    )
    grad_head_gains = jnp.stack([grad_query_gain, grad_key_gain])
    grad_wide = jnp.stack(
        [part.astype(jnp.bfloat16) for part in (grad_gate_w, grad_up_w, grad_down_w)]
    )
    grad_wide, moment_rows = lax.optimization_barrier((grad_wide, moment_rows))
    wide_moment_job = jnp.stack(
        [
            lax.dynamic_slice_in_dim(
                block_at(moment_rows, member - step),
                jnp.minimum(member, wides - 1) * wide_rows,
                wide_rows,
                0,
            )
            for step in range(members)
        ]
    )
    square_moment_job = moment_rows[:, wides * wide_rows :].reshape(
        members, squares, square_rows, D
    )
    square_moment_job = jnp.pad(
        square_moment_job, ((0, 0), (0, per_member * members - squares), (0, 0), (0, 0))
    ).reshape(members, per_member, members, square_rows, D)
    square_moment_job = lax.dynamic_index_in_dim(square_moment_job, member, 2, keepdims=False)
    square_moment_job = square_moment_job.transpose(1, 0, 2, 3).reshape(per_member, group_rows, D)
    share_wide_b = lax.psum_scatter(grad_wide, DP, scatter_dimension=1, tiled=True)
    grad_square, share_wide_b = lax.optimization_barrier((grad_square, share_wide_b))
    share_wide_b, grad_embed_b = lax.optimization_barrier((share_wide_b, grad_embed_b))
    share_wide = share_wide_b.astype(jnp.float32)
    wide_grad_job = jnp.stack(handed_out(wide_by_member(share_wide_b), "vocab"))
    group_square = lax.psum_scatter(grad_square, DP, scatter_dimension=1, tiled=True)
    square_grad_job = member_scatter(by_member(group_square))

    def from_members(values):
        values = values.reshape(per_member, members, square_rows, D).transpose(1, 0, 2, 3)
        values = placed_before(handed_out(values.astype(jnp.bfloat16), "vocab"), "vocab")
        values = values.transpose(1, 0, 2, 3).reshape(per_member * members, square_rows, D)
        return values[:squares].astype(jnp.float32)

    share_square = from_members(square_grad_job)

    def returned(row_keys, count):
        rows = outer(onehot_rows(row_keys, count), grad_embed_b)
        return exchanged(rows.astype(jnp.bfloat16))

    def put(wanted, rows):
        return outer(onehot_rows(wanted, block_rows), rows)

    def return_more(turn, total):
        later_keys, later_asked = later_round(turn)
        return total + put(later_asked, returned(later_keys, later_asked.shape[0]))

    returned_rows, wide_grad_job = lax.optimization_barrier(
        (returned(keys, devices * SLOTS), wide_grad_job)
    )
    share_table = lax.fori_loop(
        0, later_turns, return_more, grad_table + put(asked, returned_rows))
    width = vector_master.shape[1]
    vector_notes = grad_vector.reshape(-1, devices, width).transpose(1, 0, 2).reshape(devices, -1)
    vector_notes = jnp.concatenate(
        [
            vector_notes,
            jnp.broadcast_to(grad_head_gains.reshape(1, -1), (devices, grad_head_gains.size)),
        ],
        axis=1,
    )
    vector_notes = jnp.sum(exchanged(vector_notes), axis=0)
    share_vector = vector_notes[: vector_master.size].reshape(vector_master.shape)
    gains_total = vector_notes[vector_master.size :].reshape(grad_head_gains.shape)

    def job_sums(values):
        sums = jnp.sum(values, axis=(1, 2))[:, None]
        sums = jnp.where(jnp.arange(members)[None, :] == member, sums, 0.0)
        return sums.reshape(-1)[:squares]

    moment_squares = jnp.concatenate(
        [
            jnp.sum(square_moment * square_moment, axis=(1, 2)),
            jnp.sum(wide_moment * wide_moment, axis=(1, 2)),
        ]
    )
    moment_cross = jnp.concatenate(
        [
            job_sums(square_moment_job.astype(jnp.float32) * square_grad_job),
            jnp.sum(wide_moment * share_wide, axis=(1, 2)),
        ]
    )
    grad_squares = jnp.concatenate(
        [
            job_sums(square_grad_job * square_grad_job),
            jnp.sum(share_wide * share_wide, axis=(1, 2)),
        ]
    )
    moment_stats = jnp.stack([moment_squares, moment_cross, grad_squares])
    own_squares = (
        jnp.sum(grad_squares)
        + jnp.sum(share_vector * share_vector)
        + jnp.sum(share_table * share_table)
    )
    sums = jnp.concatenate([moment_stats.reshape(-1), own_squares[None]])
    sums = jnp.sum(spread(sums), axis=0)
    stats_total = sums[:-1].reshape(moment_stats.shape)
    grad_norm = jnp.sqrt(sums[-1] + jnp.sum(gains_total * gains_total))
    factor = jnp.minimum(1.0, clip_limit / grad_norm)
    square_moment_new = muon_decay * square_moment + (1.0 - muon_decay) * (factor * share_square)
    wide_moment_new = muon_decay * wide_moment + (1.0 - muon_decay) * (factor * share_wide)
    moment_norm = jnp.sqrt(
        muon_decay * muon_decay * stats_total[0]
        + 2.0 * muon_decay * (1.0 - muon_decay) * factor * stats_total[1]
        + (1.0 - muon_decay) * (1.0 - muon_decay) * factor * factor * stats_total[2]
    )
    ortho_square = square_moment_new / (moment_norm[:7][:, None, None] + ortho_epsilon)
    ortho_wide = wide_moment_new / (moment_norm[7:][:, None, None] + ortho_epsilon)
    wide_inverse = 1.0 / (moment_norm[squares:] + ortho_epsilon)
    wide_inverse = jnp.pad(wide_inverse, (0, members - wides))[member]
    square_inverse = 1.0 / (moment_norm[:squares] + ortho_epsilon)
    square_inverse = jnp.pad(square_inverse, (0, per_member * members - squares))
    square_inverse = square_inverse.reshape(per_member, members)[:, member][:, None, None]
    square_part = (muon_decay * square_inverse) * square_moment_job.astype(jnp.float32) + (
        (1.0 - muon_decay) * factor * square_inverse
    ) * square_grad_job
    square_part, wide_grad_job = lax.optimization_barrier(
        (square_part.astype(jnp.bfloat16), wide_grad_job)
    )
    square_part = jnp.pad(square_part, ((0, groups // 2 - per_member), (0, 0), (0, 0)))
    square_half = jnp.concatenate(handed_out(square_part, "chip"), axis=0)
    square_job = jnp.concatenate([square_half, other_core(square_half)], axis=0)
    wide_job = (
        (muon_decay * wide_inverse) * wide_moment_job.astype(jnp.float32)
        + ((1.0 - muon_decay) * factor * wide_inverse) * wide_grad_job.astype(jnp.float32)
    )
    wide_job = wide_job.reshape(members * wide_rows, D).astype(jnp.bfloat16)
    wide_gram = group_sum(outer(wide_job, wide_job).astype(jnp.bfloat16), core)
    square_gram = outer(square_job, square_job)
    gram = jnp.where(core == 0, wide_gram.astype(jnp.float32), square_gram)
    rest_b = ortho_rest(gram)
    power = leading_coefficient**NS_ITERS
    wide_rest = jnp.where(core == 0, rest_b, other_core(rest_b))
    back_square = square_product(square_job, rest_b).astype(jnp.bfloat16)
    half_rows = square_half.shape[0]
    back_square = jnp.where(
        core == 0, other_core(back_square[half_rows:]), back_square[:half_rows]
    )
    back_wide = square_product(wide_job, wide_rest).astype(jnp.bfloat16)
    share_table, back_square, back_wide = lax.optimization_barrier(
        (share_table, back_square, back_wide)
    )
    table_step, table_first_new, table_second_new = adam_step(
        table_master, table_first, table_second, share_table, factor, adam_count
    )
    back_square = handed_back(list(back_square.reshape(-1, group_rows, D)), "chip")
    back_square = placed_after(back_square, "chip")[:per_member]
    back_wide = handed_back(list(back_wide.reshape(members, wide_rows, D)), "vocab")
    back_wide = placed_after(back_wide, "vocab")[:wides]
    back_square = from_members(back_square)
    ortho_wide = power * ortho_wide + back_wide.astype(jnp.float32)
    ortho_square = power * ortho_square + back_square
    wide_scale = jnp.array([math.sqrt(FF / D), math.sqrt(FF / D), 1.0], jnp.float32)
    square_new = square_master - muon_rate * ortho_square
    wide_new = wide_master - muon_rate * wide_scale[:, None, None] * ortho_wide
    vector_step, vector_first_new, vector_second_new = adam_step(
        vector_master, vector_first, vector_second, share_vector, factor, adam_count
    )
    norm_step, norm_first_new, norm_second_new = adam_step(
        norm_gains, norm_first, norm_second, gains_total, factor, adam_count
    )
    return (
        pair_loss,
        grad_norm,
        square_new,
        square_moment_new,
        square_new.astype(jnp.bfloat16),
        wide_new,
        wide_moment_new,
        wide_new.astype(jnp.bfloat16),
        table_step,
        table_first_new,
        table_second_new,
        vector_step,
        vector_first_new,
        vector_second_new,
        norm_step,
        norm_first_new,
        norm_second_new,
        share_vector[3],
    )


def solution(mesh):
    groups, members = mesh.shape["dp"], mesh.shape["vocab"]
    cores = 2
    split_mesh = Mesh(mesh.devices.reshape(groups // cores, cores, members), ALL)
    return jax.shard_map(
        body,
        mesh=split_mesh,
        in_specs=(
            P(DP, None),
            P(DP, None),
            P(DP, None),
            P(ALL, None),
            P(ALL, None),
            P(ALL, None),
            P(None, ALL, None),
            P(None, ALL, None),
            P(None, ALL, None),
            P(None, ALL, None),
            P(None, ALL),
            P(None, ALL),
            P(None, ALL),
            P(),
            P(),
            P(),
            P(),
        ),
        out_specs=(
            P(),
            P(),
            P(None, ALL, None),
            P(None, ALL, None),
            P(None, ALL, None),
            P(None, ALL, None),
            P(None, ALL, None),
            P(None, ALL, None),
            P(ALL, None),
            P(ALL, None),
            P(ALL, None),
            P(None, ALL),
            P(None, ALL),
            P(None, ALL),
            P(),
            P(),
            P(),
            P(ALL),
        ),
        check_vma=False,
    )
```

```python
import math

import jax
import jax.numpy as jnp
from jax import lax
from jax.experimental import pallas as pl
from jax.experimental.pallas import tpu as pltpu
from jax.sharding import Mesh
from jax.sharding import PartitionSpec as P

D = 1024
HEADS = 16
KV = 8
HD = 64
FF = 4608
SEQ = 512
RESP = 96
NS_ITERS = 3


norm_epsilon = 1e-05
rope_base = 1000000.0
pref_beta = 2.0
clip_limit = 0.05
muon_decay = 0.95
muon_rate = 0.5
first_decay = 0.9
second_decay = 0.95
adam_rate = 0.02
adam_epsilon = 1e-08
weight_decay = 0.1
leading_coefficient = 3.4445
coef_second = -4.775
coef_third = 2.0315
ortho_epsilon = 1e-07
masked_score = -1e30


def rms_scale(inputs, gain):
    mean_square = jnp.mean(inputs * inputs, axis=-1, keepdims=True)
    return inputs * lax.rsqrt(mean_square + norm_epsilon) * gain


def rope_tables(length, half):
    position = jnp.arange(length, dtype=jnp.float32)
    inverse = rope_base ** (-jnp.arange(half, dtype=jnp.float32) / half)
    angle = position[:, None] * inverse[None, :]
    return (jnp.cos(angle)[:, None, :], jnp.sin(angle)[:, None, :])


def rotate(inputs, cosine, sine):
    half = inputs.shape[-1] // 2
    first = inputs[..., :half]
    second = inputs[..., half:]
    return jnp.concatenate(
        [first * cosine - second * sine, second * cosine + first * sine], axis=-1
    )


def dense(inputs, weight):
    return lax.dot_general(
        inputs, weight, (((1,), (1,)), ((), ())), preferred_element_type=jnp.float32
    )


def outer(grads, inputs):
    return lax.dot_general(
        grads, inputs, (((0,), (0,)), ((), ())), preferred_element_type=jnp.float32
    )


def back_dense(grads, weight):
    return jnp.dot(grads, weight, preferred_element_type=jnp.float32)


def delayed(values, offset):
    return jnp.pad(values, ((offset, 0), (0, 0)))[: values.shape[0]]


def advanced(values, offset):
    return jnp.pad(values, ((0, offset), (0, 0)))[offset:]


def norm_back(inputs, gain, grad_out):
    _, pullback = jax.vjp(rms_scale, inputs, gain)
    return pullback(grad_out)


def low_copy(values):
    return lax.optimization_barrier(values.astype(jnp.bfloat16)).astype(jnp.float32)


def adam_step(master, first, second, grad, factor, count):
    scaled = factor * grad
    first_new = first_decay * first + (1.0 - first_decay) * scaled
    second_new = second_decay * second + (1.0 - second_decay) * scaled * scaled
    steps = count.astype(jnp.float32)
    first_hat = first_new / (1.0 - first_decay**steps)
    second_hat = second_new / (1.0 - second_decay**steps)
    change = -adam_rate * (
        first_hat / (jnp.sqrt(second_hat) + adam_epsilon) + weight_decay * master
    )
    return (change, first_new, second_new)

DP = ("chip", "core")
ALL = ("chip", "core", "vocab")
SLOTS = 24
LATER_SLOTS = 8


def exchanged(rows):
    return lax.all_to_all(rows, ALL, 0, 0, tiled=True)


def spread(values):
    count = lax.axis_size(ALL)
    return lax.all_to_all(jnp.broadcast_to(values[None], (count,) + values.shape), ALL, 0, 0)


def turned(values, axis, step):
    count = lax.axis_size(axis)
    return lax.ppermute(values, axis, [(i, (i + step) % count) for i in range(count)])


def block_at(blocks, index):
    return lax.dynamic_index_in_dim(blocks, index % blocks.shape[0], 0, keepdims=False)


def handed_out(blocks, axis):
    place, count = lax.axis_index(axis), lax.axis_size(axis)
    return [block_at(blocks, place)] + [
        turned(block_at(blocks, place + step), axis, step) for step in range(1, count)
    ]


def handed_back(pieces, axis):
    return [pieces[0]] + [turned(pieces[step], axis, -step) for step in range(1, len(pieces))]


def gathered(values, axis):
    return [values] + [turned(values, axis, step) for step in range(1, lax.axis_size(axis))]


def placed_before(pieces, axis):
    pieces, place = jnp.stack(pieces), lax.axis_index(axis)
    return jnp.stack([block_at(pieces, place - j) for j in range(pieces.shape[0])])


def placed_after(pieces, axis):
    pieces, place = jnp.stack(pieces), lax.axis_index(axis)
    return jnp.stack([block_at(pieces, j - place) for j in range(pieces.shape[0])])


def added(pieces):
    total = pieces[0].astype(jnp.float32)
    for piece in pieces[1:]:
        total = total + piece.astype(jnp.float32)
    return total


def other_core(values):
    return lax.ppermute(values, "core", [(0, 1), (1, 0)])


def pair_sum(halves, core):
    given = lax.dynamic_index_in_dim(halves, 1 - core, 0, keepdims=False)
    kept = lax.dynamic_index_in_dim(halves, core, 0, keepdims=False)
    total = kept.astype(jnp.float32) + other_core(given).astype(jnp.float32)
    return total.astype(jnp.bfloat16)


def chip_sum(blocks):
    return added(handed_out(blocks, "chip"))


def group_sum(values, core):
    rows = values.shape[0] // 2
    chips = lax.axis_size("chip")
    half = pair_sum(values.reshape(2, rows, -1), core).reshape(chips, rows // chips, -1)
    part = chip_sum(half).astype(jnp.bfloat16)
    half = placed_before(gathered(part, "chip"), "chip").reshape(rows, -1)
    return half, other_core(half)


def member_gather(values):
    return jnp.concatenate(gathered(values, "vocab"), axis=0)


def member_return(pieces):
    return added(handed_back(pieces, "vocab"))


def member_scatter(blocks):
    return added(handed_out(blocks, "vocab"))


def onehot_rows(index, count):
    return (index[:, None] == jnp.arange(count)[None, :]).astype(jnp.bfloat16)


def token_slots(ids, block_rows):
    owner = ids // block_rows
    place = jnp.arange(ids.shape[0])
    earlier = place[:, None] > place[None, :]
    equal = ids[:, None] == ids[None, :]
    first = jnp.logical_not(jnp.any(equal & earlier, axis=1))
    ahead = (owner[:, None] == owner[None, :]) & earlier & first[None, :]
    rank = jnp.sum(ahead.astype(jnp.int32), axis=1)
    slot = jnp.sum(jnp.where(equal & first[None, :], rank[None, :], 0), axis=1)
    return owner, first, slot


def round_keys(owner, slot, first, count):
    within = slot - first
    return jnp.where((within >= 0) & (within < count), owner * count + within, -1)


def round_asks(keys, first_seen, local, count):
    hits = (keys[None, :] == jnp.arange(count)[:, None]) & first_seen[None, :]
    return jnp.sum(jnp.where(hits, local[None, :] + 1, 0), axis=1) - 1


def square_product(left, right):
    return jnp.dot(
        left.astype(jnp.bfloat16), right.astype(jnp.bfloat16), preferred_element_type=jnp.float32
    )


def rest_kernel(
    core_ref,
    first_ref,
    second_ref,
    square_ref,
    rest_ref,
    gram_scratch,
    change_scratch,
    rest_scratch,
    grams,
    change_b,
    rest_b,
):
    lead = leading_coefficient
    size = square_ref.shape[0]
    half = size // 2
    tile = 256

    def dot(left, right):
        return jnp.dot(left, right, preferred_element_type=jnp.float32)

    on_wide = core_ref[0] == 0
    for part, wide_ref in enumerate((first_ref, second_ref)):

        @pl.loop(0, half // tile)
        def _(step):
            rows = pl.ds(pl.multiple_of(step * tile, tile), tile)
            place = pl.ds(pl.multiple_of(part * half + step * tile, tile), tile)
            gram = jnp.where(on_wide, wide_ref[rows, :].astype(jnp.float32), square_ref[place, :])
            gram_scratch[place, :] = gram
            grams[0, place, :] = gram.astype(jnp.bfloat16)

    power = 1.0
    for turn in range(NS_ITERS):
        now, later = turn % 2, (turn + 1) % 2

        @pl.loop(0, size // tile)
        def _(step):
            rows = pl.ds(pl.multiple_of(step * tile, tile), tile)
            change = coef_second * gram_scratch[rows, :] + coef_third * dot(
                grams[now, rows, :], grams[now]
            )
            change_scratch[rows, :] = change
            change_b[rows, :] = change.astype(jnp.bfloat16)

        @pl.loop(0, size // tile)
        def _(step):
            rows = pl.ds(pl.multiple_of(step * tile, tile), tile)
            if turn == 0:
                rest = change_scratch[rows, :]
            else:
                rest = (
                    lead * rest_scratch[rows, :]
                    + power * change_scratch[rows, :]
                    + dot(rest_b[rows, :], change_b[...])
                )
            if turn + 1 < NS_ITERS:
                rest_scratch[rows, :] = rest
                rest_b[rows, :] = rest.astype(jnp.bfloat16)
                mixed = dot(change_b[rows, :], grams[now])
                gram = (
                    lead * lead * gram_scratch[rows, :]
                    + 2.0 * lead * mixed
                    + dot(mixed.astype(jnp.bfloat16), change_b[...])
                )
                gram_scratch[rows, :] = gram
                grams[later, rows, :] = gram.astype(jnp.bfloat16)
            else:
                rest_ref[rows, :] = rest.astype(jnp.bfloat16)

        power = power * lead


def ortho_rest(core, first, second, square):
    size = square.shape[0]
    wide = pltpu.VMEM((size, size), jnp.float32)
    narrow = pltpu.VMEM((size, size), jnp.bfloat16)
    return pl.pallas_call(
        rest_kernel,
        out_shape=jax.ShapeDtypeStruct((size, size), jnp.bfloat16),
        in_specs=[pl.BlockSpec(memory_space=pltpu.SMEM)]
        + [pl.BlockSpec(memory_space=pltpu.VMEM)] * 3,
        out_specs=pl.BlockSpec(memory_space=pltpu.VMEM),
        scratch_shapes=[
            wide,
            wide,
            wide,
            pltpu.VMEM((2, size, size), jnp.bfloat16),
            narrow,
            narrow,
        ],
        compiler_params=pltpu.CompilerParams(vmem_limit_bytes=44 * 1024 * 1024),
        cost_estimate=pl.CostEstimate(
            flops=18 * size**3, bytes_accessed=6 * size * size, transcendentals=0
        ),
    )(core.reshape(1), first, second, square)


def logits_kernel(target_ref, answers_ref, table_ref, shares_ref, stats_ref, logits):
    rows, width = logits.shape
    piece = 256
    target = target_ref[...]
    top = jnp.full((8, width), -jnp.inf, jnp.float32)
    total = jnp.zeros((8, width), jnp.float32)
    picked = jnp.zeros((8, width), jnp.float32)
    for first in range(0, rows, piece):
        scores = lax.dot_general(
            table_ref[first : first + piece, :],
            answers_ref[...],
            (((1,), (1,)), ((), ())),
            preferred_element_type=jnp.float32,
        )
        logits[first : first + piece, :] = scores
        top = jnp.maximum(top, jnp.max(scores.reshape(-1, 8, width), axis=0))
    top = jnp.max(top, axis=0, keepdims=True)
    for first in range(0, rows, piece):
        scores = logits[first : first + piece, :]
        share = jnp.exp(scores - top)
        shares_ref[first : first + piece, :] = share.astype(jnp.bfloat16)
        total = total + jnp.sum(share.reshape(-1, 8, width), axis=0)
        place = lax.broadcasted_iota(jnp.int32, (piece, width), 0)
        hit = jnp.where(place == target - first, scores, 0.0)
        picked = picked + jnp.sum(hit.reshape(-1, 8, width), axis=0)
    stats_ref[0:1, :] = top
    stats_ref[1:2, :] = jnp.sum(total, axis=0, keepdims=True)
    stats_ref[2:3, :] = jnp.sum(picked, axis=0, keepdims=True)
    stats_ref[3:8, :] = jnp.zeros((5, width), jnp.float32)


def answer_shares(target, answers, table):
    count, rows = answers.shape[0], table.shape[0]
    tile = 256
    return pl.pallas_call(
        logits_kernel,
        grid=(count // tile,),
        in_specs=[
            pl.BlockSpec((1, tile), lambda i: (0, i)),
            pl.BlockSpec((tile, D), lambda i: (i, 0)),
            pl.BlockSpec((rows, D), lambda i: (0, 0)),
        ],
        out_specs=[
            pl.BlockSpec((rows, tile), lambda i: (0, i)),
            pl.BlockSpec((8, tile), lambda i: (0, i)),
        ],
        out_shape=[
            jax.ShapeDtypeStruct((rows, count), jnp.bfloat16),
            jax.ShapeDtypeStruct((8, count), jnp.float32),
        ],
        scratch_shapes=[pltpu.VMEM((rows, tile), jnp.float32)],
        compiler_params=pltpu.CompilerParams(vmem_limit_bytes=40 * 1024 * 1024),
        cost_estimate=pl.CostEstimate(
            flops=2 * count * rows * D,
            bytes_accessed=2 * count * (rows + D),
            transcendentals=count * rows,
        ),
    )(target, answers, table)


def logit_grads(place, target, scale, value, shares):
    return jnp.where(place == target, value, shares.astype(jnp.float32) * scale).astype(jnp.bfloat16)


def grads_kernel(core_ref, target_ref, scale_ref, value_ref, shares_ref, table_ref, grads_ref):
    place = lax.broadcasted_iota(jnp.int32, shares_ref.shape, 0)
    grads = logit_grads(place, target_ref[...], scale_ref[...], value_ref[...], shares_ref[...])
    grads_ref[...] = lax.dot_general(
        grads, table_ref[...], (((0,), (0,)), ((), ())), preferred_element_type=jnp.float32
    ).astype(jnp.bfloat16)


def answer_grads(core, target, scale, value, shares, table, width):
    rows, count = shares.shape
    steps = count // (2 * width)
    row = pl.BlockSpec((1, width), lambda i, core_ref: (0, 2 * i + core_ref[0]))
    return pl.pallas_call(
        grads_kernel,
        grid_spec=pltpu.PrefetchScalarGridSpec(
            num_scalar_prefetch=1,
            grid=(steps,),
            in_specs=[
                row,
                row,
                row,
                pl.BlockSpec((rows, width), lambda i, core_ref: (0, 2 * i + core_ref[0])),
                pl.BlockSpec((rows, D), lambda i, core_ref: (0, 0)),
            ],
            out_specs=pl.BlockSpec((width, D), lambda i, core_ref: (i, 0)),
        ),
        out_shape=jax.ShapeDtypeStruct((steps * width, D), jnp.bfloat16),
        compiler_params=pltpu.CompilerParams(vmem_limit_bytes=40 * 1024 * 1024),
        cost_estimate=pl.CostEstimate(
            flops=2 * steps * width * rows * D,
            bytes_accessed=2 * steps * width * (rows + D),
            transcendentals=0,
        ),
    )(core.reshape(1), target, scale, value, shares, table)


def body(
    token_ids,
    seq_lengths,
    pair_order,
    table_master,
    table_first,
    table_second,
    square_master,
    square_moment,
    wide_master,
    wide_moment,
    vector_master,
    vector_first,
    vector_second,
    norm_gains,
    norm_first,
    norm_second,
    adam_count,
):
    members = lax.axis_size("vocab")
    member = lax.axis_index("vocab")
    block_rows = table_master.shape[0]
    lengths = seq_lengths[0]
    order = pair_order[0]
    groups_per = HEADS // KV
    scale = HD ** (-0.5)

    core = lax.axis_index("core")
    devices = lax.axis_size(ALL)
    device = lax.axis_index(ALL)
    groups = devices // members

    own_ids = lax.dynamic_index_in_dim(token_ids, member, 0, keepdims=False)
    own_length = lengths[member]
    start = own_length - 1 - RESP
    owner, first_seen, slot = token_slots(own_ids, block_rows)
    local_ids = own_ids % block_rows
    keys = round_keys(owner, slot, 0, SLOTS)
    asks = round_asks(keys, first_seen, local_ids, devices * SLOTS)
    own_targets = lax.dynamic_slice_in_dim(own_ids, start + 1, RESP, 0)
    vector_low = vector_master.astype(jnp.bfloat16).astype(jnp.float32)
    shared_notes = jnp.concatenate(
        [
            vector_low.reshape(-1),
            jnp.concatenate([own_targets, order, jnp.max(slot)[None] + 1]).astype(jnp.float32),
        ]
    )
    notes = jnp.concatenate(
        [
            asks.reshape(devices, SLOTS).astype(jnp.float32),
            jnp.broadcast_to(shared_notes[None, :], (devices, shared_notes.size)),
        ],
        axis=1,
    )
    notes = exchanged(notes)
    square_b = lax.all_gather(square_master.astype(jnp.bfloat16), ALL, axis=1, tiled=True)
    wide_b = lax.all_gather(wide_master.astype(jnp.bfloat16), DP, axis=1, tiled=True)
    hidden_units = wide_b.shape[1]
    asked = notes[:, :SLOTS].astype(jnp.int32).reshape(-1)
    gains = (
        notes[:, SLOTS : SLOTS + vector_low.size]
        .reshape(devices, vector_low.shape[0], vector_low.shape[1])
        .transpose(1, 0, 2)
        .reshape(vector_low.shape[0], D)
    )
    numbers = notes[:, SLOTS + vector_low.size :].astype(jnp.int32)
    targets = numbers[:, :RESP].reshape(-1)
    orders = numbers[:, RESP : RESP + members].reshape(groups, members, members)[:, 0]
    later = jnp.maximum(jnp.max(numbers[:, RESP + members]) - SLOTS, 0)
    later_turns = (later + LATER_SLOTS - 1) // LATER_SLOTS
    slots = jnp.arange(members)
    chosen_mask = (orders[:, 0::2, None] == slots[None, None, :]).astype(jnp.float32)
    rejected_mask = (orders[:, 1::2, None] == slots[None, None, :]).astype(jnp.float32)
    pair_rows = jnp.sum(
        (chosen_mask + rejected_mask)[:, :, :, None] * (chosen_mask - rejected_mask)[:, :, None, :],
        axis=1,
    )
    same_group = jnp.arange(groups)[:, None] == jnp.arange(groups)[None, :]
    pair_rows = jnp.where(same_group[:, None, :, None], pair_rows[:, :, None, :], 0.0)
    pair_rows = pair_rows.reshape(devices, devices) * (pref_beta / RESP)
    chosen_sign = jnp.sum(chosen_mask - rejected_mask, axis=1).reshape(devices, 1)
    table_b = table_master.astype(jnp.bfloat16)
    head_gains = low_copy(norm_gains)
    cosine, sine = rope_tables(SEQ, HD // 2)

    def fetched(wanted, row_keys):
        rows = jnp.dot(
            onehot_rows(wanted, block_rows), table_b, preferred_element_type=jnp.float32
        ).astype(jnp.bfloat16)
        return jnp.dot(
            onehot_rows(row_keys, wanted.shape[0]),
            exchanged(rows),
            preferred_element_type=jnp.float32,
        )

    def later_round(turn):
        count = devices * LATER_SLOTS
        later_keys = round_keys(owner, slot, SLOTS + turn * LATER_SLOTS, LATER_SLOTS)
        return later_keys, exchanged(round_asks(later_keys, first_seen, local_ids, count))

    def fetch_more(turn, rows):
        later_keys, later_asked = later_round(turn)
        return rows + fetched(later_asked, later_keys)

    hidden0 = lax.fori_loop(0, later_turns, fetch_more, fetched(asked, keys))
    act1 = rms_scale(hidden0, gains[0]).astype(jnp.bfloat16)
    entry, leave, conv_in = (dense(act1, square_b[place]) for place in range(3))
    product = entry * conv_in
    convolved = gains[4] * product + gains[5] * delayed(product, 1) + gains[6] * delayed(product, 2)
    mixer = (leave * convolved).astype(jnp.bfloat16)
    hidden1 = hidden0 + dense(mixer, square_b[3])
    act2 = rms_scale(hidden1, gains[1]).astype(jnp.bfloat16)

    def answers(values):
        return lax.dynamic_slice_in_dim(values, start, RESP, 0)

    def placed(values):
        return lax.dynamic_update_slice_in_dim(
            jnp.zeros((SEQ, values.shape[1]), values.dtype), values, start, 0
        )

    answer_act2 = answers(act2)
    query_raw = dense(answer_act2, square_b[4]).reshape(RESP, HEADS, HD)
    pair_raw = dense(act2, square_b[5])
    key_raw = pair_raw[:, : KV * HD].reshape(SEQ, KV, HD)
    value_b = pair_raw[:, KV * HD :].astype(jnp.bfloat16).reshape(SEQ, KV, HD)

    answer_cosine, answer_sine = answers(cosine), answers(sine)

    def query_prep(raw, gain):
        return rotate(rms_scale(raw, gain), answer_cosine, answer_sine)

    def key_prep(raw, gain):
        return rotate(rms_scale(raw, gain), cosine, sine)

    query_b = (
        query_prep(query_raw, head_gains[0]).astype(jnp.bfloat16).reshape(RESP, KV, groups_per, HD)
    )
    key_b = key_prep(key_raw, head_gains[1]).astype(jnp.bfloat16)
    causal = start + jnp.arange(RESP)[:, None] >= jnp.arange(SEQ)[None, :]
    scores = (
        jnp.einsum("sgrd,tgd->grst", query_b, key_b, preferred_element_type=jnp.float32) * scale
    )
    scores = jnp.where(causal, scores, masked_score)
    peak = jnp.max(scores, axis=-1, keepdims=True)
    expo = jnp.exp(scores - peak)
    total = jnp.sum(expo, axis=-1, keepdims=True)
    log_norm = peak + jnp.log(total)
    probs_b = (expo / total).astype(jnp.bfloat16)
    attended = jnp.einsum(
        "grst,tgd->sgrd", probs_b, value_b, preferred_element_type=jnp.float32
    ).reshape(RESP, D)
    attended_b = attended.astype(jnp.bfloat16)
    hidden2 = answers(hidden1) + dense(attended_b, square_b[6])
    act3 = member_gather(rms_scale(hidden2, gains[2]).astype(jnp.bfloat16))
    gate_part, up_part = dense(act3, wide_b[0]), dense(act3, wide_b[1])
    inner_b = (jax.nn.silu(gate_part) * up_part).astype(jnp.bfloat16)
    ffn_part = jnp.dot(inner_b, wide_b[2], preferred_element_type=jnp.float32)
    hidden3 = hidden2 + member_return(ffn_part.astype(jnp.bfloat16).reshape(members, RESP, D))
    final_b = rms_scale(hidden3, gains[3]).astype(jnp.bfloat16)
    squares, square_rows = square_master.shape[0], square_master.shape[1]
    wides, wide_rows = wide_master.shape[0], wide_master.shape[1]
    per_member = -(-squares // members)
    group_rows = members * square_rows

    def by_member(values):
        values = jnp.pad(values, ((0, per_member * members - squares), (0, 0), (0, 0)))
        return values.reshape(per_member, members, -1, D).transpose(1, 0, 2, 3)

    def wide_by_member(values):
        return jnp.pad(values, ((0, members - wides), (0, 0), (0, 0)))

    moment_blocks = jnp.concatenate(
        [
            wide_by_member(wide_moment.astype(jnp.bfloat16)),
            by_member(square_moment.astype(jnp.bfloat16)).reshape(members, -1, D),
        ],
        axis=1,
    )
    final_b, moment_blocks = lax.optimization_barrier((final_b, moment_blocks))
    response_tokens = lax.all_gather(final_b, ALL, axis=0, tiled=True)
    response_tokens, moment_jobs = lax.optimization_barrier(
        (response_tokens, handed_out(moment_blocks, "vocab"))
    )
    wide_moment_job = jnp.stack([piece[:wide_rows] for piece in moment_jobs])
    square_moment_job = placed_before([piece[wide_rows:] for piece in moment_jobs], "vocab")
    square_moment_job = square_moment_job.reshape(members, per_member, square_rows, D)
    square_moment_job = square_moment_job.transpose(1, 0, 2, 3).reshape(per_member, group_rows, D)
    local_target = jnp.where(targets // block_rows == device, targets % block_rows, -1)[None, :]
    shares, own_stats = answer_shares(local_target, response_tokens, table_b)
    stats = own_stats[:3].reshape(3, devices, RESP).transpose(1, 0, 2)
    stats = exchanged(stats)
    top = jnp.max(stats[:, 0], axis=0)
    exp_total = jnp.sum(stats[:, 1] * jnp.exp(stats[:, 0] - top[None, :]), axis=0)
    own_log_total = top + jnp.log(exp_total)
    own_logp = jnp.sum(jnp.sum(stats[:, 2], axis=0) - own_log_total)
    joined = spread(jnp.concatenate([own_log_total, own_logp[None]]))
    log_total = joined[:, :RESP].reshape(1, -1)
    margin = jnp.sum(pair_rows * joined[:, RESP][None, :], axis=1, keepdims=True)
    pair_loss = 0.5 * jnp.sum(jax.nn.softplus(-margin))
    grad_logp = chosen_sign * jax.nn.sigmoid(-margin) * (-pref_beta / RESP)
    row_weight = jnp.broadcast_to(grad_logp, (devices, RESP)).reshape(1, -1)
    share_scale = -row_weight * jnp.exp(own_stats[0:1] - log_total)
    target_value = row_weight * (1.0 - jnp.exp(own_stats[2:3] - log_total))
    given, kept = (
        answer_grads(
            which, local_target, share_scale, target_value, shares, table_b, members * RESP
        )
        for which in (1 - core, core)
    )
    grad_answer_pair = (kept.astype(jnp.float32) + other_core(given).astype(jnp.float32)).astype(
        jnp.bfloat16
    )
    grad_answer_group = chip_sum(grad_answer_pair.reshape(groups // 2, members * RESP, D))
    grad_table = jnp.dot(
        logit_grads(
            jnp.arange(block_rows)[:, None], local_target, share_scale, target_value, shares
        ),
        response_tokens,
        preferred_element_type=jnp.float32,
    )
    grad_answer_group, grad_table = lax.optimization_barrier(
        (grad_answer_group.astype(jnp.bfloat16), grad_table)
    )
    grad_final = member_scatter(grad_answer_group.reshape(members, RESP, D))
    grad_hidden3, grad_gain3 = norm_back(hidden3, gains[3], grad_final)
    grad_ffn_out = member_gather(grad_hidden3.astype(jnp.bfloat16))
    grad_inner = dense(grad_ffn_out, wide_b[2])
    grad_down_w = outer(inner_b, grad_ffn_out)
    _, silu_pull = jax.vjp(lambda gate_in, up_in: jax.nn.silu(gate_in) * up_in, gate_part, up_part)
    grad_gate, grad_up = silu_pull(grad_inner)
    grad_gate_b, grad_up_b = grad_gate.astype(jnp.bfloat16), grad_up.astype(jnp.bfloat16)
    grad_act3_part = back_dense(grad_gate_b, wide_b[0]) + back_dense(grad_up_b, wide_b[1])
    grad_act3 = member_return(grad_act3_part.astype(jnp.bfloat16).reshape(members, RESP, D))
    grad_gate_w, grad_up_w = outer(grad_gate_b, act3), outer(grad_up_b, act3)
    grad_norm2, grad_gain2 = norm_back(hidden2, gains[2], grad_act3)
    grad_hidden2 = grad_hidden3 + grad_norm2
    grad_attn_out = grad_hidden2.astype(jnp.bfloat16)
    grad_attended = (
        back_dense(grad_attn_out, square_b[6])
        .astype(jnp.bfloat16)
        .reshape(RESP, KV, groups_per, HD)
    )
    grad_out_w = outer(grad_attn_out, attended_b)
    scores = (
        jnp.einsum("sgrd,tgd->grst", query_b, key_b, preferred_element_type=jnp.float32) * scale
    )
    probs = jnp.exp(jnp.where(causal, scores, masked_score) - log_norm)
    grad_probs = jnp.einsum(
        "sgrd,tgd->grst", grad_attended, value_b, preferred_element_type=jnp.float32
    )
    grad_values = jnp.einsum(
        "grst,sgrd->tgd", probs_b, grad_attended, preferred_element_type=jnp.float32
    )
    delta = jnp.sum(probs * grad_probs, axis=-1, keepdims=True)
    grad_scores = (probs * (grad_probs - delta)).astype(jnp.bfloat16)
    grad_query = (
        jnp.einsum("grst,tgd->sgrd", grad_scores, key_b, preferred_element_type=jnp.float32) * scale
    ).reshape(RESP, HEADS, HD)
    grad_keys = (
        jnp.einsum("grst,sgrd->tgd", grad_scores, query_b, preferred_element_type=jnp.float32)
        * scale
    )
    _, query_pull = jax.vjp(query_prep, query_raw, head_gains[0])
    grad_query_raw, grad_query_gain = query_pull(grad_query)
    _, key_pull = jax.vjp(key_prep, key_raw, head_gains[1])
    grad_key_raw, grad_key_gain = key_pull(grad_keys)
    grad_query_b = grad_query_raw.reshape(RESP, D).astype(jnp.bfloat16)
    grad_pair_b = jnp.concatenate(
        [grad_key_raw.reshape(SEQ, KV * HD), grad_values.reshape(SEQ, KV * HD)], axis=1
    ).astype(jnp.bfloat16)
    grad_act2 = back_dense(grad_pair_b, square_b[5]) + placed(back_dense(grad_query_b, square_b[4]))
    grad_query_w = outer(grad_query_b, answer_act2)
    grad_pair_w = outer(grad_pair_b, act2)
    grad_norm1, grad_gain1 = norm_back(hidden1, gains[1], grad_act2)
    grad_hidden1 = placed(grad_hidden2) + grad_norm1
    grad_mix_out = grad_hidden1.astype(jnp.bfloat16)
    grad_mixer = back_dense(grad_mix_out, square_b[3])
    grad_mixer_w = outer(grad_mix_out, mixer)
    grad_leave = grad_mixer * convolved
    grad_conv = grad_mixer * leave
    grad_tap0 = jnp.sum(grad_conv * product, axis=0)
    grad_tap1 = jnp.sum(grad_conv * delayed(product, 1), axis=0)
    grad_tap2 = jnp.sum(grad_conv * delayed(product, 2), axis=0)
    grad_product = (
        gains[4] * grad_conv + gains[5] * advanced(grad_conv, 1) + gains[6] * advanced(grad_conv, 2)
    )
    grad_inner = [
        part.astype(jnp.bfloat16)
        for part in (grad_product * conv_in, grad_leave, grad_product * entry)
    ]
    grad_act1 = sum(back_dense(grad_inner[place], square_b[place]) for place in range(3))
    grad_inner_w = [outer(part, act1) for part in grad_inner]
    grad_norm0, grad_gain0 = norm_back(hidden0, gains[0], grad_act1)
    grad_embed_b = (grad_hidden1 + grad_norm0).astype(jnp.bfloat16)

    grad_square = jnp.stack(
        [
            part.astype(jnp.bfloat16)
            for part in (*grad_inner_w, grad_mixer_w, grad_query_w, grad_pair_w, grad_out_w)
        ]
    )
    grad_vector = jnp.stack(
        [grad_gain0, grad_gain1, grad_gain2, grad_gain3, grad_tap0, grad_tap1, grad_tap2]
    )
    grad_head_gains = jnp.stack([grad_query_gain, grad_key_gain])
    grad_wide = jnp.stack(
        [part.astype(jnp.bfloat16) for part in (grad_gate_w, grad_up_w, grad_down_w)]
    )
    share_wide_b = lax.psum_scatter(grad_wide, DP, scatter_dimension=1, tiled=True)
    grad_square, share_wide_b = lax.optimization_barrier((grad_square, share_wide_b))
    share_wide_b, grad_embed_b = lax.optimization_barrier((share_wide_b, grad_embed_b))
    share_wide = share_wide_b.astype(jnp.float32)
    wide_grad_job = jnp.stack(handed_out(wide_by_member(share_wide_b), "vocab"))
    group_square = lax.psum_scatter(grad_square, DP, scatter_dimension=1, tiled=True)
    square_grad_job = member_scatter(by_member(group_square))

    def from_members(values):
        values = values.reshape(per_member, members, square_rows, D).transpose(1, 0, 2, 3)
        values = placed_before(handed_out(values.astype(jnp.bfloat16), "vocab"), "vocab")
        values = values.transpose(1, 0, 2, 3).reshape(per_member * members, square_rows, D)
        return values[:squares].astype(jnp.float32)

    share_square = from_members(square_grad_job)

    def returned(row_keys, count):
        rows = outer(onehot_rows(row_keys, count), grad_embed_b)
        return exchanged(rows.astype(jnp.bfloat16))

    def put(wanted, rows):
        return outer(onehot_rows(wanted, block_rows), rows)

    def return_more(turn, total):
        later_keys, later_asked = later_round(turn)
        return total + put(later_asked, returned(later_keys, later_asked.shape[0]))

    returned_rows, wide_grad_job = lax.optimization_barrier(
        (returned(keys, devices * SLOTS), wide_grad_job)
    )
    share_table = lax.fori_loop(
        0, later_turns, return_more, grad_table + put(asked, returned_rows))
    width = vector_master.shape[1]
    vector_notes = grad_vector.reshape(-1, devices, width).transpose(1, 0, 2).reshape(devices, -1)
    vector_notes = jnp.concatenate(
        [
            vector_notes,
            jnp.broadcast_to(grad_head_gains.reshape(1, -1), (devices, grad_head_gains.size)),
        ],
        axis=1,
    )
    vector_notes = jnp.sum(exchanged(vector_notes), axis=0)
    share_vector = vector_notes[: vector_master.size].reshape(vector_master.shape)
    gains_total = vector_notes[vector_master.size :].reshape(grad_head_gains.shape)

    def job_sums(values):
        sums = jnp.sum(values, axis=(1, 2))[:, None]
        sums = jnp.where(jnp.arange(members)[None, :] == member, sums, 0.0)
        return sums.reshape(-1)[:squares]

    moment_squares = jnp.concatenate(
        [
            jnp.sum(square_moment * square_moment, axis=(1, 2)),
            jnp.sum(wide_moment * wide_moment, axis=(1, 2)),
        ]
    )
    moment_cross = jnp.concatenate(
        [
            job_sums(square_moment_job.astype(jnp.float32) * square_grad_job),
            jnp.sum(wide_moment * share_wide, axis=(1, 2)),
        ]
    )
    grad_squares = jnp.concatenate(
        [
            job_sums(square_grad_job * square_grad_job),
            jnp.sum(share_wide * share_wide, axis=(1, 2)),
        ]
    )
    moment_stats = jnp.stack([moment_squares, moment_cross, grad_squares])
    own_squares = (
        jnp.sum(grad_squares)
        + jnp.sum(share_vector * share_vector)
        + jnp.sum(share_table * share_table)
    )
    sums = jnp.concatenate([moment_stats.reshape(-1), own_squares[None]])
    sums = jnp.sum(spread(sums), axis=0)
    stats_total = sums[:-1].reshape(moment_stats.shape)
    grad_norm = jnp.sqrt(sums[-1] + jnp.sum(gains_total * gains_total))
    factor = jnp.minimum(1.0, clip_limit / grad_norm)
    square_moment_new = muon_decay * square_moment + (1.0 - muon_decay) * (factor * share_square)
    wide_moment_new = muon_decay * wide_moment + (1.0 - muon_decay) * (factor * share_wide)
    moment_norm = jnp.sqrt(
        muon_decay * muon_decay * stats_total[0]
        + 2.0 * muon_decay * (1.0 - muon_decay) * factor * stats_total[1]
        + (1.0 - muon_decay) * (1.0 - muon_decay) * factor * factor * stats_total[2]
    )
    ortho_square = square_moment_new / (moment_norm[:7][:, None, None] + ortho_epsilon)
    ortho_wide = wide_moment_new / (moment_norm[7:][:, None, None] + ortho_epsilon)
    wide_inverse = 1.0 / (moment_norm[squares:] + ortho_epsilon)
    wide_inverse = jnp.pad(wide_inverse, (0, members - wides))[member]
    square_inverse = 1.0 / (moment_norm[:squares] + ortho_epsilon)
    square_inverse = jnp.pad(square_inverse, (0, per_member * members - squares))
    square_inverse = square_inverse.reshape(per_member, members)[:, member][:, None, None]
    square_part = (muon_decay * square_inverse) * square_moment_job.astype(jnp.float32) + (
        (1.0 - muon_decay) * factor * square_inverse
    ) * square_grad_job
    square_part, wide_grad_job = lax.optimization_barrier(
        (square_part.astype(jnp.bfloat16), wide_grad_job)
    )
    square_part = jnp.pad(square_part, ((0, groups // 2 - per_member), (0, 0), (0, 0)))
    square_half = jnp.concatenate(handed_out(square_part, "chip"), axis=0)
    square_job = jnp.concatenate([square_half, other_core(square_half)], axis=0)
    wide_job = (
        (muon_decay * wide_inverse) * wide_moment_job.astype(jnp.float32)
        + ((1.0 - muon_decay) * factor * wide_inverse) * wide_grad_job.astype(jnp.float32)
    )
    wide_job = wide_job.reshape(members * wide_rows, D).astype(jnp.bfloat16)
    wide_first, wide_second = group_sum(outer(wide_job, wide_job).astype(jnp.bfloat16), core)
    square_gram = outer(square_job, square_job)
    rest_b = ortho_rest(core, wide_first, wide_second, square_gram)
    power = leading_coefficient**NS_ITERS
    wide_rest = jnp.where(core == 0, rest_b, other_core(rest_b))
    back_square = square_product(square_job, rest_b).astype(jnp.bfloat16)
    half_rows = square_half.shape[0]
    back_square = jnp.where(
        core == 0, other_core(back_square[half_rows:]), back_square[:half_rows]
    )
    back_wide = square_product(wide_job, wide_rest).astype(jnp.bfloat16)
    share_table, back_square, back_wide = lax.optimization_barrier(
        (share_table, back_square, back_wide)
    )
    table_step, table_first_new, table_second_new = adam_step(
        table_master, table_first, table_second, share_table, factor, adam_count
    )
    back_square = handed_back(list(back_square.reshape(-1, group_rows, D)), "chip")
    back_square = placed_after(back_square, "chip")[:per_member]
    back_wide = handed_back(list(back_wide.reshape(members, wide_rows, D)), "vocab")
    back_wide = placed_after(back_wide, "vocab")[:wides]
    back_square = from_members(back_square)
    ortho_wide = power * ortho_wide + back_wide.astype(jnp.float32)
    ortho_square = power * ortho_square + back_square
    wide_scale = jnp.array([math.sqrt(FF / D), math.sqrt(FF / D), 1.0], jnp.float32)
    square_new = square_master - muon_rate * ortho_square
    wide_new = wide_master - muon_rate * wide_scale[:, None, None] * ortho_wide
    vector_step, vector_first_new, vector_second_new = adam_step(
        vector_master, vector_first, vector_second, share_vector, factor, adam_count
    )
    norm_step, norm_first_new, norm_second_new = adam_step(
        norm_gains, norm_first, norm_second, gains_total, factor, adam_count
    )
    return (
        pair_loss,
        grad_norm,
        square_new,
        square_moment_new,
        square_new.astype(jnp.bfloat16),
        wide_new,
        wide_moment_new,
        wide_new.astype(jnp.bfloat16),
        table_step,
        table_first_new,
        table_second_new,
        vector_step,
        vector_first_new,
        vector_second_new,
        norm_step,
        norm_first_new,
        norm_second_new,
        share_vector[3],
    )


def solution(mesh):
    groups, members = mesh.shape["dp"], mesh.shape["vocab"]
    cores = 2
    split_mesh = Mesh(mesh.devices.reshape(groups // cores, cores, members), ALL)
    return jax.shard_map(
        body,
        mesh=split_mesh,
        in_specs=(
            P(DP, None),
            P(DP, None),
            P(DP, None),
            P(ALL, None),
            P(ALL, None),
            P(ALL, None),
            P(None, ALL, None),
            P(None, ALL, None),
            P(None, ALL, None),
            P(None, ALL, None),
            P(None, ALL),
            P(None, ALL),
            P(None, ALL),
            P(),
            P(),
            P(),
            P(),
        ),
        out_specs=(
            P(),
            P(),
            P(None, ALL, None),
            P(None, ALL, None),
            P(None, ALL, None),
            P(None, ALL, None),
            P(None, ALL, None),
            P(None, ALL, None),
            P(ALL, None),
            P(ALL, None),
            P(ALL, None),
            P(None, ALL),
            P(None, ALL),
            P(None, ALL),
            P(),
            P(),
            P(),
            P(ALL),
        ),
        check_vma=False,
    )
```

```python
import math

import jax
import jax.numpy as jnp
from jax import lax
from jax.experimental import pallas as pl
from jax.experimental.pallas import tpu as pltpu
from jax.sharding import Mesh
from jax.sharding import PartitionSpec as P

D = 1024
HEADS = 16
KV = 8
HD = 64
FF = 4608
SEQ = 512
RESP = 96
NS_ITERS = 3


norm_epsilon = 1e-05
rope_base = 1000000.0
pref_beta = 2.0
clip_limit = 0.05
muon_decay = 0.95
muon_rate = 0.5
first_decay = 0.9
second_decay = 0.95
adam_rate = 0.02
adam_epsilon = 1e-08
weight_decay = 0.1
leading_coefficient = 3.4445
coef_second = -4.775
coef_third = 2.0315
ortho_epsilon = 1e-07
masked_score = -1e30


def rms_scale(inputs, gain):
    mean_square = jnp.mean(inputs * inputs, axis=-1, keepdims=True)
    return inputs * lax.rsqrt(mean_square + norm_epsilon) * gain


def rope_tables(length, half):
    position = jnp.arange(length, dtype=jnp.float32)
    inverse = rope_base ** (-jnp.arange(half, dtype=jnp.float32) / half)
    angle = position[:, None] * inverse[None, :]
    return (jnp.cos(angle)[:, None, :], jnp.sin(angle)[:, None, :])


def rotate(inputs, cosine, sine):
    half = inputs.shape[-1] // 2
    first = inputs[..., :half]
    second = inputs[..., half:]
    return jnp.concatenate(
        [first * cosine - second * sine, second * cosine + first * sine], axis=-1
    )


def dense(inputs, weight):
    return lax.dot_general(
        inputs, weight, (((1,), (1,)), ((), ())), preferred_element_type=jnp.float32
    )


def outer(grads, inputs):
    return lax.dot_general(
        grads, inputs, (((0,), (0,)), ((), ())), preferred_element_type=jnp.float32
    )


def back_dense(grads, weight):
    return jnp.dot(grads, weight, preferred_element_type=jnp.float32)


def delayed(values, offset):
    return jnp.pad(values, ((offset, 0), (0, 0)))[: values.shape[0]]


def advanced(values, offset):
    return jnp.pad(values, ((0, offset), (0, 0)))[offset:]


def norm_back(inputs, gain, grad_out):
    _, pullback = jax.vjp(rms_scale, inputs, gain)
    return pullback(grad_out)


def low_copy(values):
    return lax.optimization_barrier(values.astype(jnp.bfloat16)).astype(jnp.float32)


def adam_step(master, first, second, grad, factor, count):
    scaled = factor * grad
    first_new = first_decay * first + (1.0 - first_decay) * scaled
    second_new = second_decay * second + (1.0 - second_decay) * scaled * scaled
    steps = count.astype(jnp.float32)
    first_hat = first_new / (1.0 - first_decay**steps)
    second_hat = second_new / (1.0 - second_decay**steps)
    change = -adam_rate * (
        first_hat / (jnp.sqrt(second_hat) + adam_epsilon) + weight_decay * master
    )
    return (change, first_new, second_new)

DP = ("chip", "core")
ALL = ("chip", "core", "vocab")
SLOTS = 24
LATER_SLOTS = 8


def exchanged(rows):
    return lax.all_to_all(rows, ALL, 0, 0, tiled=True)


def spread(values):
    count = lax.axis_size(ALL)
    return lax.all_to_all(jnp.broadcast_to(values[None], (count,) + values.shape), ALL, 0, 0)


def turned(values, axis, step):
    count = lax.axis_size(axis)
    return lax.ppermute(values, axis, [(i, (i + step) % count) for i in range(count)])


def block_at(blocks, index):
    return lax.dynamic_index_in_dim(blocks, index % blocks.shape[0], 0, keepdims=False)


def handed_out(blocks, axis):
    place, count = lax.axis_index(axis), lax.axis_size(axis)
    return [block_at(blocks, place)] + [
        turned(block_at(blocks, place + step), axis, step) for step in range(1, count)
    ]


def handed_back(pieces, axis):
    return [pieces[0]] + [turned(pieces[step], axis, -step) for step in range(1, len(pieces))]


def gathered(values, axis):
    return [values] + [turned(values, axis, step) for step in range(1, lax.axis_size(axis))]


def placed_before(pieces, axis):
    pieces, place = jnp.stack(pieces), lax.axis_index(axis)
    return jnp.stack([block_at(pieces, place - j) for j in range(pieces.shape[0])])


def placed_after(pieces, axis):
    pieces, place = jnp.stack(pieces), lax.axis_index(axis)
    return jnp.stack([block_at(pieces, j - place) for j in range(pieces.shape[0])])


def added(pieces):
    total = pieces[0].astype(jnp.float32)
    for piece in pieces[1:]:
        total = total + piece.astype(jnp.float32)
    return total


def other_core(values):
    return lax.ppermute(values, "core", [(0, 1), (1, 0)])


def pair_sum(halves, core):
    given = lax.dynamic_index_in_dim(halves, 1 - core, 0, keepdims=False)
    kept = lax.dynamic_index_in_dim(halves, core, 0, keepdims=False)
    total = kept.astype(jnp.float32) + other_core(given).astype(jnp.float32)
    return total.astype(jnp.bfloat16)


def chip_sum(blocks):
    return added(handed_out(blocks, "chip"))


def group_sum(values, core):
    rows = values.shape[0] // 2
    chips = lax.axis_size("chip")
    half = pair_sum(values.reshape(2, rows, -1), core).reshape(chips, rows // chips, -1)
    part = chip_sum(half).astype(jnp.bfloat16)
    half = placed_before(gathered(part, "chip"), "chip").reshape(rows, -1)
    return half, other_core(half)


def member_gather(values):
    return jnp.concatenate(gathered(values, "vocab"), axis=0)


def member_return(pieces):
    return added(handed_back(pieces, "vocab"))


def member_scatter(blocks):
    return added(handed_out(blocks, "vocab"))


def onehot_rows(index, count):
    return (index[:, None] == jnp.arange(count)[None, :]).astype(jnp.bfloat16)


def token_slots(ids, block_rows):
    owner = ids // block_rows
    place = jnp.arange(ids.shape[0])
    earlier = place[:, None] > place[None, :]
    equal = ids[:, None] == ids[None, :]
    first = jnp.logical_not(jnp.any(equal & earlier, axis=1))
    ahead = (owner[:, None] == owner[None, :]) & earlier & first[None, :]
    rank = jnp.sum(ahead.astype(jnp.int32), axis=1)
    slot = jnp.sum(jnp.where(equal & first[None, :], rank[None, :], 0), axis=1)
    return owner, first, slot


def round_keys(owner, slot, first, count):
    within = slot - first
    return jnp.where((within >= 0) & (within < count), owner * count + within, -1)


def round_asks(keys, first_seen, local, count):
    hits = (keys[None, :] == jnp.arange(count)[:, None]) & first_seen[None, :]
    return jnp.sum(jnp.where(hits, local[None, :] + 1, 0), axis=1) - 1


def square_product(left, right):
    return jnp.dot(
        left.astype(jnp.bfloat16), right.astype(jnp.bfloat16), preferred_element_type=jnp.float32
    )


def rest_kernel(
    core_ref,
    first_ref,
    second_ref,
    square_ref,
    rest_ref,
    gram_scratch,
    change_scratch,
    rest_scratch,
    grams,
    change_b,
    rest_b,
):
    lead = leading_coefficient
    size = square_ref.shape[0]
    half = size // 2
    tile = 256

    def dot(left, right):
        return jnp.dot(left, right, preferred_element_type=jnp.float32)

    on_wide = core_ref[0] == 0
    for part, wide_ref in enumerate((first_ref, second_ref)):

        @pl.loop(0, half // tile)
        def _(step):
            rows = pl.ds(pl.multiple_of(step * tile, tile), tile)
            place = pl.ds(pl.multiple_of(part * half + step * tile, tile), tile)
            gram = jnp.where(on_wide, wide_ref[rows, :].astype(jnp.float32), square_ref[place, :])
            gram_scratch[place, :] = gram
            grams[0, place, :] = gram.astype(jnp.bfloat16)

    power = 1.0
    for turn in range(NS_ITERS):
        now, later = turn % 2, (turn + 1) % 2

        @pl.loop(0, size // tile)
        def _(step):
            rows = pl.ds(pl.multiple_of(step * tile, tile), tile)
            change = coef_second * gram_scratch[rows, :] + coef_third * dot(
                grams[now, rows, :], grams[now]
            )
            change_scratch[rows, :] = change
            change_b[rows, :] = change.astype(jnp.bfloat16)

        @pl.loop(0, size // tile)
        def _(step):
            rows = pl.ds(pl.multiple_of(step * tile, tile), tile)
            if turn == 0:
                rest = change_scratch[rows, :]
            else:
                rest = (
                    lead * rest_scratch[rows, :]
                    + power * change_scratch[rows, :]
                    + dot(rest_b[rows, :], change_b[...])
                )
            if turn + 1 < NS_ITERS:
                rest_scratch[rows, :] = rest
                rest_b[rows, :] = rest.astype(jnp.bfloat16)
                mixed = dot(change_b[rows, :], grams[now])
                gram = (
                    lead * lead * gram_scratch[rows, :]
                    + 2.0 * lead * mixed
                    + dot(mixed.astype(jnp.bfloat16), change_b[...])
                )
                gram_scratch[rows, :] = gram
                grams[later, rows, :] = gram.astype(jnp.bfloat16)
            else:
                rest_ref[rows, :] = rest.astype(jnp.bfloat16)

        power = power * lead


def ortho_rest(core, first, second, square):
    size = square.shape[0]
    wide = pltpu.VMEM((size, size), jnp.float32)
    narrow = pltpu.VMEM((size, size), jnp.bfloat16)
    return pl.pallas_call(
        rest_kernel,
        out_shape=jax.ShapeDtypeStruct((size, size), jnp.bfloat16),
        in_specs=[pl.BlockSpec(memory_space=pltpu.SMEM)]
        + [pl.BlockSpec(memory_space=pltpu.VMEM)] * 3,
        out_specs=pl.BlockSpec(memory_space=pltpu.VMEM),
        scratch_shapes=[
            wide,
            wide,
            wide,
            pltpu.VMEM((2, size, size), jnp.bfloat16),
            narrow,
            narrow,
        ],
        compiler_params=pltpu.CompilerParams(vmem_limit_bytes=44 * 1024 * 1024),
        cost_estimate=pl.CostEstimate(
            flops=18 * size**3, bytes_accessed=6 * size * size, transcendentals=0
        ),
    )(core.reshape(1), first, second, square)


def logits_kernel(target_ref, answers_ref, table_ref, shares_ref, stats_ref, logits):
    rows, width = logits.shape
    piece = 256
    target = target_ref[...]
    top = jnp.full((8, width), -jnp.inf, jnp.float32)
    total = jnp.zeros((8, width), jnp.float32)
    picked = jnp.zeros((8, width), jnp.float32)
    for first in range(0, rows, piece):
        scores = lax.dot_general(
            table_ref[first : first + piece, :],
            answers_ref[...],
            (((1,), (1,)), ((), ())),
            preferred_element_type=jnp.float32,
        )
        logits[first : first + piece, :] = scores
        top = jnp.maximum(top, jnp.max(scores.reshape(-1, 8, width), axis=0))
    top = jnp.max(top, axis=0, keepdims=True)
    for first in range(0, rows, piece):
        scores = logits[first : first + piece, :]
        share = jnp.exp(scores - top)
        shares_ref[first : first + piece, :] = share.astype(jnp.bfloat16)
        total = total + jnp.sum(share.reshape(-1, 8, width), axis=0)
        place = lax.broadcasted_iota(jnp.int32, (piece, width), 0)
        hit = jnp.where(place == target - first, scores, 0.0)
        picked = picked + jnp.sum(hit.reshape(-1, 8, width), axis=0)
    stats_ref[0:1, :] = top
    stats_ref[1:2, :] = jnp.sum(total, axis=0, keepdims=True)
    stats_ref[2:3, :] = jnp.sum(picked, axis=0, keepdims=True)
    stats_ref[3:8, :] = jnp.zeros((5, width), jnp.float32)


def answer_shares(target, answers, table):
    count, rows = answers.shape[0], table.shape[0]
    tile = 256
    return pl.pallas_call(
        logits_kernel,
        grid=(count // tile,),
        in_specs=[
            pl.BlockSpec((1, tile), lambda i: (0, i)),
            pl.BlockSpec((tile, D), lambda i: (i, 0)),
            pl.BlockSpec((rows, D), lambda i: (0, 0)),
        ],
        out_specs=[
            pl.BlockSpec((rows, tile), lambda i: (0, i)),
            pl.BlockSpec((8, tile), lambda i: (0, i)),
        ],
        out_shape=[
            jax.ShapeDtypeStruct((rows, count), jnp.bfloat16),
            jax.ShapeDtypeStruct((8, count), jnp.float32),
        ],
        scratch_shapes=[pltpu.VMEM((rows, tile), jnp.float32)],
        compiler_params=pltpu.CompilerParams(vmem_limit_bytes=40 * 1024 * 1024),
        cost_estimate=pl.CostEstimate(
            flops=2 * count * rows * D,
            bytes_accessed=2 * count * (rows + D),
            transcendentals=count * rows,
        ),
    )(target, answers, table)


def logit_grads(place, target, scale, value, shares):
    return jnp.where(place == target, value, shares.astype(jnp.float32) * scale).astype(jnp.bfloat16)


def grads_kernel(target_ref, scale_ref, value_ref, shares_ref, table_ref, grads_ref):
    place = lax.broadcasted_iota(jnp.int32, shares_ref.shape, 0)
    grads = logit_grads(place, target_ref[...], scale_ref[...], value_ref[...], shares_ref[...])
    grads_ref[...] = lax.dot_general(
        grads, table_ref[...], (((0,), (0,)), ((), ())), preferred_element_type=jnp.float32
    ).astype(jnp.bfloat16)


def answer_grads(half, target, scale, value, shares, table, width):
    rows, count = shares.shape
    steps = count // (2 * width)
    first = half * steps
    row = pl.BlockSpec((1, width), lambda i: (0, first + i))
    return pl.pallas_call(
        grads_kernel,
        grid=(steps,),
        in_specs=[
            row,
            row,
            row,
            pl.BlockSpec((rows, width), lambda i: (0, first + i)),
            pl.BlockSpec((rows, D), lambda i: (0, 0)),
        ],
        out_specs=pl.BlockSpec((width, D), lambda i: (i, 0)),
        out_shape=jax.ShapeDtypeStruct((steps * width, D), jnp.bfloat16),
        compiler_params=pltpu.CompilerParams(vmem_limit_bytes=40 * 1024 * 1024),
        cost_estimate=pl.CostEstimate(
            flops=2 * steps * width * rows * D,
            bytes_accessed=2 * steps * width * (rows + D),
            transcendentals=0,
        ),
    )(target, scale, value, shares, table)


def body(
    token_ids,
    seq_lengths,
    pair_order,
    table_master,
    table_first,
    table_second,
    square_master,
    square_moment,
    wide_master,
    wide_moment,
    vector_master,
    vector_first,
    vector_second,
    norm_gains,
    norm_first,
    norm_second,
    adam_count,
):
    members = lax.axis_size("vocab")
    member = lax.axis_index("vocab")
    block_rows = table_master.shape[0]
    lengths = seq_lengths[0]
    order = pair_order[0]
    groups_per = HEADS // KV
    scale = HD ** (-0.5)

    core = lax.axis_index("core")
    devices = lax.axis_size(ALL)
    device = lax.axis_index(ALL)
    groups = devices // members

    own_ids = lax.dynamic_index_in_dim(token_ids, member, 0, keepdims=False)
    own_length = lengths[member]
    start = own_length - 1 - RESP
    owner, first_seen, slot = token_slots(own_ids, block_rows)
    local_ids = own_ids % block_rows
    keys = round_keys(owner, slot, 0, SLOTS)
    asks = round_asks(keys, first_seen, local_ids, devices * SLOTS)
    own_targets = lax.dynamic_slice_in_dim(own_ids, start + 1, RESP, 0)
    vector_low = vector_master.astype(jnp.bfloat16).astype(jnp.float32)
    shared_notes = jnp.concatenate(
        [
            vector_low.reshape(-1),
            jnp.concatenate([own_targets, order, jnp.max(slot)[None] + 1]).astype(jnp.float32),
        ]
    )
    notes = jnp.concatenate(
        [
            asks.reshape(devices, SLOTS).astype(jnp.float32),
            jnp.broadcast_to(shared_notes[None, :], (devices, shared_notes.size)),
        ],
        axis=1,
    )
    notes = exchanged(notes)
    square_b = lax.all_gather(square_master.astype(jnp.bfloat16), ALL, axis=1, tiled=True)
    wide_b = lax.all_gather(wide_master.astype(jnp.bfloat16), DP, axis=1, tiled=True)
    hidden_units = wide_b.shape[1]
    asked = notes[:, :SLOTS].astype(jnp.int32).reshape(-1)
    gains = (
        notes[:, SLOTS : SLOTS + vector_low.size]
        .reshape(devices, vector_low.shape[0], vector_low.shape[1])
        .transpose(1, 0, 2)
        .reshape(vector_low.shape[0], D)
    )
    numbers = notes[:, SLOTS + vector_low.size :].astype(jnp.int32)
    targets = numbers[:, :RESP].reshape(-1)
    orders = numbers[:, RESP : RESP + members].reshape(groups, members, members)[:, 0]
    later = jnp.maximum(jnp.max(numbers[:, RESP + members]) - SLOTS, 0)
    later_turns = (later + LATER_SLOTS - 1) // LATER_SLOTS
    slots = jnp.arange(members)
    chosen_mask = (orders[:, 0::2, None] == slots[None, None, :]).astype(jnp.float32)
    rejected_mask = (orders[:, 1::2, None] == slots[None, None, :]).astype(jnp.float32)
    pair_rows = jnp.sum(
        (chosen_mask + rejected_mask)[:, :, :, None] * (chosen_mask - rejected_mask)[:, :, None, :],
        axis=1,
    )
    same_group = jnp.arange(groups)[:, None] == jnp.arange(groups)[None, :]
    pair_rows = jnp.where(same_group[:, None, :, None], pair_rows[:, :, None, :], 0.0)
    pair_rows = pair_rows.reshape(devices, devices) * (pref_beta / RESP)
    chosen_sign = jnp.sum(chosen_mask - rejected_mask, axis=1).reshape(devices, 1)
    table_b = table_master.astype(jnp.bfloat16)
    head_gains = low_copy(norm_gains)
    cosine, sine = rope_tables(SEQ, HD // 2)

    def fetched(wanted, row_keys):
        rows = jnp.dot(
            onehot_rows(wanted, block_rows), table_b, preferred_element_type=jnp.float32
        ).astype(jnp.bfloat16)
        return jnp.dot(
            onehot_rows(row_keys, wanted.shape[0]),
            exchanged(rows),
            preferred_element_type=jnp.float32,
        )

    def later_round(turn):
        count = devices * LATER_SLOTS
        later_keys = round_keys(owner, slot, SLOTS + turn * LATER_SLOTS, LATER_SLOTS)
        return later_keys, exchanged(round_asks(later_keys, first_seen, local_ids, count))

    def fetch_more(turn, rows):
        later_keys, later_asked = later_round(turn)
        return rows + fetched(later_asked, later_keys)

    hidden0 = lax.fori_loop(0, later_turns, fetch_more, fetched(asked, keys))
    act1 = rms_scale(hidden0, gains[0]).astype(jnp.bfloat16)
    entry, leave, conv_in = (dense(act1, square_b[place]) for place in range(3))
    product = entry * conv_in
    convolved = gains[4] * product + gains[5] * delayed(product, 1) + gains[6] * delayed(product, 2)
    mixer = (leave * convolved).astype(jnp.bfloat16)
    hidden1 = hidden0 + dense(mixer, square_b[3])
    act2 = rms_scale(hidden1, gains[1]).astype(jnp.bfloat16)

    def answers(values):
        return lax.dynamic_slice_in_dim(values, start, RESP, 0)

    def placed(values):
        return lax.dynamic_update_slice_in_dim(
            jnp.zeros((SEQ, values.shape[1]), values.dtype), values, start, 0
        )

    answer_act2 = answers(act2)
    query_raw = dense(answer_act2, square_b[4]).reshape(RESP, HEADS, HD)
    pair_raw = dense(act2, square_b[5])
    key_raw = pair_raw[:, : KV * HD].reshape(SEQ, KV, HD)
    value_b = pair_raw[:, KV * HD :].astype(jnp.bfloat16).reshape(SEQ, KV, HD)

    answer_cosine, answer_sine = answers(cosine), answers(sine)

    def query_prep(raw, gain):
        return rotate(rms_scale(raw, gain), answer_cosine, answer_sine)

    def key_prep(raw, gain):
        return rotate(rms_scale(raw, gain), cosine, sine)

    query_b = (
        query_prep(query_raw, head_gains[0]).astype(jnp.bfloat16).reshape(RESP, KV, groups_per, HD)
    )
    key_b = key_prep(key_raw, head_gains[1]).astype(jnp.bfloat16)
    causal = start + jnp.arange(RESP)[:, None] >= jnp.arange(SEQ)[None, :]
    scores = (
        jnp.einsum("sgrd,tgd->grst", query_b, key_b, preferred_element_type=jnp.float32) * scale
    )
    scores = jnp.where(causal, scores, masked_score)
    peak = jnp.max(scores, axis=-1, keepdims=True)
    expo = jnp.exp(scores - peak)
    total = jnp.sum(expo, axis=-1, keepdims=True)
    log_norm = peak + jnp.log(total)
    probs_b = (expo / total).astype(jnp.bfloat16)
    attended = jnp.einsum(
        "grst,tgd->sgrd", probs_b, value_b, preferred_element_type=jnp.float32
    ).reshape(RESP, D)
    attended_b = attended.astype(jnp.bfloat16)
    hidden2 = answers(hidden1) + dense(attended_b, square_b[6])
    act3 = member_gather(rms_scale(hidden2, gains[2]).astype(jnp.bfloat16))
    gate_part, up_part = dense(act3, wide_b[0]), dense(act3, wide_b[1])
    inner_b = (jax.nn.silu(gate_part) * up_part).astype(jnp.bfloat16)
    ffn_part = jnp.dot(inner_b, wide_b[2], preferred_element_type=jnp.float32)
    hidden3 = hidden2 + member_return(ffn_part.astype(jnp.bfloat16).reshape(members, RESP, D))
    final_b = rms_scale(hidden3, gains[3]).astype(jnp.bfloat16)
    squares, square_rows = square_master.shape[0], square_master.shape[1]
    wides, wide_rows = wide_master.shape[0], wide_master.shape[1]
    per_member = -(-squares // members)
    group_rows = members * square_rows

    def by_member(values):
        values = jnp.pad(values, ((0, per_member * members - squares), (0, 0), (0, 0)))
        return values.reshape(per_member, members, -1, D).transpose(1, 0, 2, 3)

    def wide_by_member(values):
        return jnp.pad(values, ((0, members - wides), (0, 0), (0, 0)))

    half_tokens = [
        jnp.concatenate(gathered(piece, "chip"), axis=0) for piece in gathered(final_b, "vocab")
    ]
    response_tokens = jnp.concatenate(
        half_tokens + [other_core(piece) for piece in half_tokens], axis=0
    )
    chips = groups // 2
    chip = lax.axis_index("chip")
    block_core = jnp.stack([core, 1 - core])[:, None, None]
    block_member = ((member - jnp.arange(members)) % members)[None, :, None]
    block_chip = ((chip - jnp.arange(chips)) % chips)[None, None, :]
    block_device = ((block_chip * 2 + block_core) * members + block_member).reshape(-1)
    device_block = jnp.sum(
        jnp.where(
            block_device[None, :] == jnp.arange(devices)[:, None], jnp.arange(devices)[None, :], 0
        ),
        axis=1,
    )
    wide_moment_blocks, response_tokens = lax.optimization_barrier(
        (wide_by_member(wide_moment.astype(jnp.bfloat16)), response_tokens)
    )
    wide_moment_job = handed_out(wide_moment_blocks, "vocab")
    local_target = jnp.where(targets // block_rows == device, targets % block_rows, -1)
    local_target = local_target.reshape(devices, RESP)[block_device].reshape(1, -1)
    shares, own_stats = answer_shares(local_target, response_tokens, table_b)
    own_stats, wide_moment_job = lax.optimization_barrier((own_stats, wide_moment_job))
    wide_moment_job = jnp.stack(wide_moment_job)
    stats = own_stats[:3].reshape(3, devices, RESP).transpose(1, 0, 2)[device_block]
    stats = exchanged(stats)
    top = jnp.max(stats[:, 0], axis=0)
    exp_total = jnp.sum(stats[:, 1] * jnp.exp(stats[:, 0] - top[None, :]), axis=0)
    own_log_total = top + jnp.log(exp_total)
    own_logp = jnp.sum(jnp.sum(stats[:, 2], axis=0) - own_log_total)
    joined = spread(jnp.concatenate([own_log_total, own_logp[None]]))
    log_total = joined[:, :RESP][block_device].reshape(1, -1)
    margin = jnp.sum(pair_rows * joined[:, RESP][None, :], axis=1, keepdims=True)
    pair_loss = 0.5 * jnp.sum(jax.nn.softplus(-margin))
    grad_logp = chosen_sign * jax.nn.sigmoid(-margin) * (-pref_beta / RESP)
    row_weight = jnp.broadcast_to(grad_logp[block_device], (devices, RESP)).reshape(1, -1)
    share_scale = -row_weight * jnp.exp(own_stats[0:1] - log_total)
    target_value = row_weight * (1.0 - jnp.exp(own_stats[2:3] - log_total))
    given, kept = (
        answer_grads(
            half, local_target, share_scale, target_value, shares, table_b, members * RESP
        )
        for half in (1, 0)
    )
    grad_answer_pair = (kept.astype(jnp.float32) + other_core(given).astype(jnp.float32)).astype(
        jnp.bfloat16
    )
    grad_answer_pair, square_moment_blocks = lax.optimization_barrier(
        (grad_answer_pair, by_member(square_moment.astype(jnp.bfloat16)))
    )
    square_moment_job = handed_out(square_moment_blocks, "vocab")
    grad_answer_pair = grad_answer_pair.reshape(members, chips, RESP, D)
    grad_answer_group = added(
        handed_back([grad_answer_pair[:, place] for place in range(chips)], "chip")
    )
    grad_table = jnp.dot(
        logit_grads(
            jnp.arange(block_rows)[:, None], local_target, share_scale, target_value, shares
        ),
        response_tokens,
        preferred_element_type=jnp.float32,
    )
    grad_answer_group, grad_table, square_moment_job = lax.optimization_barrier(
        (grad_answer_group.astype(jnp.bfloat16), grad_table, square_moment_job)
    )
    square_moment_job = placed_before(square_moment_job, "vocab")
    square_moment_job = square_moment_job.transpose(1, 0, 2, 3).reshape(per_member, group_rows, D)
    grad_final = member_return(list(grad_answer_group))
    grad_hidden3, grad_gain3 = norm_back(hidden3, gains[3], grad_final)
    grad_ffn_out = member_gather(grad_hidden3.astype(jnp.bfloat16))
    grad_inner = dense(grad_ffn_out, wide_b[2])
    grad_down_w = outer(inner_b, grad_ffn_out)
    _, silu_pull = jax.vjp(lambda gate_in, up_in: jax.nn.silu(gate_in) * up_in, gate_part, up_part)
    grad_gate, grad_up = silu_pull(grad_inner)
    grad_gate_b, grad_up_b = grad_gate.astype(jnp.bfloat16), grad_up.astype(jnp.bfloat16)
    grad_act3_part = back_dense(grad_gate_b, wide_b[0]) + back_dense(grad_up_b, wide_b[1])
    grad_act3 = member_return(grad_act3_part.astype(jnp.bfloat16).reshape(members, RESP, D))
    grad_gate_w, grad_up_w = outer(grad_gate_b, act3), outer(grad_up_b, act3)
    grad_norm2, grad_gain2 = norm_back(hidden2, gains[2], grad_act3)
    grad_hidden2 = grad_hidden3 + grad_norm2
    grad_attn_out = grad_hidden2.astype(jnp.bfloat16)
    grad_attended = (
        back_dense(grad_attn_out, square_b[6])
        .astype(jnp.bfloat16)
        .reshape(RESP, KV, groups_per, HD)
    )
    grad_out_w = outer(grad_attn_out, attended_b)
    scores = (
        jnp.einsum("sgrd,tgd->grst", query_b, key_b, preferred_element_type=jnp.float32) * scale
    )
    probs = jnp.exp(jnp.where(causal, scores, masked_score) - log_norm)
    grad_probs = jnp.einsum(
        "sgrd,tgd->grst", grad_attended, value_b, preferred_element_type=jnp.float32
    )
    grad_values = jnp.einsum(
        "grst,sgrd->tgd", probs_b, grad_attended, preferred_element_type=jnp.float32
    )
    delta = jnp.sum(probs * grad_probs, axis=-1, keepdims=True)
    grad_scores = (probs * (grad_probs - delta)).astype(jnp.bfloat16)
    grad_query = (
        jnp.einsum("grst,tgd->sgrd", grad_scores, key_b, preferred_element_type=jnp.float32) * scale
    ).reshape(RESP, HEADS, HD)
    grad_keys = (
        jnp.einsum("grst,sgrd->tgd", grad_scores, query_b, preferred_element_type=jnp.float32)
        * scale
    )
    _, query_pull = jax.vjp(query_prep, query_raw, head_gains[0])
    grad_query_raw, grad_query_gain = query_pull(grad_query)
    _, key_pull = jax.vjp(key_prep, key_raw, head_gains[1])
    grad_key_raw, grad_key_gain = key_pull(grad_keys)
    grad_query_b = grad_query_raw.reshape(RESP, D).astype(jnp.bfloat16)
    grad_pair_b = jnp.concatenate(
        [grad_key_raw.reshape(SEQ, KV * HD), grad_values.reshape(SEQ, KV * HD)], axis=1
    ).astype(jnp.bfloat16)
    grad_act2 = back_dense(grad_pair_b, square_b[5]) + placed(back_dense(grad_query_b, square_b[4]))
    grad_query_w = outer(grad_query_b, answer_act2)
    grad_pair_w = outer(grad_pair_b, act2)
    grad_norm1, grad_gain1 = norm_back(hidden1, gains[1], grad_act2)
    grad_hidden1 = placed(grad_hidden2) + grad_norm1
    grad_mix_out = grad_hidden1.astype(jnp.bfloat16)
    grad_mixer = back_dense(grad_mix_out, square_b[3])
    grad_mixer_w = outer(grad_mix_out, mixer)
    grad_leave = grad_mixer * convolved
    grad_conv = grad_mixer * leave
    grad_tap0 = jnp.sum(grad_conv * product, axis=0)
    grad_tap1 = jnp.sum(grad_conv * delayed(product, 1), axis=0)
    grad_tap2 = jnp.sum(grad_conv * delayed(product, 2), axis=0)
    grad_product = (
        gains[4] * grad_conv + gains[5] * advanced(grad_conv, 1) + gains[6] * advanced(grad_conv, 2)
    )
    grad_inner = [
        part.astype(jnp.bfloat16)
        for part in (grad_product * conv_in, grad_leave, grad_product * entry)
    ]
    grad_act1 = sum(back_dense(grad_inner[place], square_b[place]) for place in range(3))
    grad_inner_w = [outer(part, act1) for part in grad_inner]
    grad_norm0, grad_gain0 = norm_back(hidden0, gains[0], grad_act1)
    grad_embed_b = (grad_hidden1 + grad_norm0).astype(jnp.bfloat16)

    grad_square = jnp.stack(
        [
            part.astype(jnp.bfloat16)
            for part in (*grad_inner_w, grad_mixer_w, grad_query_w, grad_pair_w, grad_out_w)
        ]
    )
    grad_vector = jnp.stack(
        [grad_gain0, grad_gain1, grad_gain2, grad_gain3, grad_tap0, grad_tap1, grad_tap2]
    )
    grad_head_gains = jnp.stack([grad_query_gain, grad_key_gain])
    grad_wide = jnp.stack(
        [part.astype(jnp.bfloat16) for part in (grad_gate_w, grad_up_w, grad_down_w)]
    )
    share_wide_b = lax.psum_scatter(grad_wide, DP, scatter_dimension=1, tiled=True)
    grad_square, share_wide_b = lax.optimization_barrier((grad_square, share_wide_b))
    share_wide_b, grad_embed_b = lax.optimization_barrier((share_wide_b, grad_embed_b))
    share_wide = share_wide_b.astype(jnp.float32)
    wide_grad_job = jnp.stack(handed_out(wide_by_member(share_wide_b), "vocab"))
    group_square = lax.psum_scatter(grad_square, DP, scatter_dimension=1, tiled=True)
    square_grad_job = member_scatter(by_member(group_square))

    def from_members(values):
        values = values.reshape(per_member, members, square_rows, D).transpose(1, 0, 2, 3)
        values = placed_before(handed_out(values.astype(jnp.bfloat16), "vocab"), "vocab")
        values = values.transpose(1, 0, 2, 3).reshape(per_member * members, square_rows, D)
        return values[:squares].astype(jnp.float32)

    share_square = from_members(square_grad_job)

    def returned(row_keys, count):
        rows = outer(onehot_rows(row_keys, count), grad_embed_b)
        return exchanged(rows.astype(jnp.bfloat16))

    def put(wanted, rows):
        return outer(onehot_rows(wanted, block_rows), rows)

    def return_more(turn, total):
        later_keys, later_asked = later_round(turn)
        return total + put(later_asked, returned(later_keys, later_asked.shape[0]))

    returned_rows, wide_grad_job = lax.optimization_barrier(
        (returned(keys, devices * SLOTS), wide_grad_job)
    )
    share_table = lax.fori_loop(
        0, later_turns, return_more, grad_table + put(asked, returned_rows))
    width = vector_master.shape[1]
    vector_notes = grad_vector.reshape(-1, devices, width).transpose(1, 0, 2).reshape(devices, -1)
    vector_notes = jnp.concatenate(
        [
            vector_notes,
            jnp.broadcast_to(grad_head_gains.reshape(1, -1), (devices, grad_head_gains.size)),
        ],
        axis=1,
    )
    vector_notes = jnp.sum(exchanged(vector_notes), axis=0)
    share_vector = vector_notes[: vector_master.size].reshape(vector_master.shape)
    gains_total = vector_notes[vector_master.size :].reshape(grad_head_gains.shape)

    def job_sums(values):
        sums = jnp.sum(values, axis=(1, 2))[:, None]
        sums = jnp.where(jnp.arange(members)[None, :] == member, sums, 0.0)
        return sums.reshape(-1)[:squares]

    moment_squares = jnp.concatenate(
        [
            jnp.sum(square_moment * square_moment, axis=(1, 2)),
            jnp.sum(wide_moment * wide_moment, axis=(1, 2)),
        ]
    )
    moment_cross = jnp.concatenate(
        [
            job_sums(square_moment_job.astype(jnp.float32) * square_grad_job),
            jnp.sum(wide_moment * share_wide, axis=(1, 2)),
        ]
    )
    grad_squares = jnp.concatenate(
        [
            job_sums(square_grad_job * square_grad_job),
            jnp.sum(share_wide * share_wide, axis=(1, 2)),
        ]
    )
    moment_stats = jnp.stack([moment_squares, moment_cross, grad_squares])
    own_squares = (
        jnp.sum(grad_squares)
        + jnp.sum(share_vector * share_vector)
        + jnp.sum(share_table * share_table)
    )
    sums = jnp.concatenate([moment_stats.reshape(-1), own_squares[None]])
    sums = jnp.sum(spread(sums), axis=0)
    stats_total = sums[:-1].reshape(moment_stats.shape)
    grad_norm = jnp.sqrt(sums[-1] + jnp.sum(gains_total * gains_total))
    factor = jnp.minimum(1.0, clip_limit / grad_norm)
    square_moment_new = muon_decay * square_moment + (1.0 - muon_decay) * (factor * share_square)
    wide_moment_new = muon_decay * wide_moment + (1.0 - muon_decay) * (factor * share_wide)
    moment_norm = jnp.sqrt(
        muon_decay * muon_decay * stats_total[0]
        + 2.0 * muon_decay * (1.0 - muon_decay) * factor * stats_total[1]
        + (1.0 - muon_decay) * (1.0 - muon_decay) * factor * factor * stats_total[2]
    )
    ortho_square = square_moment_new / (moment_norm[:7][:, None, None] + ortho_epsilon)
    ortho_wide = wide_moment_new / (moment_norm[7:][:, None, None] + ortho_epsilon)
    wide_inverse = 1.0 / (moment_norm[squares:] + ortho_epsilon)
    wide_inverse = jnp.pad(wide_inverse, (0, members - wides))[member]
    square_inverse = 1.0 / (moment_norm[:squares] + ortho_epsilon)
    square_inverse = jnp.pad(square_inverse, (0, per_member * members - squares))
    square_inverse = square_inverse.reshape(per_member, members)[:, member][:, None, None]
    square_part = (muon_decay * square_inverse) * square_moment_job.astype(jnp.float32) + (
        (1.0 - muon_decay) * factor * square_inverse
    ) * square_grad_job
    square_part, wide_grad_job = lax.optimization_barrier(
        (square_part.astype(jnp.bfloat16), wide_grad_job)
    )
    square_part = jnp.pad(square_part, ((0, groups // 2 - per_member), (0, 0), (0, 0)))
    square_half = jnp.concatenate(handed_out(square_part, "chip"), axis=0)
    square_job = jnp.concatenate([square_half, other_core(square_half)], axis=0)
    wide_job = (
        (muon_decay * wide_inverse) * wide_moment_job.astype(jnp.float32)
        + ((1.0 - muon_decay) * factor * wide_inverse) * wide_grad_job.astype(jnp.float32)
    )
    wide_job = wide_job.reshape(members * wide_rows, D).astype(jnp.bfloat16)
    wide_first, wide_second = group_sum(outer(wide_job, wide_job).astype(jnp.bfloat16), core)
    square_gram = outer(square_job, square_job)
    rest_b = ortho_rest(core, wide_first, wide_second, square_gram)
    power = leading_coefficient**NS_ITERS
    wide_rest = jnp.where(core == 0, rest_b, other_core(rest_b))
    back_square = square_product(square_job, rest_b).astype(jnp.bfloat16)
    half_rows = square_half.shape[0]
    back_square = jnp.where(
        core == 0, other_core(back_square[half_rows:]), back_square[:half_rows]
    )
    back_wide = square_product(wide_job, wide_rest).astype(jnp.bfloat16)
    share_table, back_square, back_wide = lax.optimization_barrier(
        (share_table, back_square, back_wide)
    )
    table_step, table_first_new, table_second_new = adam_step(
        table_master, table_first, table_second, share_table, factor, adam_count
    )
    back_square = handed_back(list(back_square.reshape(-1, group_rows, D)), "chip")
    back_square = placed_after(back_square, "chip")[:per_member]
    back_wide = handed_back(list(back_wide.reshape(members, wide_rows, D)), "vocab")
    back_wide = placed_after(back_wide, "vocab")[:wides]
    back_square = from_members(back_square)
    ortho_wide = power * ortho_wide + back_wide.astype(jnp.float32)
    ortho_square = power * ortho_square + back_square
    wide_scale = jnp.array([math.sqrt(FF / D), math.sqrt(FF / D), 1.0], jnp.float32)
    square_new = square_master - muon_rate * ortho_square
    wide_new = wide_master - muon_rate * wide_scale[:, None, None] * ortho_wide
    vector_step, vector_first_new, vector_second_new = adam_step(
        vector_master, vector_first, vector_second, share_vector, factor, adam_count
    )
    norm_step, norm_first_new, norm_second_new = adam_step(
        norm_gains, norm_first, norm_second, gains_total, factor, adam_count
    )
    return (
        pair_loss,
        grad_norm,
        square_new,
        square_moment_new,
        square_new.astype(jnp.bfloat16),
        wide_new,
        wide_moment_new,
        wide_new.astype(jnp.bfloat16),
        table_step,
        table_first_new,
        table_second_new,
        vector_step,
        vector_first_new,
        vector_second_new,
        norm_step,
        norm_first_new,
        norm_second_new,
        share_vector[3],
    )


def solution(mesh):
    groups, members = mesh.shape["dp"], mesh.shape["vocab"]
    cores = 2
    split_mesh = Mesh(mesh.devices.reshape(groups // cores, cores, members), ALL)
    return jax.shard_map(
        body,
        mesh=split_mesh,
        in_specs=(
            P(DP, None),
            P(DP, None),
            P(DP, None),
            P(ALL, None),
            P(ALL, None),
            P(ALL, None),
            P(None, ALL, None),
            P(None, ALL, None),
            P(None, ALL, None),
            P(None, ALL, None),
            P(None, ALL),
            P(None, ALL),
            P(None, ALL),
            P(),
            P(),
            P(),
            P(),
        ),
        out_specs=(
            P(),
            P(),
            P(None, ALL, None),
            P(None, ALL, None),
            P(None, ALL, None),
            P(None, ALL, None),
            P(None, ALL, None),
            P(None, ALL, None),
            P(ALL, None),
            P(ALL, None),
            P(ALL, None),
            P(None, ALL),
            P(None, ALL),
            P(None, ALL),
            P(),
            P(),
            P(),
            P(ALL),
        ),
        check_vma=False,
    )
```

```python
import math

import jax
import jax.numpy as jnp
from jax import lax
from jax.experimental import pallas as pl
from jax.experimental.pallas import tpu as pltpu
from jax.sharding import Mesh
from jax.sharding import PartitionSpec as P

D = 1024
HEADS = 16
KV = 8
HD = 64
FF = 4608
SEQ = 512
RESP = 96
NS_ITERS = 3


norm_epsilon = 1e-05
rope_base = 1000000.0
pref_beta = 2.0
clip_limit = 0.05
muon_decay = 0.95
muon_rate = 0.5
first_decay = 0.9
second_decay = 0.95
adam_rate = 0.02
adam_epsilon = 1e-08
weight_decay = 0.1
leading_coefficient = 3.4445
coef_second = -4.775
coef_third = 2.0315
ortho_epsilon = 1e-07
masked_score = -1e30


def rms_scale(inputs, gain):
    mean_square = jnp.mean(inputs * inputs, axis=-1, keepdims=True)
    return inputs * lax.rsqrt(mean_square + norm_epsilon) * gain


def rope_tables(length, half):
    position = jnp.arange(length, dtype=jnp.float32)
    inverse = rope_base ** (-jnp.arange(half, dtype=jnp.float32) / half)
    angle = position[:, None] * inverse[None, :]
    return (jnp.cos(angle)[:, None, :], jnp.sin(angle)[:, None, :])


def rotate(inputs, cosine, sine):
    half = inputs.shape[-1] // 2
    first = inputs[..., :half]
    second = inputs[..., half:]
    return jnp.concatenate(
        [first * cosine - second * sine, second * cosine + first * sine], axis=-1
    )


def dense(inputs, weight):
    return lax.dot_general(
        inputs, weight, (((1,), (1,)), ((), ())), preferred_element_type=jnp.float32
    )


def outer(grads, inputs):
    return lax.dot_general(
        grads, inputs, (((0,), (0,)), ((), ())), preferred_element_type=jnp.float32
    )


def back_dense(grads, weight):
    return jnp.dot(grads, weight, preferred_element_type=jnp.float32)


def delayed(values, offset):
    return jnp.pad(values, ((offset, 0), (0, 0)))[: values.shape[0]]


def advanced(values, offset):
    return jnp.pad(values, ((0, offset), (0, 0)))[offset:]


def norm_back(inputs, gain, grad_out):
    _, pullback = jax.vjp(rms_scale, inputs, gain)
    return pullback(grad_out)


def low_copy(values):
    return lax.optimization_barrier(values.astype(jnp.bfloat16)).astype(jnp.float32)


def adam_step(master, first, second, grad, factor, count):
    scaled = factor * grad
    first_new = first_decay * first + (1.0 - first_decay) * scaled
    second_new = second_decay * second + (1.0 - second_decay) * scaled * scaled
    steps = count.astype(jnp.float32)
    first_hat = first_new / (1.0 - first_decay**steps)
    second_hat = second_new / (1.0 - second_decay**steps)
    change = -adam_rate * (
        first_hat / (jnp.sqrt(second_hat) + adam_epsilon) + weight_decay * master
    )
    return (change, first_new, second_new)

DP = ("chip", "core")
ALL = ("chip", "core", "vocab")
SLOTS = 24
LATER_SLOTS = 8


def exchanged(rows):
    return lax.all_to_all(rows, ALL, 0, 0, tiled=True)


def spread(values):
    count = lax.axis_size(ALL)
    return lax.all_to_all(jnp.broadcast_to(values[None], (count,) + values.shape), ALL, 0, 0)


def turned(values, axis, step):
    count = lax.axis_size(axis)
    return lax.ppermute(values, axis, [(i, (i + step) % count) for i in range(count)])


def block_at(blocks, index):
    return lax.dynamic_index_in_dim(blocks, index % blocks.shape[0], 0, keepdims=False)


def handed_out(blocks, axis):
    place, count = lax.axis_index(axis), lax.axis_size(axis)
    return [block_at(blocks, place)] + [
        turned(block_at(blocks, place + step), axis, step) for step in range(1, count)
    ]


def handed_back(pieces, axis):
    return [pieces[0]] + [turned(pieces[step], axis, -step) for step in range(1, len(pieces))]


def gathered(values, axis):
    return [values] + [turned(values, axis, step) for step in range(1, lax.axis_size(axis))]


def placed_before(pieces, axis):
    pieces, place = jnp.stack(pieces), lax.axis_index(axis)
    return jnp.stack([block_at(pieces, place - j) for j in range(pieces.shape[0])])


def placed_after(pieces, axis):
    pieces, place = jnp.stack(pieces), lax.axis_index(axis)
    return jnp.stack([block_at(pieces, j - place) for j in range(pieces.shape[0])])


def added(pieces):
    total = pieces[0].astype(jnp.float32)
    for piece in pieces[1:]:
        total = total + piece.astype(jnp.float32)
    return total


def other_core(values):
    return lax.ppermute(values, "core", [(0, 1), (1, 0)])


def pair_sum(halves, core):
    given = lax.dynamic_index_in_dim(halves, 1 - core, 0, keepdims=False)
    kept = lax.dynamic_index_in_dim(halves, core, 0, keepdims=False)
    total = kept.astype(jnp.float32) + other_core(given).astype(jnp.float32)
    return total.astype(jnp.bfloat16)


def chip_sum(blocks):
    return added(handed_out(blocks, "chip"))


def group_sum(values, core):
    rows = values.shape[0] // 2
    chips = lax.axis_size("chip")
    half = pair_sum(values.reshape(2, rows, -1), core).reshape(chips, rows // chips, -1)
    part = chip_sum(half).astype(jnp.bfloat16)
    half = placed_before(gathered(part, "chip"), "chip").reshape(rows, -1)
    return half, other_core(half)


def member_gather(values):
    return jnp.concatenate(gathered(values, "vocab"), axis=0)


def member_return(pieces):
    return added(handed_back(pieces, "vocab"))


def member_scatter(blocks):
    return added(handed_out(blocks, "vocab"))


def onehot_rows(index, count):
    return (index[:, None] == jnp.arange(count)[None, :]).astype(jnp.bfloat16)


def token_slots(ids, block_rows):
    owner = ids // block_rows
    place = jnp.arange(ids.shape[0])
    earlier = place[:, None] > place[None, :]
    equal = ids[:, None] == ids[None, :]
    first = jnp.logical_not(jnp.any(equal & earlier, axis=1))
    ahead = (owner[:, None] == owner[None, :]) & earlier & first[None, :]
    rank = jnp.sum(ahead.astype(jnp.int32), axis=1)
    slot = jnp.sum(jnp.where(equal & first[None, :], rank[None, :], 0), axis=1)
    return owner, first, slot


def round_keys(owner, slot, first, count):
    within = slot - first
    return jnp.where((within >= 0) & (within < count), owner * count + within, -1)


def round_asks(keys, first_seen, local, count):
    hits = (keys[None, :] == jnp.arange(count)[:, None]) & first_seen[None, :]
    return jnp.sum(jnp.where(hits, local[None, :] + 1, 0), axis=1) - 1


def square_product(left, right):
    return jnp.dot(
        left.astype(jnp.bfloat16), right.astype(jnp.bfloat16), preferred_element_type=jnp.float32
    )


def rest_kernel(
    core_ref,
    first_ref,
    second_ref,
    square_ref,
    rest_ref,
    gram_scratch,
    change_scratch,
    rest_scratch,
    grams,
    change_b,
    rest_b,
):
    lead = leading_coefficient
    size = square_ref.shape[0]
    half = size // 2
    tile = 256

    def dot(left, right):
        return jnp.dot(left, right, preferred_element_type=jnp.float32)

    on_wide = core_ref[0] == 0
    for part, wide_ref in enumerate((first_ref, second_ref)):

        @pl.loop(0, half // tile)
        def _(step):
            rows = pl.ds(pl.multiple_of(step * tile, tile), tile)
            place = pl.ds(pl.multiple_of(part * half + step * tile, tile), tile)
            gram = jnp.where(on_wide, wide_ref[rows, :].astype(jnp.float32), square_ref[place, :])
            gram_scratch[place, :] = gram
            grams[0, place, :] = gram.astype(jnp.bfloat16)

    power = 1.0
    for turn in range(NS_ITERS):
        now, later = turn % 2, (turn + 1) % 2

        @pl.loop(0, size // tile)
        def _(step):
            rows = pl.ds(pl.multiple_of(step * tile, tile), tile)
            change = coef_second * gram_scratch[rows, :] + coef_third * dot(
                grams[now, rows, :], grams[now]
            )
            change_scratch[rows, :] = change
            change_b[rows, :] = change.astype(jnp.bfloat16)

        @pl.loop(0, size // tile)
        def _(step):
            rows = pl.ds(pl.multiple_of(step * tile, tile), tile)
            if turn == 0:
                rest = change_scratch[rows, :]
            else:
                rest = (
                    lead * rest_scratch[rows, :]
                    + power * change_scratch[rows, :]
                    + dot(rest_b[rows, :], change_b[...])
                )
            if turn + 1 < NS_ITERS:
                rest_scratch[rows, :] = rest
                rest_b[rows, :] = rest.astype(jnp.bfloat16)
                mixed = dot(change_b[rows, :], grams[now])
                gram = (
                    lead * lead * gram_scratch[rows, :]
                    + 2.0 * lead * mixed
                    + dot(mixed.astype(jnp.bfloat16), change_b[...])
                )
                gram_scratch[rows, :] = gram
                grams[later, rows, :] = gram.astype(jnp.bfloat16)
            else:
                rest_ref[rows, :] = rest.astype(jnp.bfloat16)

        power = power * lead


def ortho_rest(core, first, second, square):
    size = square.shape[0]
    wide = pltpu.VMEM((size, size), jnp.float32)
    narrow = pltpu.VMEM((size, size), jnp.bfloat16)
    return pl.pallas_call(
        rest_kernel,
        out_shape=jax.ShapeDtypeStruct((size, size), jnp.bfloat16),
        in_specs=[pl.BlockSpec(memory_space=pltpu.SMEM)]
        + [pl.BlockSpec(memory_space=pltpu.VMEM)] * 3,
        out_specs=pl.BlockSpec(memory_space=pltpu.VMEM),
        scratch_shapes=[
            wide,
            wide,
            wide,
            pltpu.VMEM((2, size, size), jnp.bfloat16),
            narrow,
            narrow,
        ],
        compiler_params=pltpu.CompilerParams(vmem_limit_bytes=44 * 1024 * 1024),
        cost_estimate=pl.CostEstimate(
            flops=18 * size**3, bytes_accessed=6 * size * size, transcendentals=0
        ),
    )(core.reshape(1), first, second, square)


def logits_kernel(target_ref, answers_ref, table_ref, shares_ref, stats_ref, logits):
    rows, width = logits.shape
    piece = 256
    target = target_ref[...]
    top = jnp.full((8, width), -jnp.inf, jnp.float32)
    total = jnp.zeros((8, width), jnp.float32)
    picked = jnp.zeros((8, width), jnp.float32)
    for first in range(0, rows, piece):
        scores = lax.dot_general(
            table_ref[first : first + piece, :],
            answers_ref[...],
            (((1,), (1,)), ((), ())),
            preferred_element_type=jnp.float32,
        )
        logits[first : first + piece, :] = scores
        top = jnp.maximum(top, jnp.max(scores.reshape(-1, 8, width), axis=0))
    top = jnp.max(top, axis=0, keepdims=True)
    for first in range(0, rows, piece):
        scores = logits[first : first + piece, :]
        share = jnp.exp(scores - top)
        shares_ref[first : first + piece, :] = share.astype(jnp.bfloat16)
        total = total + jnp.sum(share.reshape(-1, 8, width), axis=0)
        place = lax.broadcasted_iota(jnp.int32, (piece, width), 0)
        hit = jnp.where(place == target - first, scores, 0.0)
        picked = picked + jnp.sum(hit.reshape(-1, 8, width), axis=0)
    stats_ref[0:1, :] = top
    stats_ref[1:2, :] = jnp.sum(total, axis=0, keepdims=True)
    stats_ref[2:3, :] = jnp.sum(picked, axis=0, keepdims=True)
    stats_ref[3:8, :] = jnp.zeros((5, width), jnp.float32)


def answer_shares(target, answers, table):
    count, rows = answers.shape[0], table.shape[0]
    tile = 256
    return pl.pallas_call(
        logits_kernel,
        grid=(count // tile,),
        in_specs=[
            pl.BlockSpec((1, tile), lambda i: (0, i)),
            pl.BlockSpec((tile, D), lambda i: (i, 0)),
            pl.BlockSpec((rows, D), lambda i: (0, 0)),
        ],
        out_specs=[
            pl.BlockSpec((rows, tile), lambda i: (0, i)),
            pl.BlockSpec((8, tile), lambda i: (0, i)),
        ],
        out_shape=[
            jax.ShapeDtypeStruct((rows, count), jnp.bfloat16),
            jax.ShapeDtypeStruct((8, count), jnp.float32),
        ],
        scratch_shapes=[pltpu.VMEM((rows, tile), jnp.float32)],
        compiler_params=pltpu.CompilerParams(vmem_limit_bytes=40 * 1024 * 1024),
        cost_estimate=pl.CostEstimate(
            flops=2 * count * rows * D,
            bytes_accessed=2 * count * (rows + D),
            transcendentals=count * rows,
        ),
    )(target, answers, table)


def logit_grads(place, target, scale, value, shares):
    return jnp.where(place == target, value, shares.astype(jnp.float32) * scale).astype(jnp.bfloat16)


def grads_kernel(target_ref, scale_ref, value_ref, shares_ref, table_ref, grads_ref):
    place = lax.broadcasted_iota(jnp.int32, shares_ref.shape, 0)
    grads = logit_grads(place, target_ref[...], scale_ref[...], value_ref[...], shares_ref[...])
    grads_ref[...] = lax.dot_general(
        grads, table_ref[...], (((0,), (0,)), ((), ())), preferred_element_type=jnp.float32
    ).astype(jnp.bfloat16)


def answer_grads(half, target, scale, value, shares, table, width):
    rows, count = shares.shape
    steps = count // (2 * width)
    first = half * steps
    row = pl.BlockSpec((1, width), lambda i: (0, first + i))
    return pl.pallas_call(
        grads_kernel,
        grid=(steps,),
        in_specs=[
            row,
            row,
            row,
            pl.BlockSpec((rows, width), lambda i: (0, first + i)),
            pl.BlockSpec((rows, D), lambda i: (0, 0)),
        ],
        out_specs=pl.BlockSpec((width, D), lambda i: (i, 0)),
        out_shape=jax.ShapeDtypeStruct((steps * width, D), jnp.bfloat16),
        compiler_params=pltpu.CompilerParams(vmem_limit_bytes=40 * 1024 * 1024),
        cost_estimate=pl.CostEstimate(
            flops=2 * steps * width * rows * D,
            bytes_accessed=2 * steps * width * (rows + D),
            transcendentals=0,
        ),
    )(target, scale, value, shares, table)


def body(
    token_ids,
    seq_lengths,
    pair_order,
    table_master,
    table_first,
    table_second,
    square_master,
    square_moment,
    wide_master,
    wide_moment,
    vector_master,
    vector_first,
    vector_second,
    norm_gains,
    norm_first,
    norm_second,
    adam_count,
):
    members = lax.axis_size("vocab")
    member = lax.axis_index("vocab")
    block_rows = table_master.shape[0]
    lengths = seq_lengths[0]
    order = pair_order[0]
    groups_per = HEADS // KV
    scale = HD ** (-0.5)

    core = lax.axis_index("core")
    devices = lax.axis_size(ALL)
    device = lax.axis_index(ALL)
    groups = devices // members

    own_ids = lax.dynamic_index_in_dim(token_ids, member, 0, keepdims=False)
    own_length = lengths[member]
    start = own_length - 1 - RESP
    owner, first_seen, slot = token_slots(own_ids, block_rows)
    local_ids = own_ids % block_rows
    keys = round_keys(owner, slot, 0, SLOTS)
    asks = round_asks(keys, first_seen, local_ids, devices * SLOTS)
    own_targets = lax.dynamic_slice_in_dim(own_ids, start + 1, RESP, 0)
    vector_low = vector_master.astype(jnp.bfloat16).astype(jnp.float32)
    shared_notes = jnp.concatenate(
        [
            vector_low.reshape(-1),
            jnp.concatenate([own_targets, order, jnp.max(slot)[None] + 1]).astype(jnp.float32),
        ]
    )
    notes = jnp.concatenate(
        [
            asks.reshape(devices, SLOTS).astype(jnp.float32),
            jnp.broadcast_to(shared_notes[None, :], (devices, shared_notes.size)),
        ],
        axis=1,
    )
    notes = exchanged(notes)
    square_b = lax.all_gather(square_master.astype(jnp.bfloat16), ALL, axis=1, tiled=True)
    wide_b = lax.all_gather(wide_master.astype(jnp.bfloat16), DP, axis=1, tiled=True)
    hidden_units = wide_b.shape[1]
    asked = notes[:, :SLOTS].astype(jnp.int32).reshape(-1)
    gains = (
        notes[:, SLOTS : SLOTS + vector_low.size]
        .reshape(devices, vector_low.shape[0], vector_low.shape[1])
        .transpose(1, 0, 2)
        .reshape(vector_low.shape[0], D)
    )
    numbers = notes[:, SLOTS + vector_low.size :].astype(jnp.int32)
    targets = numbers[:, :RESP].reshape(-1)
    orders = numbers[:, RESP : RESP + members].reshape(groups, members, members)[:, 0]
    later = jnp.maximum(jnp.max(numbers[:, RESP + members]) - SLOTS, 0)
    later_turns = (later + LATER_SLOTS - 1) // LATER_SLOTS
    slots = jnp.arange(members)
    chosen_mask = (orders[:, 0::2, None] == slots[None, None, :]).astype(jnp.float32)
    rejected_mask = (orders[:, 1::2, None] == slots[None, None, :]).astype(jnp.float32)
    pair_rows = jnp.sum(
        (chosen_mask + rejected_mask)[:, :, :, None] * (chosen_mask - rejected_mask)[:, :, None, :],
        axis=1,
    )
    same_group = jnp.arange(groups)[:, None] == jnp.arange(groups)[None, :]
    pair_rows = jnp.where(same_group[:, None, :, None], pair_rows[:, :, None, :], 0.0)
    pair_rows = pair_rows.reshape(devices, devices) * (pref_beta / RESP)
    chosen_sign = jnp.sum(chosen_mask - rejected_mask, axis=1).reshape(devices, 1)
    table_b = table_master.astype(jnp.bfloat16)
    head_gains = low_copy(norm_gains)
    cosine, sine = rope_tables(SEQ, HD // 2)

    def fetched(wanted, row_keys):
        rows = jnp.dot(
            onehot_rows(wanted, block_rows), table_b, preferred_element_type=jnp.float32
        ).astype(jnp.bfloat16)
        return jnp.dot(
            onehot_rows(row_keys, wanted.shape[0]),
            exchanged(rows),
            preferred_element_type=jnp.float32,
        )

    def later_round(turn):
        count = devices * LATER_SLOTS
        later_keys = round_keys(owner, slot, SLOTS + turn * LATER_SLOTS, LATER_SLOTS)
        return later_keys, exchanged(round_asks(later_keys, first_seen, local_ids, count))

    def fetch_more(turn, rows):
        later_keys, later_asked = later_round(turn)
        return rows + fetched(later_asked, later_keys)

    hidden0 = lax.fori_loop(0, later_turns, fetch_more, fetched(asked, keys))
    act1 = rms_scale(hidden0, gains[0]).astype(jnp.bfloat16)
    entry, leave, conv_in = (dense(act1, square_b[place]) for place in range(3))
    product = entry * conv_in
    convolved = gains[4] * product + gains[5] * delayed(product, 1) + gains[6] * delayed(product, 2)
    mixer = (leave * convolved).astype(jnp.bfloat16)
    hidden1 = hidden0 + dense(mixer, square_b[3])
    act2 = rms_scale(hidden1, gains[1]).astype(jnp.bfloat16)

    def answers(values):
        return lax.dynamic_slice_in_dim(values, start, RESP, 0)

    def placed(values):
        return lax.dynamic_update_slice_in_dim(
            jnp.zeros((SEQ, values.shape[1]), values.dtype), values, start, 0
        )

    answer_act2 = answers(act2)
    query_raw = dense(answer_act2, square_b[4]).reshape(RESP, HEADS, HD)
    pair_raw = dense(act2, square_b[5])
    key_raw = pair_raw[:, : KV * HD].reshape(SEQ, KV, HD)
    value_b = pair_raw[:, KV * HD :].astype(jnp.bfloat16).reshape(SEQ, KV, HD)

    answer_cosine, answer_sine = answers(cosine), answers(sine)

    def query_prep(raw, gain):
        return rotate(rms_scale(raw, gain), answer_cosine, answer_sine)

    def key_prep(raw, gain):
        return rotate(rms_scale(raw, gain), cosine, sine)

    query_b = (
        query_prep(query_raw, head_gains[0]).astype(jnp.bfloat16).reshape(RESP, KV, groups_per, HD)
    )
    key_b = key_prep(key_raw, head_gains[1]).astype(jnp.bfloat16)
    causal = start + jnp.arange(RESP)[:, None] >= jnp.arange(SEQ)[None, :]
    scores = (
        jnp.einsum("sgrd,tgd->grst", query_b, key_b, preferred_element_type=jnp.float32) * scale
    )
    scores = jnp.where(causal, scores, masked_score)
    peak = jnp.max(scores, axis=-1, keepdims=True)
    expo = jnp.exp(scores - peak)
    total = jnp.sum(expo, axis=-1, keepdims=True)
    log_norm = peak + jnp.log(total)
    probs_b = (expo / total).astype(jnp.bfloat16)
    attended = jnp.einsum(
        "grst,tgd->sgrd", probs_b, value_b, preferred_element_type=jnp.float32
    ).reshape(RESP, D)
    attended_b = attended.astype(jnp.bfloat16)
    hidden2 = answers(hidden1) + dense(attended_b, square_b[6])
    act3 = member_gather(rms_scale(hidden2, gains[2]).astype(jnp.bfloat16))
    gate_part, up_part = dense(act3, wide_b[0]), dense(act3, wide_b[1])
    inner_b = (jax.nn.silu(gate_part) * up_part).astype(jnp.bfloat16)
    ffn_part = jnp.dot(inner_b, wide_b[2], preferred_element_type=jnp.float32)
    hidden3 = hidden2 + member_return(ffn_part.astype(jnp.bfloat16).reshape(members, RESP, D))
    final_b = rms_scale(hidden3, gains[3]).astype(jnp.bfloat16)
    squares, square_rows = square_master.shape[0], square_master.shape[1]
    wides, wide_rows = wide_master.shape[0], wide_master.shape[1]
    per_member = -(-squares // members)
    group_rows = members * square_rows

    def by_member(values):
        values = jnp.pad(values, ((0, per_member * members - squares), (0, 0), (0, 0)))
        return values.reshape(per_member, members, -1, D).transpose(1, 0, 2, 3)

    def wide_by_member(values):
        return jnp.pad(values, ((0, members - wides), (0, 0), (0, 0)))

    half_tokens = [
        jnp.concatenate(gathered(piece, "chip"), axis=0) for piece in gathered(final_b, "vocab")
    ]
    response_tokens = jnp.concatenate(
        half_tokens + [other_core(piece) for piece in half_tokens], axis=0
    )
    chips = groups // 2
    chip = lax.axis_index("chip")
    block_core = jnp.stack([core, 1 - core])[:, None, None]
    block_member = ((member - jnp.arange(members)) % members)[None, :, None]
    block_chip = ((chip - jnp.arange(chips)) % chips)[None, None, :]
    block_device = ((block_chip * 2 + block_core) * members + block_member).reshape(-1)
    device_block = jnp.sum(
        jnp.where(
            block_device[None, :] == jnp.arange(devices)[:, None], jnp.arange(devices)[None, :], 0
        ),
        axis=1,
    )
    wide_moment_blocks, response_tokens = lax.optimization_barrier(
        (wide_by_member(wide_moment.astype(jnp.bfloat16)), response_tokens)
    )
    wide_moment_job = handed_out(wide_moment_blocks, "vocab")
    local_target = jnp.where(targets // block_rows == device, targets % block_rows, -1)
    local_target = local_target.reshape(devices, RESP)[block_device].reshape(1, -1)
    shares, own_stats = answer_shares(local_target, response_tokens, table_b)
    own_stats, wide_moment_job = lax.optimization_barrier((own_stats, wide_moment_job))
    wide_moment_job = jnp.stack(wide_moment_job)
    stats = own_stats[:3].reshape(3, devices, RESP).transpose(1, 0, 2)[device_block]
    stats = exchanged(stats)
    top = jnp.max(stats[:, 0], axis=0)
    exp_total = jnp.sum(stats[:, 1] * jnp.exp(stats[:, 0] - top[None, :]), axis=0)
    own_log_total = top + jnp.log(exp_total)
    own_logp = jnp.sum(jnp.sum(stats[:, 2], axis=0) - own_log_total)
    joined = spread(jnp.concatenate([own_log_total, own_logp[None]]))
    log_total = joined[:, :RESP][block_device].reshape(1, -1)
    margin = jnp.sum(pair_rows * joined[:, RESP][None, :], axis=1, keepdims=True)
    pair_loss = 0.5 * jnp.sum(jax.nn.softplus(-margin))
    grad_logp = chosen_sign * jax.nn.sigmoid(-margin) * (-pref_beta / RESP)
    row_weight = jnp.broadcast_to(grad_logp[block_device], (devices, RESP)).reshape(1, -1)
    share_scale = -row_weight * jnp.exp(own_stats[0:1] - log_total)
    target_value = row_weight * (1.0 - jnp.exp(own_stats[2:3] - log_total))
    given, kept = (
        answer_grads(
            half, local_target, share_scale, target_value, shares, table_b, members * RESP
        )
        for half in (1, 0)
    )
    grad_answer_pair = (kept.astype(jnp.float32) + other_core(given).astype(jnp.float32)).astype(
        jnp.bfloat16
    )
    grad_answer_pair, square_moment_blocks = lax.optimization_barrier(
        (grad_answer_pair, by_member(square_moment.astype(jnp.bfloat16)))
    )
    square_moment_job = handed_out(square_moment_blocks, "vocab")
    grad_answer_pair = grad_answer_pair.reshape(members, chips, RESP, D)
    grad_answer_group = added(
        handed_back([grad_answer_pair[:, place] for place in range(chips)], "chip")
    )
    grad_table = jnp.dot(
        logit_grads(
            jnp.arange(block_rows)[:, None], local_target, share_scale, target_value, shares
        ),
        response_tokens,
        preferred_element_type=jnp.float32,
    )
    grad_answer_group, grad_table, square_moment_job = lax.optimization_barrier(
        (grad_answer_group.astype(jnp.bfloat16), grad_table, square_moment_job)
    )
    square_moment_job = placed_before(square_moment_job, "vocab")
    square_moment_job = square_moment_job.transpose(1, 0, 2, 3).reshape(per_member, group_rows, D)
    grad_final = member_return(list(grad_answer_group))
    grad_hidden3, grad_gain3 = norm_back(hidden3, gains[3], grad_final)
    grad_ffn_out = member_gather(grad_hidden3.astype(jnp.bfloat16))
    grad_inner = dense(grad_ffn_out, wide_b[2])
    grad_down_w = outer(inner_b, grad_ffn_out)
    _, silu_pull = jax.vjp(lambda gate_in, up_in: jax.nn.silu(gate_in) * up_in, gate_part, up_part)
    grad_gate, grad_up = silu_pull(grad_inner)
    grad_gate_b, grad_up_b = grad_gate.astype(jnp.bfloat16), grad_up.astype(jnp.bfloat16)
    grad_act3_part = back_dense(grad_gate_b, wide_b[0]) + back_dense(grad_up_b, wide_b[1])
    grad_act3 = member_return(grad_act3_part.astype(jnp.bfloat16).reshape(members, RESP, D))
    grad_gate_w, grad_up_w = outer(grad_gate_b, act3), outer(grad_up_b, act3)
    grad_norm2, grad_gain2 = norm_back(hidden2, gains[2], grad_act3)
    grad_hidden2 = grad_hidden3 + grad_norm2
    grad_attn_out = grad_hidden2.astype(jnp.bfloat16)
    grad_attended = (
        back_dense(grad_attn_out, square_b[6])
        .astype(jnp.bfloat16)
        .reshape(RESP, KV, groups_per, HD)
    )
    grad_out_w = outer(grad_attn_out, attended_b)
    scores = (
        jnp.einsum("sgrd,tgd->grst", query_b, key_b, preferred_element_type=jnp.float32) * scale
    )
    probs = jnp.exp(jnp.where(causal, scores, masked_score) - log_norm)
    grad_probs = jnp.einsum(
        "sgrd,tgd->grst", grad_attended, value_b, preferred_element_type=jnp.float32
    )
    grad_values = jnp.einsum(
        "grst,sgrd->tgd", probs_b, grad_attended, preferred_element_type=jnp.float32
    )
    delta = jnp.sum(probs * grad_probs, axis=-1, keepdims=True)
    grad_scores = (probs * (grad_probs - delta)).astype(jnp.bfloat16)
    grad_query = (
        jnp.einsum("grst,tgd->sgrd", grad_scores, key_b, preferred_element_type=jnp.float32) * scale
    ).reshape(RESP, HEADS, HD)
    grad_keys = (
        jnp.einsum("grst,sgrd->tgd", grad_scores, query_b, preferred_element_type=jnp.float32)
        * scale
    )
    _, query_pull = jax.vjp(query_prep, query_raw, head_gains[0])
    grad_query_raw, grad_query_gain = query_pull(grad_query)
    _, key_pull = jax.vjp(key_prep, key_raw, head_gains[1])
    grad_key_raw, grad_key_gain = key_pull(grad_keys)
    grad_query_b = grad_query_raw.reshape(RESP, D).astype(jnp.bfloat16)
    grad_pair_b = jnp.concatenate(
        [grad_key_raw.reshape(SEQ, KV * HD), grad_values.reshape(SEQ, KV * HD)], axis=1
    ).astype(jnp.bfloat16)
    grad_act2 = back_dense(grad_pair_b, square_b[5]) + placed(back_dense(grad_query_b, square_b[4]))
    grad_query_w = outer(grad_query_b, answer_act2)
    grad_pair_w = outer(grad_pair_b, act2)
    grad_norm1, grad_gain1 = norm_back(hidden1, gains[1], grad_act2)
    grad_hidden1 = placed(grad_hidden2) + grad_norm1
    grad_mix_out = grad_hidden1.astype(jnp.bfloat16)
    grad_mixer = back_dense(grad_mix_out, square_b[3])
    grad_mixer_w = outer(grad_mix_out, mixer)
    grad_leave = grad_mixer * convolved
    grad_conv = grad_mixer * leave
    grad_tap0 = jnp.sum(grad_conv * product, axis=0)
    grad_tap1 = jnp.sum(grad_conv * delayed(product, 1), axis=0)
    grad_tap2 = jnp.sum(grad_conv * delayed(product, 2), axis=0)
    grad_product = (
        gains[4] * grad_conv + gains[5] * advanced(grad_conv, 1) + gains[6] * advanced(grad_conv, 2)
    )
    grad_inner = [
        part.astype(jnp.bfloat16)
        for part in (grad_product * conv_in, grad_leave, grad_product * entry)
    ]
    grad_act1 = sum(back_dense(grad_inner[place], square_b[place]) for place in range(3))
    grad_inner_w = [outer(part, act1) for part in grad_inner]
    grad_norm0, grad_gain0 = norm_back(hidden0, gains[0], grad_act1)
    grad_embed_b = (grad_hidden1 + grad_norm0).astype(jnp.bfloat16)

    grad_first = (*grad_inner_w, grad_mixer_w)
    grad_square = jnp.stack(
        [part.astype(jnp.bfloat16) for part in (grad_query_w, grad_pair_w, grad_out_w)]
    )
    grad_vector = jnp.stack(
        [grad_gain0, grad_gain1, grad_gain2, grad_gain3, grad_tap0, grad_tap1, grad_tap2]
    )
    grad_head_gains = jnp.stack([grad_query_gain, grad_key_gain])
    grad_wide = jnp.stack(
        [part.astype(jnp.bfloat16) for part in (grad_gate_w, grad_up_w, grad_down_w)]
    )
    share_wide_b = lax.psum_scatter(grad_wide, DP, scatter_dimension=1, tiled=True)
    grad_square, share_wide_b = lax.optimization_barrier((grad_square, share_wide_b))
    share_wide_b, grad_embed_b = lax.optimization_barrier((share_wide_b, grad_embed_b))
    share_wide = share_wide_b.astype(jnp.float32)
    wide_grad_job = jnp.stack(handed_out(wide_by_member(share_wide_b), "vocab"))
    group_square = lax.psum_scatter(grad_square, DP, scatter_dimension=1, tiled=True)

    def permuted_sum(values):
        blocks = values.astype(jnp.bfloat16).reshape(chips, 2, group_rows, D)
        given = lax.dynamic_index_in_dim(blocks, 1 - core, 1, keepdims=False)
        kept = lax.dynamic_index_in_dim(blocks, core, 1, keepdims=False)
        pair = kept.astype(jnp.float32) + other_core(given).astype(jnp.float32)
        return chip_sum(pair.astype(jnp.bfloat16)).astype(jnp.bfloat16)

    group_square = jnp.pad(group_square, ((0, per_member * members - squares), (0, 0), (0, 0)))
    square_grad_job = jnp.stack(
        [
            member_scatter(jnp.stack([permuted_sum(part) for part in grad_first])),
            member_scatter(group_square),
        ]
    )

    def from_members(values):
        values = values.reshape(per_member, members, square_rows, D).transpose(1, 0, 2, 3)
        values = placed_before(handed_out(values.astype(jnp.bfloat16), "vocab"), "vocab")
        values = values.transpose(1, 0, 2, 3).reshape(per_member * members, square_rows, D)
        return values[:squares].astype(jnp.float32)

    share_square = from_members(square_grad_job)

    def returned(row_keys, count):
        rows = outer(onehot_rows(row_keys, count), grad_embed_b)
        return exchanged(rows.astype(jnp.bfloat16))

    def put(wanted, rows):
        return outer(onehot_rows(wanted, block_rows), rows)

    def return_more(turn, total):
        later_keys, later_asked = later_round(turn)
        return total + put(later_asked, returned(later_keys, later_asked.shape[0]))

    returned_rows, wide_grad_job = lax.optimization_barrier(
        (returned(keys, devices * SLOTS), wide_grad_job)
    )
    share_table = lax.fori_loop(
        0, later_turns, return_more, grad_table + put(asked, returned_rows))
    width = vector_master.shape[1]
    vector_notes = grad_vector.reshape(-1, devices, width).transpose(1, 0, 2).reshape(devices, -1)
    vector_notes = jnp.concatenate(
        [
            vector_notes,
            jnp.broadcast_to(grad_head_gains.reshape(1, -1), (devices, grad_head_gains.size)),
        ],
        axis=1,
    )
    vector_notes = jnp.sum(exchanged(vector_notes), axis=0)
    share_vector = vector_notes[: vector_master.size].reshape(vector_master.shape)
    gains_total = vector_notes[vector_master.size :].reshape(grad_head_gains.shape)

    def job_sums(values):
        sums = jnp.sum(values, axis=(1, 2))[:, None]
        sums = jnp.where(jnp.arange(members)[None, :] == member, sums, 0.0)
        return sums.reshape(-1)[:squares]

    moment_squares = jnp.concatenate(
        [
            jnp.sum(square_moment * square_moment, axis=(1, 2)),
            jnp.sum(wide_moment * wide_moment, axis=(1, 2)),
        ]
    )
    moment_cross = jnp.concatenate(
        [
            job_sums(square_moment_job.astype(jnp.float32) * square_grad_job),
            jnp.sum(wide_moment * share_wide, axis=(1, 2)),
        ]
    )
    grad_squares = jnp.concatenate(
        [
            job_sums(square_grad_job * square_grad_job),
            jnp.sum(share_wide * share_wide, axis=(1, 2)),
        ]
    )
    moment_stats = jnp.stack([moment_squares, moment_cross, grad_squares])
    own_squares = (
        jnp.sum(grad_squares)
        + jnp.sum(share_vector * share_vector)
        + jnp.sum(share_table * share_table)
    )
    sums = jnp.concatenate([moment_stats.reshape(-1), own_squares[None]])
    sums = jnp.sum(spread(sums), axis=0)
    stats_total = sums[:-1].reshape(moment_stats.shape)
    grad_norm = jnp.sqrt(sums[-1] + jnp.sum(gains_total * gains_total))
    factor = jnp.minimum(1.0, clip_limit / grad_norm)
    square_moment_new = muon_decay * square_moment + (1.0 - muon_decay) * (factor * share_square)
    wide_moment_new = muon_decay * wide_moment + (1.0 - muon_decay) * (factor * share_wide)
    moment_norm = jnp.sqrt(
        muon_decay * muon_decay * stats_total[0]
        + 2.0 * muon_decay * (1.0 - muon_decay) * factor * stats_total[1]
        + (1.0 - muon_decay) * (1.0 - muon_decay) * factor * factor * stats_total[2]
    )
    ortho_square = square_moment_new / (moment_norm[:7][:, None, None] + ortho_epsilon)
    ortho_wide = wide_moment_new / (moment_norm[7:][:, None, None] + ortho_epsilon)
    wide_inverse = 1.0 / (moment_norm[squares:] + ortho_epsilon)
    wide_inverse = jnp.pad(wide_inverse, (0, members - wides))[member]
    square_inverse = 1.0 / (moment_norm[:squares] + ortho_epsilon)
    square_inverse = jnp.pad(square_inverse, (0, per_member * members - squares))
    square_inverse = square_inverse.reshape(per_member, members)[:, member][:, None, None]
    square_part = (muon_decay * square_inverse) * square_moment_job.astype(jnp.float32) + (
        (1.0 - muon_decay) * factor * square_inverse
    ) * square_grad_job
    square_part, wide_grad_job = lax.optimization_barrier(
        (square_part.astype(jnp.bfloat16), wide_grad_job)
    )
    square_part = jnp.pad(square_part, ((0, groups // 2 - per_member), (0, 0), (0, 0)))
    square_half = jnp.concatenate(handed_out(square_part, "chip"), axis=0)
    square_job = jnp.concatenate([square_half, other_core(square_half)], axis=0)
    wide_job = (
        (muon_decay * wide_inverse) * wide_moment_job.astype(jnp.float32)
        + ((1.0 - muon_decay) * factor * wide_inverse) * wide_grad_job.astype(jnp.float32)
    )
    wide_job = wide_job.reshape(members * wide_rows, D).astype(jnp.bfloat16)
    wide_first, wide_second = group_sum(outer(wide_job, wide_job).astype(jnp.bfloat16), core)
    square_gram = outer(square_job, square_job)
    rest_b = ortho_rest(core, wide_first, wide_second, square_gram)
    power = leading_coefficient**NS_ITERS
    wide_rest = jnp.where(core == 0, rest_b, other_core(rest_b))
    back_square = square_product(square_job, rest_b).astype(jnp.bfloat16)
    half_rows = square_half.shape[0]
    back_square = jnp.where(
        core == 0, other_core(back_square[half_rows:]), back_square[:half_rows]
    )
    back_wide = square_product(wide_job, wide_rest).astype(jnp.bfloat16)
    share_table, back_square, back_wide = lax.optimization_barrier(
        (share_table, back_square, back_wide)
    )
    table_step, table_first_new, table_second_new = adam_step(
        table_master, table_first, table_second, share_table, factor, adam_count
    )
    back_square = handed_back(list(back_square.reshape(-1, group_rows, D)), "chip")
    back_square = placed_after(back_square, "chip")[:per_member]
    back_wide = handed_back(list(back_wide.reshape(members, wide_rows, D)), "vocab")
    back_wide = placed_after(back_wide, "vocab")[:wides]
    back_square = from_members(back_square)
    ortho_wide = power * ortho_wide + back_wide.astype(jnp.float32)
    ortho_square = power * ortho_square + back_square
    wide_scale = jnp.array([math.sqrt(FF / D), math.sqrt(FF / D), 1.0], jnp.float32)
    square_new = square_master - muon_rate * ortho_square
    wide_new = wide_master - muon_rate * wide_scale[:, None, None] * ortho_wide
    vector_step, vector_first_new, vector_second_new = adam_step(
        vector_master, vector_first, vector_second, share_vector, factor, adam_count
    )
    norm_step, norm_first_new, norm_second_new = adam_step(
        norm_gains, norm_first, norm_second, gains_total, factor, adam_count
    )
    return (
        pair_loss,
        grad_norm,
        square_new,
        square_moment_new,
        square_new.astype(jnp.bfloat16),
        wide_new,
        wide_moment_new,
        wide_new.astype(jnp.bfloat16),
        table_step,
        table_first_new,
        table_second_new,
        vector_step,
        vector_first_new,
        vector_second_new,
        norm_step,
        norm_first_new,
        norm_second_new,
        share_vector[3],
    )


def solution(mesh):
    groups, members = mesh.shape["dp"], mesh.shape["vocab"]
    cores = 2
    split_mesh = Mesh(mesh.devices.reshape(groups // cores, cores, members), ALL)
    return jax.shard_map(
        body,
        mesh=split_mesh,
        in_specs=(
            P(DP, None),
            P(DP, None),
            P(DP, None),
            P(ALL, None),
            P(ALL, None),
            P(ALL, None),
            P(None, ALL, None),
            P(None, ALL, None),
            P(None, ALL, None),
            P(None, ALL, None),
            P(None, ALL),
            P(None, ALL),
            P(None, ALL),
            P(),
            P(),
            P(),
            P(),
        ),
        out_specs=(
            P(),
            P(),
            P(None, ALL, None),
            P(None, ALL, None),
            P(None, ALL, None),
            P(None, ALL, None),
            P(None, ALL, None),
            P(None, ALL, None),
            P(ALL, None),
            P(ALL, None),
            P(ALL, None),
            P(None, ALL),
            P(None, ALL),
            P(None, ALL),
            P(),
            P(),
            P(),
            P(ALL),
        ),
        check_vma=False,
    )
```

```python
import math

import jax
import jax.numpy as jnp
from jax import lax
from jax.experimental import pallas as pl
from jax.experimental.pallas import tpu as pltpu
from jax.sharding import Mesh
from jax.sharding import PartitionSpec as P

D = 1024
HEADS = 16
KV = 8
HD = 64
FF = 4608
SEQ = 512
RESP = 96
NS_ITERS = 3


norm_epsilon = 1e-05
rope_base = 1000000.0
pref_beta = 2.0
clip_limit = 0.05
muon_decay = 0.95
muon_rate = 0.5
first_decay = 0.9
second_decay = 0.95
adam_rate = 0.02
adam_epsilon = 1e-08
weight_decay = 0.1
leading_coefficient = 3.4445
coef_second = -4.775
coef_third = 2.0315
ortho_epsilon = 1e-07
masked_score = -1e30


def rms_scale(inputs, gain):
    mean_square = jnp.mean(inputs * inputs, axis=-1, keepdims=True)
    return inputs * lax.rsqrt(mean_square + norm_epsilon) * gain


def rope_tables(length, half):
    position = jnp.arange(length, dtype=jnp.float32)
    inverse = rope_base ** (-jnp.arange(half, dtype=jnp.float32) / half)
    angle = position[:, None] * inverse[None, :]
    return (jnp.cos(angle)[:, None, :], jnp.sin(angle)[:, None, :])


def rotate(inputs, cosine, sine):
    half = inputs.shape[-1] // 2
    first = inputs[..., :half]
    second = inputs[..., half:]
    return jnp.concatenate(
        [first * cosine - second * sine, second * cosine + first * sine], axis=-1
    )


def dense(inputs, weight):
    return lax.dot_general(
        inputs, weight, (((1,), (1,)), ((), ())), preferred_element_type=jnp.float32
    )


def outer(grads, inputs):
    return lax.dot_general(
        grads, inputs, (((0,), (0,)), ((), ())), preferred_element_type=jnp.float32
    )


def back_dense(grads, weight):
    return jnp.dot(grads, weight, preferred_element_type=jnp.float32)


def delayed(values, offset):
    return jnp.pad(values, ((offset, 0), (0, 0)))[: values.shape[0]]


def advanced(values, offset):
    return jnp.pad(values, ((0, offset), (0, 0)))[offset:]


def norm_back(inputs, gain, grad_out):
    _, pullback = jax.vjp(rms_scale, inputs, gain)
    return pullback(grad_out)


def low_copy(values):
    return lax.optimization_barrier(values.astype(jnp.bfloat16)).astype(jnp.float32)


def adam_step(master, first, second, grad, factor, count):
    scaled = factor * grad
    first_new = first_decay * first + (1.0 - first_decay) * scaled
    second_new = second_decay * second + (1.0 - second_decay) * scaled * scaled
    steps = count.astype(jnp.float32)
    first_hat = first_new / (1.0 - first_decay**steps)
    second_hat = second_new / (1.0 - second_decay**steps)
    change = -adam_rate * (
        first_hat / (jnp.sqrt(second_hat) + adam_epsilon) + weight_decay * master
    )
    return (change, first_new, second_new)

DP = ("chip", "core")
ALL = ("chip", "core", "vocab")
SLOTS = 24
LATER_SLOTS = 8


def exchanged(rows):
    return lax.all_to_all(rows, ALL, 0, 0, tiled=True)


def spread(values):
    count = lax.axis_size(ALL)
    return lax.all_to_all(jnp.broadcast_to(values[None], (count,) + values.shape), ALL, 0, 0)


def turned(values, axis, step):
    count = lax.axis_size(axis)
    return lax.ppermute(values, axis, [(i, (i + step) % count) for i in range(count)])


def block_at(blocks, index):
    return lax.dynamic_index_in_dim(blocks, index % blocks.shape[0], 0, keepdims=False)


def handed_out(blocks, axis):
    place, count = lax.axis_index(axis), lax.axis_size(axis)
    return [block_at(blocks, place)] + [
        turned(block_at(blocks, place + step), axis, step) for step in range(1, count)
    ]


def handed_back(pieces, axis):
    return [pieces[0]] + [turned(pieces[step], axis, -step) for step in range(1, len(pieces))]


def gathered(values, axis):
    return [values] + [turned(values, axis, step) for step in range(1, lax.axis_size(axis))]


def placed_before(pieces, axis):
    pieces, place = jnp.stack(pieces), lax.axis_index(axis)
    return jnp.stack([block_at(pieces, place - j) for j in range(pieces.shape[0])])


def placed_after(pieces, axis):
    pieces, place = jnp.stack(pieces), lax.axis_index(axis)
    return jnp.stack([block_at(pieces, j - place) for j in range(pieces.shape[0])])


def added(pieces):
    total = pieces[0].astype(jnp.float32)
    for piece in pieces[1:]:
        total = total + piece.astype(jnp.float32)
    return total


def other_core(values):
    return lax.ppermute(values, "core", [(0, 1), (1, 0)])


def pair_sum(halves, core):
    given = lax.dynamic_index_in_dim(halves, 1 - core, 0, keepdims=False)
    kept = lax.dynamic_index_in_dim(halves, core, 0, keepdims=False)
    total = kept.astype(jnp.float32) + other_core(given).astype(jnp.float32)
    return total.astype(jnp.bfloat16)


def chip_sum(blocks):
    return added(handed_out(blocks, "chip"))


def group_sum(values, core):
    rows = values.shape[0] // 2
    chips = lax.axis_size("chip")
    half = pair_sum(values.reshape(2, rows, -1), core).reshape(chips, rows // chips, -1)
    part = chip_sum(half).astype(jnp.bfloat16)
    half = placed_before(gathered(part, "chip"), "chip").reshape(rows, -1)
    return half, other_core(half)


def member_gather(values):
    return jnp.concatenate(gathered(values, "vocab"), axis=0)


def member_return(pieces):
    return added(handed_back(pieces, "vocab"))


def member_scatter(blocks):
    return added(handed_out(blocks, "vocab"))


def onehot_rows(index, count):
    return (index[:, None] == jnp.arange(count)[None, :]).astype(jnp.bfloat16)


def token_slots(ids, block_rows):
    owner = ids // block_rows
    place = jnp.arange(ids.shape[0])
    earlier = place[:, None] > place[None, :]
    equal = ids[:, None] == ids[None, :]
    first = jnp.logical_not(jnp.any(equal & earlier, axis=1))
    ahead = (owner[:, None] == owner[None, :]) & earlier & first[None, :]
    rank = jnp.sum(ahead.astype(jnp.int32), axis=1)
    slot = jnp.sum(jnp.where(equal & first[None, :], rank[None, :], 0), axis=1)
    return owner, first, slot


def round_keys(owner, slot, first, count):
    within = slot - first
    return jnp.where((within >= 0) & (within < count), owner * count + within, -1)


def round_asks(keys, first_seen, local, count):
    hits = (keys[None, :] == jnp.arange(count)[:, None]) & first_seen[None, :]
    return jnp.sum(jnp.where(hits, local[None, :] + 1, 0), axis=1) - 1


def square_product(left, right):
    return jnp.dot(
        left.astype(jnp.bfloat16), right.astype(jnp.bfloat16), preferred_element_type=jnp.float32
    )


def rest_kernel(
    core_ref,
    first_ref,
    second_ref,
    square_ref,
    rest_ref,
    gram_scratch,
    change_scratch,
    rest_scratch,
    grams,
    change_b,
    rest_b,
):
    lead = leading_coefficient
    size = square_ref.shape[0]
    half = size // 2
    tile = 256

    def dot(left, right):
        return jnp.dot(left, right, preferred_element_type=jnp.float32)

    on_wide = core_ref[0] == 0
    for part, wide_ref in enumerate((first_ref, second_ref)):

        @pl.loop(0, half // tile)
        def _(step):
            rows = pl.ds(pl.multiple_of(step * tile, tile), tile)
            place = pl.ds(pl.multiple_of(part * half + step * tile, tile), tile)
            gram = jnp.where(on_wide, wide_ref[rows, :].astype(jnp.float32), square_ref[place, :])
            gram_scratch[place, :] = gram
            grams[0, place, :] = gram.astype(jnp.bfloat16)

    power = 1.0
    for turn in range(NS_ITERS):
        now, later = turn % 2, (turn + 1) % 2

        @pl.loop(0, size // tile)
        def _(step):
            rows = pl.ds(pl.multiple_of(step * tile, tile), tile)
            change = coef_second * gram_scratch[rows, :] + coef_third * dot(
                grams[now, rows, :], grams[now]
            )
            change_scratch[rows, :] = change
            change_b[rows, :] = change.astype(jnp.bfloat16)

        @pl.loop(0, size // tile)
        def _(step):
            rows = pl.ds(pl.multiple_of(step * tile, tile), tile)
            if turn == 0:
                rest = change_scratch[rows, :]
            else:
                rest = (
                    lead * rest_scratch[rows, :]
                    + power * change_scratch[rows, :]
                    + dot(rest_b[rows, :], change_b[...])
                )
            if turn + 1 < NS_ITERS:
                rest_scratch[rows, :] = rest
                rest_b[rows, :] = rest.astype(jnp.bfloat16)
                mixed = dot(change_b[rows, :], grams[now])
                gram = (
                    lead * lead * gram_scratch[rows, :]
                    + 2.0 * lead * mixed
                    + dot(mixed.astype(jnp.bfloat16), change_b[...])
                )
                gram_scratch[rows, :] = gram
                grams[later, rows, :] = gram.astype(jnp.bfloat16)
            else:
                rest_ref[rows, :] = rest.astype(jnp.bfloat16)

        power = power * lead


def ortho_rest(core, first, second, square):
    size = square.shape[0]
    wide = pltpu.VMEM((size, size), jnp.float32)
    narrow = pltpu.VMEM((size, size), jnp.bfloat16)
    return pl.pallas_call(
        rest_kernel,
        out_shape=jax.ShapeDtypeStruct((size, size), jnp.bfloat16),
        in_specs=[pl.BlockSpec(memory_space=pltpu.SMEM)]
        + [pl.BlockSpec(memory_space=pltpu.VMEM)] * 3,
        out_specs=pl.BlockSpec(memory_space=pltpu.VMEM),
        scratch_shapes=[
            wide,
            wide,
            wide,
            pltpu.VMEM((2, size, size), jnp.bfloat16),
            narrow,
            narrow,
        ],
        compiler_params=pltpu.CompilerParams(vmem_limit_bytes=44 * 1024 * 1024),
        cost_estimate=pl.CostEstimate(
            flops=18 * size**3, bytes_accessed=6 * size * size, transcendentals=0
        ),
    )(core.reshape(1), first, second, square)


def logits_kernel(target_ref, answers_ref, table_ref, shares_ref, stats_ref, logits):
    rows, width = logits.shape
    piece = 256
    target = target_ref[...]
    top = jnp.full((8, width), -jnp.inf, jnp.float32)
    total = jnp.zeros((8, width), jnp.float32)
    picked = jnp.zeros((8, width), jnp.float32)
    for first in range(0, rows, piece):
        scores = lax.dot_general(
            table_ref[first : first + piece, :],
            answers_ref[...],
            (((1,), (1,)), ((), ())),
            preferred_element_type=jnp.float32,
        )
        logits[first : first + piece, :] = scores
        top = jnp.maximum(top, jnp.max(scores.reshape(-1, 8, width), axis=0))
    top = jnp.max(top, axis=0, keepdims=True)
    for first in range(0, rows, piece):
        scores = logits[first : first + piece, :]
        share = jnp.exp(scores - top)
        shares_ref[first : first + piece, :] = share.astype(jnp.bfloat16)
        total = total + jnp.sum(share.reshape(-1, 8, width), axis=0)
        place = lax.broadcasted_iota(jnp.int32, (piece, width), 0)
        hit = jnp.where(place == target - first, scores, 0.0)
        picked = picked + jnp.sum(hit.reshape(-1, 8, width), axis=0)
    stats_ref[0:1, :] = top
    stats_ref[1:2, :] = jnp.sum(total, axis=0, keepdims=True)
    stats_ref[2:3, :] = jnp.sum(picked, axis=0, keepdims=True)
    stats_ref[3:8, :] = jnp.zeros((5, width), jnp.float32)


def answer_shares(target, answers, table):
    count, rows = answers.shape[0], table.shape[0]
    tile = 256
    return pl.pallas_call(
        logits_kernel,
        grid=(count // tile,),
        in_specs=[
            pl.BlockSpec((1, tile), lambda i: (0, i)),
            pl.BlockSpec((tile, D), lambda i: (i, 0)),
            pl.BlockSpec((rows, D), lambda i: (0, 0)),
        ],
        out_specs=[
            pl.BlockSpec((rows, tile), lambda i: (0, i)),
            pl.BlockSpec((8, tile), lambda i: (0, i)),
        ],
        out_shape=[
            jax.ShapeDtypeStruct((rows, count), jnp.bfloat16),
            jax.ShapeDtypeStruct((8, count), jnp.float32),
        ],
        scratch_shapes=[pltpu.VMEM((rows, tile), jnp.float32)],
        compiler_params=pltpu.CompilerParams(vmem_limit_bytes=40 * 1024 * 1024),
        cost_estimate=pl.CostEstimate(
            flops=2 * count * rows * D,
            bytes_accessed=2 * count * (rows + D),
            transcendentals=count * rows,
        ),
    )(target, answers, table)


def logit_grads(place, target, scale, value, shares):
    return jnp.where(place == target, value, shares.astype(jnp.float32) * scale).astype(jnp.bfloat16)


def grads_kernel(target_ref, scale_ref, value_ref, shares_ref, table_ref, grads_ref):
    place = lax.broadcasted_iota(jnp.int32, shares_ref.shape, 0)
    grads = logit_grads(place, target_ref[...], scale_ref[...], value_ref[...], shares_ref[...])
    grads_ref[...] = lax.dot_general(
        grads, table_ref[...], (((0,), (0,)), ((), ())), preferred_element_type=jnp.float32
    ).astype(jnp.bfloat16)


def answer_grads(half, target, scale, value, shares, table, width):
    rows, count = shares.shape
    steps = count // (2 * width)
    first = half * steps
    row = pl.BlockSpec((1, width), lambda i: (0, first + i))
    return pl.pallas_call(
        grads_kernel,
        grid=(steps,),
        in_specs=[
            row,
            row,
            row,
            pl.BlockSpec((rows, width), lambda i: (0, first + i)),
            pl.BlockSpec((rows, D), lambda i: (0, 0)),
        ],
        out_specs=pl.BlockSpec((width, D), lambda i: (i, 0)),
        out_shape=jax.ShapeDtypeStruct((steps * width, D), jnp.bfloat16),
        compiler_params=pltpu.CompilerParams(vmem_limit_bytes=40 * 1024 * 1024),
        cost_estimate=pl.CostEstimate(
            flops=2 * steps * width * rows * D,
            bytes_accessed=2 * steps * width * (rows + D),
            transcendentals=0,
        ),
    )(target, scale, value, shares, table)


def body(
    token_ids,
    seq_lengths,
    pair_order,
    table_master,
    table_first,
    table_second,
    square_master,
    square_moment,
    wide_master,
    wide_moment,
    vector_master,
    vector_first,
    vector_second,
    norm_gains,
    norm_first,
    norm_second,
    adam_count,
):
    members = lax.axis_size("vocab")
    member = lax.axis_index("vocab")
    block_rows = table_master.shape[0]
    lengths = seq_lengths[0]
    order = pair_order[0]
    groups_per = HEADS // KV
    scale = HD ** (-0.5)

    core = lax.axis_index("core")
    devices = lax.axis_size(ALL)
    device = lax.axis_index(ALL)
    groups = devices // members

    own_ids = lax.dynamic_index_in_dim(token_ids, member, 0, keepdims=False)
    own_length = lengths[member]
    start = own_length - 1 - RESP
    owner, first_seen, slot = token_slots(own_ids, block_rows)
    local_ids = own_ids % block_rows
    keys = round_keys(owner, slot, 0, SLOTS)
    asks = round_asks(keys, first_seen, local_ids, devices * SLOTS)
    own_targets = lax.dynamic_slice_in_dim(own_ids, start + 1, RESP, 0)
    vector_low = vector_master.astype(jnp.bfloat16).astype(jnp.float32)
    shared_notes = jnp.concatenate(
        [
            vector_low.reshape(-1),
            jnp.concatenate([own_targets, order, jnp.max(slot)[None] + 1]).astype(jnp.float32),
        ]
    )
    notes = jnp.concatenate(
        [
            asks.reshape(devices, SLOTS).astype(jnp.float32),
            jnp.broadcast_to(shared_notes[None, :], (devices, shared_notes.size)),
        ],
        axis=1,
    )
    notes = exchanged(notes)
    square_b = lax.all_gather(square_master.astype(jnp.bfloat16), ALL, axis=1, tiled=True)
    wide_b = lax.all_gather(wide_master.astype(jnp.bfloat16), DP, axis=1, tiled=True)
    hidden_units = wide_b.shape[1]
    asked = notes[:, :SLOTS].astype(jnp.int32).reshape(-1)
    gains = (
        notes[:, SLOTS : SLOTS + vector_low.size]
        .reshape(devices, vector_low.shape[0], vector_low.shape[1])
        .transpose(1, 0, 2)
        .reshape(vector_low.shape[0], D)
    )
    numbers = notes[:, SLOTS + vector_low.size :].astype(jnp.int32)
    targets = numbers[:, :RESP].reshape(-1)
    orders = numbers[:, RESP : RESP + members].reshape(groups, members, members)[:, 0]
    later = jnp.maximum(jnp.max(numbers[:, RESP + members]) - SLOTS, 0)
    later_turns = (later + LATER_SLOTS - 1) // LATER_SLOTS
    slots = jnp.arange(members)
    chosen_mask = (orders[:, 0::2, None] == slots[None, None, :]).astype(jnp.float32)
    rejected_mask = (orders[:, 1::2, None] == slots[None, None, :]).astype(jnp.float32)
    pair_rows = jnp.sum(
        (chosen_mask + rejected_mask)[:, :, :, None] * (chosen_mask - rejected_mask)[:, :, None, :],
        axis=1,
    )
    same_group = jnp.arange(groups)[:, None] == jnp.arange(groups)[None, :]
    pair_rows = jnp.where(same_group[:, None, :, None], pair_rows[:, :, None, :], 0.0)
    pair_rows = pair_rows.reshape(devices, devices) * (pref_beta / RESP)
    chosen_sign = jnp.sum(chosen_mask - rejected_mask, axis=1).reshape(devices, 1)
    table_b = table_master.astype(jnp.bfloat16)
    head_gains = low_copy(norm_gains)
    cosine, sine = rope_tables(SEQ, HD // 2)

    def fetched(wanted, row_keys):
        rows = jnp.dot(
            onehot_rows(wanted, block_rows), table_b, preferred_element_type=jnp.float32
        ).astype(jnp.bfloat16)
        return jnp.dot(
            onehot_rows(row_keys, wanted.shape[0]),
            exchanged(rows),
            preferred_element_type=jnp.float32,
        )

    def later_round(turn):
        count = devices * LATER_SLOTS
        later_keys = round_keys(owner, slot, SLOTS + turn * LATER_SLOTS, LATER_SLOTS)
        return later_keys, exchanged(round_asks(later_keys, first_seen, local_ids, count))

    def fetch_more(turn, rows):
        later_keys, later_asked = later_round(turn)
        return rows + fetched(later_asked, later_keys)

    hidden0 = lax.fori_loop(0, later_turns, fetch_more, fetched(asked, keys))
    act1 = rms_scale(hidden0, gains[0]).astype(jnp.bfloat16)
    entry, leave, conv_in = (dense(act1, square_b[place]) for place in range(3))
    product = entry * conv_in
    convolved = gains[4] * product + gains[5] * delayed(product, 1) + gains[6] * delayed(product, 2)
    mixer = (leave * convolved).astype(jnp.bfloat16)
    hidden1 = hidden0 + dense(mixer, square_b[3])
    act2 = rms_scale(hidden1, gains[1]).astype(jnp.bfloat16)

    def answers(values):
        return lax.dynamic_slice_in_dim(values, start, RESP, 0)

    def placed(values):
        return lax.dynamic_update_slice_in_dim(
            jnp.zeros((SEQ, values.shape[1]), values.dtype), values, start, 0
        )

    answer_act2 = answers(act2)
    query_raw = dense(answer_act2, square_b[4]).reshape(RESP, HEADS, HD)
    pair_raw = dense(act2, square_b[5])
    key_raw = pair_raw[:, : KV * HD].reshape(SEQ, KV, HD)
    value_b = pair_raw[:, KV * HD :].astype(jnp.bfloat16).reshape(SEQ, KV, HD)

    answer_cosine, answer_sine = answers(cosine), answers(sine)

    def query_prep(raw, gain):
        return rotate(rms_scale(raw, gain), answer_cosine, answer_sine)

    def key_prep(raw, gain):
        return rotate(rms_scale(raw, gain), cosine, sine)

    query_b = (
        query_prep(query_raw, head_gains[0]).astype(jnp.bfloat16).reshape(RESP, KV, groups_per, HD)
    )
    key_b = key_prep(key_raw, head_gains[1]).astype(jnp.bfloat16)
    causal = start + jnp.arange(RESP)[:, None] >= jnp.arange(SEQ)[None, :]
    scores = (
        jnp.einsum("sgrd,tgd->grst", query_b, key_b, preferred_element_type=jnp.float32) * scale
    )
    scores = jnp.where(causal, scores, masked_score)
    peak = jnp.max(scores, axis=-1, keepdims=True)
    expo = jnp.exp(scores - peak)
    total = jnp.sum(expo, axis=-1, keepdims=True)
    log_norm = peak + jnp.log(total)
    probs_b = (expo / total).astype(jnp.bfloat16)
    attended = jnp.einsum(
        "grst,tgd->sgrd", probs_b, value_b, preferred_element_type=jnp.float32
    ).reshape(RESP, D)
    attended_b = attended.astype(jnp.bfloat16)
    hidden2 = answers(hidden1) + dense(attended_b, square_b[6])
    act3 = member_gather(rms_scale(hidden2, gains[2]).astype(jnp.bfloat16))
    gate_part, up_part = dense(act3, wide_b[0]), dense(act3, wide_b[1])
    inner_b = (jax.nn.silu(gate_part) * up_part).astype(jnp.bfloat16)
    ffn_part = jnp.dot(inner_b, wide_b[2], preferred_element_type=jnp.float32)
    hidden3 = hidden2 + member_return(ffn_part.astype(jnp.bfloat16).reshape(members, RESP, D))
    final_b = rms_scale(hidden3, gains[3]).astype(jnp.bfloat16)
    squares, square_rows = square_master.shape[0], square_master.shape[1]
    wides, wide_rows = wide_master.shape[0], wide_master.shape[1]
    per_member = -(-squares // members)
    group_rows = members * square_rows

    def by_member(values):
        values = jnp.pad(values, ((0, per_member * members - squares), (0, 0), (0, 0)))
        return values.reshape(per_member, members, -1, D).transpose(1, 0, 2, 3)

    def wide_by_member(values):
        return jnp.pad(values, ((0, members - wides), (0, 0), (0, 0)))

    half_tokens = [
        jnp.concatenate(gathered(piece, "chip"), axis=0) for piece in gathered(final_b, "vocab")
    ]
    response_tokens = jnp.concatenate(
        half_tokens + [other_core(piece) for piece in half_tokens], axis=0
    )
    chips = groups // 2
    chip = lax.axis_index("chip")
    block_core = jnp.stack([core, 1 - core])[:, None, None]
    block_member = ((member - jnp.arange(members)) % members)[None, :, None]
    block_chip = ((chip - jnp.arange(chips)) % chips)[None, None, :]
    block_device = ((block_chip * 2 + block_core) * members + block_member).reshape(-1)
    device_block = jnp.sum(
        jnp.where(
            block_device[None, :] == jnp.arange(devices)[:, None], jnp.arange(devices)[None, :], 0
        ),
        axis=1,
    )
    wide_moment_blocks, response_tokens = lax.optimization_barrier(
        (wide_by_member(wide_moment.astype(jnp.bfloat16)), response_tokens)
    )
    wide_moment_job = handed_out(wide_moment_blocks, "vocab")
    local_target = jnp.where(targets // block_rows == device, targets % block_rows, -1)
    local_target = local_target.reshape(devices, RESP)[block_device].reshape(1, -1)
    shares, own_stats = answer_shares(local_target, response_tokens, table_b)
    own_stats, wide_moment_job = lax.optimization_barrier((own_stats, wide_moment_job))
    wide_moment_job = jnp.stack(wide_moment_job)
    stats = own_stats[:3].reshape(3, devices, RESP).transpose(1, 0, 2)[device_block]
    stats = exchanged(stats)
    top = jnp.max(stats[:, 0], axis=0)
    exp_total = jnp.sum(stats[:, 1] * jnp.exp(stats[:, 0] - top[None, :]), axis=0)
    own_log_total = top + jnp.log(exp_total)
    own_logp = jnp.sum(jnp.sum(stats[:, 2], axis=0) - own_log_total)
    joined = spread(jnp.concatenate([own_log_total, own_logp[None]]))
    log_total = joined[:, :RESP][block_device].reshape(1, -1)
    margin = jnp.sum(pair_rows * joined[:, RESP][None, :], axis=1, keepdims=True)
    pair_loss = 0.5 * jnp.sum(jax.nn.softplus(-margin))
    grad_logp = chosen_sign * jax.nn.sigmoid(-margin) * (-pref_beta / RESP)
    row_weight = jnp.broadcast_to(grad_logp[block_device], (devices, RESP)).reshape(1, -1)
    share_scale = -row_weight * jnp.exp(own_stats[0:1] - log_total)
    target_value = row_weight * (1.0 - jnp.exp(own_stats[2:3] - log_total))
    given, kept = (
        answer_grads(
            half, local_target, share_scale, target_value, shares, table_b, members * RESP
        )
        for half in (1, 0)
    )
    grad_answer_pair = (kept.astype(jnp.float32) + other_core(given).astype(jnp.float32)).astype(
        jnp.bfloat16
    )
    grad_answer_pair, square_moment_blocks = lax.optimization_barrier(
        (grad_answer_pair, by_member(square_moment.astype(jnp.bfloat16)))
    )
    square_moment_job = handed_out(square_moment_blocks, "vocab")
    grad_answer_pair = grad_answer_pair.reshape(members, chips, RESP, D)
    grad_answer_group = added(
        handed_back([grad_answer_pair[:, place] for place in range(chips)], "chip")
    )
    grad_table = jnp.dot(
        logit_grads(
            jnp.arange(block_rows)[:, None], local_target, share_scale, target_value, shares
        ),
        response_tokens,
        preferred_element_type=jnp.float32,
    )
    grad_answer_group, grad_table, square_moment_job = lax.optimization_barrier(
        (grad_answer_group.astype(jnp.bfloat16), grad_table, square_moment_job)
    )
    square_moment_job = placed_before(square_moment_job, "vocab")
    square_moment_job = square_moment_job.transpose(1, 0, 2, 3).reshape(per_member, group_rows, D)
    grad_final = member_return(list(grad_answer_group))
    grad_hidden3, grad_gain3 = norm_back(hidden3, gains[3], grad_final)
    grad_ffn_out = member_gather(grad_hidden3.astype(jnp.bfloat16))
    grad_inner = dense(grad_ffn_out, wide_b[2])
    grad_down_w = outer(inner_b, grad_ffn_out)
    _, silu_pull = jax.vjp(lambda gate_in, up_in: jax.nn.silu(gate_in) * up_in, gate_part, up_part)
    grad_gate, grad_up = silu_pull(grad_inner)
    grad_gate_b, grad_up_b = grad_gate.astype(jnp.bfloat16), grad_up.astype(jnp.bfloat16)
    grad_act3_part = back_dense(grad_gate_b, wide_b[0]) + back_dense(grad_up_b, wide_b[1])
    grad_act3 = member_return(grad_act3_part.astype(jnp.bfloat16).reshape(members, RESP, D))
    grad_gate_w, grad_up_w = outer(grad_gate_b, act3), outer(grad_up_b, act3)
    grad_norm2, grad_gain2 = norm_back(hidden2, gains[2], grad_act3)
    grad_hidden2 = grad_hidden3 + grad_norm2
    grad_attn_out = grad_hidden2.astype(jnp.bfloat16)
    grad_attended = (
        back_dense(grad_attn_out, square_b[6])
        .astype(jnp.bfloat16)
        .reshape(RESP, KV, groups_per, HD)
    )
    grad_out_w = outer(grad_attn_out, attended_b)
    scores = (
        jnp.einsum("sgrd,tgd->grst", query_b, key_b, preferred_element_type=jnp.float32) * scale
    )
    probs = jnp.exp(jnp.where(causal, scores, masked_score) - log_norm)
    grad_probs = jnp.einsum(
        "sgrd,tgd->grst", grad_attended, value_b, preferred_element_type=jnp.float32
    )
    grad_values = jnp.einsum(
        "grst,sgrd->tgd", probs_b, grad_attended, preferred_element_type=jnp.float32
    )
    delta = jnp.sum(probs * grad_probs, axis=-1, keepdims=True)
    grad_scores = (probs * (grad_probs - delta)).astype(jnp.bfloat16)
    grad_query = (
        jnp.einsum("grst,tgd->sgrd", grad_scores, key_b, preferred_element_type=jnp.float32) * scale
    ).reshape(RESP, HEADS, HD)
    grad_keys = (
        jnp.einsum("grst,sgrd->tgd", grad_scores, query_b, preferred_element_type=jnp.float32)
        * scale
    )
    _, query_pull = jax.vjp(query_prep, query_raw, head_gains[0])
    grad_query_raw, grad_query_gain = query_pull(grad_query)
    _, key_pull = jax.vjp(key_prep, key_raw, head_gains[1])
    grad_key_raw, grad_key_gain = key_pull(grad_keys)
    grad_query_b = grad_query_raw.reshape(RESP, D).astype(jnp.bfloat16)
    grad_pair_b = jnp.concatenate(
        [grad_key_raw.reshape(SEQ, KV * HD), grad_values.reshape(SEQ, KV * HD)], axis=1
    ).astype(jnp.bfloat16)
    grad_act2 = back_dense(grad_pair_b, square_b[5]) + placed(back_dense(grad_query_b, square_b[4]))
    grad_query_w = outer(grad_query_b, answer_act2)
    grad_pair_w = outer(grad_pair_b, act2)
    grad_norm1, grad_gain1 = norm_back(hidden1, gains[1], grad_act2)
    grad_hidden1 = placed(grad_hidden2) + grad_norm1
    grad_mix_out = grad_hidden1.astype(jnp.bfloat16)
    grad_mixer = back_dense(grad_mix_out, square_b[3])
    grad_mixer_w = outer(grad_mix_out, mixer)
    grad_leave = grad_mixer * convolved
    grad_conv = grad_mixer * leave
    grad_tap0 = jnp.sum(grad_conv * product, axis=0)
    grad_tap1 = jnp.sum(grad_conv * delayed(product, 1), axis=0)
    grad_tap2 = jnp.sum(grad_conv * delayed(product, 2), axis=0)
    grad_product = (
        gains[4] * grad_conv + gains[5] * advanced(grad_conv, 1) + gains[6] * advanced(grad_conv, 2)
    )
    grad_inner = [
        part.astype(jnp.bfloat16)
        for part in (grad_product * conv_in, grad_leave, grad_product * entry)
    ]
    grad_act1 = sum(back_dense(grad_inner[place], square_b[place]) for place in range(3))
    grad_inner_w = [outer(part, act1) for part in grad_inner]
    grad_norm0, grad_gain0 = norm_back(hidden0, gains[0], grad_act1)
    grad_embed_b = (grad_hidden1 + grad_norm0).astype(jnp.bfloat16)

    grad_square = jnp.stack(
        [
            part.astype(jnp.bfloat16)
            for part in (*grad_inner_w, grad_mixer_w, grad_query_w, grad_pair_w, grad_out_w)
        ]
    )
    grad_vector = jnp.stack(
        [grad_gain0, grad_gain1, grad_gain2, grad_gain3, grad_tap0, grad_tap1, grad_tap2]
    )
    grad_head_gains = jnp.stack([grad_query_gain, grad_key_gain])
    grad_wide = jnp.stack(
        [part.astype(jnp.bfloat16) for part in (grad_gate_w, grad_up_w, grad_down_w)]
    )
    share_wide_b = lax.psum_scatter(grad_wide, DP, scatter_dimension=1, tiled=True)
    grad_square, share_wide_b = lax.optimization_barrier((grad_square, share_wide_b))
    share_wide_b, grad_embed_b = lax.optimization_barrier((share_wide_b, grad_embed_b))
    share_wide = share_wide_b.astype(jnp.float32)
    wide_grad_job = jnp.stack(handed_out(wide_by_member(share_wide_b), "vocab"))
    group_square = lax.psum_scatter(grad_square, DP, scatter_dimension=1, tiled=True)
    square_grad_job = member_scatter(by_member(group_square))

    def from_members(values):
        values = values.reshape(per_member, members, square_rows, D).transpose(1, 0, 2, 3)
        values = placed_before(handed_out(values.astype(jnp.bfloat16), "vocab"), "vocab")
        values = values.transpose(1, 0, 2, 3).reshape(per_member * members, square_rows, D)
        return values[:squares].astype(jnp.float32)

    share_square = from_members(square_grad_job)

    def returned(row_keys, count):
        rows = outer(onehot_rows(row_keys, count), grad_embed_b)
        return exchanged(rows.astype(jnp.bfloat16))

    def put(wanted, rows):
        return outer(onehot_rows(wanted, block_rows), rows)

    def return_more(turn, total):
        later_keys, later_asked = later_round(turn)
        return total + put(later_asked, returned(later_keys, later_asked.shape[0]))

    returned_rows, wide_grad_job = lax.optimization_barrier(
        (returned(keys, devices * SLOTS), wide_grad_job)
    )
    share_table = lax.fori_loop(
        0, later_turns, return_more, grad_table + put(asked, returned_rows))
    width = vector_master.shape[1]
    vector_notes = grad_vector.reshape(-1, devices, width).transpose(1, 0, 2).reshape(devices, -1)
    vector_notes = jnp.concatenate(
        [
            vector_notes,
            jnp.broadcast_to(grad_head_gains.reshape(1, -1), (devices, grad_head_gains.size)),
        ],
        axis=1,
    )
    vector_notes = jnp.sum(exchanged(vector_notes), axis=0)
    share_vector = vector_notes[: vector_master.size].reshape(vector_master.shape)
    gains_total = vector_notes[vector_master.size :].reshape(grad_head_gains.shape)

    def job_sums(values):
        sums = jnp.sum(values, axis=(1, 2))[:, None]
        sums = jnp.where(jnp.arange(members)[None, :] == member, sums, 0.0)
        return sums.reshape(-1)[:squares]

    moment_squares = jnp.concatenate(
        [
            jnp.sum(square_moment * square_moment, axis=(1, 2)),
            jnp.sum(wide_moment * wide_moment, axis=(1, 2)),
        ]
    )
    moment_cross = jnp.concatenate(
        [
            job_sums(square_moment_job.astype(jnp.float32) * square_grad_job),
            jnp.sum(wide_moment * share_wide, axis=(1, 2)),
        ]
    )
    grad_squares = jnp.concatenate(
        [
            job_sums(square_grad_job * square_grad_job),
            jnp.sum(share_wide * share_wide, axis=(1, 2)),
        ]
    )
    moment_stats = jnp.stack([moment_squares, moment_cross, grad_squares])
    own_squares = (
        jnp.sum(grad_squares)
        + jnp.sum(share_vector * share_vector)
        + jnp.sum(share_table * share_table)
    )
    sums = jnp.concatenate([moment_stats.reshape(-1), own_squares[None]])
    sums = jnp.sum(spread(sums), axis=0)
    stats_total = sums[:-1].reshape(moment_stats.shape)
    grad_norm = jnp.sqrt(sums[-1] + jnp.sum(gains_total * gains_total))
    factor = jnp.minimum(1.0, clip_limit / grad_norm)
    square_moment_new = muon_decay * square_moment + (1.0 - muon_decay) * (factor * share_square)
    wide_moment_new = muon_decay * wide_moment + (1.0 - muon_decay) * (factor * share_wide)
    moment_norm = jnp.sqrt(
        muon_decay * muon_decay * stats_total[0]
        + 2.0 * muon_decay * (1.0 - muon_decay) * factor * stats_total[1]
        + (1.0 - muon_decay) * (1.0 - muon_decay) * factor * factor * stats_total[2]
    )
    ortho_square = square_moment_new / (moment_norm[:7][:, None, None] + ortho_epsilon)
    ortho_wide = wide_moment_new / (moment_norm[7:][:, None, None] + ortho_epsilon)
    wide_inverse = 1.0 / (moment_norm[squares:] + ortho_epsilon)
    wide_inverse = jnp.pad(wide_inverse, (0, members - wides))[member]
    square_inverse = 1.0 / (moment_norm[:squares] + ortho_epsilon)
    square_inverse = jnp.pad(square_inverse, (0, per_member * members - squares))
    square_inverse = square_inverse.reshape(per_member, members)[:, member][:, None, None]
    square_part = (muon_decay * square_inverse) * square_moment_job.astype(jnp.float32) + (
        (1.0 - muon_decay) * factor * square_inverse
    ) * square_grad_job
    square_part, wide_grad_job = lax.optimization_barrier(
        (square_part.astype(jnp.bfloat16), wide_grad_job)
    )
    square_part = jnp.pad(square_part, ((0, groups // 2 - per_member), (0, 0), (0, 0)))
    square_half = jnp.concatenate(handed_out(square_part, "chip"), axis=0)
    square_job = jnp.concatenate([square_half, other_core(square_half)], axis=0)
    wide_job = (
        (muon_decay * wide_inverse) * wide_moment_job.astype(jnp.float32)
        + ((1.0 - muon_decay) * factor * wide_inverse) * wide_grad_job.astype(jnp.float32)
    )
    wide_job = wide_job.reshape(members * wide_rows, D).astype(jnp.bfloat16)
    wide_first, wide_second = group_sum(outer(wide_job, wide_job).astype(jnp.bfloat16), core)
    square_gram = outer(square_job, square_job)
    rest_b = ortho_rest(core, wide_first, wide_second, square_gram)
    power = leading_coefficient**NS_ITERS
    wide_rest = jnp.where(core == 0, rest_b, other_core(rest_b))
    half_rows = square_half.shape[0]
    given = square_product(square_job[half_rows:], rest_b).astype(jnp.bfloat16)
    kept = square_product(square_half, rest_b).astype(jnp.bfloat16)
    back_square = jnp.where(core == 0, other_core(given), kept)
    back_wide = square_product(wide_job, wide_rest).astype(jnp.bfloat16)
    back_square, back_wide = lax.optimization_barrier((back_square, back_wide))
    back_square = handed_back(list(back_square.reshape(-1, group_rows, D)), "chip")
    share_table, back_square = lax.optimization_barrier((share_table, back_square))
    table_step, table_first_new, table_second_new = adam_step(
        table_master, table_first, table_second, share_table, factor, adam_count
    )
    back_square = placed_after(back_square, "chip")[:per_member]
    back_square = from_members(back_square)
    back_wide = handed_back(list(back_wide.reshape(members, wide_rows, D)), "vocab")
    back_wide = placed_after(back_wide, "vocab")[:wides]
    ortho_wide = power * ortho_wide + back_wide.astype(jnp.float32)
    ortho_square = power * ortho_square + back_square
    wide_scale = jnp.array([math.sqrt(FF / D), math.sqrt(FF / D), 1.0], jnp.float32)
    square_new = square_master - muon_rate * ortho_square
    wide_new = wide_master - muon_rate * wide_scale[:, None, None] * ortho_wide
    vector_step, vector_first_new, vector_second_new = adam_step(
        vector_master, vector_first, vector_second, share_vector, factor, adam_count
    )
    norm_step, norm_first_new, norm_second_new = adam_step(
        norm_gains, norm_first, norm_second, gains_total, factor, adam_count
    )
    return (
        pair_loss,
        grad_norm,
        square_new,
        square_moment_new,
        square_new.astype(jnp.bfloat16),
        wide_new,
        wide_moment_new,
        wide_new.astype(jnp.bfloat16),
        table_step,
        table_first_new,
        table_second_new,
        vector_step,
        vector_first_new,
        vector_second_new,
        norm_step,
        norm_first_new,
        norm_second_new,
        share_vector[3],
    )


def solution(mesh):
    groups, members = mesh.shape["dp"], mesh.shape["vocab"]
    cores = 2
    split_mesh = Mesh(mesh.devices.reshape(groups // cores, cores, members), ALL)
    return jax.shard_map(
        body,
        mesh=split_mesh,
        in_specs=(
            P(DP, None),
            P(DP, None),
            P(DP, None),
            P(ALL, None),
            P(ALL, None),
            P(ALL, None),
            P(None, ALL, None),
            P(None, ALL, None),
            P(None, ALL, None),
            P(None, ALL, None),
            P(None, ALL),
            P(None, ALL),
            P(None, ALL),
            P(),
            P(),
            P(),
            P(),
        ),
        out_specs=(
            P(),
            P(),
            P(None, ALL, None),
            P(None, ALL, None),
            P(None, ALL, None),
            P(None, ALL, None),
            P(None, ALL, None),
            P(None, ALL, None),
            P(ALL, None),
            P(ALL, None),
            P(ALL, None),
            P(None, ALL),
            P(None, ALL),
            P(None, ALL),
            P(),
            P(),
            P(),
            P(ALL),
        ),
        check_vma=False,
    )
```

```python
import math

import jax
import jax.numpy as jnp
from jax import lax
from jax.experimental import pallas as pl
from jax.experimental.pallas import tpu as pltpu
from jax.sharding import Mesh
from jax.sharding import PartitionSpec as P

D = 1024
HEADS = 16
KV = 8
HD = 64
FF = 4608
SEQ = 512
RESP = 96
NS_ITERS = 3


norm_epsilon = 1e-05
rope_base = 1000000.0
pref_beta = 2.0
clip_limit = 0.05
muon_decay = 0.95
muon_rate = 0.5
first_decay = 0.9
second_decay = 0.95
adam_rate = 0.02
adam_epsilon = 1e-08
weight_decay = 0.1
leading_coefficient = 3.4445
coef_second = -4.775
coef_third = 2.0315
ortho_epsilon = 1e-07
masked_score = -1e30


def rms_scale(inputs, gain):
    mean_square = jnp.mean(inputs * inputs, axis=-1, keepdims=True)
    return inputs * lax.rsqrt(mean_square + norm_epsilon) * gain


def rope_tables(length, half):
    position = jnp.arange(length, dtype=jnp.float32)
    inverse = rope_base ** (-jnp.arange(half, dtype=jnp.float32) / half)
    angle = position[:, None] * inverse[None, :]
    return (jnp.cos(angle)[:, None, :], jnp.sin(angle)[:, None, :])


def rotate(inputs, cosine, sine):
    half = inputs.shape[-1] // 2
    first = inputs[..., :half]
    second = inputs[..., half:]
    return jnp.concatenate(
        [first * cosine - second * sine, second * cosine + first * sine], axis=-1
    )


def dense(inputs, weight):
    return lax.dot_general(
        inputs, weight, (((1,), (1,)), ((), ())), preferred_element_type=jnp.float32
    )


def outer(grads, inputs):
    return lax.dot_general(
        grads, inputs, (((0,), (0,)), ((), ())), preferred_element_type=jnp.float32
    )


def back_dense(grads, weight):
    return jnp.dot(grads, weight, preferred_element_type=jnp.float32)


def delayed(values, offset):
    return jnp.pad(values, ((offset, 0), (0, 0)))[: values.shape[0]]


def advanced(values, offset):
    return jnp.pad(values, ((0, offset), (0, 0)))[offset:]


def norm_back(inputs, gain, grad_out):
    _, pullback = jax.vjp(rms_scale, inputs, gain)
    return pullback(grad_out)


def low_copy(values):
    return lax.optimization_barrier(values.astype(jnp.bfloat16)).astype(jnp.float32)


def adam_step(master, first, second, grad, factor, count):
    scaled = factor * grad
    first_new = first_decay * first + (1.0 - first_decay) * scaled
    second_new = second_decay * second + (1.0 - second_decay) * scaled * scaled
    steps = count.astype(jnp.float32)
    first_hat = first_new / (1.0 - first_decay**steps)
    second_hat = second_new / (1.0 - second_decay**steps)
    change = -adam_rate * (
        first_hat / (jnp.sqrt(second_hat) + adam_epsilon) + weight_decay * master
    )
    return (change, first_new, second_new)

DP = ("chip", "core")
ALL = ("chip", "core", "vocab")
SLOTS = 24
LATER_SLOTS = 8


def exchanged(rows):
    return lax.all_to_all(rows, ALL, 0, 0, tiled=True)


def spread(values):
    count = lax.axis_size(ALL)
    return lax.all_to_all(jnp.broadcast_to(values[None], (count,) + values.shape), ALL, 0, 0)


def turned(values, axis, step):
    count = lax.axis_size(axis)
    return lax.ppermute(values, axis, [(i, (i + step) % count) for i in range(count)])


def block_at(blocks, index):
    return lax.dynamic_index_in_dim(blocks, index % blocks.shape[0], 0, keepdims=False)


def handed_out(blocks, axis):
    place, count = lax.axis_index(axis), lax.axis_size(axis)
    return [block_at(blocks, place)] + [
        turned(block_at(blocks, place + step), axis, step) for step in range(1, count)
    ]


def handed_back(pieces, axis):
    return [pieces[0]] + [turned(pieces[step], axis, -step) for step in range(1, len(pieces))]


def gathered(values, axis):
    return [values] + [turned(values, axis, step) for step in range(1, lax.axis_size(axis))]


def placed_before(pieces, axis):
    pieces, place = jnp.stack(pieces), lax.axis_index(axis)
    return jnp.stack([block_at(pieces, place - j) for j in range(pieces.shape[0])])


def placed_after(pieces, axis):
    pieces, place = jnp.stack(pieces), lax.axis_index(axis)
    return jnp.stack([block_at(pieces, j - place) for j in range(pieces.shape[0])])


def added(pieces):
    total = pieces[0].astype(jnp.float32)
    for piece in pieces[1:]:
        total = total + piece.astype(jnp.float32)
    return total


def other_core(values):
    return lax.ppermute(values, "core", [(0, 1), (1, 0)])


def pair_sum(halves, core):
    given = lax.dynamic_index_in_dim(halves, 1 - core, 0, keepdims=False)
    kept = lax.dynamic_index_in_dim(halves, core, 0, keepdims=False)
    total = kept.astype(jnp.float32) + other_core(given).astype(jnp.float32)
    return total.astype(jnp.bfloat16)


def chip_sum(blocks):
    return added(handed_out(blocks, "chip"))


def group_sum(values, core):
    rows = values.shape[0] // 2
    chips = lax.axis_size("chip")
    half = pair_sum(values.reshape(2, rows, -1), core).reshape(chips, rows // chips, -1)
    part = chip_sum(half).astype(jnp.bfloat16)
    half = placed_before(gathered(part, "chip"), "chip").reshape(rows, -1)
    return half, other_core(half)


def member_gather(values):
    return jnp.concatenate(gathered(values, "vocab"), axis=0)


def member_return(pieces):
    return added(handed_back(pieces, "vocab"))


def member_scatter(blocks):
    return added(handed_out(blocks, "vocab"))


def member_scatter_halves(blocks):
    if blocks.shape[0] != 4:
        return member_scatter(blocks)
    member = lax.axis_index("vocab")
    near, half = member % 2, member // 2
    far_first = (1 - half) * 2
    neighbours = [(0, 1), (1, 0), (2, 3), (3, 2)]
    across = [(0, 2), (2, 0), (1, 3), (3, 1)]
    far = lax.ppermute(block_at(blocks, far_first + 1 - near), "vocab", neighbours)
    far = added([block_at(blocks, far_first + near), far]).astype(jnp.bfloat16)
    far = lax.ppermute(far, "vocab", across)
    close = lax.ppermute(block_at(blocks, half * 2 + 1 - near), "vocab", neighbours)
    return added([block_at(blocks, member), close, far])


def onehot_rows(index, count):
    return (index[:, None] == jnp.arange(count)[None, :]).astype(jnp.bfloat16)


def token_slots(ids, block_rows):
    owner = ids // block_rows
    place = jnp.arange(ids.shape[0])
    earlier = place[:, None] > place[None, :]
    equal = ids[:, None] == ids[None, :]
    first = jnp.logical_not(jnp.any(equal & earlier, axis=1))
    ahead = (owner[:, None] == owner[None, :]) & earlier & first[None, :]
    rank = jnp.sum(ahead.astype(jnp.int32), axis=1)
    slot = jnp.sum(jnp.where(equal & first[None, :], rank[None, :], 0), axis=1)
    return owner, first, slot


def round_keys(owner, slot, first, count):
    within = slot - first
    return jnp.where((within >= 0) & (within < count), owner * count + within, -1)


def round_asks(keys, first_seen, local, count):
    hits = (keys[None, :] == jnp.arange(count)[:, None]) & first_seen[None, :]
    return jnp.sum(jnp.where(hits, local[None, :] + 1, 0), axis=1) - 1


def square_product(left, right):
    return jnp.dot(
        left.astype(jnp.bfloat16), right.astype(jnp.bfloat16), preferred_element_type=jnp.float32
    )


def rest_kernel(
    core_ref,
    first_ref,
    second_ref,
    square_ref,
    rest_ref,
    gram_scratch,
    change_scratch,
    rest_scratch,
    grams,
    change_b,
    rest_b,
):
    lead = leading_coefficient
    size = square_ref.shape[0]
    half = size // 2
    tile = 256

    def dot(left, right):
        return jnp.dot(left, right, preferred_element_type=jnp.float32)

    on_wide = core_ref[0] == 0
    for part, wide_ref in enumerate((first_ref, second_ref)):

        @pl.loop(0, half // tile)
        def _(step):
            rows = pl.ds(pl.multiple_of(step * tile, tile), tile)
            place = pl.ds(pl.multiple_of(part * half + step * tile, tile), tile)
            gram = jnp.where(on_wide, wide_ref[rows, :].astype(jnp.float32), square_ref[place, :])
            gram_scratch[place, :] = gram
            grams[0, place, :] = gram.astype(jnp.bfloat16)

    power = 1.0
    for turn in range(NS_ITERS):
        now, later = turn % 2, (turn + 1) % 2

        @pl.loop(0, size // tile)
        def _(step):
            rows = pl.ds(pl.multiple_of(step * tile, tile), tile)
            change = coef_second * gram_scratch[rows, :] + coef_third * dot(
                grams[now, rows, :], grams[now]
            )
            change_scratch[rows, :] = change
            change_b[rows, :] = change.astype(jnp.bfloat16)

        @pl.loop(0, size // tile)
        def _(step):
            rows = pl.ds(pl.multiple_of(step * tile, tile), tile)
            if turn == 0:
                rest = change_scratch[rows, :]
            else:
                rest = (
                    lead * rest_scratch[rows, :]
                    + power * change_scratch[rows, :]
                    + dot(rest_b[rows, :], change_b[...])
                )
            if turn + 1 < NS_ITERS:
                rest_scratch[rows, :] = rest
                rest_b[rows, :] = rest.astype(jnp.bfloat16)
                mixed = dot(change_b[rows, :], grams[now])
                gram = (
                    lead * lead * gram_scratch[rows, :]
                    + 2.0 * lead * mixed
                    + dot(mixed.astype(jnp.bfloat16), change_b[...])
                )
                gram_scratch[rows, :] = gram
                grams[later, rows, :] = gram.astype(jnp.bfloat16)
            else:
                rest_ref[rows, :] = rest.astype(jnp.bfloat16)

        power = power * lead


def ortho_rest(core, first, second, square):
    size = square.shape[0]
    wide = pltpu.VMEM((size, size), jnp.float32)
    narrow = pltpu.VMEM((size, size), jnp.bfloat16)
    return pl.pallas_call(
        rest_kernel,
        out_shape=jax.ShapeDtypeStruct((size, size), jnp.bfloat16),
        in_specs=[pl.BlockSpec(memory_space=pltpu.SMEM)]
        + [pl.BlockSpec(memory_space=pltpu.VMEM)] * 3,
        out_specs=pl.BlockSpec(memory_space=pltpu.VMEM),
        scratch_shapes=[
            wide,
            wide,
            wide,
            pltpu.VMEM((2, size, size), jnp.bfloat16),
            narrow,
            narrow,
        ],
        compiler_params=pltpu.CompilerParams(vmem_limit_bytes=44 * 1024 * 1024),
        cost_estimate=pl.CostEstimate(
            flops=18 * size**3, bytes_accessed=6 * size * size, transcendentals=0
        ),
    )(core.reshape(1), first, second, square)


def logits_kernel(target_ref, answers_ref, table_ref, shares_ref, stats_ref, logits):
    rows, width = logits.shape
    piece = 256
    target = target_ref[...]
    top = jnp.full((8, width), -jnp.inf, jnp.float32)
    total = jnp.zeros((8, width), jnp.float32)
    picked = jnp.zeros((8, width), jnp.float32)
    for first in range(0, rows, piece):
        scores = lax.dot_general(
            table_ref[first : first + piece, :],
            answers_ref[...],
            (((1,), (1,)), ((), ())),
            preferred_element_type=jnp.float32,
        )
        logits[first : first + piece, :] = scores
        top = jnp.maximum(top, jnp.max(scores.reshape(-1, 8, width), axis=0))
    top = jnp.max(top, axis=0, keepdims=True)
    for first in range(0, rows, piece):
        scores = logits[first : first + piece, :]
        share = jnp.exp(scores - top)
        shares_ref[first : first + piece, :] = share.astype(jnp.bfloat16)
        total = total + jnp.sum(share.reshape(-1, 8, width), axis=0)
        place = lax.broadcasted_iota(jnp.int32, (piece, width), 0)
        hit = jnp.where(place == target - first, scores, 0.0)
        picked = picked + jnp.sum(hit.reshape(-1, 8, width), axis=0)
    stats_ref[0:1, :] = top
    stats_ref[1:2, :] = jnp.sum(total, axis=0, keepdims=True)
    stats_ref[2:3, :] = jnp.sum(picked, axis=0, keepdims=True)
    stats_ref[3:8, :] = jnp.zeros((5, width), jnp.float32)


def answer_shares(target, answers, table):
    count, rows = answers.shape[0], table.shape[0]
    tile = 256
    return pl.pallas_call(
        logits_kernel,
        grid=(count // tile,),
        in_specs=[
            pl.BlockSpec((1, tile), lambda i: (0, i)),
            pl.BlockSpec((tile, D), lambda i: (i, 0)),
            pl.BlockSpec((rows, D), lambda i: (0, 0)),
        ],
        out_specs=[
            pl.BlockSpec((rows, tile), lambda i: (0, i)),
            pl.BlockSpec((8, tile), lambda i: (0, i)),
        ],
        out_shape=[
            jax.ShapeDtypeStruct((rows, count), jnp.bfloat16),
            jax.ShapeDtypeStruct((8, count), jnp.float32),
        ],
        scratch_shapes=[pltpu.VMEM((rows, tile), jnp.float32)],
        compiler_params=pltpu.CompilerParams(vmem_limit_bytes=40 * 1024 * 1024),
        cost_estimate=pl.CostEstimate(
            flops=2 * count * rows * D,
            bytes_accessed=2 * count * (rows + D),
            transcendentals=count * rows,
        ),
    )(target, answers, table)


def logit_grads(place, target, scale, value, shares):
    return jnp.where(place == target, value, shares.astype(jnp.float32) * scale).astype(jnp.bfloat16)


def grads_kernel(target_ref, scale_ref, value_ref, shares_ref, table_ref, grads_ref):
    place = lax.broadcasted_iota(jnp.int32, shares_ref.shape, 0)
    grads = logit_grads(place, target_ref[...], scale_ref[...], value_ref[...], shares_ref[...])
    grads_ref[...] = lax.dot_general(
        grads, table_ref[...], (((0,), (0,)), ((), ())), preferred_element_type=jnp.float32
    ).astype(jnp.bfloat16)


def answer_grads(half, target, scale, value, shares, table, width):
    rows, count = shares.shape
    steps = count // (2 * width)
    first = half * steps
    row = pl.BlockSpec((1, width), lambda i: (0, first + i))
    return pl.pallas_call(
        grads_kernel,
        grid=(steps,),
        in_specs=[
            row,
            row,
            row,
            pl.BlockSpec((rows, width), lambda i: (0, first + i)),
            pl.BlockSpec((rows, D), lambda i: (0, 0)),
        ],
        out_specs=pl.BlockSpec((width, D), lambda i: (i, 0)),
        out_shape=jax.ShapeDtypeStruct((steps * width, D), jnp.bfloat16),
        compiler_params=pltpu.CompilerParams(vmem_limit_bytes=40 * 1024 * 1024),
        cost_estimate=pl.CostEstimate(
            flops=2 * steps * width * rows * D,
            bytes_accessed=2 * steps * width * (rows + D),
            transcendentals=0,
        ),
    )(target, scale, value, shares, table)


def body(
    token_ids,
    seq_lengths,
    pair_order,
    table_master,
    table_first,
    table_second,
    square_master,
    square_moment,
    wide_master,
    wide_moment,
    vector_master,
    vector_first,
    vector_second,
    norm_gains,
    norm_first,
    norm_second,
    adam_count,
):
    members = lax.axis_size("vocab")
    member = lax.axis_index("vocab")
    block_rows = table_master.shape[0]
    lengths = seq_lengths[0]
    order = pair_order[0]
    groups_per = HEADS // KV
    scale = HD ** (-0.5)

    core = lax.axis_index("core")
    devices = lax.axis_size(ALL)
    device = lax.axis_index(ALL)
    groups = devices // members

    own_ids = lax.dynamic_index_in_dim(token_ids, member, 0, keepdims=False)
    own_length = lengths[member]
    start = own_length - 1 - RESP
    owner, first_seen, slot = token_slots(own_ids, block_rows)
    local_ids = own_ids % block_rows
    keys = round_keys(owner, slot, 0, SLOTS)
    asks = round_asks(keys, first_seen, local_ids, devices * SLOTS)
    own_targets = lax.dynamic_slice_in_dim(own_ids, start + 1, RESP, 0)
    vector_low = vector_master.astype(jnp.bfloat16).astype(jnp.float32)
    shared_notes = jnp.concatenate(
        [
            vector_low.reshape(-1),
            jnp.concatenate([own_targets, order, jnp.max(slot)[None] + 1]).astype(jnp.float32),
        ]
    )
    notes = jnp.concatenate(
        [
            asks.reshape(devices, SLOTS).astype(jnp.float32),
            jnp.broadcast_to(shared_notes[None, :], (devices, shared_notes.size)),
        ],
        axis=1,
    )
    notes = exchanged(notes)
    square_b = lax.all_gather(square_master.astype(jnp.bfloat16), ALL, axis=1, tiled=True)
    wide_b = lax.all_gather(wide_master.astype(jnp.bfloat16), DP, axis=1, tiled=True)
    hidden_units = wide_b.shape[1]
    asked = notes[:, :SLOTS].astype(jnp.int32).reshape(-1)
    gains = (
        notes[:, SLOTS : SLOTS + vector_low.size]
        .reshape(devices, vector_low.shape[0], vector_low.shape[1])
        .transpose(1, 0, 2)
        .reshape(vector_low.shape[0], D)
    )
    numbers = notes[:, SLOTS + vector_low.size :].astype(jnp.int32)
    targets = numbers[:, :RESP].reshape(-1)
    orders = numbers[:, RESP : RESP + members].reshape(groups, members, members)[:, 0]
    later = jnp.maximum(jnp.max(numbers[:, RESP + members]) - SLOTS, 0)
    later_turns = (later + LATER_SLOTS - 1) // LATER_SLOTS
    slots = jnp.arange(members)
    chosen_mask = (orders[:, 0::2, None] == slots[None, None, :]).astype(jnp.float32)
    rejected_mask = (orders[:, 1::2, None] == slots[None, None, :]).astype(jnp.float32)
    pair_rows = jnp.sum(
        (chosen_mask + rejected_mask)[:, :, :, None] * (chosen_mask - rejected_mask)[:, :, None, :],
        axis=1,
    )
    same_group = jnp.arange(groups)[:, None] == jnp.arange(groups)[None, :]
    pair_rows = jnp.where(same_group[:, None, :, None], pair_rows[:, :, None, :], 0.0)
    pair_rows = pair_rows.reshape(devices, devices) * (pref_beta / RESP)
    chosen_sign = jnp.sum(chosen_mask - rejected_mask, axis=1).reshape(devices, 1)
    table_b = table_master.astype(jnp.bfloat16)
    head_gains = low_copy(norm_gains)
    cosine, sine = rope_tables(SEQ, HD // 2)

    def fetched(wanted, row_keys):
        rows = jnp.dot(
            onehot_rows(wanted, block_rows), table_b, preferred_element_type=jnp.float32
        ).astype(jnp.bfloat16)
        return jnp.dot(
            onehot_rows(row_keys, wanted.shape[0]),
            exchanged(rows),
            preferred_element_type=jnp.float32,
        )

    def later_round(turn):
        count = devices * LATER_SLOTS
        later_keys = round_keys(owner, slot, SLOTS + turn * LATER_SLOTS, LATER_SLOTS)
        return later_keys, exchanged(round_asks(later_keys, first_seen, local_ids, count))

    def fetch_more(turn, rows):
        later_keys, later_asked = later_round(turn)
        return rows + fetched(later_asked, later_keys)

    hidden0 = lax.fori_loop(0, later_turns, fetch_more, fetched(asked, keys))
    act1 = rms_scale(hidden0, gains[0]).astype(jnp.bfloat16)
    entry, leave, conv_in = (dense(act1, square_b[place]) for place in range(3))
    product = entry * conv_in
    convolved = gains[4] * product + gains[5] * delayed(product, 1) + gains[6] * delayed(product, 2)
    mixer = (leave * convolved).astype(jnp.bfloat16)
    hidden1 = hidden0 + dense(mixer, square_b[3])
    act2 = rms_scale(hidden1, gains[1]).astype(jnp.bfloat16)

    def answers(values):
        return lax.dynamic_slice_in_dim(values, start, RESP, 0)

    def placed(values):
        return lax.dynamic_update_slice_in_dim(
            jnp.zeros((SEQ, values.shape[1]), values.dtype), values, start, 0
        )

    answer_act2 = answers(act2)
    query_raw = dense(answer_act2, square_b[4]).reshape(RESP, HEADS, HD)
    pair_raw = dense(act2, square_b[5])
    key_raw = pair_raw[:, : KV * HD].reshape(SEQ, KV, HD)
    value_b = pair_raw[:, KV * HD :].astype(jnp.bfloat16).reshape(SEQ, KV, HD)

    answer_cosine, answer_sine = answers(cosine), answers(sine)

    def query_prep(raw, gain):
        return rotate(rms_scale(raw, gain), answer_cosine, answer_sine)

    def key_prep(raw, gain):
        return rotate(rms_scale(raw, gain), cosine, sine)

    query_b = (
        query_prep(query_raw, head_gains[0]).astype(jnp.bfloat16).reshape(RESP, KV, groups_per, HD)
    )
    key_b = key_prep(key_raw, head_gains[1]).astype(jnp.bfloat16)
    causal = start + jnp.arange(RESP)[:, None] >= jnp.arange(SEQ)[None, :]
    scores = (
        jnp.einsum("sgrd,tgd->grst", query_b, key_b, preferred_element_type=jnp.float32) * scale
    )
    scores = jnp.where(causal, scores, masked_score)
    peak = jnp.max(scores, axis=-1, keepdims=True)
    expo = jnp.exp(scores - peak)
    total = jnp.sum(expo, axis=-1, keepdims=True)
    log_norm = peak + jnp.log(total)
    probs_b = (expo / total).astype(jnp.bfloat16)
    attended = jnp.einsum(
        "grst,tgd->sgrd", probs_b, value_b, preferred_element_type=jnp.float32
    ).reshape(RESP, D)
    attended_b = attended.astype(jnp.bfloat16)
    hidden2 = answers(hidden1) + dense(attended_b, square_b[6])
    act3 = member_gather(rms_scale(hidden2, gains[2]).astype(jnp.bfloat16))
    gate_part, up_part = dense(act3, wide_b[0]), dense(act3, wide_b[1])
    inner_b = (jax.nn.silu(gate_part) * up_part).astype(jnp.bfloat16)
    ffn_part = jnp.dot(inner_b, wide_b[2], preferred_element_type=jnp.float32)
    hidden3 = hidden2 + member_return(ffn_part.astype(jnp.bfloat16).reshape(members, RESP, D))
    final_b = rms_scale(hidden3, gains[3]).astype(jnp.bfloat16)
    squares, square_rows = square_master.shape[0], square_master.shape[1]
    wides, wide_rows = wide_master.shape[0], wide_master.shape[1]
    per_member = -(-squares // members)
    group_rows = members * square_rows

    def by_member(values):
        values = jnp.pad(values, ((0, per_member * members - squares), (0, 0), (0, 0)))
        return values.reshape(per_member, members, -1, D).transpose(1, 0, 2, 3)

    def wide_by_member(values):
        return jnp.pad(values, ((0, members - wides), (0, 0), (0, 0)))

    half_tokens = [
        jnp.concatenate(gathered(piece, "chip"), axis=0) for piece in gathered(final_b, "vocab")
    ]
    response_tokens = jnp.concatenate(
        half_tokens + [other_core(piece) for piece in half_tokens], axis=0
    )
    chips = groups // 2
    chip = lax.axis_index("chip")
    block_core = jnp.stack([core, 1 - core])[:, None, None]
    block_member = ((member - jnp.arange(members)) % members)[None, :, None]
    block_chip = ((chip - jnp.arange(chips)) % chips)[None, None, :]
    block_device = ((block_chip * 2 + block_core) * members + block_member).reshape(-1)
    device_block = jnp.sum(
        jnp.where(
            block_device[None, :] == jnp.arange(devices)[:, None], jnp.arange(devices)[None, :], 0
        ),
        axis=1,
    )
    wide_moment_blocks, response_tokens = lax.optimization_barrier(
        (wide_by_member(wide_moment.astype(jnp.bfloat16)), response_tokens)
    )
    wide_moment_job = handed_out(wide_moment_blocks, "vocab")
    local_target = jnp.where(targets // block_rows == device, targets % block_rows, -1)
    local_target = local_target.reshape(devices, RESP)[block_device].reshape(1, -1)
    shares, own_stats = answer_shares(local_target, response_tokens, table_b)
    own_stats, wide_moment_job = lax.optimization_barrier((own_stats, wide_moment_job))
    wide_moment_job = jnp.stack(wide_moment_job)
    stats = own_stats[:3].reshape(3, devices, RESP).transpose(1, 0, 2)[device_block]
    stats = exchanged(stats)
    top = jnp.max(stats[:, 0], axis=0)
    exp_total = jnp.sum(stats[:, 1] * jnp.exp(stats[:, 0] - top[None, :]), axis=0)
    own_log_total = top + jnp.log(exp_total)
    own_logp = jnp.sum(jnp.sum(stats[:, 2], axis=0) - own_log_total)
    joined = spread(jnp.concatenate([own_log_total, own_logp[None]]))
    log_total = joined[:, :RESP][block_device].reshape(1, -1)
    margin = jnp.sum(pair_rows * joined[:, RESP][None, :], axis=1, keepdims=True)
    pair_loss = 0.5 * jnp.sum(jax.nn.softplus(-margin))
    grad_logp = chosen_sign * jax.nn.sigmoid(-margin) * (-pref_beta / RESP)
    row_weight = jnp.broadcast_to(grad_logp[block_device], (devices, RESP)).reshape(1, -1)
    share_scale = -row_weight * jnp.exp(own_stats[0:1] - log_total)
    target_value = row_weight * (1.0 - jnp.exp(own_stats[2:3] - log_total))
    given, kept = (
        answer_grads(
            half, local_target, share_scale, target_value, shares, table_b, members * RESP
        )
        for half in (1, 0)
    )
    grad_answer_pair = (kept.astype(jnp.float32) + other_core(given).astype(jnp.float32)).astype(
        jnp.bfloat16
    )
    grad_answer_pair, square_moment_blocks = lax.optimization_barrier(
        (grad_answer_pair, by_member(square_moment.astype(jnp.bfloat16)))
    )
    square_moment_job = handed_out(square_moment_blocks, "vocab")
    grad_answer_pair = grad_answer_pair.reshape(members, chips, RESP, D)
    grad_answer_group = added(
        handed_back([grad_answer_pair[:, place] for place in range(chips)], "chip")
    )
    grad_table = jnp.dot(
        logit_grads(
            jnp.arange(block_rows)[:, None], local_target, share_scale, target_value, shares
        ),
        response_tokens,
        preferred_element_type=jnp.float32,
    )
    grad_answer_group, grad_table, square_moment_job = lax.optimization_barrier(
        (grad_answer_group.astype(jnp.bfloat16), grad_table, square_moment_job)
    )
    square_moment_job = placed_before(square_moment_job, "vocab")
    square_moment_job = square_moment_job.transpose(1, 0, 2, 3).reshape(per_member, group_rows, D)
    grad_final = member_return(list(grad_answer_group))
    grad_hidden3, grad_gain3 = norm_back(hidden3, gains[3], grad_final)
    grad_ffn_out = member_gather(grad_hidden3.astype(jnp.bfloat16))
    grad_inner = dense(grad_ffn_out, wide_b[2])
    grad_down_w = outer(inner_b, grad_ffn_out)
    _, silu_pull = jax.vjp(lambda gate_in, up_in: jax.nn.silu(gate_in) * up_in, gate_part, up_part)
    grad_gate, grad_up = silu_pull(grad_inner)
    grad_gate_b, grad_up_b = grad_gate.astype(jnp.bfloat16), grad_up.astype(jnp.bfloat16)
    grad_act3_part = back_dense(grad_gate_b, wide_b[0]) + back_dense(grad_up_b, wide_b[1])
    grad_act3 = member_return(grad_act3_part.astype(jnp.bfloat16).reshape(members, RESP, D))
    grad_gate_w, grad_up_w = outer(grad_gate_b, act3), outer(grad_up_b, act3)
    grad_norm2, grad_gain2 = norm_back(hidden2, gains[2], grad_act3)
    grad_hidden2 = grad_hidden3 + grad_norm2
    grad_attn_out = grad_hidden2.astype(jnp.bfloat16)
    grad_attended = (
        back_dense(grad_attn_out, square_b[6])
        .astype(jnp.bfloat16)
        .reshape(RESP, KV, groups_per, HD)
    )
    grad_out_w = outer(grad_attn_out, attended_b)
    scores = (
        jnp.einsum("sgrd,tgd->grst", query_b, key_b, preferred_element_type=jnp.float32) * scale
    )
    probs = jnp.exp(jnp.where(causal, scores, masked_score) - log_norm)
    grad_probs = jnp.einsum(
        "sgrd,tgd->grst", grad_attended, value_b, preferred_element_type=jnp.float32
    )
    grad_values = jnp.einsum(
        "grst,sgrd->tgd", probs_b, grad_attended, preferred_element_type=jnp.float32
    )
    delta = jnp.sum(probs * grad_probs, axis=-1, keepdims=True)
    grad_scores = (probs * (grad_probs - delta)).astype(jnp.bfloat16)
    grad_query = (
        jnp.einsum("grst,tgd->sgrd", grad_scores, key_b, preferred_element_type=jnp.float32) * scale
    ).reshape(RESP, HEADS, HD)
    grad_keys = (
        jnp.einsum("grst,sgrd->tgd", grad_scores, query_b, preferred_element_type=jnp.float32)
        * scale
    )
    _, query_pull = jax.vjp(query_prep, query_raw, head_gains[0])
    grad_query_raw, grad_query_gain = query_pull(grad_query)
    _, key_pull = jax.vjp(key_prep, key_raw, head_gains[1])
    grad_key_raw, grad_key_gain = key_pull(grad_keys)
    grad_query_b = grad_query_raw.reshape(RESP, D).astype(jnp.bfloat16)
    grad_pair_b = jnp.concatenate(
        [grad_key_raw.reshape(SEQ, KV * HD), grad_values.reshape(SEQ, KV * HD)], axis=1
    ).astype(jnp.bfloat16)
    grad_act2 = back_dense(grad_pair_b, square_b[5]) + placed(back_dense(grad_query_b, square_b[4]))
    grad_query_w = outer(grad_query_b, answer_act2)
    grad_pair_w = outer(grad_pair_b, act2)
    grad_norm1, grad_gain1 = norm_back(hidden1, gains[1], grad_act2)
    grad_hidden1 = placed(grad_hidden2) + grad_norm1
    grad_mix_out = grad_hidden1.astype(jnp.bfloat16)
    grad_mixer = back_dense(grad_mix_out, square_b[3])
    grad_mixer_w = outer(grad_mix_out, mixer)
    grad_leave = grad_mixer * convolved
    grad_conv = grad_mixer * leave
    grad_tap0 = jnp.sum(grad_conv * product, axis=0)
    grad_tap1 = jnp.sum(grad_conv * delayed(product, 1), axis=0)
    grad_tap2 = jnp.sum(grad_conv * delayed(product, 2), axis=0)
    grad_product = (
        gains[4] * grad_conv + gains[5] * advanced(grad_conv, 1) + gains[6] * advanced(grad_conv, 2)
    )
    grad_inner = [
        part.astype(jnp.bfloat16)
        for part in (grad_product * conv_in, grad_leave, grad_product * entry)
    ]
    grad_act1 = sum(back_dense(grad_inner[place], square_b[place]) for place in range(3))
    grad_inner_w = [outer(part, act1) for part in grad_inner]
    grad_norm0, grad_gain0 = norm_back(hidden0, gains[0], grad_act1)
    grad_embed_b = (grad_hidden1 + grad_norm0).astype(jnp.bfloat16)

    grad_square = jnp.stack(
        [
            part.astype(jnp.bfloat16)
            for part in (*grad_inner_w, grad_mixer_w, grad_query_w, grad_pair_w, grad_out_w)
        ]
    )
    grad_vector = jnp.stack(
        [grad_gain0, grad_gain1, grad_gain2, grad_gain3, grad_tap0, grad_tap1, grad_tap2]
    )
    grad_head_gains = jnp.stack([grad_query_gain, grad_key_gain])
    grad_wide = jnp.stack(
        [part.astype(jnp.bfloat16) for part in (grad_gate_w, grad_up_w, grad_down_w)]
    )
    share_wide_b = lax.psum_scatter(grad_wide, DP, scatter_dimension=1, tiled=True)
    grad_square, share_wide_b = lax.optimization_barrier((grad_square, share_wide_b))
    share_wide_b, grad_embed_b = lax.optimization_barrier((share_wide_b, grad_embed_b))
    share_wide = share_wide_b.astype(jnp.float32)
    wide_grad_job = jnp.stack(handed_out(wide_by_member(share_wide_b), "vocab"))
    group_square = lax.psum_scatter(grad_square, DP, scatter_dimension=1, tiled=True)

    def from_members(values):
        values = values.reshape(per_member, members, square_rows, D).transpose(1, 0, 2, 3)
        values = placed_before(handed_out(values.astype(jnp.bfloat16), "vocab"), "vocab")
        values = values.transpose(1, 0, 2, 3).reshape(per_member * members, square_rows, D)
        return values[:squares].astype(jnp.float32)


    def returned(row_keys, count):
        rows = outer(onehot_rows(row_keys, count), grad_embed_b)
        return exchanged(rows.astype(jnp.bfloat16))

    def put(wanted, rows):
        return outer(onehot_rows(wanted, block_rows), rows)

    def return_more(turn, total):
        later_keys, later_asked = later_round(turn)
        return total + put(later_asked, returned(later_keys, later_asked.shape[0]))

    returned_rows, wide_grad_job = lax.optimization_barrier(
        (returned(keys, devices * SLOTS), wide_grad_job)
    )
    share_table = lax.fori_loop(
        0, later_turns, return_more, grad_table + put(asked, returned_rows))
    width = vector_master.shape[1]
    vector_notes = grad_vector.reshape(-1, devices, width).transpose(1, 0, 2).reshape(devices, -1)
    vector_notes = jnp.concatenate(
        [
            vector_notes,
            jnp.broadcast_to(grad_head_gains.reshape(1, -1), (devices, grad_head_gains.size)),
        ],
        axis=1,
    )
    group_square, share_table = lax.optimization_barrier((group_square, share_table))
    square_grad_job = member_scatter_halves(by_member(group_square))
    share_square = from_members(square_grad_job)
    vector_notes = jnp.sum(exchanged(vector_notes), axis=0)
    share_vector = vector_notes[: vector_master.size].reshape(vector_master.shape)
    gains_total = vector_notes[vector_master.size :].reshape(grad_head_gains.shape)

    def job_sums(values):
        sums = jnp.sum(values, axis=(1, 2))[:, None]
        sums = jnp.where(jnp.arange(members)[None, :] == member, sums, 0.0)
        return sums.reshape(-1)[:squares]

    moment_squares = jnp.concatenate(
        [
            jnp.sum(square_moment * square_moment, axis=(1, 2)),
            jnp.sum(wide_moment * wide_moment, axis=(1, 2)),
        ]
    )
    moment_cross = jnp.concatenate(
        [
            job_sums(square_moment_job.astype(jnp.float32) * square_grad_job),
            jnp.sum(wide_moment * share_wide, axis=(1, 2)),
        ]
    )
    grad_squares = jnp.concatenate(
        [
            job_sums(square_grad_job * square_grad_job),
            jnp.sum(share_wide * share_wide, axis=(1, 2)),
        ]
    )
    moment_stats = jnp.stack([moment_squares, moment_cross, grad_squares])
    own_squares = (
        jnp.sum(grad_squares)
        + jnp.sum(share_vector * share_vector)
        + jnp.sum(share_table * share_table)
    )
    sums = jnp.concatenate([moment_stats.reshape(-1), own_squares[None]])
    sums = jnp.sum(spread(sums), axis=0)
    stats_total = sums[:-1].reshape(moment_stats.shape)
    grad_norm = jnp.sqrt(sums[-1] + jnp.sum(gains_total * gains_total))
    factor = jnp.minimum(1.0, clip_limit / grad_norm)
    square_moment_new = muon_decay * square_moment + (1.0 - muon_decay) * (factor * share_square)
    wide_moment_new = muon_decay * wide_moment + (1.0 - muon_decay) * (factor * share_wide)
    moment_norm = jnp.sqrt(
        muon_decay * muon_decay * stats_total[0]
        + 2.0 * muon_decay * (1.0 - muon_decay) * factor * stats_total[1]
        + (1.0 - muon_decay) * (1.0 - muon_decay) * factor * factor * stats_total[2]
    )
    ortho_square = square_moment_new / (moment_norm[:7][:, None, None] + ortho_epsilon)
    ortho_wide = wide_moment_new / (moment_norm[7:][:, None, None] + ortho_epsilon)
    wide_inverse = 1.0 / (moment_norm[squares:] + ortho_epsilon)
    wide_inverse = jnp.pad(wide_inverse, (0, members - wides))[member]
    square_inverse = 1.0 / (moment_norm[:squares] + ortho_epsilon)
    square_inverse = jnp.pad(square_inverse, (0, per_member * members - squares))
    square_inverse = square_inverse.reshape(per_member, members)[:, member][:, None, None]
    square_part = (muon_decay * square_inverse) * square_moment_job.astype(jnp.float32) + (
        (1.0 - muon_decay) * factor * square_inverse
    ) * square_grad_job
    square_part, wide_grad_job = lax.optimization_barrier(
        (square_part.astype(jnp.bfloat16), wide_grad_job)
    )
    square_part = jnp.pad(square_part, ((0, groups // 2 - per_member), (0, 0), (0, 0)))
    square_half = jnp.concatenate(handed_out(square_part, "chip"), axis=0)
    square_job = jnp.concatenate([square_half, other_core(square_half)], axis=0)
    wide_job = (
        (muon_decay * wide_inverse) * wide_moment_job.astype(jnp.float32)
        + ((1.0 - muon_decay) * factor * wide_inverse) * wide_grad_job.astype(jnp.float32)
    )
    wide_job = wide_job.reshape(members * wide_rows, D).astype(jnp.bfloat16)
    wide_first, wide_second = group_sum(outer(wide_job, wide_job).astype(jnp.bfloat16), core)
    square_gram = outer(square_job, square_job)
    rest_b = ortho_rest(core, wide_first, wide_second, square_gram)
    power = leading_coefficient**NS_ITERS
    wide_rest = jnp.where(core == 0, rest_b, other_core(rest_b))
    half_rows = square_half.shape[0]
    given = square_product(square_job[half_rows:], rest_b).astype(jnp.bfloat16)
    kept = square_product(square_half, rest_b).astype(jnp.bfloat16)
    back_square = jnp.where(core == 0, other_core(given), kept)
    back_wide = square_product(wide_job, wide_rest).astype(jnp.bfloat16)
    back_square, back_wide = lax.optimization_barrier((back_square, back_wide))
    back_square = handed_back(list(back_square.reshape(-1, group_rows, D)), "chip")
    share_table, back_square = lax.optimization_barrier((share_table, back_square))
    table_step, table_first_new, table_second_new = adam_step(
        table_master, table_first, table_second, share_table, factor, adam_count
    )
    back_square = placed_after(back_square, "chip")[:per_member]
    back_square = from_members(back_square)
    back_wide = handed_back(list(back_wide.reshape(members, wide_rows, D)), "vocab")
    back_wide = placed_after(back_wide, "vocab")[:wides]
    ortho_wide = power * ortho_wide + back_wide.astype(jnp.float32)
    ortho_square = power * ortho_square + back_square
    wide_scale = jnp.array([math.sqrt(FF / D), math.sqrt(FF / D), 1.0], jnp.float32)
    square_new = square_master - muon_rate * ortho_square
    wide_new = wide_master - muon_rate * wide_scale[:, None, None] * ortho_wide
    vector_step, vector_first_new, vector_second_new = adam_step(
        vector_master, vector_first, vector_second, share_vector, factor, adam_count
    )
    norm_step, norm_first_new, norm_second_new = adam_step(
        norm_gains, norm_first, norm_second, gains_total, factor, adam_count
    )
    return (
        pair_loss,
        grad_norm,
        square_new,
        square_moment_new,
        square_new.astype(jnp.bfloat16),
        wide_new,
        wide_moment_new,
        wide_new.astype(jnp.bfloat16),
        table_step,
        table_first_new,
        table_second_new,
        vector_step,
        vector_first_new,
        vector_second_new,
        norm_step,
        norm_first_new,
        norm_second_new,
        share_vector[3],
    )


def solution(mesh):
    groups, members = mesh.shape["dp"], mesh.shape["vocab"]
    cores = 2
    split_mesh = Mesh(mesh.devices.reshape(groups // cores, cores, members), ALL)
    return jax.shard_map(
        body,
        mesh=split_mesh,
        in_specs=(
            P(DP, None),
            P(DP, None),
            P(DP, None),
            P(ALL, None),
            P(ALL, None),
            P(ALL, None),
            P(None, ALL, None),
            P(None, ALL, None),
            P(None, ALL, None),
            P(None, ALL, None),
            P(None, ALL),
            P(None, ALL),
            P(None, ALL),
            P(),
            P(),
            P(),
            P(),
        ),
        out_specs=(
            P(),
            P(),
            P(None, ALL, None),
            P(None, ALL, None),
            P(None, ALL, None),
            P(None, ALL, None),
            P(None, ALL, None),
            P(None, ALL, None),
            P(ALL, None),
            P(ALL, None),
            P(ALL, None),
            P(None, ALL),
            P(None, ALL),
            P(None, ALL),
            P(),
            P(),
            P(),
            P(ALL),
        ),
        check_vma=False,
    )
```
